32 devices in a mesh: dp: 8 (over z, x), seq: 4 (over y, core).
Axes of the slice: x: 2, y: 2, z: 4, core: 2. Of those that a mesh axis runs over, the one named last changes fastest.
Arguments:
- patches: float32 [8192, 768], P(('dp', 'seq')), may hold values from -6 to 6
- specials: float32 [64, 768], P(('dp', 'seq')), may hold values from -6 to 6
- lengths: int32 [8, 4], P('dp'), may hold values from 232 to 280, as said below
- keep_mask: int32 [8, 4, 4], P('dp'), may hold values 0 or 1
- norm1_gain: bfloat16 [2, 768], P(None, 'dp'), may hold values from 0.099609375 to 1.8984375
- norm1_bias: bfloat16 [2, 768], P(None, 'dp'), may hold values from -4 to 4
- qkv_weight: bfloat16 [2, 768, 2304], P(None, 'dp'), may hold values from -0.21875 to 0.21875
- query_bias: bfloat16 [2, 768], P(None, 'dp'), may hold values from -4 to 4
- value_bias: bfloat16 [2, 768], P(None, 'dp'), may hold values from -4 to 4
- proj_weight: bfloat16 [2, 768, 768], P(None, 'dp'), may hold values from -1.25 to 1.25
- proj_bias: bfloat16 [2, 768], P(None, 'dp'), may hold values from -4 to 4
- norm2_gain: bfloat16 [2, 768], P(None, 'dp'), may hold values from 0.099609375 to 1.8984375
- norm2_bias: bfloat16 [2, 768], P(None, 'dp'), may hold values from -4 to 4
- fc1_weight: bfloat16 [2, 768, 3072], P(None, 'dp'), may hold values from -0.21875 to 0.21875
- fc1_bias: bfloat16 [2, 3072], P(None, 'dp'), may hold values from -6 to 6
- fc2_weight: bfloat16 [2, 3072, 768], P(None, 'dp'), may hold values from -0.21875 to 0.21875
- fc2_bias: bfloat16 [2, 768], P(None, 'dp'), may hold values from -4 to 4
- cot_patches: float32 [8192, 768], P(('dp', 'seq')), may hold values from -6 to 6
- cot_specials: float32 [64, 768], P(('dp', 'seq')), may hold values from -6 to 6
Outputs:
- out_patches: float32 [8192, 768], P(('dp', 'seq'))
- out_specials: float32 [64, 768], P(('dp', 'seq'))
- grad_patches: float32 [8192, 768], P(('dp', 'seq'))
- grad_specials: float32 [64, 768], P(('dp', 'seq'))
- grad_norm1_gain: float32 [2, 768], P(None, 'dp')
- grad_norm1_bias: float32 [2, 768], P(None, 'dp')
- grad_qkv_weight: float32 [2, 768, 2304], P(None, 'dp', 'seq')
- grad_query_bias: float32 [2, 768], P(None, 'dp')
- grad_value_bias: float32 [2, 768], P(None, 'dp')
- grad_proj_weight: float32 [2, 768, 768], P(None, 'dp', 'seq')
- grad_proj_bias: float32 [2, 768], P(None, 'dp')
- grad_norm2_gain: float32 [2, 768], P(None, 'dp')
- grad_norm2_bias: float32 [2, 768], P(None, 'dp')
- grad_fc1_weight: float32 [2, 768, 3072], P(None, 'dp', 'seq')
- grad_fc1_bias: float32 [2, 3072], P(None, 'dp')
- grad_fc2_weight: float32 [2, 3072, 768], P(None, 'dp', 'seq')
- grad_fc2_bias: float32 [2, 768], P(None, 'dp')
The draws below stay inside these ranges and needn't reach their ends.
Inputs may be any that keep to these rules, and one draw needn't show every extreme that they name: `lengths`: each row holds the patch counts of the 4 images of one group in packing order; they sum to 1024, one image of each row has exactly 280 patches and one exactly 232. `keep_mask`: last index 2 l is layer l's attention branch, 2 l + 1 its feed-forward branch.
All inputs are finite; a program needn't handle non-finite values. No bound on the sum of `keep_mask` on one device may be relied on, other than what follows from the above.
Results may differ from the reference program's by a relative error of at most 0.014.
Values may be sent and summed in bfloat16 or wider, within the bound.
No kernel may reach another device: no remote copies, remote signals or barrier semaphores. Data moves between devices by JAX's collectives and lax.ppermute only.
A program may use at most 256 MiB of HBM per device.

```python
import jax
import jax.numpy as jnp
from jax import lax

D = 768
HEADS = 12
HD = 64
FF = 3072
LAYERS = 2
MEAN_LEN = 256
MOST = 280
IMGS = 4
PACK = 1024
TOKENS = 8192
SPECIALS = 64
N_DP = 8


def draw_lengths(key, part):
    key = jax.random.fold_in(key, 11)
    reach = MOST - MEAN_LEN
    half_count = IMGS // 2

    def one_row(row_key):
        offset_key, order_key = jax.random.split(row_key)
        offsets = jax.random.randint(offset_key, (half_count,), -reach, reach + 1, dtype=jnp.int32)
        offsets = jnp.where(jnp.arange(half_count, dtype=jnp.int32) == 0, reach, offsets)
        paired = jnp.stack([MEAN_LEN + offsets, MEAN_LEN - offsets], axis=1).reshape(IMGS)
        order = jax.random.permutation(order_key, IMGS)
        return paired[order]
    return jax.vmap(one_row)(jax.random.split(key, N_DP)).astype(jnp.int32)


def with_ends(values, rng, smallest, high):
    longest = values.shape.index(max(values.shape))
    spots = []
    for shift in (0, 1):
        where = [jax.random.randint(jax.random.fold_in(rng, axis), (), 0, length) for axis, length in enumerate(values.shape)]
        where[longest] = (where[longest] + shift) % values.shape[longest]
        spots.append(tuple(where))
    return values.at[spots[0]].set(smallest).at[spots[1]].set(high)


def levels(rng, shape, pieces, low, high):
    loudness = 1.0
    for position, parts in pieces:
        heights = jax.random.uniform(jax.random.fold_in(jax.random.fold_in(rng, 6), position), (parts,), jnp.float32, low / len(pieces), high / len(pieces))
        loudness = loudness * jnp.repeat(jnp.exp(heights), shape[position] // parts).reshape((-1,) + (1,) * (len(shape) - 1 - position))
    return loudness


def bell_draw(rng, shape, scale, limit, pieces=(), held_as=jnp.bfloat16):
    factor_of = levels(rng, shape, pieces, -0.22, 0.18) if pieces else 1.0
    array = jax.random.normal(rng, shape, jnp.float32) * scale * factor_of
    return jnp.minimum(jnp.maximum(array, -limit), limit).astype(held_as)


def setup_inputs(seed: int = 0) -> dict:
    streams_of = jax.random.split(jax.random.key(seed), 20)
    return {
        "patches": bell_draw(streams_of[0], (TOKENS, D), 1.0, 6.0, ((0, 32),), jnp.float32),
        "specials": bell_draw(streams_of[1], (SPECIALS, D), 1.0, 6.0, ((0, 32),), jnp.float32),
        "lengths": draw_lengths(jax.random.fold_in(streams_of[19], 71), 0),
        "keep_mask": with_ends((jax.random.randint(streams_of[3], (N_DP, IMGS, 2 * LAYERS), 0, 10) < 9).astype(jnp.int32), jax.random.fold_in(streams_of[3], 1), 0, 1),
        "norm1_gain": jnp.clip(1.0 + 0.18 * jax.random.normal(streams_of[4], (LAYERS, D), jnp.float32), 0.099609375, 1.8984375).astype(jnp.bfloat16),
        "norm1_bias": bell_draw(streams_of[5], (LAYERS, D), 0.3, 4.0, ((1, 8),)),
        "qkv_weight": bell_draw(streams_of[6], (LAYERS, D, 3 * D), D ** -0.5, 0.21875, ((1, 8),)),
        "query_bias": bell_draw(streams_of[7], (LAYERS, D), 0.3, 4.0, ((1, 8),)),
        "value_bias": bell_draw(streams_of[8], (LAYERS, D), 0.3, 4.0, ((1, 8),)),
        "proj_weight": bell_draw(streams_of[9], (LAYERS, D, D), (D // 32) ** -0.5, 1.25, ((1, 8),)),
        "proj_bias": bell_draw(streams_of[10], (LAYERS, D), 0.3, 4.0, ((1, 8),)),
        "norm2_gain": jnp.clip(1.0 + 0.18 * jax.random.normal(streams_of[11], (LAYERS, D), jnp.float32), 0.099609375, 1.8984375).astype(jnp.bfloat16),
        "norm2_bias": bell_draw(streams_of[12], (LAYERS, D), 0.3, 4.0, ((1, 8),)),
        "fc1_weight": bell_draw(streams_of[13], (LAYERS, D, FF), D ** -0.5, 0.21875, ((1, 8),)),
        "fc1_bias": bell_draw(streams_of[14], (LAYERS, FF), 0.5, 6.0, ((1, 8),)),
        "fc2_weight": bell_draw(streams_of[15], (LAYERS, FF, D), (FF // 4) ** -0.5, 0.21875, ((1, 8),)),
        "fc2_bias": bell_draw(streams_of[16], (LAYERS, D), 0.3, 4.0, ((1, 8),)),
        "cot_patches": bell_draw(streams_of[17], (TOKENS, D), 1.0, 6.0, ((0, 32),), jnp.float32),
        "cot_specials": bell_draw(streams_of[18], (SPECIALS, D), 1.0, 6.0, ((0, 32),), jnp.float32),
    }


@jax.custom_vjp
def low(v):
    return lax.optimization_barrier(v.astype(jnp.bfloat16)).astype(jnp.float32)

@jax.custom_vjp
def low_back(v):
    return v

def low_keep(v):
    return (low(v), None)

def low_pass(kept, grad):
    return (grad,)

def back_keep(v):
    return (v, None)

def back_low(kept, grad):
    return (low(grad),)
low.defvjp(low_keep, low_pass)
low_back.defvjp(back_keep, back_low)
HIGHEST_PRECISION = lax.Precision.HIGHEST
KEEP_RATE = 0.9
EPSILON = 1e-06
MASKED = -1e+30

def layer_norm(values, gain_vector, shift_vector):
    center = values - lax.optimization_barrier(jnp.mean(values, axis=-1, keepdims=True))
    spread = lax.optimization_barrier(jnp.mean(center * center, axis=-1, keepdims=True))
    return center * lax.rsqrt(spread + EPSILON) * gain_vector + shift_vector

def matmul(left_side, right_side):
    return jnp.dot(left_side, right_side, precision=HIGHEST_PRECISION)

def encoder_layer(stream, params, keep_pair, same_image):
    gain_one, shift_one, w_mixed, bias_query, bias_value, w_proj, bias_proj, gain_two, shift_two, w_up, bias_up, w_down, bias_down = params
    row_count = stream.shape[0]
    normed = low(layer_norm(stream, gain_one, shift_one))
    bias_mixed = jnp.concatenate([bias_query, jnp.zeros_like(bias_query), bias_value])
    mixed = low(low_back(matmul(normed, w_mixed) + bias_mixed))
    mixed = mixed.reshape(row_count, 3, HEADS, HD)
    scores = jnp.einsum('qhd,khd->hqk', mixed[:, 0], mixed[:, 1], precision=HIGHEST_PRECISION) * 0.125
    scores = low_back(scores)
    scores = jnp.where(same_image[None], scores, MASKED)
    probs = low(jax.nn.softmax(scores, axis=-1))
    attended = jnp.einsum('hqk,khd->qhd', probs, mixed[:, 2], precision=HIGHEST_PRECISION)
    attended = low(low_back(attended.reshape(row_count, D)))
    branch = low_back(matmul(attended, w_proj) + bias_proj)
    middle = stream + keep_pair[:, 0:1] * branch / KEEP_RATE
    normed_two = low(layer_norm(middle, gain_two, shift_two))
    hidden = low_back(matmul(normed_two, w_up) + bias_up)
    hidden = low(jax.nn.gelu(hidden, approximate=False))
    branch_two = low_back(matmul(hidden, w_down) + bias_down)
    return middle + keep_pair[:, 1:2] * branch_two / KEEP_RATE

def reference(patches, specials, lengths, keep_mask, norm1_gain, norm1_bias, qkv_weight, query_bias, value_bias, proj_weight, proj_bias, norm2_gain, norm2_bias, fc1_weight, fc1_bias, fc2_weight, fc2_bias, cot_patches, cot_specials):
    params = tuple((weight.astype(jnp.float32) for weight in (norm1_gain, norm1_bias, qkv_weight, query_bias, value_bias, proj_weight, proj_bias, norm2_gain, norm2_bias, fc1_weight, fc1_bias, fc2_weight, fc2_bias)))
    groups = lengths.shape[0]
    patch_all = patches.astype(jnp.float32).reshape(groups, PACK, D)
    spec_all = specials.astype(jnp.float32).reshape(groups, 2 * IMGS, D)
    cot_patch_all = cot_patches.astype(jnp.float32).reshape(groups, PACK, D)
    cot_spec_all = cot_specials.astype(jnp.float32).reshape(groups, 2 * IMGS, D)
    positions = jnp.arange(PACK, dtype=jnp.int32)
    spec_image = jnp.arange(2 * IMGS, dtype=jnp.int32) // 2

    def one_group(totals, inputs):
        patch_rows, spec_rows, group_lengths, group_keep, cot_patch, cot_spec = inputs
        image_ends = jnp.cumsum(group_lengths).astype(jnp.int32)
        patch_image = lax.optimization_barrier(jnp.sum((positions[:, None] >= image_ends[None, :]).astype(jnp.int32), axis=1)).astype(jnp.int32)
        image_ids = jnp.concatenate([patch_image, spec_image]).astype(jnp.int32)
        same_image = image_ids[:, None] == image_ids[None, :]
        keep_rows = group_keep.astype(jnp.float32)[image_ids]

        def forward(stream, weights):
            for layer_index in range(LAYERS):
                layer_params = tuple((weight[layer_index] for weight in weights))
                stream = encoder_layer(stream, layer_params, keep_rows[:, 2 * layer_index:2 * layer_index + 2], same_image)
            return stream
        start = jnp.concatenate([patch_rows, spec_rows])
        result, pull = jax.vjp(forward, start, params)
        grad_stream, grad_params = pull(jnp.concatenate([cot_patch, cot_spec]))
        totals = jax.tree.map(jnp.add, totals, grad_params)
        return (totals, (result[:PACK], result[PACK:], grad_stream[:PACK], grad_stream[PACK:]))
    zero_grads = tuple((jnp.zeros_like(weight) for weight in params))
    totals, outputs = lax.scan(one_group, zero_grads, (patch_all, spec_all, lengths, keep_mask, cot_patch_all, cot_spec_all))
    out_patch, out_spec, grad_patch, grad_spec = outputs
    return (out_patch.reshape(-1, D), out_spec.reshape(-1, D), grad_patch.reshape(-1, D), grad_spec.reshape(-1, D), totals[0], totals[1], totals[2], totals[3], totals[4], totals[5], totals[6], totals[7], totals[8], totals[9], totals[10], totals[11], totals[12])
```

```python
from functools import partial

import jax
import jax.numpy as jnp
from jax import lax
from jax.sharding import PartitionSpec as P

HD = 64
LAYERS = 2
MOST = 280
KEEP_RATE = 0.9
EPSILON = 1e-06
MASKED = -1e30
ROOT_HALF = 0.7071067811865476
ROOT_TWO_PI = 0.3989422804014327
BF = jnp.bfloat16
F32 = jnp.float32


def dot_nn(left, right):
    return lax.dot_general(left, right, (((1,), (0,)), ((), ())), preferred_element_type=F32)


def dot_nt(left, right):
    return lax.dot_general(left, right, (((1,), (1,)), ((), ())), preferred_element_type=F32)


def dot_tn(left, right):
    return lax.dot_general(left, right, (((0,), (0,)), ((), ())), preferred_element_type=F32)


class Place:
    def __init__(self):
        self.n_dp = lax.axis_size("dp")
        self.n_seq = lax.axis_size("seq")
        self.walked = self.n_dp == 8 and self.n_seq == 4
        self.dp = lax.axis_index("dp")
        self.seq = lax.axis_index("seq")
        if self.walked:
            self.core = self.seq % 2
            self.y = self.seq // 2
            self.x = self.dp % 2
            self.z = self.dp // 2
            self.nz = self.n_dp // 2

    def swap_seq(self, values, mask):
        return lax.ppermute(values, "seq", [(i, i ^ mask) for i in range(self.n_seq)])

    def swap_x(self, values):
        return lax.ppermute(values, "dp", [(i, i ^ 1) for i in range(self.n_dp)])

    def ring_z(self, values):
        return lax.ppermute(values, "dp", [(i, (i + 2) % self.n_dp) for i in range(self.n_dp)])

    def own_half(self, values, which, axis):
        low, high = jnp.split(values, 2, axis=axis)
        return jnp.where(which == 0, low, high)

    def in_order(self, which, mine, other, axis):
        return jnp.where(
            which == 0,
            jnp.concatenate([mine, other], axis=axis),
            jnp.concatenate([other, mine], axis=axis),
        )


def gather_matrix(place, shard):
    if not place.walked:
        whole = lax.all_gather(shard, "dp", axis=0, tiled=True)
        half = whole.shape[1] // 2
        return (whole[:, :half], whole[:, half:])
    rows, columns = shard.shape
    blocks = [place.own_half(shard, place.core, 1)]
    for _ in range(place.nz - 1):
        blocks.append(place.ring_z(blocks[-1]))
    halves = [place.own_half(block, place.y, 0) for block in blocks]
    first = place.swap_x(halves[0])
    rest = place.swap_x(jnp.stack(halves[1:]))
    first_back = place.swap_seq(first, 2)
    rest_back = place.swap_seq(rest, 2)
    crossed = [place.in_order(place.y, first, first_back, 0)]
    rest_all = place.in_order(place.y, rest, rest_back, 1)
    crossed += [rest_all[i] for i in range(place.nz - 1)]
    mine = jnp.zeros((place.nz, 2, rows, columns // 2), shard.dtype)
    for step in range(place.nz):
        at = (place.z - step) % place.nz
        mine = lax.dynamic_update_slice(mine, blocks[step][None, None], (at, place.x, 0, 0))
        mine = lax.dynamic_update_slice(mine, crossed[step][None, None], (at, 1 - place.x, 0, 0))
    mine = mine.reshape(place.n_dp * rows, columns // 2)
    return (mine, place.swap_seq(mine, 1))


def times(place, values, halves):
    low = dot_nn(values, halves[0])
    high = dot_nn(values, halves[1])
    if not place.walked:
        return jnp.concatenate([low, high], axis=1)
    return place.in_order(place.core, low, high, 1)


def times_back(place, values, halves):
    if not place.walked:
        low, high = jnp.split(values, 2, axis=1)
    else:
        low = place.own_half(values, place.core, 1)
        high = place.own_half(values, 1 - place.core, 1)
    return dot_nt(low, halves[0]) + dot_nt(high, halves[1])


def quarter(place, values, y, core):
    pieces = jnp.split(values, 4, axis=1)
    low = jnp.where(core == 0, pieces[0], pieces[1])
    high = jnp.where(core == 0, pieces[2], pieces[3])
    return jnp.where(y == 0, low, high)


def reduce_matrix(place, acts, grads):
    if not place.walked:
        part = dot_tn(acts, grads).astype(BF)
        part = lax.psum_scatter(part, "dp", scatter_dimension=0, tiled=True)
        return lax.psum_scatter(part, "seq", scatter_dimension=1, tiled=True).astype(F32)
    y, core, nz = place.y, place.core, place.nz
    rows = acts.shape[1] // place.n_dp
    wide = grads.shape[1] // 4
    sent = jnp.concatenate([quarter(place, grads, y, 1 - core), quarter(place, grads, 1 - y, 1 - core)], 1)
    kept = jnp.concatenate([quarter(place, grads, y, core), quarter(place, grads, 1 - y, core)], 1)
    got = place.swap_seq(dot_tn(acts, sent).astype(BF), 1)
    pair = (dot_tn(acts, kept) + got).astype(BF).reshape(nz, 2, rows, 2 * wide)
    near = lax.dynamic_index_in_dim(pair, place.x, 1, keepdims=False)
    far = lax.dynamic_index_in_dim(pair, 1 - place.x, 1, keepdims=False)
    got = place.swap_seq(far[:, :, wide:], 2)
    far = (far[:, :, :wide].astype(F32) + got).astype(BF)
    got = place.swap_x(far)
    near = jnp.concatenate(
        [(near[:, :, :wide].astype(F32) + got).astype(BF), near[:, :, wide:]], axis=2
    )

    def block(step):
        return lax.dynamic_index_in_dim(near, (place.z - step) % nz, 0, keepdims=False)

    total = block(1)
    for step in range(2, nz + 1):
        total = (place.ring_z(total).astype(F32) + block(step)).astype(BF)
    got = place.swap_seq(total[:, wide:], 2)
    return total[:, :wide].astype(F32) + got


def reduce_vectors(place, vectors):
    packed = jnp.concatenate(
        [vector.reshape(place.n_dp, vector.shape[0] // place.n_dp) for vector in vectors], axis=1
    )
    mask = 1
    while mask < place.n_seq:
        packed = packed + place.swap_seq(packed, mask)
        mask *= 2
    packed = lax.all_to_all(packed, "dp", split_axis=0, concat_axis=0, tiled=True)
    total = jnp.sum(packed, axis=0)
    results, at = [], 0
    for vector in vectors:
        width = vector.shape[0] // place.n_dp
        results.append(total[at : at + width])
        at += width
    return results


def gather_vectors(place, shards):
    widths = [shard.shape[1] for shard in shards]
    packed = jnp.concatenate(shards, axis=1)
    rows = packed.shape[0]
    spread = jnp.broadcast_to(packed[None], (place.n_dp,) + packed.shape)
    spread = lax.all_to_all(spread, "dp", split_axis=0, concat_axis=0, tiled=True)
    results, at = [], 0
    for width in widths:
        piece = spread[:, :, at : at + width]
        results.append(jnp.transpose(piece, (1, 0, 2)).reshape(rows, place.n_dp * width).astype(F32))
        at += width
    return results


def normalize(values):
    center = values - jnp.mean(values, axis=-1, keepdims=True)
    spread = jnp.mean(center * center, axis=-1, keepdims=True)
    scale = lax.rsqrt(spread + EPSILON)
    return (center * scale, scale)


def normalize_back(hat, scale, gain, grad):
    scaled = grad * gain
    first = jnp.mean(scaled, axis=-1, keepdims=True)
    second = jnp.mean(scaled * hat, axis=-1, keepdims=True)
    back = scale * (scaled - first - hat * second)
    return (back, jnp.sum(grad * hat, axis=0), jnp.sum(grad, axis=0))


def heads_of(mixed):
    rows = mixed.shape[0]
    width = mixed.shape[1] // 3
    split = mixed.reshape(rows, 3, width // HD, HD)
    return (split[:, 0], split[:, 1], split[:, 2])


def attend(mixed, key_ok):
    queries, keys, values = heads_of(mixed)
    scores = jnp.einsum("qhd,khd->hqk", queries, keys, preferred_element_type=F32) * 0.125
    scores = jnp.where(key_ok[None, None, :], scores, MASKED)
    top = jnp.max(scores, axis=2, keepdims=True)
    powers = jnp.exp(scores - top)
    probs = powers / jnp.sum(powers, axis=2, keepdims=True)
    out = jnp.einsum("hqk,khd->qhd", probs.astype(BF), values, preferred_element_type=F32)
    return (out.reshape(mixed.shape[0], -1).astype(BF), probs)


def attend_back(mixed, probs, grad_out):
    queries, keys, values = heads_of(mixed)
    rows = mixed.shape[0]
    grads = grad_out.reshape(queries.shape)
    grad_probs = jnp.einsum("qhd,khd->hqk", grads, values, preferred_element_type=F32)
    inner = jnp.sum(probs * grad_probs, axis=2, keepdims=True)
    grad_scores = (probs * (grad_probs - inner)).astype(BF)
    grad_values = jnp.einsum("hqk,qhd->khd", probs.astype(BF), grads, preferred_element_type=F32)
    grad_queries = (
        jnp.einsum("hqk,khd->qhd", grad_scores, keys, preferred_element_type=F32) * 0.125
    )
    grad_keys = (
        jnp.einsum("hqk,qhd->khd", grad_scores, queries, preferred_element_type=F32) * 0.125
    )
    return jnp.concatenate(
        [grad.reshape(rows, -1).astype(BF) for grad in (grad_queries, grad_keys, grad_values)], axis=1
    )


def layer_forward(place, stream, vectors, matrices, keeps, key_ok):
    gain_one, shift_one, bias_query, bias_value, bias_proj, gain_two, shift_two, bias_down, bias_up = vectors
    w_mixed, w_proj, w_up, w_down = matrices
    hat_one, scale_one = normalize(stream)
    normed_one = (hat_one * gain_one + shift_one).astype(BF)
    bias_mixed = jnp.concatenate([bias_query, jnp.zeros_like(bias_query), bias_value])
    mixed = (times(place, normed_one, w_mixed) + bias_mixed).astype(BF)
    attended, probs = attend(mixed, key_ok)
    middle = stream + keeps[0] * (times(place, attended, w_proj) + bias_proj) / KEEP_RATE
    hat_two, scale_two = normalize(middle)
    normed_two = (hat_two * gain_two + shift_two).astype(BF)
    hidden_pre = times(place, normed_two, w_up) + bias_up
    share = 0.5 * (1.0 + lax.erf(hidden_pre * ROOT_HALF))
    hidden = (hidden_pre * share).astype(BF)
    slope = share + hidden_pre * jnp.exp(-0.5 * hidden_pre * hidden_pre) * ROOT_TWO_PI
    output = middle + keeps[1] * (times(place, hidden, w_down) + bias_down) / KEEP_RATE
    saved = (hat_one, scale_one, normed_one, mixed, probs, attended, hat_two, scale_two, normed_two, hidden, slope)
    return (output, saved)


def layer_back(place, grad_stream, saved, vectors, matrices, keeps):
    hat_one, scale_one, normed_one, mixed, probs, attended, hat_two, scale_two, normed_two, hidden, slope = saved
    gain_one, gain_two = (vectors[0], vectors[5])
    w_mixed, w_proj, w_up, w_down = matrices
    width = grad_stream.shape[1]
    grad_down = (keeps[1] * grad_stream / KEEP_RATE).astype(BF)
    total_down = reduce_matrix(place, hidden, grad_down)
    grad_up = (times_back(place, grad_down, w_down) * slope).astype(BF)
    total_up = reduce_matrix(place, normed_two, grad_up)
    back_two, grad_gain_two, grad_shift_two = normalize_back(
        hat_two, scale_two, gain_two, times_back(place, grad_up, w_up)
    )
    grad_middle = grad_stream + back_two
    grad_proj = (keeps[0] * grad_middle / KEEP_RATE).astype(BF)
    total_proj = reduce_matrix(place, attended, grad_proj)
    grad_attended = times_back(place, grad_proj, w_proj).astype(BF)
    grad_mixed = attend_back(mixed, probs, grad_attended)
    total_mixed = reduce_matrix(place, normed_one, grad_mixed)
    back_one, grad_gain_one, grad_shift_one = normalize_back(
        hat_one, scale_one, gain_one, times_back(place, grad_mixed, w_mixed)
    )
    grad_input = grad_middle + back_one
    sum_mixed = jnp.sum(grad_mixed, axis=0, dtype=F32)
    totals = reduce_vectors(
        place,
        (
            grad_gain_one,
            grad_shift_one,
            sum_mixed[:width],
            sum_mixed[2 * width :],
            jnp.sum(grad_proj, axis=0, dtype=F32),
            grad_gain_two,
            grad_shift_two,
            jnp.sum(grad_down, axis=0, dtype=F32),
            jnp.sum(grad_up, axis=0, dtype=F32),
        ),
    )
    return (grad_input, totals, (total_mixed, total_proj, total_up, total_down))


def shift_seq(place, values, by):
    count = place.n_seq
    return lax.ppermute(values, "seq", [(i, i + by) for i in range(count) if 0 <= i + by < count])


def to_image(place, patches, specials, halo, start, length, rows):
    count, width = patches.shape
    before = shift_seq(place, patches[count - halo :], 1)
    after = shift_seq(place, patches[:halo], -1)
    spare = jnp.zeros((MOST + 2 * halo - count - 2 * halo, width), patches.dtype)
    window = jnp.concatenate([before, patches, after, spare])
    image = lax.dynamic_slice_in_dim(window, start, MOST)
    inside = jnp.arange(MOST, dtype=jnp.int32)[:, None] < length
    image = jnp.where(inside, image, 0.0)
    spare = jnp.zeros((rows - MOST - specials.shape[0], width), patches.dtype)
    return jnp.concatenate([image, specials, spare])


def from_image(place, stream, halo, start, length, count, specials):
    width = stream.shape[1]
    inside = jnp.arange(MOST, dtype=jnp.int32)[:, None] < length
    image = jnp.where(inside, stream[:MOST], 0.0)
    window = jnp.zeros((MOST + 2 * halo, width), stream.dtype)
    window = lax.dynamic_update_slice_in_dim(window, image, start, 0)
    own = window[halo : halo + count]
    from_before = shift_seq(place, window[halo + count : count + 2 * halo], 1)
    from_after = shift_seq(place, window[:halo], -1)
    blank = jnp.zeros((count - halo, width), stream.dtype)
    own = own + jnp.concatenate([from_before, blank]) + jnp.concatenate([blank, from_after])
    return (own, stream[MOST : MOST + specials])


def local(
    patches,
    specials,
    lengths,
    keep_mask,
    norm1_gain,
    norm1_bias,
    qkv_weight,
    query_bias,
    value_bias,
    proj_weight,
    proj_bias,
    norm2_gain,
    norm2_bias,
    fc1_weight,
    fc1_bias,
    fc2_weight,
    fc2_bias,
    cot_patches,
    cot_specials,
):
    place = Place()
    count = patches.shape[0]
    special_count = specials.shape[0]
    images = lengths.shape[1]
    halo = (MOST - count) * (images // 2)
    rows = -(-(MOST + special_count) // 16) * 16
    before = jnp.sum(jnp.where(jnp.arange(images) < place.seq, lengths[0], 0))
    length = lax.dynamic_index_in_dim(lengths[0], place.seq, 0, keepdims=False)
    start = before - place.seq * count + halo
    keeps = lax.dynamic_index_in_dim(keep_mask[0], place.seq, 0, keepdims=False).astype(F32)
    row_ids = jnp.arange(rows, dtype=jnp.int32)
    key_ok = (row_ids < length) | ((row_ids >= MOST) & (row_ids < MOST + special_count))

    shards = (norm1_gain, norm1_bias, query_bias, value_bias, proj_bias, norm2_gain, norm2_bias, fc2_bias, fc1_bias)
    vectors_all = gather_vectors(place, shards)
    stream = to_image(place, patches, specials, halo, start, length, rows)
    matrices = []
    for layer in range(LAYERS):
        matrices.append(
            tuple(
                gather_matrix(place, shard[layer])
                for shard in (qkv_weight, proj_weight, fc1_weight, fc2_weight)
            )
        )
    vectors = [tuple(vector[layer] for vector in vectors_all) for layer in range(LAYERS)]
    saved = []
    for layer in range(LAYERS):
        stream, kept = layer_forward(
            place, stream, vectors[layer], matrices[layer], keeps[2 * layer : 2 * layer + 2], key_ok
        )
        saved.append(kept)
    out_patches, out_specials = from_image(place, stream, halo, start, length, count, special_count)
    grad = to_image(place, cot_patches, cot_specials, halo, start, length, rows)
    vector_totals, matrix_totals = ([None] * LAYERS, [None] * LAYERS)
    for layer in reversed(range(LAYERS)):
        grad, vector_totals[layer], matrix_totals[layer] = layer_back(
            place, grad, saved[layer], vectors[layer], matrices[layer], keeps[2 * layer : 2 * layer + 2]
        )
    grad_patches, grad_specials = from_image(place, grad, halo, start, length, count, special_count)
    vector_out = [jnp.stack([vector_totals[layer][i] for layer in range(LAYERS)]) for i in range(9)]
    matrix_out = [jnp.stack([matrix_totals[layer][i] for layer in range(LAYERS)]) for i in range(4)]
    g1, s1, bq, bv, bp, g2, s2, bd, bu = vector_out
    wm, wp, wu, wd = matrix_out
    return (
        out_patches,
        out_specials,
        grad_patches,
        grad_specials,
        g1,
        s1,
        wm,
        bq,
        bv,
        wp,
        bp,
        g2,
        s2,
        wu,
        bu,
        wd,
        bd,
    )


def solution(mesh):
    in_specs = (
        P(("dp", "seq"), None),
        P(("dp", "seq"), None),
        P("dp", None),
        P("dp", None, None),
        P(None, "dp"),
        P(None, "dp"),
        P(None, "dp", None),
        P(None, "dp"),
        P(None, "dp"),
        P(None, "dp", None),
        P(None, "dp"),
        P(None, "dp"),
        P(None, "dp"),
        P(None, "dp", None),
        P(None, "dp"),
        P(None, "dp", None),
        P(None, "dp"),
        P(("dp", "seq"), None),
        P(("dp", "seq"), None),
    )
    out_specs = (
        P(("dp", "seq"), None),
        P(("dp", "seq"), None),
        P(("dp", "seq"), None),
        P(("dp", "seq"), None),
        P(None, "dp"),
        P(None, "dp"),
        P(None, "dp", "seq"),
        P(None, "dp"),
        P(None, "dp"),
        P(None, "dp", "seq"),
        P(None, "dp"),
        P(None, "dp"),
        P(None, "dp"),
        P(None, "dp", "seq"),
        P(None, "dp"),
        P(None, "dp", "seq"),
        P(None, "dp"),
    )
    return jax.shard_map(local, mesh=mesh, in_specs=in_specs, out_specs=out_specs, check_vma=False)
```

```python
from functools import partial

import jax
import jax.numpy as jnp
from jax import lax
from jax.experimental import pallas as pl
from jax.experimental.pallas import tpu as pltpu
from jax.sharding import PartitionSpec as P

HD = 64
LAYERS = 2
MOST = 280
KEEP_RATE = 0.9
EPSILON = 1e-06
MASKED = -1e30
GAIN_ONE, SHIFT_ONE, BIAS_QUERY, BIAS_VALUE, BIAS_PROJ, GAIN_TWO, SHIFT_TWO, BIAS_DOWN = range(8)
MIB = 1024 * 1024
ROOT_HALF = 0.7071067811865476
ROOT_TWO_PI = 0.3989422804014327
BF = jnp.bfloat16
F32 = jnp.float32


def dot_nn(left, right):
    return lax.dot_general(left, right, (((1,), (0,)), ((), ())), preferred_element_type=F32)


def dot_nt(left, right):
    return lax.dot_general(left, right, (((1,), (1,)), ((), ())), preferred_element_type=F32)


def dot_tn(left, right):
    return lax.dot_general(left, right, (((0,), (0,)), ((), ())), preferred_element_type=F32)


class Place:
    def __init__(self):
        self.n_dp = lax.axis_size("dp")
        self.n_seq = lax.axis_size("seq")
        self.walked = self.n_dp == 8 and self.n_seq == 4
        self.dp = lax.axis_index("dp")
        self.seq = lax.axis_index("seq")
        if self.walked:
            self.core = self.seq % 2
            self.y = self.seq // 2
            self.x = self.dp % 2
            self.z = self.dp // 2
            self.nz = self.n_dp // 2

    def swap_seq(self, values, mask):
        return lax.ppermute(values, "seq", [(i, i ^ mask) for i in range(self.n_seq)])

    def swap_x(self, values):
        return lax.ppermute(values, "dp", [(i, i ^ 1) for i in range(self.n_dp)])

    def ring_z(self, values):
        return lax.ppermute(values, "dp", [(i, (i + 2) % self.n_dp) for i in range(self.n_dp)])


def gather_matrix(shard):
    return lax.all_gather(shard, "dp", axis=0, tiled=True)


def reduce_matrix(acts, grads):
    part = dot_tn(acts, grads).astype(BF)
    part = lax.psum_scatter(part, "dp", scatter_dimension=0, tiled=True)
    return lax.psum_scatter(part, "seq", scatter_dimension=1, tiled=True).astype(F32)


def reduce_vectors(place, vectors):
    packed = jnp.concatenate(
        [vector.reshape(place.n_dp, vector.shape[0] // place.n_dp) for vector in vectors], axis=1
    )
    mask = 1
    while mask < place.n_seq:
        packed = packed + place.swap_seq(packed, mask)
        mask *= 2
    packed = lax.all_to_all(packed, "dp", split_axis=0, concat_axis=0, tiled=True)
    total = jnp.sum(packed, axis=0)
    results, at = [], 0
    for vector in vectors:
        width = vector.shape[0] // place.n_dp
        results.append(total[at : at + width])
        at += width
    return results


def gather_vectors(place, shards):
    widths = [shard.shape[1] for shard in shards]
    packed = jnp.concatenate(shards, axis=1)
    rows = packed.shape[0]
    spread = jnp.broadcast_to(packed[None], (place.n_dp,) + packed.shape)
    spread = lax.all_to_all(spread, "dp", split_axis=0, concat_axis=0, tiled=True)
    results, at = [], 0
    for width in widths:
        piece = spread[:, :, at : at + width]
        results.append(jnp.transpose(piece, (1, 0, 2)).reshape(rows, place.n_dp * width).astype(F32))
        at += width
    return results


def normalize(values):
    center = values - jnp.mean(values, axis=-1, keepdims=True)
    spread = jnp.mean(center * center, axis=-1, keepdims=True)
    scale = lax.rsqrt(spread + EPSILON)
    return (center * scale, scale)


def normalize_back(hat, scale, gain, grad):
    scaled = grad * gain
    first = jnp.mean(scaled, axis=-1, keepdims=True)
    second = jnp.mean(scaled * hat, axis=-1, keepdims=True)
    back = scale * (scaled - first - hat * second)
    return (back, jnp.sum(grad * hat, axis=0), jnp.sum(grad, axis=0))


def heads_of(mixed):
    rows = mixed.shape[0]
    width = mixed.shape[1] // 3
    split = mixed.reshape(rows, 3, width // HD, HD)
    return (split[:, 0], split[:, 1], split[:, 2])


def attend(mixed, key_ok):
    queries, keys, values = heads_of(mixed)
    scores = jnp.einsum("qhd,khd->hqk", queries, keys, preferred_element_type=F32) * 0.125
    scores = jnp.where(key_ok[None, None, :], scores, MASKED)
    top = jnp.max(scores, axis=2, keepdims=True)
    powers = jnp.exp(scores - top)
    probs = powers / jnp.sum(powers, axis=2, keepdims=True)
    out = jnp.einsum("hqk,khd->qhd", probs.astype(BF), values, preferred_element_type=F32)
    return (out.reshape(mixed.shape[0], -1).astype(BF), probs)


def attend_back(mixed, probs, grad_out):
    queries, keys, values = heads_of(mixed)
    rows = mixed.shape[0]
    grads = grad_out.reshape(queries.shape)
    grad_probs = jnp.einsum("qhd,khd->hqk", grads, values, preferred_element_type=F32)
    inner = jnp.sum(probs * grad_probs, axis=2, keepdims=True)
    grad_scores = (probs * (grad_probs - inner)).astype(BF)
    grad_values = jnp.einsum("hqk,qhd->khd", probs.astype(BF), grads, preferred_element_type=F32)
    grad_queries = (
        jnp.einsum("hqk,khd->qhd", grad_scores, keys, preferred_element_type=F32) * 0.125
    )
    grad_keys = (
        jnp.einsum("hqk,qhd->khd", grad_scores, queries, preferred_element_type=F32) * 0.125
    )
    return jnp.concatenate(
        [grad.reshape(rows, -1).astype(BF) for grad in (grad_queries, grad_keys, grad_values)], axis=1
    )


def layer_forward(stream, vectors, matrices, keeps, key_ok):
    gain_one, shift_one, bias_query, bias_value, bias_proj, gain_two, shift_two, bias_down, bias_up = vectors
    w_mixed, w_proj, w_up, w_down = matrices
    hat_one, scale_one = normalize(stream)
    normed_one = (hat_one * gain_one + shift_one).astype(BF)
    bias_mixed = jnp.concatenate([bias_query, jnp.zeros_like(bias_query), bias_value])
    mixed = (dot_nn(normed_one, w_mixed) + bias_mixed).astype(BF)
    attended, probs = attend(mixed, key_ok)
    middle = stream + keeps[0] * (dot_nn(attended, w_proj) + bias_proj) / KEEP_RATE
    hat_two, scale_two = normalize(middle)
    normed_two = (hat_two * gain_two + shift_two).astype(BF)
    hidden_pre = dot_nn(normed_two, w_up) + bias_up
    share = 0.5 * (1.0 + lax.erf(hidden_pre * ROOT_HALF))
    hidden = (hidden_pre * share).astype(BF)
    slope = share + hidden_pre * jnp.exp(-0.5 * hidden_pre * hidden_pre) * ROOT_TWO_PI
    output = middle + keeps[1] * (dot_nn(hidden, w_down) + bias_down) / KEEP_RATE
    saved = (hat_one, scale_one, normed_one, mixed, probs, attended, hat_two, scale_two, normed_two, hidden, slope)
    return (output, saved)


def layer_back(place, grad_stream, saved, vectors, matrices, keeps):
    hat_one, scale_one, normed_one, mixed, probs, attended, hat_two, scale_two, normed_two, hidden, slope = saved
    gain_one, gain_two = (vectors[0], vectors[5])
    w_mixed, w_proj, w_up, w_down = matrices
    width = grad_stream.shape[1]
    grad_down = (keeps[1] * grad_stream / KEEP_RATE).astype(BF)
    total_down = reduce_matrix(hidden, grad_down)
    grad_up = (dot_nt(grad_down, w_down) * slope).astype(BF)
    total_up = reduce_matrix(normed_two, grad_up)
    back_two, grad_gain_two, grad_shift_two = normalize_back(
        hat_two, scale_two, gain_two, dot_nt(grad_up, w_up)
    )
    grad_middle = grad_stream + back_two
    grad_proj = (keeps[0] * grad_middle / KEEP_RATE).astype(BF)
    total_proj = reduce_matrix(attended, grad_proj)
    grad_attended = dot_nt(grad_proj, w_proj).astype(BF)
    grad_mixed = attend_back(mixed, probs, grad_attended)
    total_mixed = reduce_matrix(normed_one, grad_mixed)
    back_one, grad_gain_one, grad_shift_one = normalize_back(
        hat_one, scale_one, gain_one, dot_nt(grad_mixed, w_mixed)
    )
    grad_input = grad_middle + back_one
    sum_mixed = jnp.sum(grad_mixed, axis=0, dtype=F32)
    totals = reduce_vectors(
        place,
        (
            grad_gain_one,
            grad_shift_one,
            sum_mixed[:width],
            sum_mixed[2 * width :],
            jnp.sum(grad_proj, axis=0, dtype=F32),
            grad_gain_two,
            grad_shift_two,
            jnp.sum(grad_down, axis=0, dtype=F32),
            jnp.sum(grad_up, axis=0, dtype=F32),
        ),
    )
    return (grad_input, totals, (total_mixed, total_proj, total_up, total_down))


def shift_seq(place, values, by):
    count = place.n_seq
    return lax.ppermute(values, "seq", [(i, i + by) for i in range(count) if 0 <= i + by < count])


def to_image(place, patches, specials, halo, start, length, rows):
    count, width = patches.shape
    before = shift_seq(place, patches[count - halo :], 1)
    after = shift_seq(place, patches[:halo], -1)
    spare = jnp.zeros((MOST + 2 * halo - count - 2 * halo, width), patches.dtype)
    window = jnp.concatenate([before, patches, after, spare])
    image = lax.dynamic_slice_in_dim(window, start, MOST)
    inside = jnp.arange(MOST, dtype=jnp.int32)[:, None] < length
    image = jnp.where(inside, image, 0.0)
    spare = jnp.zeros((rows - MOST - specials.shape[0], width), patches.dtype)
    return jnp.concatenate([image, specials, spare])


def from_image(place, stream, halo, start, length, count, specials):
    width = stream.shape[1]
    inside = jnp.arange(MOST, dtype=jnp.int32)[:, None] < length
    image = jnp.where(inside, stream[:MOST], 0.0)
    window = jnp.zeros((MOST + 2 * halo, width), stream.dtype)
    window = lax.dynamic_update_slice_in_dim(window, image, start, 0)
    own = window[halo : halo + count]
    from_before = shift_seq(place, window[halo + count : count + 2 * halo], 1)
    from_after = shift_seq(place, window[:halo], -1)
    blank = jnp.zeros((count - halo, width), stream.dtype)
    own = own + jnp.concatenate([from_before, blank]) + jnp.concatenate([blank, from_after])
    return (own, stream[MOST : MOST + specials])


def local_plain(
    place,
    patches,
    specials,
    lengths,
    keep_mask,
    norm1_gain,
    norm1_bias,
    qkv_weight,
    query_bias,
    value_bias,
    proj_weight,
    proj_bias,
    norm2_gain,
    norm2_bias,
    fc1_weight,
    fc1_bias,
    fc2_weight,
    fc2_bias,
    cot_patches,
    cot_specials,
):
    count = patches.shape[0]
    special_count = specials.shape[0]
    images = lengths.shape[1]
    halo = (MOST - count) * (images // 2)
    rows = -(-(MOST + special_count) // 16) * 16
    before = jnp.sum(jnp.where(jnp.arange(images) < place.seq, lengths[0], 0))
    length = lax.dynamic_index_in_dim(lengths[0], place.seq, 0, keepdims=False)
    start = before - place.seq * count + halo
    keeps = lax.dynamic_index_in_dim(keep_mask[0], place.seq, 0, keepdims=False).astype(F32)
    row_ids = jnp.arange(rows, dtype=jnp.int32)
    key_ok = (row_ids < length) | ((row_ids >= MOST) & (row_ids < MOST + special_count))

    shards = (norm1_gain, norm1_bias, query_bias, value_bias, proj_bias, norm2_gain, norm2_bias, fc2_bias, fc1_bias)
    vectors_all = gather_vectors(place, shards)
    stream = to_image(place, patches, specials, halo, start, length, rows)
    matrices = []
    for layer in range(LAYERS):
        matrices.append(
            tuple(
                gather_matrix(shard[layer])
                for shard in (qkv_weight, proj_weight, fc1_weight, fc2_weight)
            )
        )
    vectors = [tuple(vector[layer] for vector in vectors_all) for layer in range(LAYERS)]
    saved = []
    for layer in range(LAYERS):
        stream, kept = layer_forward(
            stream, vectors[layer], matrices[layer], keeps[2 * layer : 2 * layer + 2], key_ok
        )
        saved.append(kept)
    out_patches, out_specials = from_image(place, stream, halo, start, length, count, special_count)
    grad = to_image(place, cot_patches, cot_specials, halo, start, length, rows)
    vector_totals, matrix_totals = ([None] * LAYERS, [None] * LAYERS)
    for layer in reversed(range(LAYERS)):
        grad, vector_totals[layer], matrix_totals[layer] = layer_back(
            place, grad, saved[layer], vectors[layer], matrices[layer], keeps[2 * layer : 2 * layer + 2]
        )
    grad_patches, grad_specials = from_image(place, grad, halo, start, length, count, special_count)
    vector_out = [jnp.stack([vector_totals[layer][i] for layer in range(LAYERS)]) for i in range(9)]
    matrix_out = [jnp.stack([matrix_totals[layer][i] for layer in range(LAYERS)]) for i in range(4)]
    g1, s1, bq, bv, bp, g2, s2, bd, bu = vector_out
    wm, wp, wu, wd = matrix_out
    return (
        out_patches,
        out_specials,
        grad_patches,
        grad_specials,
        g1,
        s1,
        wm,
        bq,
        bv,
        wp,
        bp,
        g2,
        s2,
        wu,
        bu,
        wd,
        bd,
    )


def whole_vmem(count):
    return [pl.BlockSpec(memory_space=pltpu.VMEM)] * count


def in_smem(count):
    return [pl.BlockSpec(memory_space=pltpu.SMEM)] * count


def kernel_params(mib):
    return pltpu.CompilerParams(vmem_limit_bytes=mib * MIB)


def place_pieces(spot, parts, crossed, split, first, quarter):
    z, x, y, core = (spot[i] for i in range(4))
    steps = len(parts) // 2
    for side in range(2):
        at_core = core if side == 0 else 1 - core
        for step in range(steps):
            part = parts[side * steps + step]
            at_z = lax.rem(z - step + steps, steps)
            for far_x in range(2):
                row = 2 * at_z + lax.rem(x + far_x, 2)
                if crossed is not None:
                    base = far_x * (first + 2 * quarter)
                    for j in range(first):
                        crossed[at_core, row, j] = part[base + j]
                if split is not None:
                    for far_y in range(2):
                        base = first + far_y * (first + 2 * quarter) + far_x * quarter
                        for j in range(quarter):
                            split[at_core, row, lax.rem(y + far_y, 2) * quarter + j] = part[base + j]


def flat(block):
    return block.reshape(-1, block.shape[-1])


def moments(values):
    center = values - jnp.mean(values, axis=-1, keepdims=True)
    scale = lax.rsqrt(jnp.mean(center * center, axis=-1, keepdims=True) + EPSILON)
    return (center * scale, scale)


def norm_back(hat, scale, gain, grad):
    scaled = grad * gain
    first = jnp.mean(scaled, axis=-1, keepdims=True)
    second = jnp.mean(scaled * hat, axis=-1, keepdims=True)
    return scale * (scaled - first - hat * second)


def erf_of(values):
    v = jnp.clip(values, -3.7439211627767994, 3.7439211627767994)
    s = v * v
    top = s * 0.00022905065861350646 + 0.0034082910107109506
    top = top * s + 0.050955695062380861
    top = top * s + 0.18520832239976145
    top = top * s + 1.128379143519084
    low = s * -1.1791602954361697e-7 + 0.000023547966471313185
    low = low * s + 0.0010179625278914885
    low = low * s + 0.014070470171167667
    low = low * s + 0.11098505178285362
    low = low * s + 0.49746925110067538
    low = low * s + 1.0
    return v * top / low


def head_probs(queries, keys, blocked):
    scores = dot_nt(queries, keys) * 0.125 + blocked
    powers = jnp.exp(scores - jnp.max(scores, axis=1, keepdims=True))
    return powers / jnp.sum(powers, axis=1, keepdims=True)


def forward_attention_kernel(
    spot, keep, stream, vectors, blocked, *refs
):
    parts, refs = refs[:8], refs[8:]
    middle, normed_two, normed_one_t, normed_two_t, mixed, attended, attended_t, crossed, split = refs
    place_pieces(spot, parts, crossed, split, 2, 1)
    hat, _ = moments(stream[...])
    normed = (hat * vectors[GAIN_ONE : GAIN_ONE + 1] + vectors[SHIFT_ONE : SHIFT_ONE + 1]).astype(BF)
    normed_one_t[...] = normed.T
    width = stream.shape[1]
    half = width // 2
    for core in range(2):
        for j in range(3):
            weight = crossed[core, :, j] if j < 2 else split[core, :, 0]
            columns = pl.ds(j * width + core * half, half)
            ahead = dot_nn(normed, flat(weight))
            if j != 1:
                row = BIAS_QUERY if j == 0 else BIAS_VALUE
                ahead = ahead + vectors[row : row + 1, core * half : (core + 1) * half]
            mixed[:, columns] = ahead.astype(BF)
    lane = lax.broadcasted_iota(jnp.int32, (1, 2 * HD), 1)
    for pair in range(width // (2 * HD)):
        queries, keys, values = (
            mixed[:, pl.ds(j * width + pair * 2 * HD, 2 * HD)] for j in range(3)
        )
        outs = []
        for side in range(2):
            mine = ((lane < HD) if side == 0 else (lane >= HD)).astype(F32).astype(BF)
            probs = head_probs(queries * mine, keys, blocked[...])
            outs.append(dot_nn(probs.astype(BF), values))
        attended[:, pl.ds(pair * 2 * HD, 2 * HD)] = jnp.where(lane < HD, outs[0], outs[1]).astype(BF)
    ahead = attended[...]
    attended_t[...] = ahead.T
    for core in range(2):
        columns = pl.ds(core * half, half)
        branch = dot_nn(ahead, flat(split[core, :, 1])) + vectors[BIAS_PROJ : BIAS_PROJ + 1, columns]
        middle[:, columns] = stream[:, columns] + keep[0] * branch
    hat, _ = moments(middle[...])
    normed = (hat * vectors[GAIN_TWO : GAIN_TWO + 1] + vectors[SHIFT_TWO : SHIFT_TWO + 1]).astype(BF)
    normed_two[...] = normed
    normed_two_t[...] = normed.T


def forward_attention(place, spot, keep, stream, vectors, parts, blocked):
    rows, width = stream.shape
    group = parts[0].shape[1:]
    shapes = [
        jax.ShapeDtypeStruct((rows, width), F32),
        jax.ShapeDtypeStruct((rows, width), BF),
        jax.ShapeDtypeStruct((width, rows), BF),
        jax.ShapeDtypeStruct((width, rows), BF),
        jax.ShapeDtypeStruct((rows, 3 * width), BF),
        jax.ShapeDtypeStruct((rows, width), BF),
        jax.ShapeDtypeStruct((width, rows), BF),
    ]
    return pl.pallas_call(
        forward_attention_kernel,
        in_specs=in_smem(2) + whole_vmem(3) + whole_vmem(8),
        out_specs=whole_vmem(len(shapes)),
        out_shape=shapes,
        scratch_shapes=[
            pltpu.VMEM((2, place.n_dp, 2) + group, BF),
            pltpu.VMEM((2, place.n_dp, 2) + group, BF),
        ],
        compiler_params=kernel_params(14),
        name="forward_attention",
    )(spot, keep, stream, vectors, blocked, *parts)


def forward_feed_kernel(spot, keep, middle, normed, bias_up, vectors, *refs):
    parts, refs = refs[:8], refs[8:]
    output, hidden, slope, crossed, split = refs
    place_pieces(spot, parts, crossed, split, 4, 2)
    values = normed[...]
    half = values.shape[1] // 2
    for core in range(2):
        for j in range(4):
            columns = pl.ds((core * 4 + j) * half, half)
            pre = dot_nn(values, flat(crossed[core, :, j])) + bias_up[:, columns]
            share = 0.5 + 0.5 * erf_of(pre * ROOT_HALF)
            hidden[:, columns] = (pre * share).astype(BF)
            slope[:, columns] = (share + pre * jnp.exp(-0.5 * pre * pre) * ROOT_TWO_PI).astype(BF)
    ahead = hidden[...]
    for core in range(2):
        columns = pl.ds(core * half, half)
        branch = dot_nn(ahead, flat(split[core])) + vectors[BIAS_DOWN : BIAS_DOWN + 1, columns]
        output[:, columns] = middle[:, columns] + keep[0] * branch


def forward_feed(place, spot, keep, middle, normed, bias_up, vectors, parts):
    rows, width = middle.shape
    group = parts[0].shape[1:]
    shapes = [
        jax.ShapeDtypeStruct((rows, width), F32),
        jax.ShapeDtypeStruct((rows, 4 * width), BF),
        jax.ShapeDtypeStruct((rows, 4 * width), BF),
    ]
    return pl.pallas_call(
        forward_feed_kernel,
        in_specs=in_smem(2) + whole_vmem(4) + whole_vmem(8),
        out_specs=whole_vmem(len(shapes)),
        out_shape=shapes,
        scratch_shapes=[
            pltpu.VMEM((2, place.n_dp, 4) + group, BF),
            pltpu.VMEM((2, place.n_dp, 4) + group, BF),
        ],
        compiler_params=kernel_params(20),
        name="forward_feed",
    )(spot, keep, middle, normed, bias_up, vectors, *parts)


def backward_feed_kernel(spot, keep, grad, slope, *refs):
    parts, refs = refs[:8], refs[8:]
    grad_down_t, grad_up, sum_down, sum_up, split = refs
    place_pieces(spot, parts, None, split, 4, 2)
    down = (keep[0] * grad[...]).astype(BF)
    grad_down_t[...] = down.T
    sum_down[...] = jnp.sum(down.astype(F32), axis=0, keepdims=True)
    half = grad.shape[1] // 2
    for row in range(split.shape[1]):
        columns = pl.ds(row * half, half)
        ahead = dot_nt(down[:, :half], flat(split[0, row])) + dot_nt(down[:, half:], flat(split[1, row]))
        up = (ahead * slope[:, columns].astype(F32)).astype(BF)
        grad_up[:, columns] = up
        sum_up[:, columns] = jnp.sum(up.astype(F32), axis=0, keepdims=True)


def backward_feed(place, spot, keep, grad, slope, parts):
    rows, width = grad.shape
    group = parts[0].shape[1:]
    shapes = [
        jax.ShapeDtypeStruct((width, rows), BF),
        jax.ShapeDtypeStruct((rows, 4 * width), BF),
        jax.ShapeDtypeStruct((1, width), F32),
        jax.ShapeDtypeStruct((1, 4 * width), F32),
    ]
    return pl.pallas_call(
        backward_feed_kernel,
        in_specs=in_smem(2) + whole_vmem(2) + whole_vmem(8),
        out_specs=whole_vmem(len(shapes)),
        out_shape=shapes,
        scratch_shapes=[
            pltpu.VMEM((2, place.n_dp, 4) + group, BF),
        ],
        compiler_params=kernel_params(14),
        name="backward_feed",
    )(spot, keep, grad, slope, *parts)


def backward_middle_kernel(spot, keep, grad, grad_up, middle, vectors, *refs):
    parts, refs = refs[:8], refs[8:]
    grad_middle, grad_proj, sum_proj, grad_gain, grad_shift, crossed = refs
    place_pieces(spot, parts, crossed, None, 4, 2)
    hat, scale = moments(middle[...])
    half = grad.shape[1] // 2
    total = jnp.zeros(grad.shape, F32)
    for core in range(2):
        for j in range(4):
            total += dot_nt(grad_up[:, pl.ds((core * 4 + j) * half, half)], flat(crossed[core, :, j]))
    grad_gain[...] = jnp.sum(total * hat, axis=0, keepdims=True)
    grad_shift[...] = jnp.sum(total, axis=0, keepdims=True)
    after = grad[...] + norm_back(hat, scale, vectors[GAIN_TWO : GAIN_TWO + 1], total)
    grad_middle[...] = after
    proj = (keep[0] * after).astype(BF)
    grad_proj[...] = proj
    sum_proj[...] = jnp.sum(proj.astype(F32), axis=0, keepdims=True)


def backward_middle(place, spot, keep, grad, grad_up, middle, vectors, parts):
    rows, width = grad.shape
    group = parts[0].shape[1:]
    shapes = [
        jax.ShapeDtypeStruct((rows, width), F32),
        jax.ShapeDtypeStruct((rows, width), BF),
    ] + [jax.ShapeDtypeStruct((1, width), F32)] * 3
    return pl.pallas_call(
        backward_middle_kernel,
        in_specs=in_smem(2) + whole_vmem(4) + whole_vmem(8),
        out_specs=whole_vmem(len(shapes)),
        out_shape=shapes,
        scratch_shapes=[
            pltpu.VMEM((2, place.n_dp, 4) + group, BF),
        ],
        compiler_params=kernel_params(14),
        name="backward_middle",
    )(spot, keep, grad, grad_up, middle, vectors, *parts)


def backward_attention_kernel(spot, grad_middle, grad_proj, mixed, stream, vectors, blocked, *refs):
    others, parts, refs = refs[:5], refs[5:13], refs[13:]
    grad_stream, grad_mixed, sums, ahead, crossed, split = refs
    sum_proj, gain_two, shift_two, sum_down, sum_up = others
    place_pieces(spot, parts, crossed, split, 2, 1)
    hat, scale = moments(stream[...])
    width = stream.shape[1]
    half = width // 2
    proj = grad_proj[...]
    ahead[...] = (
        dot_nt(proj[:, :half], flat(split[0, :, 1])) + dot_nt(proj[:, half:], flat(split[1, :, 1]))
    ).astype(BF)
    lane = lax.broadcasted_iota(jnp.int32, (1, 2 * HD), 1)
    for pair in range(width // (2 * HD)):
        queries, keys, values = (
            mixed[:, pl.ds(j * width + pair * 2 * HD, 2 * HD)] for j in range(3)
        )
        grads = ahead[:, pl.ds(pair * 2 * HD, 2 * HD)]
        found = []
        for side in range(2):
            mine = ((lane < HD) if side == 0 else (lane >= HD)).astype(F32).astype(BF)
            probs = head_probs(queries * mine, keys, blocked[...])
            grad_probs = dot_nt(grads * mine, values)
            inner = jnp.sum(probs * grad_probs, axis=1, keepdims=True)
            grad_scores = (probs * (grad_probs - inner)).astype(BF)
            found.append(
                (
                    dot_nn(grad_scores, keys) * 0.125,
                    dot_tn(grad_scores, queries) * 0.125,
                    dot_tn(probs.astype(BF), grads),
                )
            )
        for j in range(3):
            grad_mixed[:, pl.ds(j * width + pair * 2 * HD, 2 * HD)] = jnp.where(
                lane < HD, found[0][j], found[1][j]
            ).astype(BF)
    total = jnp.zeros(stream.shape, F32)
    for core in range(2):
        for j in range(3):
            weight = crossed[core, :, j] if j < 2 else split[core, :, 0]
            total += dot_nt(grad_mixed[:, pl.ds(j * width + core * half, half)], flat(weight))

    def put(row, values):
        sums[row : row + 1, :] = values

    put(GAIN_ONE, jnp.sum(total * hat, axis=0, keepdims=True))
    put(SHIFT_ONE, jnp.sum(total, axis=0, keepdims=True))
    put(BIAS_QUERY, jnp.sum(grad_mixed[:, :width].astype(F32), axis=0, keepdims=True))
    put(BIAS_VALUE, jnp.sum(grad_mixed[:, 2 * width :].astype(F32), axis=0, keepdims=True))
    put(BIAS_PROJ, sum_proj[...])
    put(GAIN_TWO, gain_two[...])
    put(SHIFT_TWO, shift_two[...])
    put(BIAS_DOWN, sum_down[...])
    for j in range(4):
        put(BIAS_DOWN + 1 + j, sum_up[:, j * width : (j + 1) * width])
    sums[BIAS_DOWN + 5 :, :] = jnp.zeros((sums.shape[0] - BIAS_DOWN - 5, width), F32)
    grad_stream[...] = grad_middle[...] + norm_back(hat, scale, vectors[GAIN_ONE : GAIN_ONE + 1], total)


def backward_attention(place, spot, grad_middle, grad_proj, mixed, stream, vectors, blocked, others, parts):
    rows, width = stream.shape
    group = parts[0].shape[1:]
    shapes = [
        jax.ShapeDtypeStruct((rows, width), F32),
        jax.ShapeDtypeStruct((rows, 3 * width), BF),
        jax.ShapeDtypeStruct((16, width), F32),
    ]
    return pl.pallas_call(
        backward_attention_kernel,
        in_specs=in_smem(1) + whole_vmem(6 + 5 + 8),
        out_specs=whole_vmem(len(shapes)),
        out_shape=shapes,
        scratch_shapes=[
            pltpu.VMEM((rows, width), BF),
            pltpu.VMEM((2, place.n_dp, 2) + group, BF),
            pltpu.VMEM((2, place.n_dp, 2) + group, BF),
        ],
        compiler_params=kernel_params(16),
        name="backward_attention",
    )(spot, grad_middle, grad_proj, mixed, stream, vectors, blocked, *others, *parts)


def row_of(spot, step, far_x, steps):
    return 2 * lax.rem(spot[0] - step + steps, steps) + lax.rem(spot[1] + far_x, 2)


def feed_group(spot, core, part, far_y, j, normed_t, grad_up, grad_down_t, hidden, spare):
    half = spare.shape[2]
    column = 2 * lax.rem(spot[2] + far_y, 2) + core
    if part == 0:
        at = pl.multiple_of((column * 2 + j) * half, half)
        out = dot_nn(normed_t[...], grad_up[:, pl.ds(at, half)])
        spare[...] = out.reshape(spare.shape).astype(BF)
    else:
        rows = spare.shape[1]
        at = pl.multiple_of((column * 2 + j) * rows, rows)
        left = grad_down_t[pl.ds(at, rows), :]
        for row in range(spare.shape[0]):
            spare[row] = dot_nn(left, hidden[:, pl.ds(row * half, half)]).astype(BF)


def attention_group(spot, core, part, far_y, j, normed_t, grad_mixed, attended_t, grad_proj, spare):
    half = spare.shape[2]
    column = 2 * lax.rem(spot[2] + far_y, 2) + core
    if part == 0:
        out = dot_nn(normed_t[...], grad_mixed[column, :, :half])
    else:
        out = dot_nn(normed_t[...], grad_mixed[column, :, half:]) + dot_nn(
            attended_t[...], grad_proj[column]
        )
    spare[...] = out.reshape(spare.shape).astype(BF)


def sent_kernel(fill, wide, steps, spot, *refs):
    operands, out, spare = refs[:4], refs[4], refs[5]
    for part in range(2):
        for far_y in range(2):
            for j in range(wide):
                fill(spot, 1 - spot[3], part, far_y, j, *operands, spare)
                for step in range(steps):
                    for far_x in range(2):
                        if part == 0:
                            at = (far_x * 2 + far_y) * wide + j
                        else:
                            at = (4 + far_y * 2 + far_x) * wide + j
                        out[step, at] = spare[row_of(spot, step, far_x, steps)]


def kept_kernel(fill, wide, steps, spot, *refs):
    operands, got, outs, spare = refs[:4], refs[4], refs[5 : 5 + 3 * steps], refs[5 + 3 * steps]
    for part in range(2):
        for far_y in range(2):
            for j in range(wide):
                fill(spot, spot[3], part, far_y, j, *operands, spare)
                for step in range(steps):
                    for far_x in range(2):
                        if part == 0:
                            at = (far_x * 2 + far_y) * wide + j
                        else:
                            at = (4 + far_y * 2 + far_x) * wide + j
                        total = spare[row_of(spot, step, far_x, steps)].astype(F32) + got[step, at].astype(F32)
                        total = total.astype(BF)
                        across, aside, stays = outs[3 * step : 3 * step + 3]
                        if part == 0:
                            target, index = (across, far_y * wide + j) if far_x else (stays, far_y * wide + j)
                        else:
                            index = far_x * wide + j
                            target, index = (aside, index) if far_y else (stays, 2 * wide + index)
                        target[index] = total


def sent_part(place, spot, fill, wide, operands):
    rows, half = (operands[0].shape[0] // place.n_dp, operands[0].shape[0] // 2)
    return pl.pallas_call(
        partial(sent_kernel, fill, wide, place.nz),
        in_specs=in_smem(1) + whole_vmem(4),
        out_specs=whole_vmem(1)[0],
        out_shape=jax.ShapeDtypeStruct((place.nz, 8 * wide, rows, half), BF),
        scratch_shapes=[pltpu.VMEM((place.n_dp, rows, half), BF)],
        compiler_params=kernel_params(10),
        name="gradient_sent",
    )(spot, *operands)


def kept_part(place, spot, fill, wide, operands, got):
    rows, half = (operands[0].shape[0] // place.n_dp, operands[0].shape[0] // 2)
    shapes = [
        jax.ShapeDtypeStruct((size * wide, rows, half), BF)
        for _ in range(place.nz)
        for size in (2, 2, 4)
    ]
    outs = pl.pallas_call(
        partial(kept_kernel, fill, wide, place.nz),
        in_specs=in_smem(1) + whole_vmem(5),
        out_specs=whole_vmem(len(shapes)),
        out_shape=shapes,
        scratch_shapes=[pltpu.VMEM((place.n_dp, rows, half), BF)],
        compiler_params=kernel_params(10),
        name="gradient_kept",
    )(spot, *operands, got)
    return [outs[3 * step : 3 * step + 3] for step in range(place.nz)]


def ring_kernel(stays, across, aside, *refs):
    out = refs[-1]
    count = across.shape[0]
    for at in range(2 * count):
        side = across[at] if at < count else aside[at - count]
        total = stays[at].astype(F32) + side.astype(F32)
        if len(refs) == 2:
            total = total + refs[0][at].astype(F32)
        out[at] = total.astype(BF)


def ring_block(stays, across, aside, running):
    operands = [stays, across, aside] + ([] if running is None else [running])
    return pl.pallas_call(
        ring_kernel,
        in_specs=whole_vmem(len(operands)),
        out_specs=whole_vmem(1)[0],
        out_shape=jax.ShapeDtypeStruct(stays.shape, BF),
        compiler_params=kernel_params(4),
        name="ring_block",
    )(*operands)


def fence(trees):
    flat = [list(tree.values()) if isinstance(tree, dict) else tree for tree in trees]
    flat = lax.optimization_barrier(flat)
    return [
        dict(zip(tree, values)) if isinstance(tree, dict) else values
        for tree, values in zip(trees, flat)
    ]


def pick(which, low, high):
    return jnp.where(which == 0, low, high)


def own_groups(place, qkv, proj, up, down):
    rows, half = proj.shape[0], proj.shape[1] // 2
    wide = 2 * half

    def attention_groups(core):
        parts = [qkv[:, j * wide + core * half : j * wide + (core + 1) * half] for j in range(3)]
        return jnp.stack(parts + [proj[:, core * half : (core + 1) * half]])

    def feed_groups(core):
        parts = [up[:, (core * 4 + j) * half : (core * 4 + j + 1) * half] for j in range(4)]
        return jnp.concatenate(
            [jnp.stack(parts), down[:, core * half : (core + 1) * half].reshape(4, rows, half)]
        )

    return (
        pick(place.core, attention_groups(0), attention_groups(1)),
        pick(place.core, feed_groups(0), feed_groups(1)),
    )


class Gathered:
    def __init__(self, own, place):
        groups = own.shape[0]
        self.first = groups // 2
        self.quarter = groups // 4
        self.own = own
        self.mine = pick(
            place.y,
            own[self.first : self.first + self.quarter],
            own[self.first + self.quarter :],
        )
        self.blocks = []
        self.whole = []
        self.mate = []

    def begin(self, crossed):
        self.blocks.append(jnp.concatenate([self.own[: self.first], self.mine, crossed]))

    def parts(self):
        return self.whole + self.mate


class Reduced:
    def __init__(self, place):
        self.place = place
        self.operands = None
        self.sent = None
        self.kept = None
        self.sides = {}
        self.running = None
        self.last = None

    def block(self, step):
        return ring_block(self.kept[step][2], *self.sides[step], self.running)


def gather_vectors_packed(place, vectors, bias_up):
    rows, part = vectors[0].shape
    packed = jnp.concatenate([jnp.stack(vectors, axis=1), bias_up.reshape(rows, -1, part)], axis=1)
    spread = jnp.broadcast_to(packed[None], (place.n_dp,) + packed.shape)
    spread = lax.all_to_all(spread, "dp", split_axis=0, concat_axis=0, tiled=True).astype(F32)
    count = len(vectors)
    return (
        jnp.transpose(spread[:, :, :count], (1, 2, 0, 3)).reshape(rows, count, -1),
        jnp.transpose(spread[:, :, count:], (1, 0, 2, 3)).reshape(rows, 1, -1),
    )


def image_kernel(frame, before, patches, after, specials, out, window):
    halo, count = before.shape[0], patches.shape[0]
    window[:halo] = before[...]
    window[halo : halo + count] = patches[...]
    window[halo + count : 2 * halo + count] = after[...]
    spare = window.shape[0] - 2 * halo - count
    window[2 * halo + count :] = jnp.zeros((spare, window.shape[1]), F32)
    inside = lax.broadcasted_iota(jnp.int32, (MOST, 1), 0) < frame[1]
    turned = pltpu.roll(window[...], lax.rem(window.shape[0] - frame[0], window.shape[0]), 0)
    out[:MOST] = jnp.where(inside, turned[:MOST], 0.0)
    last = out.shape[0] - MOST
    out[MOST:] = jnp.zeros((last, out.shape[1]), F32)
    out[MOST : MOST + specials.shape[0]] = specials[...]


def take_image(place, frame, patches, specials, halo, rows):
    count, width = patches.shape
    before = shift_seq(place, patches[count - halo :], 1)
    after = shift_seq(place, patches[:halo], -1)

    def build(before, patches, after, specials):
        return pl.pallas_call(
            image_kernel,
            in_specs=in_smem(1) + whole_vmem(4),
            out_specs=whole_vmem(1)[0],
            out_shape=jax.ShapeDtypeStruct((rows, width), F32),
            scratch_shapes=[pltpu.VMEM((MOST + 2 * halo, width), F32)],
            compiler_params=kernel_params(6),
            name="take_image",
        )(frame, before, patches, after, specials)

    return (before, patches, after, specials), build


def block_kernel(frame, stream, own, before, after, specials, window):
    halo, count = before.shape[0], own.shape[0]
    window[MOST:] = jnp.zeros((window.shape[0] - MOST, window.shape[1]), F32)
    inside = lax.broadcasted_iota(jnp.int32, (MOST, 1), 0) < frame[1]
    window[:MOST] = jnp.where(inside, stream[:MOST], 0.0)
    window[...] = pltpu.roll(window[...], frame[0], 0)
    before[...] = window[:halo]
    own[...] = window[halo : halo + count]
    after[...] = window[halo + count : 2 * halo + count]
    specials[...] = stream[MOST : MOST + specials.shape[0]]


def give_image(place, frame, stream, halo, count, special_count):
    width = stream.shape[1]
    own, before, after, specials = pl.pallas_call(
        block_kernel,
        in_specs=in_smem(1) + whole_vmem(1),
        out_specs=whole_vmem(4),
        out_shape=[
            jax.ShapeDtypeStruct((size, width), F32) for size in (count, halo, halo, special_count)
        ],
        scratch_shapes=[pltpu.VMEM((MOST + 2 * halo, width), F32)],
        compiler_params=kernel_params(6),
        name="give_image",
    )(frame, stream)
    return (own, shift_seq(place, after, 1), shift_seq(place, before, -1), specials)


def join_image(own, from_before, from_after, specials):
    halo = from_before.shape[0]
    blank = jnp.zeros((own.shape[0] - halo, own.shape[1]), own.dtype)
    return (
        own + jnp.concatenate([from_before, blank]) + jnp.concatenate([blank, from_after]),
        specials,
    )


def finish_kernel(*refs):
    inputs, (out_mixed, out_proj, out_up, out_down) = refs[:-4], refs[-4:]
    layers = len(inputs) // 6
    for layer in range(layers):
        last, aside, across = inputs[6 * layer : 6 * layer + 3]
        one = last[0].astype(F32) + aside[0].astype(F32)
        two = last[2].astype(F32) + across[0].astype(F32)
        cut = one.shape[1] // 2
        out_mixed[layer] = jnp.concatenate([one, two[:, :cut]], axis=1)
        out_proj[layer] = two[:, cut:]
        last, aside, across = inputs[6 * layer + 3 : 6 * layer + 6]
        half = last.shape[2]
        for j in range(2):
            out_up[layer, :, j * half : (j + 1) * half] = last[j].astype(F32) + aside[j].astype(F32)
        downs = [last[4 + j].astype(F32) + across[j].astype(F32) for j in range(2)]
        out_down[layer] = jnp.concatenate(downs, axis=0).T


def finish(place, parts, rows, width):
    shapes = [
        jax.ShapeDtypeStruct((LAYERS, rows, columns), F32)
        for rows, columns in (
            (rows, 3 * width // 4),
            (rows, width // 4),
            (rows, width),
            (4 * rows, width // 4),
        )
    ]
    flat_parts = [array for layer in parts for array in layer]
    return pl.pallas_call(
        finish_kernel,
        in_specs=whole_vmem(len(flat_parts)),
        out_specs=whole_vmem(len(shapes)),
        out_shape=shapes,
        compiler_params=kernel_params(10),
        name="finish",
    )(*flat_parts)


def local_walked(
    place,
    patches,
    specials,
    lengths,
    keep_mask,
    norm1_gain,
    norm1_bias,
    qkv_weight,
    query_bias,
    value_bias,
    proj_weight,
    proj_bias,
    norm2_gain,
    norm2_bias,
    fc1_weight,
    fc1_bias,
    fc2_weight,
    fc2_bias,
    cot_patches,
    cot_specials,
):
    count, width = patches.shape
    special_count = specials.shape[0]
    images = lengths.shape[1]
    halo = (MOST - count) * (images // 2)
    rows = -(-(MOST + special_count) // 16) * 16
    nz = place.nz
    part_rows = proj_weight.shape[1]
    before = jnp.sum(jnp.where(jnp.arange(images) < place.seq, lengths[0], 0))
    length = lax.dynamic_index_in_dim(lengths[0], place.seq, 0, keepdims=False)
    frame = jnp.stack([before - place.seq * count + halo, length]).astype(jnp.int32)
    keeps = lax.dynamic_index_in_dim(keep_mask[0], place.seq, 0, keepdims=False).astype(F32)
    keeps = [keeps[i : i + 1] / KEEP_RATE for i in range(2 * LAYERS)]
    row_ids = jnp.arange(rows, dtype=jnp.int32)
    key_ok = (row_ids < length) | ((row_ids >= MOST) & (row_ids < MOST + special_count))
    blocked = jnp.where(key_ok, 0.0, MASKED).astype(F32)[None]
    spot = jnp.stack([place.z, place.x, place.y, place.core]).astype(jnp.int32)

    units = []
    for layer in range(LAYERS):
        attention_own, feed_own = own_groups(
            place, qkv_weight[layer], proj_weight[layer], fc1_weight[layer], fc2_weight[layer]
        )
        units.append(Gathered(attention_own, place))
        units.append(Gathered(feed_own, place))

    first_cross = place.swap_x(units[0].mine)
    inputs = {
        "later": [unit.mine for unit in units[1:]],
        "own": [unit.own for unit in units[1:]],
        "rows": (patches, specials),
        "cots": (cot_patches, cot_specials),
        "vectors": (norm1_gain, norm1_bias, query_bias, value_bias, proj_bias, norm2_gain, norm2_bias, fc2_bias),
        "bias": fc1_bias,
    }
    first_cross, inputs = fence((first_cross, inputs))
    units[0].begin(first_cross)
    for unit, own in zip(units[1:], inputs.pop("own")):
        unit.own = own

    vectors, bias_up = (None, None)
    streams = [None] * (LAYERS + 1)
    middles, normed_one_ts, normed_two_ts, mixeds, attended_ts, hiddens, slopes = (
        [None] * LAYERS for _ in range(7)
    )
    cores = []
    carried = {}
    grad = None
    for slot in range(3 * len(units) + 2):
        new = {}
        index, step = divmod(slot, 3)
        todo = []
        if index < len(units):
            new["z"] = place.ring_z(units[index].blocks[step])
            todo.append((index, step))
        if step == 0 and index > 0:
            todo.append((index - 1, 3))
        for which, at in todo:
            unit = units[which]
            new["x", which, at] = place.swap_x(unit.blocks[at][: unit.first])
            new["y", which, at] = place.swap_seq(unit.blocks[at][unit.first :], 2)
        for which, at in cores:
            new["core", which, at] = place.swap_seq(units[which].whole[at], 1)
        if slot == 0:
            new["later"] = place.swap_x(jnp.concatenate(inputs["later"]))
        if slot in (1, 4):
            new["image"], build = take_image(place, frame, *inputs["rows" if slot == 1 else "cots"], halo, rows)
        if slot == 2:
            carried["stream"] = build(*image)
        if slot == 5:
            grad = build(*image)
        if slot == 3:
            new["vectors"] = gather_vectors_packed(place, inputs["vectors"], inputs["bias"])
        if slot in (5, 11):
            layer = slot // 6
            new["forward"] = forward_attention(
                place, spot, keeps[2 * layer], carried["stream"], vectors[layer], units[2 * layer].parts(), blocked
            )
        if slot == 9:
            new["feed"] = forward_feed(
                place, spot, keeps[1], carried["middle"], carried["normed"], bias_up[0], vectors[0], units[1].parts()
            )
        after = (slot + 1) // 3
        if slot % 3 == 2 and after < len(units):
            carried["begin"] = units[after].blocks[0]
        gate = inputs if slot < 4 else {}
        new, carried, gate = fence((new, carried, gate))
        inputs.update(gate)
        if "begin" in carried:
            units[after].blocks[0] = carried.pop("begin")
        if "image" in new:
            image = new["image"]
        if "vectors" in new:
            vectors, bias_up = new["vectors"]
        if "later" in new:
            at = 0
            for unit in units[1:]:
                unit.begin(new["later"][at : at + unit.quarter])
                at += unit.quarter
        if "z" in new:
            units[index].blocks.append(new["z"])
        for which, at in cores:
            units[which].mate.append(new["core", which, at])
        cores = todo
        for which, at in todo:
            unit = units[which]
            unit.whole.append(
                jnp.concatenate([unit.blocks[at], new["x", which, at], new["y", which, at]])
            )
        if "forward" in new:
            streams[layer] = carried.pop("stream")
            middle, normed, normed_one_ts[layer], normed_two_ts[layer], mixeds[layer], _, attended_ts[layer] = new["forward"]
            middles[layer] = middle
            carried["middle"], carried["normed"] = middle, normed
        if "feed" in new:
            carried["stream"], hiddens[0], slopes[0] = new["feed"]
            del carried["middle"], carried["normed"]
    streams[LAYERS], hiddens[1], slopes[1] = forward_feed(
        place, spot, keeps[3], carried["middle"], carried["normed"], bias_up[1], vectors[1], units[3].parts()
    )

    reduces = [Reduced(place) for _ in range(2 * LAYERS)]
    lasts = [None] * (2 * LAYERS)
    back = [{} for _ in range(LAYERS)]

    def feed_back(layer, grad):
        found = back[layer]
        found["down_t"], found["up"], found["sum_down"], found["sum_up"] = backward_feed(
            place, spot, keeps[2 * layer + 1], grad, slopes[layer], units[2 * layer + 1].parts()
        )

    def feed_sent(layer):
        unit = reduces[2 * (LAYERS - 1 - layer)]
        unit.operands = (normed_two_ts[layer], back[layer]["up"], back[layer]["down_t"], hiddens[layer])
        unit.sent = sent_part(place, spot, feed_group, 2, unit.operands)

    def middle_back(layer, grad):
        found = back[layer]
        found["middle"], found["proj"], found["sum_proj"], found["gain"], found["shift"] = backward_middle(
            place, spot, keeps[2 * layer], grad, found["up"], middles[layer], vectors[layer], units[2 * layer + 1].parts()
        )

    def attention_back(layer):
        found = back[layer]
        others = [found[name] for name in ("sum_proj", "gain", "shift", "sum_down", "sum_up")]
        found["grad"], found["mixed"], found["sums"] = backward_attention(
            place, spot, found["middle"], found["proj"], mixeds[layer], streams[layer], vectors[layer], blocked, others, units[2 * layer].parts()
        )

    def attention_sent(layer):
        found = back[layer]
        wide = 3 * width // 4
        cut = width // 4
        mixed = jnp.stack(
            [jnp.pad(found["mixed"][:, i * wide : (i + 1) * wide], ((0, 0), (0, cut))) for i in range(4)]
        )
        proj = jnp.stack([jnp.pad(found["proj"][:, i * cut : (i + 1) * cut], ((0, 0), (cut, 0))) for i in range(4)])
        unit = reduces[2 * (LAYERS - 1 - layer) + 1]
        unit.operands = (normed_one_ts[layer], mixed, attended_ts[layer], proj)
        unit.sent = sent_part(place, spot, attention_group, 1, unit.operands)

    feed_back(1, grad)
    feed_sent(1)
    back[1], back_sent, output = fence((back[1], [reduces[0].sent], streams[LAYERS]))
    reduces[0].sent = back_sent[0]
    final_slot = 3 * len(reduces)
    outs = {}
    total = None
    ringing = None
    for slot in range(-2, final_slot + 1):
        new = {}
        for which, unit in enumerate(reduces):
            at = slot - 3 * which
            fill, wide = (attention_group, 1) if which % 2 else (feed_group, 2)
            if at == -2:
                new["core", which] = place.swap_seq(unit.sent, 1)
            if at == -1:
                unit.kept = kept_part(place, spot, fill, wide, unit.operands, unit.got)
            if -1 <= at <= 2:
                step = (at + 2) % nz
                new["side", which] = (
                    place.swap_x(unit.kept[step][0]),
                    place.swap_seq(unit.kept[step][1], 2),
                )
            if 0 <= at <= 2:
                new["z", which] = place.ring_z(unit.block(at + 1))
            if at == 3:
                last = unit.block(0)
                part = last.shape[0] // 4
                lasts[which] = [
                    last,
                    place.swap_seq(last[part : 2 * part], 2),
                    place.swap_x(last[3 * part :]),
                ]
                if which < len(reduces) - 1:
                    new["last", which] = lasts[which]
        work = {}
        if slot == -2:
            middle_back(1, grad)
            work["back", 1] = back[1]
        if slot == -1:
            attention_back(1)
            work["back", 1] = back[1]
        if slot == 0:
            attention_sent(1)
            work["sent", 1] = reduces[1].sent
            feed_back(0, back[1]["grad"])
            work["back", 0] = back[0]
        if slot == 1:
            feed_sent(0)
            work["sent", 2] = reduces[2].sent
            middle_back(0, back[1]["grad"])
            work["back", 0] = back[0]
        if slot == 2:
            attention_back(0)
            work["back", 0] = back[0]
        if slot == 3:
            attention_sent(0)
            work["sent", 3] = reduces[3].sent
            new["give", "out"] = give_image(place, frame, output, halo, count, special_count)
            total = jnp.concatenate([back[layer]["sums"] for layer in range(LAYERS)])
            new["total"] = total + place.swap_seq(total, 1)
        if slot == 4:
            new["give", "back"] = give_image(place, frame, back[0]["grad"], halo, count, special_count)
            new["total"] = total + place.swap_seq(total, 2)
        if slot == 5:
            new["total"] = total + place.swap_x(total)
            outs["out"] = join_image(*outs["out"])
            outs["back"] = join_image(*outs["back"])
        if slot in (6, 7, 8):
            ringing = place.ring_z(total if slot == 6 else ringing)
            new["ringing"] = ringing
        pending = {}
        for which, unit in enumerate(reduces):
            at = slot + 1 - 3 * which
            if at == -2:
                pending["sent", which] = unit.sent
            if 0 <= at <= 2:
                pending["kept", which] = unit.kept[(at + 2) % nz]
        if slot == -1:
            pending["output"] = output
        for key in list(work):
            pending.pop(key, None)
        new, work, pending = fence((new, work, pending))
        for found in (work, pending):
            for key, value in found.items():
                if key[0] == "sent":
                    reduces[key[1]].sent = value
                if key[0] == "kept":
                    reduces[key[1]].kept[(slot + 1 - 3 * key[1] + 2) % nz] = value
                if key[0] == "back":
                    back[key[1]] = value
        output = pending.get("output", output)
        for which, unit in enumerate(reduces):
            at = slot - 3 * which
            if at == -2:
                unit.got = new["core", which]
            if -1 <= at <= 2:
                unit.sides[(at + 2) % nz] = new["side", which]
            if 0 <= at <= 2:
                unit.running = new["z", which]
            if at == 3 and ("last", which) in new:
                lasts[which] = new["last", which]
        if "total" in new:
            total = new["total"]
        if "ringing" in new:
            ringing = new["ringing"]
            summed = ringing + (total if slot == 6 else summed)
        for name in ("out", "back"):
            if ("give", name) in new:
                outs[name] = new["give", name]

    wm, wp, wu, wd = finish(
        place, [lasts[3] + lasts[2], lasts[1] + lasts[0]], part_rows, width
    )
    summed = summed.reshape(LAYERS, -1, place.n_dp, part_rows)
    eight = lax.dynamic_index_in_dim(summed[:, :8], place.dp, 2, keepdims=False)
    g1, s1, bq, bv, bp, g2, s2, bd = (eight[:, i] for i in range(8))
    bu = summed[:, 8:12].reshape(LAYERS, place.n_dp, 4 * part_rows)
    bu = lax.dynamic_index_in_dim(bu, place.dp, 1, keepdims=False)
    return (
        *outs["out"],
        *outs["back"],
        g1,
        s1,
        wm,
        bq,
        bv,
        wp,
        bp,
        g2,
        s2,
        wu,
        bu,
        wd,
        bd,
    )


def local(*args):
    place = Place()
    if place.walked:
        return local_walked(place, *args)
    return local_plain(place, *args)


def solution(mesh):
    in_specs = (
        P(("dp", "seq"), None),
        P(("dp", "seq"), None),
        P("dp", None),
        P("dp", None, None),
        P(None, "dp"),
        P(None, "dp"),
        P(None, "dp", None),
        P(None, "dp"),
        P(None, "dp"),
        P(None, "dp", None),
        P(None, "dp"),
        P(None, "dp"),
        P(None, "dp"),
        P(None, "dp", None),
        P(None, "dp"),
        P(None, "dp", None),
        P(None, "dp"),
        P(("dp", "seq"), None),
        P(("dp", "seq"), None),
    )
    out_specs = (
        P(("dp", "seq"), None),
        P(("dp", "seq"), None),
        P(("dp", "seq"), None),
        P(("dp", "seq"), None),
        P(None, "dp"),
        P(None, "dp"),
        P(None, "dp", "seq"),
        P(None, "dp"),
        P(None, "dp"),
        P(None, "dp", "seq"),
        P(None, "dp"),
        P(None, "dp"),
        P(None, "dp"),
        P(None, "dp", "seq"),
        P(None, "dp"),
        P(None, "dp", "seq"),
        P(None, "dp"),
    )
    return jax.shard_map(local, mesh=mesh, in_specs=in_specs, out_specs=out_specs, check_vma=False)
```

```python
from functools import partial

import jax
import jax.numpy as jnp
from jax import lax
from jax.experimental import pallas as pl
from jax.experimental.pallas import tpu as pltpu
from jax.sharding import PartitionSpec as P

HD = 64
LAYERS = 2
MOST = 280
KEEP_RATE = 0.9
EPSILON = 1e-06
MASKED = -1e30
GAIN_ONE, SHIFT_ONE, BIAS_QUERY, BIAS_VALUE, BIAS_PROJ, GAIN_TWO, SHIFT_TWO, BIAS_DOWN = range(8)
VECTOR_PIECES = 12
EXTRA_ROWS = 16
MIB = 1024 * 1024
ROOT_HALF = 0.7071067811865476
ROOT_TWO_PI = 0.3989422804014327
BF = jnp.bfloat16
F32 = jnp.float32


def dot_nn(left, right):
    return lax.dot_general(left, right, (((1,), (0,)), ((), ())), preferred_element_type=F32)


def dot_nt(left, right):
    return lax.dot_general(left, right, (((1,), (1,)), ((), ())), preferred_element_type=F32)


def dot_tn(left, right):
    return lax.dot_general(left, right, (((0,), (0,)), ((), ())), preferred_element_type=F32)


class Place:
    def __init__(self):
        self.n_dp = lax.axis_size("dp")
        self.n_seq = lax.axis_size("seq")
        self.walked = self.n_dp == 8 and self.n_seq == 4
        self.dp = lax.axis_index("dp")
        self.seq = lax.axis_index("seq")
        if self.walked:
            self.core = self.seq % 2
            self.y = self.seq // 2
            self.x = self.dp % 2
            self.z = self.dp // 2
            self.nz = self.n_dp // 2

    def swap_seq(self, values, mask):
        return lax.ppermute(values, "seq", [(i, i ^ mask) for i in range(self.n_seq)])

    def swap_x(self, values):
        return lax.ppermute(values, "dp", [(i, i ^ 1) for i in range(self.n_dp)])

    def ring_z(self, values, by=1):
        return lax.ppermute(values, "dp", [(i, (i + 2 * by) % self.n_dp) for i in range(self.n_dp)])


def gather_matrix(shard):
    return lax.all_gather(shard, "dp", axis=0, tiled=True)


def reduce_matrix(acts, grads):
    part = dot_tn(acts, grads).astype(BF)
    part = lax.psum_scatter(part, "dp", scatter_dimension=0, tiled=True)
    return lax.psum_scatter(part, "seq", scatter_dimension=1, tiled=True).astype(F32)


def reduce_vectors(place, vectors):
    packed = jnp.concatenate(
        [vector.reshape(place.n_dp, vector.shape[0] // place.n_dp) for vector in vectors], axis=1
    )
    mask = 1
    while mask < place.n_seq:
        packed = packed + place.swap_seq(packed, mask)
        mask *= 2
    packed = lax.all_to_all(packed, "dp", split_axis=0, concat_axis=0, tiled=True)
    total = jnp.sum(packed, axis=0)
    results, at = [], 0
    for vector in vectors:
        width = vector.shape[0] // place.n_dp
        results.append(total[at : at + width])
        at += width
    return results


def gather_vectors(place, shards):
    widths = [shard.shape[1] for shard in shards]
    packed = jnp.concatenate(shards, axis=1)
    rows = packed.shape[0]
    spread = jnp.broadcast_to(packed[None], (place.n_dp,) + packed.shape)
    spread = lax.all_to_all(spread, "dp", split_axis=0, concat_axis=0, tiled=True)
    results, at = [], 0
    for width in widths:
        piece = spread[:, :, at : at + width]
        results.append(jnp.transpose(piece, (1, 0, 2)).reshape(rows, place.n_dp * width).astype(F32))
        at += width
    return results


def normalize(values):
    center = values - jnp.mean(values, axis=-1, keepdims=True)
    spread = jnp.mean(center * center, axis=-1, keepdims=True)
    scale = lax.rsqrt(spread + EPSILON)
    return (center * scale, scale)


def normalize_back(hat, scale, gain, grad):
    scaled = grad * gain
    first = jnp.mean(scaled, axis=-1, keepdims=True)
    second = jnp.mean(scaled * hat, axis=-1, keepdims=True)
    back = scale * (scaled - first - hat * second)
    return (back, jnp.sum(grad * hat, axis=0), jnp.sum(grad, axis=0))


def heads_of(mixed):
    rows = mixed.shape[0]
    width = mixed.shape[1] // 3
    split = mixed.reshape(rows, 3, width // HD, HD)
    return (split[:, 0], split[:, 1], split[:, 2])


def attend(mixed, key_ok):
    queries, keys, values = heads_of(mixed)
    scores = jnp.einsum("qhd,khd->hqk", queries, keys, preferred_element_type=F32) * 0.125
    scores = jnp.where(key_ok[None, None, :], scores, MASKED)
    top = jnp.max(scores, axis=2, keepdims=True)
    powers = jnp.exp(scores - top)
    probs = powers / jnp.sum(powers, axis=2, keepdims=True)
    out = jnp.einsum("hqk,khd->qhd", probs.astype(BF), values, preferred_element_type=F32)
    return (out.reshape(mixed.shape[0], -1).astype(BF), probs)


def attend_back(mixed, probs, grad_out):
    queries, keys, values = heads_of(mixed)
    rows = mixed.shape[0]
    grads = grad_out.reshape(queries.shape)
    grad_probs = jnp.einsum("qhd,khd->hqk", grads, values, preferred_element_type=F32)
    inner = jnp.sum(probs * grad_probs, axis=2, keepdims=True)
    grad_scores = (probs * (grad_probs - inner)).astype(BF)
    grad_values = jnp.einsum("hqk,qhd->khd", probs.astype(BF), grads, preferred_element_type=F32)
    grad_queries = (
        jnp.einsum("hqk,khd->qhd", grad_scores, keys, preferred_element_type=F32) * 0.125
    )
    grad_keys = (
        jnp.einsum("hqk,qhd->khd", grad_scores, queries, preferred_element_type=F32) * 0.125
    )
    return jnp.concatenate(
        [grad.reshape(rows, -1).astype(BF) for grad in (grad_queries, grad_keys, grad_values)], axis=1
    )


def layer_forward(stream, vectors, matrices, keeps, key_ok):
    gain_one, shift_one, bias_query, bias_value, bias_proj, gain_two, shift_two, bias_down, bias_up = vectors
    w_mixed, w_proj, w_up, w_down = matrices
    hat_one, scale_one = normalize(stream)
    normed_one = (hat_one * gain_one + shift_one).astype(BF)
    bias_mixed = jnp.concatenate([bias_query, jnp.zeros_like(bias_query), bias_value])
    mixed = (dot_nn(normed_one, w_mixed) + bias_mixed).astype(BF)
    attended, probs = attend(mixed, key_ok)
    middle = stream + keeps[0] * (dot_nn(attended, w_proj) + bias_proj) / KEEP_RATE
    hat_two, scale_two = normalize(middle)
    normed_two = (hat_two * gain_two + shift_two).astype(BF)
    hidden_pre = dot_nn(normed_two, w_up) + bias_up
    share = 0.5 * (1.0 + lax.erf(hidden_pre * ROOT_HALF))
    hidden = (hidden_pre * share).astype(BF)
    slope = share + hidden_pre * jnp.exp(-0.5 * hidden_pre * hidden_pre) * ROOT_TWO_PI
    output = middle + keeps[1] * (dot_nn(hidden, w_down) + bias_down) / KEEP_RATE
    saved = (hat_one, scale_one, normed_one, mixed, probs, attended, hat_two, scale_two, normed_two, hidden, slope)
    return (output, saved)


def layer_back(place, grad_stream, saved, vectors, matrices, keeps):
    hat_one, scale_one, normed_one, mixed, probs, attended, hat_two, scale_two, normed_two, hidden, slope = saved
    gain_one, gain_two = (vectors[0], vectors[5])
    w_mixed, w_proj, w_up, w_down = matrices
    width = grad_stream.shape[1]
    grad_down = (keeps[1] * grad_stream / KEEP_RATE).astype(BF)
    total_down = reduce_matrix(hidden, grad_down)
    grad_up = (dot_nt(grad_down, w_down) * slope).astype(BF)
    total_up = reduce_matrix(normed_two, grad_up)
    back_two, grad_gain_two, grad_shift_two = normalize_back(
        hat_two, scale_two, gain_two, dot_nt(grad_up, w_up)
    )
    grad_middle = grad_stream + back_two
    grad_proj = (keeps[0] * grad_middle / KEEP_RATE).astype(BF)
    total_proj = reduce_matrix(attended, grad_proj)
    grad_attended = dot_nt(grad_proj, w_proj).astype(BF)
    grad_mixed = attend_back(mixed, probs, grad_attended)
    total_mixed = reduce_matrix(normed_one, grad_mixed)
    back_one, grad_gain_one, grad_shift_one = normalize_back(
        hat_one, scale_one, gain_one, dot_nt(grad_mixed, w_mixed)
    )
    grad_input = grad_middle + back_one
    sum_mixed = jnp.sum(grad_mixed, axis=0, dtype=F32)
    totals = reduce_vectors(
        place,
        (
            grad_gain_one,
            grad_shift_one,
            sum_mixed[:width],
            sum_mixed[2 * width :],
            jnp.sum(grad_proj, axis=0, dtype=F32),
            grad_gain_two,
            grad_shift_two,
            jnp.sum(grad_down, axis=0, dtype=F32),
            jnp.sum(grad_up, axis=0, dtype=F32),
        ),
    )
    return (grad_input, totals, (total_mixed, total_proj, total_up, total_down))


def shift_seq(place, values, by):
    count = place.n_seq
    return lax.ppermute(values, "seq", [(i, i + by) for i in range(count) if 0 <= i + by < count])


def to_image(place, patches, specials, halo, start, length, rows):
    count, width = patches.shape
    before = shift_seq(place, patches[count - halo :], 1)
    after = shift_seq(place, patches[:halo], -1)
    spare = jnp.zeros((MOST + 2 * halo - count - 2 * halo, width), patches.dtype)
    window = jnp.concatenate([before, patches, after, spare])
    image = lax.dynamic_slice_in_dim(window, start, MOST)
    inside = jnp.arange(MOST, dtype=jnp.int32)[:, None] < length
    image = jnp.where(inside, image, 0.0)
    spare = jnp.zeros((rows - MOST - specials.shape[0], width), patches.dtype)
    return jnp.concatenate([image, specials, spare])


def from_image(place, stream, halo, start, length, count, specials):
    width = stream.shape[1]
    inside = jnp.arange(MOST, dtype=jnp.int32)[:, None] < length
    image = jnp.where(inside, stream[:MOST], 0.0)
    window = jnp.zeros((MOST + 2 * halo, width), stream.dtype)
    window = lax.dynamic_update_slice_in_dim(window, image, start, 0)
    own = window[halo : halo + count]
    from_before = shift_seq(place, window[halo + count : count + 2 * halo], 1)
    from_after = shift_seq(place, window[:halo], -1)
    blank = jnp.zeros((count - halo, width), stream.dtype)
    own = own + jnp.concatenate([from_before, blank]) + jnp.concatenate([blank, from_after])
    return (own, stream[MOST : MOST + specials])


def local_plain(
    place,
    patches,
    specials,
    lengths,
    keep_mask,
    norm1_gain,
    norm1_bias,
    qkv_weight,
    query_bias,
    value_bias,
    proj_weight,
    proj_bias,
    norm2_gain,
    norm2_bias,
    fc1_weight,
    fc1_bias,
    fc2_weight,
    fc2_bias,
    cot_patches,
    cot_specials,
):
    count = patches.shape[0]
    special_count = specials.shape[0]
    images = lengths.shape[1]
    halo = (MOST - count) * (images // 2)
    rows = -(-(MOST + special_count) // 16) * 16
    before = jnp.sum(jnp.where(jnp.arange(images) < place.seq, lengths[0], 0))
    length = lax.dynamic_index_in_dim(lengths[0], place.seq, 0, keepdims=False)
    start = before - place.seq * count + halo
    keeps = lax.dynamic_index_in_dim(keep_mask[0], place.seq, 0, keepdims=False).astype(F32)
    row_ids = jnp.arange(rows, dtype=jnp.int32)
    key_ok = (row_ids < length) | ((row_ids >= MOST) & (row_ids < MOST + special_count))

    shards = (norm1_gain, norm1_bias, query_bias, value_bias, proj_bias, norm2_gain, norm2_bias, fc2_bias, fc1_bias)
    vectors_all = gather_vectors(place, shards)
    stream = to_image(place, patches, specials, halo, start, length, rows)
    matrices = []
    for layer in range(LAYERS):
        matrices.append(
            tuple(
                gather_matrix(shard[layer])
                for shard in (qkv_weight, proj_weight, fc1_weight, fc2_weight)
            )
        )
    vectors = [tuple(vector[layer] for vector in vectors_all) for layer in range(LAYERS)]
    saved = []
    for layer in range(LAYERS):
        stream, kept = layer_forward(
            stream, vectors[layer], matrices[layer], keeps[2 * layer : 2 * layer + 2], key_ok
        )
        saved.append(kept)
    out_patches, out_specials = from_image(place, stream, halo, start, length, count, special_count)
    grad = to_image(place, cot_patches, cot_specials, halo, start, length, rows)
    vector_totals, matrix_totals = ([None] * LAYERS, [None] * LAYERS)
    for layer in reversed(range(LAYERS)):
        grad, vector_totals[layer], matrix_totals[layer] = layer_back(
            place, grad, saved[layer], vectors[layer], matrices[layer], keeps[2 * layer : 2 * layer + 2]
        )
    grad_patches, grad_specials = from_image(place, grad, halo, start, length, count, special_count)
    vector_out = [jnp.stack([vector_totals[layer][i] for layer in range(LAYERS)]) for i in range(9)]
    matrix_out = [jnp.stack([matrix_totals[layer][i] for layer in range(LAYERS)]) for i in range(4)]
    g1, s1, bq, bv, bp, g2, s2, bd, bu = vector_out
    wm, wp, wu, wd = matrix_out
    return (
        out_patches,
        out_specials,
        grad_patches,
        grad_specials,
        g1,
        s1,
        wm,
        bq,
        bv,
        wp,
        bp,
        g2,
        s2,
        wu,
        bu,
        wd,
        bd,
    )


def whole_vmem(count):
    return [pl.BlockSpec(memory_space=pltpu.VMEM)] * count


def in_smem(count):
    return [pl.BlockSpec(memory_space=pltpu.SMEM)] * count


def kernel_params(mib):
    return pltpu.CompilerParams(vmem_limit_bytes=mib * MIB)


def place_pieces(spot, parts, chunks, crossed, split, extra, turned):
    z, x, y, core = (spot[i] for i in range(4))
    steps = sum(len(chunk) for chunk in chunks)
    first, rows = crossed.shape[2:4]
    quarter = split.shape[2] // 2
    more = 0 if extra is None else extra.shape[1]
    wide, piece = first * rows + more, quarter * rows
    block = wide + (piece if turned else 2 * piece)
    spots = {
        (0, 0): wide,
        (1, 0): block + wide if turned else wide + piece,
        (0, 1): 2 * wide + 2 * piece,
        (1, 1): 2 * wide + 3 * piece,
    }
    for side in range(2):
        at_core = core if side == 0 else 1 - core
        for step in range(steps):
            which = next(i for i, chunk in enumerate(chunks) if step in chunk)
            part = parts[side * len(chunks) + which]
            start = chunks[which].index(step) * (2 * wide + 4 * piece)
            at_z = lax.rem(z - step + steps, steps)
            for far_x in range(2):
                row = 2 * at_z + lax.rem(x + far_x, 2)
                base = start + far_x * block
                for j in range(first):
                    crossed[at_core, row, j] = part[base + j * rows : base + (j + 1) * rows]
                if extra is not None and side == 0:
                    extra[row] = part[base + first * rows : base + wide]
                for far_y in range(2):
                    base = start + spots[far_x, far_y]
                    for j in range(quarter):
                        split[at_core, row, lax.rem(y + far_y, 2) * quarter + j] = part[
                            base + j * rows : base + (j + 1) * rows
                        ]


def flat(block):
    return block.reshape(-1, block.shape[-1])


def moments(values):
    center = values - jnp.mean(values, axis=-1, keepdims=True)
    scale = lax.rsqrt(jnp.mean(center * center, axis=-1, keepdims=True) + EPSILON)
    return (center * scale, scale)


def norm_back(hat, scale, gain, grad):
    scaled = grad * gain
    first = jnp.mean(scaled, axis=-1, keepdims=True)
    second = jnp.mean(scaled * hat, axis=-1, keepdims=True)
    return scale * (scaled - first - hat * second)


def erf_of(values):
    v = jnp.clip(values, -3.7439211627767994, 3.7439211627767994)
    s = v * v
    top = s * 0.00022905065861350646 + 0.0034082910107109506
    top = top * s + 0.050955695062380861
    top = top * s + 0.18520832239976145
    top = top * s + 1.128379143519084
    low = s * -1.1791602954361697e-7 + 0.000023547966471313185
    low = low * s + 0.0010179625278914885
    low = low * s + 0.014070470171167667
    low = low * s + 0.11098505178285362
    low = low * s + 0.49746925110067538
    low = low * s + 1.0
    return v * top / low


def head_probs(queries, keys, blocked):
    scores = dot_nt(queries, keys) * 0.125 + blocked
    powers = jnp.exp(scores - jnp.max(scores, axis=1, keepdims=True))
    return powers / jnp.sum(powers, axis=1, keepdims=True)


def forward_attention_kernel(turned, chunks, spot, keep, stream, blocked, *refs):
    parts, refs = refs[: 2 * len(chunks)], refs[2 * len(chunks) :]
    middle, normed_two, normed_one_t, normed_two_t, mixed, attended, attended_t, crossed, split, vectors, bias_up, extra = refs
    place_pieces(spot, parts, chunks, crossed, split, extra, turned)
    rows = crossed.shape[3]
    each = extra.shape[2] // rows
    for row in range(extra.shape[0]):
        block = extra[row].astype(F32)
        for piece in range(VECTOR_PIECES):
            values = block[piece // each : piece // each + 1, (piece % each) * rows : (piece % each + 1) * rows]
            if piece < vectors.shape[0]:
                vectors[piece : piece + 1, row * rows : (row + 1) * rows] = values
            else:
                column = (row * (VECTOR_PIECES - vectors.shape[0]) + piece - vectors.shape[0]) * rows
                bias_up[:, column : column + rows] = values
    hat, _ = moments(stream[...])
    normed = (hat * vectors[GAIN_ONE : GAIN_ONE + 1] + vectors[SHIFT_ONE : SHIFT_ONE + 1]).astype(BF)
    normed_one_t[...] = normed.T
    width = stream.shape[1]
    half = width // 2
    for core in range(2):
        for j in range(3):
            weight = crossed[core, :, j] if j < 2 else split[core, :, 0]
            columns = pl.ds(j * width + core * half, half)
            ahead = dot_nn(normed, flat(weight))
            if j != 1:
                row = BIAS_QUERY if j == 0 else BIAS_VALUE
                ahead = ahead + vectors[row : row + 1, core * half : (core + 1) * half]
            mixed[:, columns] = ahead.astype(BF)
    lane = lax.broadcasted_iota(jnp.int32, (1, 2 * HD), 1)
    for pair in range(width // (2 * HD)):
        queries, keys, values = (
            mixed[:, pl.ds(j * width + pair * 2 * HD, 2 * HD)] for j in range(3)
        )
        outs = []
        for side in range(2):
            mine = ((lane < HD) if side == 0 else (lane >= HD)).astype(F32).astype(BF)
            probs = head_probs(queries * mine, keys, blocked[...])
            outs.append(dot_nn(probs.astype(BF), values))
        attended[:, pl.ds(pair * 2 * HD, 2 * HD)] = jnp.where(lane < HD, outs[0], outs[1]).astype(BF)
    ahead = attended[...]
    attended_t[...] = ahead.T
    for core in range(2):
        columns = pl.ds(core * half, half)
        branch = dot_nn(ahead, flat(split[core, :, 1])) + vectors[BIAS_PROJ : BIAS_PROJ + 1, columns]
        middle[:, columns] = stream[:, columns] + keep[0] * branch
    hat, _ = moments(middle[...])
    normed = (hat * vectors[GAIN_TWO : GAIN_TWO + 1] + vectors[SHIFT_TWO : SHIFT_TWO + 1]).astype(BF)
    normed_two[...] = normed
    normed_two_t[...] = normed.T


def forward_attention(place, spot, keep, stream, unit, blocked, extra_rows):
    parts = unit.parts()
    rows, width = stream.shape
    group = (width // place.n_dp, width // 2)
    shapes = [
        jax.ShapeDtypeStruct((rows, width), F32),
        jax.ShapeDtypeStruct((rows, width), BF),
        jax.ShapeDtypeStruct((width, rows), BF),
        jax.ShapeDtypeStruct((width, rows), BF),
        jax.ShapeDtypeStruct((rows, 3 * width), BF),
        jax.ShapeDtypeStruct((rows, width), BF),
        jax.ShapeDtypeStruct((width, rows), BF),
    ] + [jax.ShapeDtypeStruct((2, place.n_dp, 2) + group, BF)] * 2
    shapes += [
        jax.ShapeDtypeStruct((BIAS_DOWN + 1, width), F32),
        jax.ShapeDtypeStruct((1, 4 * width), F32),
    ]
    return pl.pallas_call(
        partial(forward_attention_kernel, unit.turned, unit.chunks),
        in_specs=in_smem(2) + whole_vmem(2 + len(parts)),
        out_specs=whole_vmem(len(shapes)),
        out_shape=shapes,
        scratch_shapes=[pltpu.VMEM((place.n_dp, extra_rows, width // 2), BF)],
        compiler_params=kernel_params(12),
        cost_estimate=pl.CostEstimate(flops=0, bytes_accessed=0, transcendentals=0),
        name="forward_attention",
    )(spot, keep, stream, blocked, *parts)


def forward_up_kernel(turned, chunks, spot, normed, bias_up, *refs):
    parts, refs = refs[: 2 * len(chunks)], refs[2 * len(chunks) :]
    hidden, slope, crossed, split = refs
    place_pieces(spot, parts, chunks, crossed, split, None, turned)
    values = normed[...]
    half = values.shape[1] // 2
    for core in range(2):
        for j in range(4):
            columns = pl.ds((core * 4 + j) * half, half)
            pre = dot_nn(values, flat(crossed[core, :, j])) + bias_up[:, columns]
            share = 0.5 + 0.5 * erf_of(pre * ROOT_HALF)
            hidden[:, columns] = (pre * share).astype(BF)
            slope[:, columns] = (share + pre * jnp.exp(-0.5 * pre * pre) * ROOT_TWO_PI).astype(BF)


def forward_up(place, spot, normed, bias_up, unit):
    parts = unit.parts()
    rows, width = normed.shape
    group = (width // place.n_dp, width // 2)
    return pl.pallas_call(
        partial(forward_up_kernel, unit.turned, unit.chunks),
        in_specs=in_smem(1) + whole_vmem(2 + len(parts)),
        out_specs=whole_vmem(4),
        out_shape=[jax.ShapeDtypeStruct((rows, 4 * width), BF)] * 2
        + [jax.ShapeDtypeStruct((2, place.n_dp, 4) + group, BF)] * 2,
        compiler_params=kernel_params(8),
        cost_estimate=pl.CostEstimate(flops=0, bytes_accessed=0, transcendentals=0),
        name="forward_up",
    )(spot, normed, bias_up, *parts)


def forward_down_kernel(keep, middle, hidden, vectors, split, output):
    ahead = hidden[...]
    half = middle.shape[1] // 2
    for core in range(2):
        columns = pl.ds(core * half, half)
        branch = dot_nn(ahead, flat(split[core])) + vectors[BIAS_DOWN : BIAS_DOWN + 1, columns]
        output[:, columns] = middle[:, columns] + keep[0] * branch


def forward_down(keep, middle, hidden, vectors, split):
    return pl.pallas_call(
        forward_down_kernel,
        in_specs=in_smem(1) + whole_vmem(4),
        out_specs=whole_vmem(1)[0],
        out_shape=jax.ShapeDtypeStruct(middle.shape, F32),
        compiler_params=kernel_params(8),
        cost_estimate=pl.CostEstimate(flops=0, bytes_accessed=0, transcendentals=0),
        name="forward_down",
    )(keep, middle, hidden, vectors, split)


def backward_feed_kernel(keep, grad, slope, split, grad_down_t, grad_up, sum_down, sum_up):
    down = (keep[0] * grad[...]).astype(BF)
    grad_down_t[...] = down.T
    sum_down[...] = jnp.sum(down.astype(F32), axis=0, keepdims=True)
    half = grad.shape[1] // 2
    for row in range(split.shape[1]):
        columns = pl.ds(row * half, half)
        ahead = dot_nt(down[:, :half], flat(split[0, row])) + dot_nt(down[:, half:], flat(split[1, row]))
        up = (ahead * slope[:, columns].astype(F32)).astype(BF)
        grad_up[:, columns] = up
        sum_up[:, columns] = jnp.sum(up.astype(F32), axis=0, keepdims=True)


def backward_feed(keep, grad, slope, split):
    rows, width = grad.shape
    shapes = [
        jax.ShapeDtypeStruct((width, rows), BF),
        jax.ShapeDtypeStruct((rows, 4 * width), BF),
        jax.ShapeDtypeStruct((1, width), F32),
        jax.ShapeDtypeStruct((1, 4 * width), F32),
    ]
    return pl.pallas_call(
        backward_feed_kernel,
        in_specs=in_smem(1) + whole_vmem(3),
        out_specs=whole_vmem(len(shapes)),
        out_shape=shapes,
        compiler_params=kernel_params(8),
        cost_estimate=pl.CostEstimate(flops=0, bytes_accessed=0, transcendentals=0),
        name="backward_feed",
    )(keep, grad, slope, split)


def backward_middle_kernel(keep, grad, grad_up, middle, vectors, crossed, *refs):
    grad_middle, grad_proj, sum_proj, grad_gain, grad_shift = refs
    hat, scale = moments(middle[...])
    half = grad.shape[1] // 2
    total = jnp.zeros(grad.shape, F32)
    for core in range(2):
        for j in range(4):
            total += dot_nt(grad_up[:, pl.ds((core * 4 + j) * half, half)], flat(crossed[core, :, j]))
    grad_gain[...] = jnp.sum(total * hat, axis=0, keepdims=True)
    grad_shift[...] = jnp.sum(total, axis=0, keepdims=True)
    after = grad[...] + norm_back(hat, scale, vectors[GAIN_TWO : GAIN_TWO + 1], total)
    grad_middle[...] = after
    proj = (keep[0] * after).astype(BF)
    grad_proj[...] = proj
    sum_proj[...] = jnp.sum(proj.astype(F32), axis=0, keepdims=True)


def backward_middle(keep, grad, grad_up, middle, vectors, crossed):
    rows, width = grad.shape
    shapes = [
        jax.ShapeDtypeStruct((rows, width), F32),
        jax.ShapeDtypeStruct((rows, width), BF),
    ] + [jax.ShapeDtypeStruct((1, width), F32)] * 3
    return pl.pallas_call(
        backward_middle_kernel,
        in_specs=in_smem(1) + whole_vmem(5),
        out_specs=whole_vmem(len(shapes)),
        out_shape=shapes,
        compiler_params=kernel_params(10),
        cost_estimate=pl.CostEstimate(flops=0, bytes_accessed=0, transcendentals=0),
        name="backward_middle",
    )(keep, grad, grad_up, middle, vectors, crossed)


def backward_feed_middle_kernel(keep_down, keep_up, grad, slope, split, middle, vectors, crossed, *refs):
    backward_feed_kernel(keep_down, grad, slope, split, *refs[:4])
    backward_middle_kernel(keep_up, grad, refs[1], middle, vectors, crossed, *refs[4:])


def backward_feed_middle(keep_down, keep_up, grad, slope, split, middle, vectors, crossed):
    rows, width = grad.shape
    shapes = [
        jax.ShapeDtypeStruct((width, rows), BF),
        jax.ShapeDtypeStruct((rows, 4 * width), BF),
        jax.ShapeDtypeStruct((1, width), F32),
        jax.ShapeDtypeStruct((1, 4 * width), F32),
        jax.ShapeDtypeStruct((rows, width), F32),
        jax.ShapeDtypeStruct((rows, width), BF),
    ] + [jax.ShapeDtypeStruct((1, width), F32)] * 3
    return pl.pallas_call(
        backward_feed_middle_kernel,
        in_specs=in_smem(2) + whole_vmem(6),
        out_specs=whole_vmem(len(shapes)),
        out_shape=shapes,
        compiler_params=kernel_params(12),
        name="backward_feed_middle",
    )(keep_down, keep_up, grad, slope, split, middle, vectors, crossed)


def backward_attention_kernel(grad_middle, grad_proj, mixed, stream, vectors, blocked, *refs):
    others, (crossed, split), refs = refs[:5], refs[5:7], refs[7:]
    grad_stream, grad_mixed, sums, ahead = refs
    sum_proj, gain_two, shift_two, sum_down, sum_up = others
    hat, scale = moments(stream[...])
    width = stream.shape[1]
    half = width // 2
    proj = grad_proj[...]
    ahead[...] = (
        dot_nt(proj[:, :half], flat(split[0, :, 1])) + dot_nt(proj[:, half:], flat(split[1, :, 1]))
    ).astype(BF)
    lane = lax.broadcasted_iota(jnp.int32, (1, 2 * HD), 1)
    for pair in range(width // (2 * HD)):
        queries, keys, values = (
            mixed[:, pl.ds(j * width + pair * 2 * HD, 2 * HD)] for j in range(3)
        )
        grads = ahead[:, pl.ds(pair * 2 * HD, 2 * HD)]
        found = []
        for side in range(2):
            mine = ((lane < HD) if side == 0 else (lane >= HD)).astype(F32).astype(BF)
            probs = head_probs(queries * mine, keys, blocked[...])
            grad_probs = dot_nt(grads * mine, values)
            inner = jnp.sum(probs * grad_probs, axis=1, keepdims=True)
            grad_scores = (probs * (grad_probs - inner)).astype(BF)
            found.append(
                (
                    dot_nn(grad_scores, keys) * 0.125,
                    dot_tn(grad_scores, queries) * 0.125,
                    dot_tn(probs.astype(BF), grads),
                )
            )
        for j in range(3):
            grad_mixed[:, pl.ds(j * width + pair * 2 * HD, 2 * HD)] = jnp.where(
                lane < HD, found[0][j], found[1][j]
            ).astype(BF)
    total = jnp.zeros(stream.shape, F32)
    for core in range(2):
        for j in range(3):
            weight = crossed[core, :, j] if j < 2 else split[core, :, 0]
            total += dot_nt(grad_mixed[:, pl.ds(j * width + core * half, half)], flat(weight))

    def put(row, values):
        sums[row : row + 1, :] = values

    put(GAIN_ONE, jnp.sum(total * hat, axis=0, keepdims=True))
    put(SHIFT_ONE, jnp.sum(total, axis=0, keepdims=True))
    put(BIAS_QUERY, jnp.sum(grad_mixed[:, :width].astype(F32), axis=0, keepdims=True))
    put(BIAS_VALUE, jnp.sum(grad_mixed[:, 2 * width :].astype(F32), axis=0, keepdims=True))
    put(BIAS_PROJ, sum_proj[...])
    put(GAIN_TWO, gain_two[...])
    put(SHIFT_TWO, shift_two[...])
    put(BIAS_DOWN, sum_down[...])
    for j in range(4):
        put(BIAS_DOWN + 1 + j, sum_up[:, j * width : (j + 1) * width])
    sums[BIAS_DOWN + 5 :, :] = jnp.zeros((sums.shape[0] - BIAS_DOWN - 5, width), F32)
    grad_stream[...] = grad_middle[...] + norm_back(hat, scale, vectors[GAIN_ONE : GAIN_ONE + 1], total)


def backward_attention(grad_middle, grad_proj, mixed, stream, vectors, blocked, others, crossed, split):
    rows, width = stream.shape
    shapes = [
        jax.ShapeDtypeStruct((rows, width), F32),
        jax.ShapeDtypeStruct((rows, 3 * width), BF),
        jax.ShapeDtypeStruct((16, width), F32),
    ]
    return pl.pallas_call(
        backward_attention_kernel,
        in_specs=whole_vmem(6 + 5 + 2),
        out_specs=whole_vmem(len(shapes)),
        out_shape=shapes,
        scratch_shapes=[pltpu.VMEM((rows, width), BF)],
        compiler_params=kernel_params(12),
        cost_estimate=pl.CostEstimate(flops=0, bytes_accessed=0, transcendentals=0),
        name="backward_attention",
    )(grad_middle, grad_proj, mixed, stream, vectors, blocked, *others, crossed, split)


def row_of(spot, step, far_x, steps):
    return 2 * lax.rem(spot[0] - step + steps, steps) + lax.rem(spot[1] + far_x, 2)


def feed_group(spot, core, part, far_y, at_z, normed_t, grad_up, grad_down_t, hidden, spare):
    count, wide, rows, half = spare.shape
    column = 2 * lax.rem(spot[2] + far_y, 2) + core
    if part == 0:
        left = normed_t[...] if at_z is None else normed_t[pl.ds(pl.multiple_of(at_z * 2 * rows, 2 * rows), 2 * rows), :]
        for j in range(wide):
            at = pl.multiple_of((column * wide + j) * half, half)
            out = dot_nn(left, grad_up[:, pl.ds(at, half)])
            spare[:, j] = out.reshape(count, rows, half).astype(BF)
    else:
        at = pl.multiple_of(column * wide * rows, wide * rows)
        left = grad_down_t[pl.ds(at, wide * rows), :]
        for row in range(count):
            columns = row * half if at_z is None else pl.multiple_of((at_z * 2 + row) * half, half)
            out = dot_nn(left, hidden[:, pl.ds(columns, half)])
            spare[row] = out.reshape(wide, rows, half).astype(BF)


def attention_group(spot, core, part, far_y, at_z, normed_t, grad_mixed, attended_t, grad_proj, spare):
    count, _, rows, half = spare.shape
    column = 2 * lax.rem(spot[2] + far_y, 2) + core
    if part == 0:
        out = dot_nn(normed_t[...], grad_mixed[column, :, :half])
    else:
        out = dot_nn(normed_t[...], grad_mixed[column, :, half:]) + dot_nn(
            attended_t[...], grad_proj[column]
        )
    spare[:, 0] = out.reshape(count, rows, half).astype(BF)


def each_group(fill, steps, ring, spot, core, operands, spare):
    wide = spare.shape[1]
    at_z = lax.rem(spot[0] - steps[0] + ring, ring) if len(steps) == 1 else None
    for part in range(2):
        for far_y in range(2):
            fill(spot, core, part, far_y, at_z, *operands, spare)
            for index, step in enumerate(steps):
                for far_x in range(2):
                    row = row_of(spot, step, far_x, ring) if at_z is None else lax.rem(spot[1] + far_x, 2)
                    for j in range(wide):
                        yield index, part, far_y, far_x, j, spare[row, j]


def place_in(part, far_y, far_x, j, wide):
    return (far_x * 2 + far_y) * wide + j if part == 0 else (4 + far_y * 2 + far_x) * wide + j


def sent_kernel(fill, steps, ring, spot, *refs):
    operands, out, spare = refs[:4], refs[4], refs[5]
    for index, part, far_y, far_x, j, block in each_group(fill, steps, ring, spot, 1 - spot[3], operands, spare):
        out[index, place_in(part, far_y, far_x, j, spare.shape[1])] = block


def kept_kernel(fill, steps, ring, spot, *refs):
    operands, got, outs, spare = refs[:4], refs[4], refs[5:-1], refs[-1]
    wide = spare.shape[1]
    for index, part, far_y, far_x, j, block in each_group(fill, steps, ring, spot, spot[3], operands, spare):
        total = block.astype(F32) + got[index, place_in(part, far_y, far_x, j, wide)].astype(F32)
        across, aside, stays = outs[3 * index : 3 * index + 3]
        if part == 0:
            at = far_y * wide + j
            target = across if far_x else stays
        else:
            at = far_x * wide + j
            target = aside if far_y else stays
            at = at if far_y else 2 * wide + at
        target[at] = total.astype(BF)


def spare_shape(place, steps, wide, rows, half):
    return pltpu.VMEM((2 if len(steps) == 1 else place.n_dp, wide, rows, half), BF)


def sent_part(place, spot, fill, wide, steps, operands):
    rows, half = (operands[0].shape[0] // place.n_dp, operands[0].shape[0] // 2)
    return pl.pallas_call(
        partial(sent_kernel, fill, steps, place.nz),
        in_specs=in_smem(1) + whole_vmem(4),
        out_specs=whole_vmem(1)[0],
        out_shape=jax.ShapeDtypeStruct((len(steps), 8 * wide, rows, half), BF),
        scratch_shapes=[spare_shape(place, steps, wide, rows, half)],
        compiler_params=kernel_params(10),
        cost_estimate=pl.CostEstimate(flops=0, bytes_accessed=0, transcendentals=0),
        name="gradient_sent",
    )(spot, *operands)


def kept_part(place, spot, fill, wide, steps, operands, got):
    rows, half = (operands[0].shape[0] // place.n_dp, operands[0].shape[0] // 2)
    shapes = [
        jax.ShapeDtypeStruct((size * wide, rows, half), BF) for _ in steps for size in (2, 2, 4)
    ]
    outs = pl.pallas_call(
        partial(kept_kernel, fill, steps, place.nz),
        in_specs=in_smem(1) + whole_vmem(5),
        out_specs=whole_vmem(len(shapes)),
        out_shape=shapes,
        scratch_shapes=[spare_shape(place, steps, wide, rows, half)],
        compiler_params=kernel_params(10),
        cost_estimate=pl.CostEstimate(flops=0, bytes_accessed=0, transcendentals=0),
        name="gradient_kept",
    )(spot, *operands, got)
    return {step: list(outs[3 * i : 3 * i + 3]) for i, step in enumerate(steps)}


def ring_kernel(stays, across, aside, *refs):
    out = refs[-1]
    count = across.shape[0]
    for at in range(2 * count):
        side = across[at] if at < count else aside[at - count]
        total = stays[at].astype(F32) + side.astype(F32)
        if len(refs) == 2:
            total = total + refs[0][at].astype(F32)
        out[at] = total.astype(BF)


def ring_block(stays, across, aside, running):
    operands = [stays, across, aside] + ([] if running is None else [running])
    return pl.pallas_call(
        ring_kernel,
        in_specs=whole_vmem(len(operands)),
        out_specs=whole_vmem(1)[0],
        out_shape=jax.ShapeDtypeStruct(stays.shape, BF),
        compiler_params=kernel_params(4),
        cost_estimate=pl.CostEstimate(flops=0, bytes_accessed=0, transcendentals=0),
        name="ring_block",
    )(*operands)


def fence(trees):
    flat = [list(tree.values()) if isinstance(tree, dict) else tree for tree in trees]
    flat = lax.optimization_barrier(flat)
    return [
        dict(zip(tree, values)) if isinstance(tree, dict) else values
        for tree, values in zip(trees, flat)
    ]


def pick(which, low, high):
    return jnp.where(which == 0, low, high)


def attention_groups(place, qkv, proj):
    half = proj.shape[1] // 2

    def of(core):
        parts = [qkv[:, (2 * j + core) * half : (2 * j + core + 1) * half] for j in range(3)]
        return jnp.stack(parts + [proj[:, core * half : (core + 1) * half]])

    return pick(place.core, of(0), of(1))


def feed_groups(place, up, down):
    rows, half = up.shape[0], down.shape[1] // 2

    def of(core):
        parts = [up[:, (core * 4 + j) * half : (core * 4 + j + 1) * half] for j in range(4)]
        return jnp.concatenate(
            [jnp.stack(parts), down[:, core * half : (core + 1) * half].reshape(4, rows, half)]
        )

    return pick(place.core, of(0), of(1))


class Gathered:
    def __init__(self, place, own, extra, turned, chunks):
        groups, rows, half = own.shape
        self.turned = turned
        self.chunks = chunks
        self.first = jnp.concatenate([own[: groups // 2].reshape(-1, half)] + extra)
        self.wide = self.first.shape[0]
        self.mine = pick(
            place.y,
            own[groups // 2 : groups // 2 + groups // 4],
            own[groups // 2 + groups // 4 :],
        ).reshape(-1, half)
        self.blocks = []
        self.across = {}
        self.aside = {}
        self.whole = []
        self.mate = []
        if turned:
            self.begin([])

    def begin(self, crossed):
        self.blocks.append(jnp.concatenate([self.first, self.mine] + crossed))

    def over_x(self, step):
        return self.blocks[step] if self.turned else self.blocks[step][: self.wide]

    def over_y(self, step):
        tails = [self.blocks[step][self.wide :]]
        if self.turned:
            tails.append(self.across[step][self.wide :])
        return tails

    def chunk(self, which, across, aside):
        return jnp.concatenate(
            [
                piece
                for step in self.chunks[which]
                for piece in (self.blocks[step], across.get(step), aside.get(step))
            ]
        )

    def parts(self):
        return self.whole + self.mate


class Reduced:
    def __init__(self, place):
        self.place = place
        self.operands = None
        self.kept = {}
        self.sides = {}
        self.running = None
        self.last = None

    def block(self, step):
        return ring_block(self.kept[step][2], *self.sides[step], self.running)


def pack_vectors(vectors, bias_up, half, rows):
    packed = jnp.concatenate(vectors + [bias_up]).reshape(-1, half)
    return jnp.pad(packed, ((0, rows - packed.shape[0]), (0, 0)))


def image_kernel(frame, before, patches, after, specials, out, window):
    halo, count = before.shape[0], patches.shape[0]
    window[:halo] = before[...]
    window[halo : halo + count] = patches[...]
    window[halo + count : 2 * halo + count] = after[...]
    spare = window.shape[0] - 2 * halo - count
    window[2 * halo + count :] = jnp.zeros((spare, window.shape[1]), F32)
    inside = lax.broadcasted_iota(jnp.int32, (MOST, 1), 0) < frame[1]
    turned = pltpu.roll(window[...], lax.rem(window.shape[0] - frame[0], window.shape[0]), 0)
    out[:MOST] = jnp.where(inside, turned[:MOST], 0.0)
    last = out.shape[0] - MOST
    out[MOST:] = jnp.zeros((last, out.shape[1]), F32)
    out[MOST : MOST + specials.shape[0]] = specials[...]


def take_image(place, frame, patches, specials, halo, rows):
    count, width = patches.shape
    before = shift_seq(place, patches[count - halo :], 1)
    after = shift_seq(place, patches[:halo], -1)

    def build(before, patches, after, specials):
        return pl.pallas_call(
            image_kernel,
            in_specs=in_smem(1) + whole_vmem(4),
            out_specs=whole_vmem(1)[0],
            out_shape=jax.ShapeDtypeStruct((rows, width), F32),
            scratch_shapes=[pltpu.VMEM((MOST + 2 * halo, width), F32)],
            compiler_params=kernel_params(6),
        cost_estimate=pl.CostEstimate(flops=0, bytes_accessed=0, transcendentals=0),
            name="take_image",
        )(frame, before, patches, after, specials)

    return (before, patches, after, specials), build


def block_kernel(frame, *refs):
    streams, (before, after), owns, window = refs[:2], refs[2:4], refs[4:8], refs[8]
    for at, stream in enumerate(streams):
        own, specials = owns[2 * at : 2 * at + 2]
        halo, count = before.shape[0] // 2, own.shape[0]
        window[MOST:] = jnp.zeros((window.shape[0] - MOST, window.shape[1]), F32)
        inside = lax.broadcasted_iota(jnp.int32, (MOST, 1), 0) < frame[1]
        window[:MOST] = jnp.where(inside, stream[:MOST], 0.0)
        window[...] = pltpu.roll(window[...], frame[0], 0)
        before[at * halo : (at + 1) * halo] = window[:halo]
        own[...] = window[halo : halo + count]
        after[at * halo : (at + 1) * halo] = window[halo + count : 2 * halo + count]
        specials[...] = stream[MOST : MOST + specials.shape[0]]


def give_images(frame, streams, halo, count, special_count):
    width = streams[0].shape[1]
    return pl.pallas_call(
        block_kernel,
        in_specs=in_smem(1) + whole_vmem(2),
        out_specs=whole_vmem(6),
        out_shape=[
            jax.ShapeDtypeStruct((size, width), F32)
            for size in (2 * halo, 2 * halo, count, special_count, count, special_count)
        ],
        scratch_shapes=[pltpu.VMEM((MOST + 2 * halo, width), F32)],
        compiler_params=kernel_params(6),
        cost_estimate=pl.CostEstimate(flops=0, bytes_accessed=0, transcendentals=0),
        name="give_images",
    )(frame, *streams)


def finish_kernel(*refs):
    spot, refs = refs[0], refs[1:]
    inputs, outs = refs[: 6 * LAYERS], refs[6 * LAYERS :]
    sums, (own_one, own_two, from_before, from_after), outs = outs[:4], outs[4:8], outs[8:]
    (out_mixed, out_proj, out_up, out_down), (image_one, image_two), out_rows = outs[:4], outs[4:6], outs[6:]
    halo = from_before.shape[0] // 2
    for at, (own, image) in enumerate(((own_one, image_one), (own_two, image_two))):
        count = own.shape[0]
        image[:halo] = own[:halo] + from_before[at * halo : (at + 1) * halo]
        image[halo : count - halo] = own[halo : count - halo]
        image[count - halo :] = own[count - halo :] + from_after[at * halo : (at + 1) * halo]
    layers = LAYERS
    total = sums[0][...]
    for other in sums[1:]:
        total = total + other[...]
    place_dp = 2 * spot[0] + spot[1]
    each, width = total.shape[0] // layers, total.shape[1]
    part = out_rows[0].shape[1]
    turned = pltpu.roll(total, lax.rem(width - place_dp * part, width), 1)
    more = VECTOR_PIECES - BIAS_DOWN - 1
    row_ids = lax.broadcasted_iota(jnp.int32, total.shape, 0)
    half_turned = pltpu.roll(total, lax.rem(width - lax.rem(place_dp * more * part, width), width), 1)
    for layer in range(layers):
        for row in range(BIAS_DOWN + 1):
            at = layer * each + row
            out_rows[row][layer : layer + 1, :] = turned[at : at + 1, :part]
        at = layer * each + BIAS_DOWN + 1 + place_dp * more * part // width
        row = jnp.sum(jnp.where(row_ids == at, half_turned, 0.0), axis=0, keepdims=True)
        out_rows[-1][layer : layer + 1, :] = row[:, : more * part]
    for layer in range(layers):
        last, aside, across = inputs[6 * layer : 6 * layer + 3]
        one = last[0].astype(F32) + aside[0].astype(F32)
        two = last[2].astype(F32) + across[0].astype(F32)
        cut = one.shape[1] // 2
        out_mixed[layer] = jnp.concatenate([one, two[:, :cut]], axis=1)
        out_proj[layer] = two[:, cut:]
        last, aside, across = inputs[6 * layer + 3 : 6 * layer + 6]
        half = last.shape[2]
        for j in range(2):
            out_up[layer, :, j * half : (j + 1) * half] = last[j].astype(F32) + aside[j].astype(F32)
        downs = [last[4 + j].astype(F32) + across[j].astype(F32) for j in range(2)]
        for j in range(2):
            out_down[layer, j * downs[j].shape[0] : (j + 1) * downs[j].shape[0]] = downs[j]


def finish(place, spot, parts, sums, images, rows, width):
    shapes = [
        jax.ShapeDtypeStruct((LAYERS, rows, columns), F32)
        for rows, columns in (
            (rows, 3 * width // 4),
            (rows, width // 4),
            (rows, width),
            (width // 4, 4 * rows),
        )
    ]
    shapes += [jax.ShapeDtypeStruct(images[0].shape, F32)] * 2
    more = VECTOR_PIECES - BIAS_DOWN - 1
    shapes += [jax.ShapeDtypeStruct((LAYERS, rows), F32)] * (BIAS_DOWN + 1)
    shapes += [jax.ShapeDtypeStruct((LAYERS, more * rows), F32)]
    flat_parts = [array for layer in parts for array in layer] + sums + images
    return pl.pallas_call(
        finish_kernel,
        in_specs=in_smem(1) + whole_vmem(len(flat_parts)),
        out_specs=whole_vmem(len(shapes)),
        out_shape=shapes,
        compiler_params=kernel_params(10),
        cost_estimate=pl.CostEstimate(flops=0, bytes_accessed=0, transcendentals=0),
        name="finish",
    )(spot, *flat_parts)


def local_walked(
    place,
    patches,
    specials,
    lengths,
    keep_mask,
    norm1_gain,
    norm1_bias,
    qkv_weight,
    query_bias,
    value_bias,
    proj_weight,
    proj_bias,
    norm2_gain,
    norm2_bias,
    fc1_weight,
    fc1_bias,
    fc2_weight,
    fc2_bias,
    cot_patches,
    cot_specials,
):
    count, width = patches.shape
    special_count = specials.shape[0]
    images = lengths.shape[1]
    halo = (MOST - count) * (images // 2)
    rows = -(-(MOST + special_count) // 16) * 16
    nz = place.nz
    pairs = ((0, 1), (2, 3))
    part_rows = proj_weight.shape[1]
    before = jnp.sum(jnp.where(jnp.arange(images) < place.seq, lengths[0], 0))
    length = lax.dynamic_index_in_dim(lengths[0], place.seq, 0, keepdims=False)
    frame = jnp.stack([before - place.seq * count + halo, length]).astype(jnp.int32)
    keeps = lax.dynamic_index_in_dim(keep_mask[0], place.seq, 0, keepdims=False).astype(F32)
    keeps = [keeps[i : i + 1] / KEEP_RATE for i in range(2 * LAYERS)]
    row_ids = jnp.arange(rows, dtype=jnp.int32)
    key_ok = (row_ids < length) | ((row_ids >= MOST) & (row_ids < MOST + special_count))
    blocked = jnp.where(key_ok, 0.0, MASKED).astype(F32)[None]
    spot = jnp.stack([place.z, place.x, place.y, place.core]).astype(jnp.int32)

    shards = (norm1_gain, norm1_bias, query_bias, value_bias, proj_bias, norm2_gain, norm2_bias, fc2_bias)

    def attention_unit(layer, qkv, proj):
        extra = pack_vectors([shard[layer] for shard in shards], fc1_bias[layer], width // 2, EXTRA_ROWS)
        return Gathered(place, attention_groups(place, qkv, proj), [extra], layer == 0, pairs)

    units = [attention_unit(0, qkv_weight[0], proj_weight[0])]
    image, build = take_image(place, frame, patches, specials, halo, rows)
    inputs = {
        "weights": (fc1_weight[0], fc2_weight[0], qkv_weight[1], proj_weight[1], fc1_weight[1], fc2_weight[1]),
        "cots": (cot_patches, cot_specials),
    }
    vectors, bias_up = ([None] * LAYERS, [None] * LAYERS)
    streams = [None] * (LAYERS + 1)
    middles, normed_one_ts, normed_two_ts, mixeds, attended_ts, hiddens, slopes = (
        [None] * LAYERS for _ in range(7)
    )
    weights = [None] * (2 * LAYERS)
    unit_count = 2 * LAYERS
    last_slot = 3 * unit_count + 1
    at_x, at_y = ([[] for _ in range(last_slot + 2)] for _ in range(2))
    for which in range(unit_count):
        for step in range(nz):
            slot = 3 * which + step
            at_x[slot].append((which, step))
            at_y[slot + (which == 0)].append((which, step))
    at_core = {4: [(0, 0)], 5: [(0, 1), (1, 0)], 7: [(1, 1)], 8: [(2, 0)], 10: [(2, 1)], 11: [(3, 0)], 12: [(3, 1)], 13: [(3, 2)]}
    carried = {}
    grad = None
    for slot in range(last_slot + 1):
        new = {}
        index, step = divmod(slot, 3)
        if index < unit_count:
            new["z"] = place.ring_z(units[index].blocks[step])
        for which, at in at_x[slot]:
            new["x", which, at] = place.swap_x(units[which].over_x(at))
        for which, at in at_y[slot]:
            tails = units[which].over_y(at)
            new["y", which, at] = place.swap_seq(tails[0] if len(tails) == 1 else jnp.concatenate(tails), 2)
        for which, at in at_core.get(slot, []):
            new["core", which, at] = place.swap_seq(units[which].whole[at], 1)
        for which, at in at_y[slot]:
            for index_of, chunk in enumerate(units[which].chunks):
                if chunk[-1] == at:
                    unit = units[which]
                    across = {**unit.across, **{k[2]: v for k, v in new.items() if k[:2] == ("x", which)}}
                    aside = {**unit.aside, **{k[2]: v for k, v in new.items() if k[:2] == ("y", which)}}
                    new["chunk", which, index_of] = unit.chunk(index_of, across, aside)
        later = {1: 1, 2: 2, 8: 3}.get(slot)
        if later:
            new["later"] = place.swap_x(units[later].mine)
        if slot == 0:
            new["image"] = image
        if slot == 5:
            carried["stream"] = build(*image)
        if slot == 3 * unit_count:
            new["image"], build = take_image(place, frame, *inputs["cots"], halo, rows)
        if slot == 3 * unit_count + 1:
            grad = build(*image)
        if slot in (9, 11):
            layer = slot // 11
            new["forward"] = forward_attention(
                place, spot, keeps[2 * layer], carried["stream"], units[2 * layer], blocked, EXTRA_ROWS
            )
        if slot == 10:
            hidden, slope, crossed, split = forward_up(place, spot, carried["normed"], bias_up[0], units[1])
            output = forward_down(keeps[1], carried["middle"], hidden, vectors[0], split)
            new["feed"] = (output, hidden, slope, crossed, split)
        if step == 2 and index + 1 < unit_count and units[index + 1].blocks:
            carried["begin"] = units[index + 1].blocks[0]
        gate = inputs if slot in (0, 3 * unit_count - 1) else {}
        new, carried, gate = fence((new, carried, gate))
        inputs.update(gate)
        if slot == 0:
            up_0, down_0, qkv_1, proj_1, up_1, down_1 = inputs.pop("weights")
            units.append(Gathered(place, feed_groups(place, up_0, down_0), [], False, pairs))
            units.append(attention_unit(1, qkv_1, proj_1))
            units.append(Gathered(place, feed_groups(place, up_1, down_1), [], False, ((0, 1), (2,), (3,))))
        if "begin" in carried:
            units[index + 1].blocks[0] = carried.pop("begin")
        if "image" in new:
            image = new["image"]
        if "later" in new:
            units[later].begin([new["later"]])
        if "z" in new:
            units[index].blocks.append(new["z"])
        for which, at in at_core.get(slot, []):
            units[which].mate.append(new["core", which, at])
        for which, at in at_x[slot]:
            units[which].across[at] = new["x", which, at]
        for which, at in at_y[slot]:
            units[which].aside[at] = new["y", which, at]
        for key in new:
            if key[0] == "chunk":
                units[key[1]].whole.append(new[key])
        if "forward" in new:
            streams[layer] = carried.pop("stream")
            middle, normed, normed_one_ts[layer], normed_two_ts[layer], mixeds[layer], _, attended_ts[layer], crossed, split, vectors[layer], bias_up[layer] = new["forward"]
            weights[2 * layer] = [crossed, split]
            middles[layer] = middle
            carried["middle"], carried["normed"] = middle, normed
        if "feed" in new:
            carried["stream"], hiddens[0], slopes[0], *weights[1] = new["feed"]
            del carried["middle"], carried["normed"]
    hiddens[1], slopes[1], *weights[3] = forward_up(
        place, spot, carried["normed"], bias_up[1], units[3]
    )

    reduces = [Reduced(place) for _ in range(2 * LAYERS)]
    lasts = [None] * (2 * LAYERS)
    back = [{} for _ in range(LAYERS)]

    def feed_back(layer, grad):
        found = back[layer]
        found["down_t"], found["up"], found["sum_down"], found["sum_up"] = backward_feed(
            keeps[2 * layer + 1], grad, slopes[layer], weights[2 * layer + 1][1]
        )

    def feed_operands(layer):
        reduces[2 * (LAYERS - 1 - layer)].operands = (
            normed_two_ts[layer], back[layer]["up"], back[layer]["down_t"], hiddens[layer]
        )

    def middle_back(layer, grad):
        found = back[layer]
        found["middle"], found["proj"], found["sum_proj"], found["gain"], found["shift"] = backward_middle(
            keeps[2 * layer], grad, found["up"], middles[layer], vectors[layer], weights[2 * layer + 1][0]
        )

    def attention_back(layer):
        found = back[layer]
        others = [found[name] for name in ("sum_proj", "gain", "shift", "sum_down", "sum_up")]
        found["grad"], found["mixed"], found["sums"] = backward_attention(
            found["middle"], found["proj"], mixeds[layer], streams[layer], vectors[layer], blocked, others, *weights[2 * layer]
        )

    def attention_operands(layer):
        found = back[layer]
        wide = 3 * width // 4
        cut = width // 4
        mixed = jnp.stack(
            [jnp.pad(found["mixed"][:, i * wide : (i + 1) * wide], ((0, 0), (0, cut))) for i in range(4)]
        )
        proj = jnp.stack([jnp.pad(found["proj"][:, i * cut : (i + 1) * cut], ((0, 0), (cut, 0))) for i in range(4)])
        unit = reduces[2 * (LAYERS - 1 - layer) + 1]
        unit.operands = (normed_one_ts[layer], mixed, attended_ts[layer], proj)

    fills = [(feed_group, 2), (attention_group, 1)] * LAYERS
    all_steps = (1, 2, 3, 0)
    cuts = [((1,), (2, 3, 0))] + [(all_steps,)] * (len(reduces) - 1)

    def sent_cut(which, cut):
        fill, wide = fills[which]
        return sent_part(place, spot, fill, wide, cuts[which][cut], reduces[which].operands)

    def keep_cut(which, cut, got):
        fill, wide = fills[which]
        unit = reduces[which]
        unit.kept.update(kept_part(place, spot, fill, wide, cuts[which][cut], unit.operands, got))

    feed_back(1, grad)
    feed_operands(1)
    sent = [sent_cut(0, 0), None]
    back[1], sent = fence((back[1], sent[:1]))
    final_slot = 3 * len(reduces)
    total = given = None
    rung = []
    got = {}
    sending = {(0, 0): sent[0]}
    for slot in range(-2, final_slot + 1):
        new = {}
        work = {}
        for which, unit in enumerate(reduces):
            at = slot - 3 * which
            if 0 <= at <= 2:
                new["z", which] = place.ring_z(unit.block(at + 1))
            if at == 3:
                unit.last = unit.block(0)
                work["last", which] = unit.last
        for base, group in ((final_slot - 2, range(len(reduces) - 1)), (final_slot, [len(reduces) - 1])):
            if slot == base:
                ends = [reduces[which].last for which in group]
                parts = [end.shape[0] // 4 for end in ends]
                aside = place.swap_seq(
                    jnp.concatenate([end[part : 2 * part] for end, part in zip(ends, parts)]), 2
                )
                across = place.swap_x(jnp.concatenate([end[3 * part :] for end, part in zip(ends, parts)]))
                begins = 0
                for which, end, part in zip(group, ends, parts):
                    lasts[which] = [end, aside[begins : begins + part], across[begins : begins + part]]
                    begins += part
                if slot < final_slot:
                    new["lasts"] = [lasts[which] for which in group]
        if slot == -2:
            sending[0, 1] = sent_cut(0, 1)
            work["sending"] = sending[0, 1]
        if slot == 0:
            keep_cut(0, 1, got.pop((0, 1)))
        if slot == -1:
            keep_cut(0, 0, got.pop((0, 0)))
        for which, base in ((1, 2), (2, 5), (3, 8)):
            if slot == base:
                keep_cut(which, 0, got.pop((which, 0)))
        for key, base in (((0, 0), -2), ((0, 1), -1), ((2, 0), 4), ((3, 0), 6)):
            if slot == base:
                new["core", key] = place.swap_seq(sending.pop(key), 1)
        for which, unit in enumerate(reduces):
            at = slot - 3 * which
            if -1 <= at <= 2:
                step = (at + 2) % nz
                new["side", which] = (
                    place.swap_x(unit.kept[step][0]),
                    place.swap_seq(unit.kept[step][1], 2),
                )
        if slot == 3:
            feed_operands(0)
            attention_operands(0)
            work["sending"] = (sent_cut(2, 0), sent_cut(3, 0))
        if slot == -1:
            middle_back(1, grad)
            streams[LAYERS] = forward_down(keeps[3], carried["middle"], hiddens[1], vectors[1], weights[3][1])
            work["output"] = streams[LAYERS]
        if slot == 0:
            attention_back(1)
        if slot == 1:
            attention_operands(1)
            new["core", (1, 0)] = place.swap_seq(sent_cut(1, 0), 1)
            names = ("down_t", "up", "sum_down", "sum_up", "middle", "proj", "sum_proj", "gain", "shift")
            back[0] = dict(
                zip(
                    names,
                    backward_feed_middle(
                        keeps[1], keeps[0], back[1]["grad"], slopes[0], weights[1][1], middles[0], vectors[0], weights[1][0]
                    ),
                )
            )
        if slot == 2:
            attention_back(0)
        if slot in (-1, 0):
            work["back", 1] = back[1]
        if slot in (1, 2):
            work["back", 0] = back[0]
        if slot == 3:
            total = jnp.concatenate([back[layer]["sums"] for layer in range(LAYERS)])
            new["sum"] = place.swap_seq(total, 1)
        if slot == 4:
            new["sum"] = place.swap_seq(total, 2)
        if slot == 6:
            new["sum"] = place.swap_x(total)
        if slot in (7, 9):
            new["ringing"] = [place.ring_z(total, by) for by in ((1,) if slot == 7 else (2, 3))]
        if slot == final_slot - 2:
            work["images"] = give_images(frame, given, halo, count, special_count)
        if slot == final_slot - 1:
            images_before, images_after, *owns = images
            new["images"] = (shift_seq(place, images_after, 1), shift_seq(place, images_before, -1))
        pending = {}
        for which, unit in enumerate(reduces):
            at = slot + 1 - 3 * which
            if 0 <= at <= 2:
                step = (at + 2) % nz
                if step in unit.kept:
                    pending["kept", which] = unit.kept[step]
        if slot == final_slot - 3:
            pending["give"] = [streams[LAYERS], back[0]["grad"]]
        for key, base in (((3, 0), 5),):
            if slot == base:
                pending["sending", key] = sending[key]
        for key, base in (((0, 1), 0), ((1, 0), 2), ((2, 0), 5), ((3, 0), 8)):
            if slot == base - 1 and key in got:
                pending["got", key] = got[key]
        new, work, pending = fence((new, work, pending))
        if "sending" in work:
            if slot == 3:
                sending[2, 0], sending[3, 0] = work.pop("sending")
            else:
                sending[0, 1] = work.pop("sending")
        for key in [key for key in pending if key[0] == "sending"]:
            sending[key[1]] = pending.pop(key)
        if "output" in work:
            streams[LAYERS] = work.pop("output")
        for key, value in work.items():
            if key[0] == "back":
                back[key[1]] = value
            if key[0] == "last":
                reduces[key[1]].last = value
            if key == "images":
                images = value
        if "give" in pending:
            given = pending.pop("give")
        for key in [key for key in pending if key[0] == "got"]:
            got[key[1]] = pending.pop(key)
        for key, value in pending.items():
            reduces[key[1]].kept[(slot + 1 - 3 * key[1] + 2) % nz] = value
        for key, value in new.items():
            if key[0] == "core":
                got[key[1]] = value
            if key[0] == "z":
                reduces[key[1]].running = value
            if key[0] == "side":
                reduces[key[1]].sides[(slot - 3 * key[1] + 2) % nz] = value
        if "images" in new:
            sides = new["images"]
        if "lasts" in new:
            lasts[: len(new["lasts"])] = new["lasts"]
        if "sum" in new:
            total = total + new["sum"]
        if "ringing" in new:
            rung += new["ringing"]

    wm, wp, wu, wd, out_patches, grad_patches, g1, s1, bq, bv, bp, g2, s2, bd, bu = finish(
        place,
        spot,
        [lasts[3] + lasts[2], lasts[1] + lasts[0]],
        [total] + rung,
        [owns[0], owns[2], *sides],
        part_rows,
        width,
    )
    wd = jnp.transpose(wd, (0, 2, 1))
    return (
        out_patches,
        owns[1],
        grad_patches,
        owns[3],
        g1,
        s1,
        wm,
        bq,
        bv,
        wp,
        bp,
        g2,
        s2,
        wu,
        bu,
        wd,
        bd,
    )


def local(*args):
    place = Place()
    if place.walked:
        return local_walked(place, *args)
    return local_plain(place, *args)


def solution(mesh):
    in_specs = (
        P(("dp", "seq"), None),
        P(("dp", "seq"), None),
        P("dp", None),
        P("dp", None, None),
        P(None, "dp"),
        P(None, "dp"),
        P(None, "dp", None),
        P(None, "dp"),
        P(None, "dp"),
        P(None, "dp", None),
        P(None, "dp"),
        P(None, "dp"),
        P(None, "dp"),
        P(None, "dp", None),
        P(None, "dp"),
        P(None, "dp", None),
        P(None, "dp"),
        P(("dp", "seq"), None),
        P(("dp", "seq"), None),
    )
    out_specs = (
        P(("dp", "seq"), None),
        P(("dp", "seq"), None),
        P(("dp", "seq"), None),
        P(("dp", "seq"), None),
        P(None, "dp"),
        P(None, "dp"),
        P(None, "dp", "seq"),
        P(None, "dp"),
        P(None, "dp"),
        P(None, "dp", "seq"),
        P(None, "dp"),
        P(None, "dp"),
        P(None, "dp"),
        P(None, "dp", "seq"),
        P(None, "dp"),
        P(None, "dp", "seq"),
        P(None, "dp"),
    )
    return jax.shard_map(local, mesh=mesh, in_specs=in_specs, out_specs=out_specs, check_vma=False)
```

```python
from functools import partial

import jax
import jax.numpy as jnp
from jax import lax
from jax.experimental import pallas as pl
from jax.experimental.pallas import tpu as pltpu
from jax.sharding import PartitionSpec as P

HD = 64
LAYERS = 2
MOST = 280
KEEP_RATE = 0.9
EPSILON = 1e-06
MASKED = -1e30
GAIN_ONE, SHIFT_ONE, BIAS_QUERY, BIAS_VALUE, BIAS_PROJ, GAIN_TWO, SHIFT_TWO, BIAS_DOWN = range(8)
VECTOR_PIECES = 12
EXTRA_ROWS = 16
MIB = 1024 * 1024
ROOT_HALF = 0.7071067811865476
ROOT_TWO_PI = 0.3989422804014327
BF = jnp.bfloat16
F32 = jnp.float32


def dot_nn(left, right):
    return lax.dot_general(left, right, (((1,), (0,)), ((), ())), preferred_element_type=F32)


def dot_nt(left, right):
    return lax.dot_general(left, right, (((1,), (1,)), ((), ())), preferred_element_type=F32)


def dot_tn(left, right):
    return lax.dot_general(left, right, (((0,), (0,)), ((), ())), preferred_element_type=F32)


class Place:
    def __init__(self):
        self.n_dp = lax.axis_size("dp")
        self.n_seq = lax.axis_size("seq")
        self.walked = self.n_dp == 8 and self.n_seq == 4
        self.dp = lax.axis_index("dp")
        self.seq = lax.axis_index("seq")
        if self.walked:
            self.core = self.seq % 2
            self.y = self.seq // 2
            self.x = self.dp % 2
            self.z = self.dp // 2
            self.nz = self.n_dp // 2

    def swap_seq(self, values, mask):
        return lax.ppermute(values, "seq", [(i, i ^ mask) for i in range(self.n_seq)])

    def swap_x(self, values):
        return lax.ppermute(values, "dp", [(i, i ^ 1) for i in range(self.n_dp)])

    def ring_z(self, values, by=1):
        return lax.ppermute(values, "dp", [(i, (i + 2 * by) % self.n_dp) for i in range(self.n_dp)])


def gather_matrix(shard):
    return lax.all_gather(shard, "dp", axis=0, tiled=True)


def reduce_matrix(acts, grads):
    part = dot_tn(acts, grads).astype(BF)
    part = lax.psum_scatter(part, "dp", scatter_dimension=0, tiled=True)
    return lax.psum_scatter(part, "seq", scatter_dimension=1, tiled=True).astype(F32)


def reduce_vectors(place, vectors):
    packed = jnp.concatenate(
        [vector.reshape(place.n_dp, vector.shape[0] // place.n_dp) for vector in vectors], axis=1
    )
    mask = 1
    while mask < place.n_seq:
        packed = packed + place.swap_seq(packed, mask)
        mask *= 2
    packed = lax.all_to_all(packed, "dp", split_axis=0, concat_axis=0, tiled=True)
    total = jnp.sum(packed, axis=0)
    results, at = [], 0
    for vector in vectors:
        width = vector.shape[0] // place.n_dp
        results.append(total[at : at + width])
        at += width
    return results


def gather_vectors(place, shards):
    widths = [shard.shape[1] for shard in shards]
    packed = jnp.concatenate(shards, axis=1)
    rows = packed.shape[0]
    spread = jnp.broadcast_to(packed[None], (place.n_dp,) + packed.shape)
    spread = lax.all_to_all(spread, "dp", split_axis=0, concat_axis=0, tiled=True)
    results, at = [], 0
    for width in widths:
        piece = spread[:, :, at : at + width]
        results.append(jnp.transpose(piece, (1, 0, 2)).reshape(rows, place.n_dp * width).astype(F32))
        at += width
    return results


def normalize(values):
    center = values - jnp.mean(values, axis=-1, keepdims=True)
    spread = jnp.mean(center * center, axis=-1, keepdims=True)
    scale = lax.rsqrt(spread + EPSILON)
    return (center * scale, scale)


def normalize_back(hat, scale, gain, grad):
    scaled = grad * gain
    first = jnp.mean(scaled, axis=-1, keepdims=True)
    second = jnp.mean(scaled * hat, axis=-1, keepdims=True)
    back = scale * (scaled - first - hat * second)
    return (back, jnp.sum(grad * hat, axis=0), jnp.sum(grad, axis=0))


def heads_of(mixed):
    rows = mixed.shape[0]
    width = mixed.shape[1] // 3
    split = mixed.reshape(rows, 3, width // HD, HD)
    return (split[:, 0], split[:, 1], split[:, 2])


def attend(mixed, key_ok):
    queries, keys, values = heads_of(mixed)
    scores = jnp.einsum("qhd,khd->hqk", queries, keys, preferred_element_type=F32) * 0.125
    scores = jnp.where(key_ok[None, None, :], scores, MASKED)
    top = jnp.max(scores, axis=2, keepdims=True)
    powers = jnp.exp(scores - top)
    probs = powers / jnp.sum(powers, axis=2, keepdims=True)
    out = jnp.einsum("hqk,khd->qhd", probs.astype(BF), values, preferred_element_type=F32)
    return (out.reshape(mixed.shape[0], -1).astype(BF), probs)


def attend_back(mixed, probs, grad_out):
    queries, keys, values = heads_of(mixed)
    rows = mixed.shape[0]
    grads = grad_out.reshape(queries.shape)
    grad_probs = jnp.einsum("qhd,khd->hqk", grads, values, preferred_element_type=F32)
    inner = jnp.sum(probs * grad_probs, axis=2, keepdims=True)
    grad_scores = (probs * (grad_probs - inner)).astype(BF)
    grad_values = jnp.einsum("hqk,qhd->khd", probs.astype(BF), grads, preferred_element_type=F32)
    grad_queries = (
        jnp.einsum("hqk,khd->qhd", grad_scores, keys, preferred_element_type=F32) * 0.125
    )
    grad_keys = (
        jnp.einsum("hqk,qhd->khd", grad_scores, queries, preferred_element_type=F32) * 0.125
    )
    return jnp.concatenate(
        [grad.reshape(rows, -1).astype(BF) for grad in (grad_queries, grad_keys, grad_values)], axis=1
    )


def layer_forward(stream, vectors, matrices, keeps, key_ok):
    gain_one, shift_one, bias_query, bias_value, bias_proj, gain_two, shift_two, bias_down, bias_up = vectors
    w_mixed, w_proj, w_up, w_down = matrices
    hat_one, scale_one = normalize(stream)
    normed_one = (hat_one * gain_one + shift_one).astype(BF)
    bias_mixed = jnp.concatenate([bias_query, jnp.zeros_like(bias_query), bias_value])
    mixed = (dot_nn(normed_one, w_mixed) + bias_mixed).astype(BF)
    attended, probs = attend(mixed, key_ok)
    middle = stream + keeps[0] * (dot_nn(attended, w_proj) + bias_proj) / KEEP_RATE
    hat_two, scale_two = normalize(middle)
    normed_two = (hat_two * gain_two + shift_two).astype(BF)
    hidden_pre = dot_nn(normed_two, w_up) + bias_up
    share = 0.5 * (1.0 + lax.erf(hidden_pre * ROOT_HALF))
    hidden = (hidden_pre * share).astype(BF)
    slope = share + hidden_pre * jnp.exp(-0.5 * hidden_pre * hidden_pre) * ROOT_TWO_PI
    output = middle + keeps[1] * (dot_nn(hidden, w_down) + bias_down) / KEEP_RATE
    saved = (hat_one, scale_one, normed_one, mixed, probs, attended, hat_two, scale_two, normed_two, hidden, slope)
    return (output, saved)


def layer_back(place, grad_stream, saved, vectors, matrices, keeps):
    hat_one, scale_one, normed_one, mixed, probs, attended, hat_two, scale_two, normed_two, hidden, slope = saved
    gain_one, gain_two = (vectors[0], vectors[5])
    w_mixed, w_proj, w_up, w_down = matrices
    width = grad_stream.shape[1]
    grad_down = (keeps[1] * grad_stream / KEEP_RATE).astype(BF)
    total_down = reduce_matrix(hidden, grad_down)
    grad_up = (dot_nt(grad_down, w_down) * slope).astype(BF)
    total_up = reduce_matrix(normed_two, grad_up)
    back_two, grad_gain_two, grad_shift_two = normalize_back(
        hat_two, scale_two, gain_two, dot_nt(grad_up, w_up)
    )
    grad_middle = grad_stream + back_two
    grad_proj = (keeps[0] * grad_middle / KEEP_RATE).astype(BF)
    total_proj = reduce_matrix(attended, grad_proj)
    grad_attended = dot_nt(grad_proj, w_proj).astype(BF)
    grad_mixed = attend_back(mixed, probs, grad_attended)
    total_mixed = reduce_matrix(normed_one, grad_mixed)
    back_one, grad_gain_one, grad_shift_one = normalize_back(
        hat_one, scale_one, gain_one, dot_nt(grad_mixed, w_mixed)
    )
    grad_input = grad_middle + back_one
    sum_mixed = jnp.sum(grad_mixed, axis=0, dtype=F32)
    totals = reduce_vectors(
        place,
        (
            grad_gain_one,
            grad_shift_one,
            sum_mixed[:width],
            sum_mixed[2 * width :],
            jnp.sum(grad_proj, axis=0, dtype=F32),
            grad_gain_two,
            grad_shift_two,
            jnp.sum(grad_down, axis=0, dtype=F32),
            jnp.sum(grad_up, axis=0, dtype=F32),
        ),
    )
    return (grad_input, totals, (total_mixed, total_proj, total_up, total_down))


def shift_seq(place, values, by):
    count = place.n_seq
    return lax.ppermute(values, "seq", [(i, i + by) for i in range(count) if 0 <= i + by < count])


def to_image(place, patches, specials, halo, start, length, rows):
    count, width = patches.shape
    before = shift_seq(place, patches[count - halo :], 1)
    after = shift_seq(place, patches[:halo], -1)
    spare = jnp.zeros((MOST + 2 * halo - count - 2 * halo, width), patches.dtype)
    window = jnp.concatenate([before, patches, after, spare])
    image = lax.dynamic_slice_in_dim(window, start, MOST)
    inside = jnp.arange(MOST, dtype=jnp.int32)[:, None] < length
    image = jnp.where(inside, image, 0.0)
    spare = jnp.zeros((rows - MOST - specials.shape[0], width), patches.dtype)
    return jnp.concatenate([image, specials, spare])


def from_image(place, stream, halo, start, length, count, specials):
    width = stream.shape[1]
    inside = jnp.arange(MOST, dtype=jnp.int32)[:, None] < length
    image = jnp.where(inside, stream[:MOST], 0.0)
    window = jnp.zeros((MOST + 2 * halo, width), stream.dtype)
    window = lax.dynamic_update_slice_in_dim(window, image, start, 0)
    own = window[halo : halo + count]
    from_before = shift_seq(place, window[halo + count : count + 2 * halo], 1)
    from_after = shift_seq(place, window[:halo], -1)
    blank = jnp.zeros((count - halo, width), stream.dtype)
    own = own + jnp.concatenate([from_before, blank]) + jnp.concatenate([blank, from_after])
    return (own, stream[MOST : MOST + specials])


def local_plain(
    place,
    patches,
    specials,
    lengths,
    keep_mask,
    norm1_gain,
    norm1_bias,
    qkv_weight,
    query_bias,
    value_bias,
    proj_weight,
    proj_bias,
    norm2_gain,
    norm2_bias,
    fc1_weight,
    fc1_bias,
    fc2_weight,
    fc2_bias,
    cot_patches,
    cot_specials,
):
    count = patches.shape[0]
    special_count = specials.shape[0]
    images = lengths.shape[1]
    halo = (MOST - count) * (images // 2)
    rows = -(-(MOST + special_count) // 16) * 16
    before = jnp.sum(jnp.where(jnp.arange(images) < place.seq, lengths[0], 0))
    length = lax.dynamic_index_in_dim(lengths[0], place.seq, 0, keepdims=False)
    start = before - place.seq * count + halo
    keeps = lax.dynamic_index_in_dim(keep_mask[0], place.seq, 0, keepdims=False).astype(F32)
    row_ids = jnp.arange(rows, dtype=jnp.int32)
    key_ok = (row_ids < length) | ((row_ids >= MOST) & (row_ids < MOST + special_count))

    shards = (norm1_gain, norm1_bias, query_bias, value_bias, proj_bias, norm2_gain, norm2_bias, fc2_bias, fc1_bias)
    vectors_all = gather_vectors(place, shards)
    stream = to_image(place, patches, specials, halo, start, length, rows)
    matrices = []
    for layer in range(LAYERS):
        matrices.append(
            tuple(
                gather_matrix(shard[layer])
                for shard in (qkv_weight, proj_weight, fc1_weight, fc2_weight)
            )
        )
    vectors = [tuple(vector[layer] for vector in vectors_all) for layer in range(LAYERS)]
    saved = []
    for layer in range(LAYERS):
        stream, kept = layer_forward(
            stream, vectors[layer], matrices[layer], keeps[2 * layer : 2 * layer + 2], key_ok
        )
        saved.append(kept)
    out_patches, out_specials = from_image(place, stream, halo, start, length, count, special_count)
    grad = to_image(place, cot_patches, cot_specials, halo, start, length, rows)
    vector_totals, matrix_totals = ([None] * LAYERS, [None] * LAYERS)
    for layer in reversed(range(LAYERS)):
        grad, vector_totals[layer], matrix_totals[layer] = layer_back(
            place, grad, saved[layer], vectors[layer], matrices[layer], keeps[2 * layer : 2 * layer + 2]
        )
    grad_patches, grad_specials = from_image(place, grad, halo, start, length, count, special_count)
    vector_out = [jnp.stack([vector_totals[layer][i] for layer in range(LAYERS)]) for i in range(9)]
    matrix_out = [jnp.stack([matrix_totals[layer][i] for layer in range(LAYERS)]) for i in range(4)]
    g1, s1, bq, bv, bp, g2, s2, bd, bu = vector_out
    wm, wp, wu, wd = matrix_out
    return (
        out_patches,
        out_specials,
        grad_patches,
        grad_specials,
        g1,
        s1,
        wm,
        bq,
        bv,
        wp,
        bp,
        g2,
        s2,
        wu,
        bu,
        wd,
        bd,
    )


def whole_vmem(count):
    return [pl.BlockSpec(memory_space=pltpu.VMEM)] * count


def in_smem(count):
    return [pl.BlockSpec(memory_space=pltpu.SMEM)] * count


def kernel_params(mib):
    return pltpu.CompilerParams(vmem_limit_bytes=mib * MIB)


def place_pieces(spot, parts, chunks, crossed, split, extra, turned):
    z, x, y, core = (spot[i] for i in range(4))
    steps = sum(len(chunk) for chunk in chunks)
    first, rows = crossed.shape[2:4]
    quarter = split.shape[2] // 2
    more = 0 if extra is None else extra.shape[1]
    wide, piece = first * rows + more, quarter * rows
    block = wide + (piece if turned else 2 * piece)
    spots = {
        (0, 0): wide,
        (1, 0): block + wide if turned else wide + piece,
        (0, 1): 2 * wide + 2 * piece,
        (1, 1): 2 * wide + 3 * piece,
    }
    for side in range(2):
        at_core = core if side == 0 else 1 - core
        for step in range(steps):
            which = next(i for i, chunk in enumerate(chunks) if step in chunk)
            part = parts[side * len(chunks) + which]
            start = chunks[which].index(step) * (2 * wide + 4 * piece)
            at_z = lax.rem(z - step + steps, steps)
            for far_x in range(2):
                row = 2 * at_z + lax.rem(x + far_x, 2)
                base = start + far_x * block
                for j in range(first):
                    crossed[at_core, row, j] = part[base + j * rows : base + (j + 1) * rows]
                if extra is not None and side == 0:
                    extra[row] = part[base + first * rows : base + wide]
                for far_y in range(2):
                    base = start + spots[far_x, far_y]
                    for j in range(quarter):
                        split[at_core, row, lax.rem(y + far_y, 2) * quarter + j] = part[
                            base + j * rows : base + (j + 1) * rows
                        ]


def keep_factor(spot, keep_mask, branch):
    return keep_mask[spot[4], branch].astype(F32) * (1.0 / KEEP_RATE)


def key_block(spot, lengths, rows, special_count):
    ids = lax.broadcasted_iota(jnp.int32, (1, rows), 1)
    inside = (ids < lengths[0, spot[4]]) | ((ids >= MOST) & (ids < MOST + special_count))
    return jnp.where(inside, 0.0, MASKED).astype(F32)


def image_frame(spot, lengths, count, halo):
    before = jnp.int32(0)
    for image in range(lengths.shape[1]):
        before = before + jnp.where(image < spot[4], lengths[0, image], 0)
    return before - spot[4] * count + halo, lengths[0, spot[4]]


def flat(block):
    return block.reshape(-1, block.shape[-1])


def moments(values):
    center = values - jnp.mean(values, axis=-1, keepdims=True)
    scale = lax.rsqrt(jnp.mean(center * center, axis=-1, keepdims=True) + EPSILON)
    return (center * scale, scale)


def norm_back(hat, scale, gain, grad):
    scaled = grad * gain
    first = jnp.mean(scaled, axis=-1, keepdims=True)
    second = jnp.mean(scaled * hat, axis=-1, keepdims=True)
    return scale * (scaled - first - hat * second)


def erf_of(values):
    v = jnp.clip(values, -3.7439211627767994, 3.7439211627767994)
    s = v * v
    top = s * 0.00022905065861350646 + 0.0034082910107109506
    top = top * s + 0.050955695062380861
    top = top * s + 0.18520832239976145
    top = top * s + 1.128379143519084
    low = s * -1.1791602954361697e-7 + 0.000023547966471313185
    low = low * s + 0.0010179625278914885
    low = low * s + 0.014070470171167667
    low = low * s + 0.11098505178285362
    low = low * s + 0.49746925110067538
    low = low * s + 1.0
    return v * top / low


def head_probs(queries, keys, blocked):
    scores = dot_nt(queries, keys) * 0.125 + blocked
    powers = jnp.exp(scores - jnp.max(scores, axis=1, keepdims=True))
    return powers / jnp.sum(powers, axis=1, keepdims=True)


def forward_attention_kernel(turned, chunks, branch, special_count, spot, lengths, keep_mask, stream, *refs):
    keep = keep_factor(spot, keep_mask, branch)
    blocked = key_block(spot, lengths, stream.shape[0], special_count)
    parts, refs = refs[: 2 * len(chunks)], refs[2 * len(chunks) :]
    middle, normed_two, normed_one_t, normed_two_t, mixed, attended, attended_t, crossed, split, vectors, bias_up, extra = refs
    place_pieces(spot, parts, chunks, crossed, split, extra, turned)
    rows = crossed.shape[3]
    for row in range(extra.shape[0]):
        block = extra[row].astype(F32)
        for piece in range(VECTOR_PIECES):
            values = block[piece : piece + 1, :rows]
            if piece < vectors.shape[0]:
                vectors[piece : piece + 1, row * rows : (row + 1) * rows] = values
            else:
                column = (row * (VECTOR_PIECES - vectors.shape[0]) + piece - vectors.shape[0]) * rows
                bias_up[:, column : column + rows] = values
    hat, _ = moments(stream[...])
    normed = (hat * vectors[GAIN_ONE : GAIN_ONE + 1] + vectors[SHIFT_ONE : SHIFT_ONE + 1]).astype(BF)
    normed_one_t[...] = normed.T
    width = stream.shape[1]
    half = width // 2
    for core in range(2):
        for j in range(3):
            weight = crossed[core, :, j] if j < 2 else split[core, :, 0]
            columns = pl.ds(j * width + core * half, half)
            ahead = dot_nn(normed, flat(weight))
            if j != 1:
                row = BIAS_QUERY if j == 0 else BIAS_VALUE
                ahead = ahead + vectors[row : row + 1, core * half : (core + 1) * half]
            mixed[:, columns] = ahead.astype(BF)
    lane = lax.broadcasted_iota(jnp.int32, (1, 2 * HD), 1)
    for pair in range(width // (2 * HD)):
        queries, keys, values = (
            mixed[:, pl.ds(j * width + pair * 2 * HD, 2 * HD)] for j in range(3)
        )
        outs = []
        for side in range(2):
            mine = ((lane < HD) if side == 0 else (lane >= HD)).astype(F32).astype(BF)
            probs = head_probs(queries * mine, keys, blocked)
            outs.append(dot_nn(probs.astype(BF), values))
        attended[:, pl.ds(pair * 2 * HD, 2 * HD)] = jnp.where(lane < HD, outs[0], outs[1]).astype(BF)
    ahead = attended[...]
    attended_t[...] = ahead.T
    for core in range(2):
        columns = pl.ds(core * half, half)
        added = dot_nn(ahead, flat(split[core, :, 1])) + vectors[BIAS_PROJ : BIAS_PROJ + 1, columns]
        middle[:, columns] = stream[:, columns] + keep * added
    hat, _ = moments(middle[...])
    normed = (hat * vectors[GAIN_TWO : GAIN_TWO + 1] + vectors[SHIFT_TWO : SHIFT_TWO + 1]).astype(BF)
    normed_two[...] = normed
    normed_two_t[...] = normed.T


def forward_attention(place, where, branch, special_count, stream, unit, extra_rows):
    parts = unit.parts()
    rows, width = stream.shape
    group = (width // place.n_dp, width // 2)
    shapes = [
        jax.ShapeDtypeStruct((rows, width), F32),
        jax.ShapeDtypeStruct((rows, width), BF),
        jax.ShapeDtypeStruct((width, rows), BF),
        jax.ShapeDtypeStruct((width, rows), BF),
        jax.ShapeDtypeStruct((rows, 3 * width), BF),
        jax.ShapeDtypeStruct((rows, width), BF),
        jax.ShapeDtypeStruct((width, rows), BF),
    ] + [jax.ShapeDtypeStruct((2, place.n_dp, 2) + group, BF)] * 2
    shapes += [
        jax.ShapeDtypeStruct((BIAS_DOWN + 1, width), F32),
        jax.ShapeDtypeStruct((1, 4 * width), F32),
    ]
    return pl.pallas_call(
        partial(forward_attention_kernel, unit.turned, unit.chunks, branch, special_count),
        in_specs=in_smem(3) + whole_vmem(1 + len(parts)),
        out_specs=whole_vmem(len(shapes)),
        out_shape=shapes,
        scratch_shapes=[pltpu.VMEM((place.n_dp, extra_rows, width // 2), BF)],
        compiler_params=kernel_params(12),
        cost_estimate=pl.CostEstimate(flops=0, bytes_accessed=0, transcendentals=0),
        name="forward_attention",
    )(*where, stream, *parts)


def forward_up_kernel(turned, chunks, spot, normed, bias_up, *refs):
    parts, refs = refs[: 2 * len(chunks)], refs[2 * len(chunks) :]
    hidden, slope, crossed, split = refs
    place_pieces(spot, parts, chunks, crossed, split, None, turned)
    values = normed[...]
    half = values.shape[1] // 2
    for core in range(2):
        for j in range(4):
            columns = pl.ds((core * 4 + j) * half, half)
            pre = dot_nn(values, flat(crossed[core, :, j])) + bias_up[:, columns]
            share = 0.5 + 0.5 * erf_of(pre * ROOT_HALF)
            hidden[:, columns] = (pre * share).astype(BF)
            slope[:, columns] = (share + pre * jnp.exp(-0.5 * pre * pre) * ROOT_TWO_PI).astype(BF)


def forward_up(place, spot, normed, bias_up, unit):
    parts = unit.parts()
    rows, width = normed.shape
    group = (width // place.n_dp, width // 2)
    return pl.pallas_call(
        partial(forward_up_kernel, unit.turned, unit.chunks),
        in_specs=in_smem(1) + whole_vmem(2 + len(parts)),
        out_specs=whole_vmem(4),
        out_shape=[jax.ShapeDtypeStruct((rows, 4 * width), BF)] * 2
        + [jax.ShapeDtypeStruct((2, place.n_dp, 4) + group, BF)] * 2,
        compiler_params=kernel_params(8),
        cost_estimate=pl.CostEstimate(flops=0, bytes_accessed=0, transcendentals=0),
        name="forward_up",
    )(spot, normed, bias_up, *parts)


def forward_down_kernel(branch, spot, keep_mask, middle, hidden, vectors, split, output):
    keep = keep_factor(spot, keep_mask, branch)
    ahead = hidden[...]
    half = middle.shape[1] // 2
    for core in range(2):
        columns = pl.ds(core * half, half)
        added = dot_nn(ahead, flat(split[core])) + vectors[BIAS_DOWN : BIAS_DOWN + 1, columns]
        output[:, columns] = middle[:, columns] + keep * added


def forward_down(where, branch, middle, hidden, vectors, split):
    return pl.pallas_call(
        partial(forward_down_kernel, branch),
        in_specs=in_smem(2) + whole_vmem(4),
        out_specs=whole_vmem(1)[0],
        out_shape=jax.ShapeDtypeStruct(middle.shape, F32),
        compiler_params=kernel_params(8),
        cost_estimate=pl.CostEstimate(flops=0, bytes_accessed=0, transcendentals=0),
        name="forward_down",
    )(where[0], where[2], middle, hidden, vectors, split)


def backward_feed_kernel(branch, spot, keep_mask, grad, slope, split, grad_down_t, grad_up, sum_down, sum_up):
    keep = keep_factor(spot, keep_mask, branch)
    down = (keep * grad[...]).astype(BF)
    grad_down_t[...] = down.T
    sum_down[...] = jnp.sum(down.astype(F32), axis=0, keepdims=True)
    half = grad.shape[1] // 2
    for row in range(split.shape[1]):
        columns = pl.ds(row * half, half)
        ahead = dot_nt(down[:, :half], flat(split[0, row])) + dot_nt(down[:, half:], flat(split[1, row]))
        up = (ahead * slope[:, columns].astype(F32)).astype(BF)
        grad_up[:, columns] = up
        sum_up[:, columns] = jnp.sum(up.astype(F32), axis=0, keepdims=True)


def backward_feed(where, branch, grad, slope, split):
    rows, width = grad.shape
    shapes = [
        jax.ShapeDtypeStruct((width, rows), BF),
        jax.ShapeDtypeStruct((rows, 4 * width), BF),
        jax.ShapeDtypeStruct((1, width), F32),
        jax.ShapeDtypeStruct((1, 4 * width), F32),
    ]
    return pl.pallas_call(
        partial(backward_feed_kernel, branch),
        in_specs=in_smem(2) + whole_vmem(3),
        out_specs=whole_vmem(len(shapes)),
        out_shape=shapes,
        compiler_params=kernel_params(8),
        cost_estimate=pl.CostEstimate(flops=0, bytes_accessed=0, transcendentals=0),
        name="backward_feed",
    )(where[0], where[2], grad, slope, split)


def backward_middle_kernel(branch, spot, keep_mask, grad, grad_up, middle, vectors, crossed, *refs):
    keep = keep_factor(spot, keep_mask, branch)
    grad_middle, grad_proj, sum_proj, grad_gain, grad_shift = refs
    hat, scale = moments(middle[...])
    half = grad.shape[1] // 2
    total = jnp.zeros(grad.shape, F32)
    for core in range(2):
        for j in range(4):
            total += dot_nt(grad_up[:, pl.ds((core * 4 + j) * half, half)], flat(crossed[core, :, j]))
    grad_gain[...] = jnp.sum(total * hat, axis=0, keepdims=True)
    grad_shift[...] = jnp.sum(total, axis=0, keepdims=True)
    after = grad[...] + norm_back(hat, scale, vectors[GAIN_TWO : GAIN_TWO + 1], total)
    grad_middle[...] = after
    proj = (keep * after).astype(BF)
    grad_proj[...] = proj
    sum_proj[...] = jnp.sum(proj.astype(F32), axis=0, keepdims=True)


def backward_middle(where, branch, grad, grad_up, middle, vectors, crossed):
    rows, width = grad.shape
    shapes = [
        jax.ShapeDtypeStruct((rows, width), F32),
        jax.ShapeDtypeStruct((rows, width), BF),
    ] + [jax.ShapeDtypeStruct((1, width), F32)] * 3
    return pl.pallas_call(
        partial(backward_middle_kernel, branch),
        in_specs=in_smem(2) + whole_vmem(5),
        out_specs=whole_vmem(len(shapes)),
        out_shape=shapes,
        compiler_params=kernel_params(10),
        cost_estimate=pl.CostEstimate(flops=0, bytes_accessed=0, transcendentals=0),
        name="backward_middle",
    )(where[0], where[2], grad, grad_up, middle, vectors, crossed)


def backward_feed_middle_kernel(branches, spot, keep_mask, grad, slope, split, middle, vectors, crossed, *refs):
    backward_feed_kernel(branches[1], spot, keep_mask, grad, slope, split, *refs[:4])
    backward_middle_kernel(branches[0], spot, keep_mask, grad, refs[1], middle, vectors, crossed, *refs[4:])


def backward_feed_middle(where, branches, grad, slope, split, middle, vectors, crossed):
    rows, width = grad.shape
    shapes = [
        jax.ShapeDtypeStruct((width, rows), BF),
        jax.ShapeDtypeStruct((rows, 4 * width), BF),
        jax.ShapeDtypeStruct((1, width), F32),
        jax.ShapeDtypeStruct((1, 4 * width), F32),
        jax.ShapeDtypeStruct((rows, width), F32),
        jax.ShapeDtypeStruct((rows, width), BF),
    ] + [jax.ShapeDtypeStruct((1, width), F32)] * 3
    return pl.pallas_call(
        partial(backward_feed_middle_kernel, branches),
        in_specs=in_smem(2) + whole_vmem(6),
        out_specs=whole_vmem(len(shapes)),
        out_shape=shapes,
        compiler_params=kernel_params(12),
        name="backward_feed_middle",
    )(where[0], where[2], grad, slope, split, middle, vectors, crossed)


def backward_attention_kernel(special_count, spot, lengths, grad_middle, grad_proj, mixed, stream, vectors, *refs):
    blocked = key_block(spot, lengths, stream.shape[0], special_count)
    others, (crossed, split), refs = refs[:5], refs[5:7], refs[7:]
    grad_stream, grad_mixed, sums, ahead = refs
    sum_proj, gain_two, shift_two, sum_down, sum_up = others
    hat, scale = moments(stream[...])
    width = stream.shape[1]
    half = width // 2
    proj = grad_proj[...]
    ahead[...] = (
        dot_nt(proj[:, :half], flat(split[0, :, 1])) + dot_nt(proj[:, half:], flat(split[1, :, 1]))
    ).astype(BF)
    lane = lax.broadcasted_iota(jnp.int32, (1, 2 * HD), 1)
    for pair in range(width // (2 * HD)):
        queries, keys, values = (
            mixed[:, pl.ds(j * width + pair * 2 * HD, 2 * HD)] for j in range(3)
        )
        grads = ahead[:, pl.ds(pair * 2 * HD, 2 * HD)]
        found = []
        for side in range(2):
            mine = ((lane < HD) if side == 0 else (lane >= HD)).astype(F32).astype(BF)
            probs = head_probs(queries * mine, keys, blocked)
            grad_probs = dot_nt(grads * mine, values)
            inner = jnp.sum(probs * grad_probs, axis=1, keepdims=True)
            grad_scores = (probs * (grad_probs - inner)).astype(BF)
            found.append(
                (
                    dot_nn(grad_scores, keys) * 0.125,
                    dot_tn(grad_scores, queries) * 0.125,
                    dot_tn(probs.astype(BF), grads),
                )
            )
        for j in range(3):
            grad_mixed[:, pl.ds(j * width + pair * 2 * HD, 2 * HD)] = jnp.where(
                lane < HD, found[0][j], found[1][j]
            ).astype(BF)
    total = jnp.zeros(stream.shape, F32)
    for core in range(2):
        for j in range(3):
            weight = crossed[core, :, j] if j < 2 else split[core, :, 0]
            total += dot_nt(grad_mixed[:, pl.ds(j * width + core * half, half)], flat(weight))

    def put(row, values):
        sums[row : row + 1, :] = values

    put(GAIN_ONE, jnp.sum(total * hat, axis=0, keepdims=True))
    put(SHIFT_ONE, jnp.sum(total, axis=0, keepdims=True))
    put(BIAS_QUERY, jnp.sum(grad_mixed[:, :width].astype(F32), axis=0, keepdims=True))
    put(BIAS_VALUE, jnp.sum(grad_mixed[:, 2 * width :].astype(F32), axis=0, keepdims=True))
    put(BIAS_PROJ, sum_proj[...])
    put(GAIN_TWO, gain_two[...])
    put(SHIFT_TWO, shift_two[...])
    put(BIAS_DOWN, sum_down[...])
    for j in range(4):
        put(BIAS_DOWN + 1 + j, sum_up[:, j * width : (j + 1) * width])
    sums[BIAS_DOWN + 5 :, :] = jnp.zeros((sums.shape[0] - BIAS_DOWN - 5, width), F32)
    grad_stream[...] = grad_middle[...] + norm_back(hat, scale, vectors[GAIN_ONE : GAIN_ONE + 1], total)


def backward_attention(where, special_count, grad_middle, grad_proj, mixed, stream, vectors, others, crossed, split):
    rows, width = stream.shape
    shapes = [
        jax.ShapeDtypeStruct((rows, width), F32),
        jax.ShapeDtypeStruct((rows, 3 * width), BF),
        jax.ShapeDtypeStruct((16, width), F32),
    ]
    return pl.pallas_call(
        partial(backward_attention_kernel, special_count),
        in_specs=in_smem(2) + whole_vmem(5 + 5 + 2),
        out_specs=whole_vmem(len(shapes)),
        out_shape=shapes,
        scratch_shapes=[pltpu.VMEM((rows, width), BF)],
        compiler_params=kernel_params(12),
        cost_estimate=pl.CostEstimate(flops=0, bytes_accessed=0, transcendentals=0),
        name="backward_attention",
    )(where[0], where[1], grad_middle, grad_proj, mixed, stream, vectors, *others, crossed, split)


def row_of(spot, step, far_x, steps):
    return 2 * lax.rem(spot[0] - step + steps, steps) + lax.rem(spot[1] + far_x, 2)


def feed_group(spot, core, part, far_y, at_z, normed_t, grad_up, grad_down_t, hidden, spare):
    count, wide, rows, half = spare.shape
    column = 2 * lax.rem(spot[2] + far_y, 2) + core
    if part == 0:
        left = normed_t[...] if at_z is None else normed_t[pl.ds(pl.multiple_of(at_z * 2 * rows, 2 * rows), 2 * rows), :]
        for j in range(wide):
            at = pl.multiple_of((column * wide + j) * half, half)
            out = dot_nn(left, grad_up[:, pl.ds(at, half)])
            spare[:, j] = out.reshape(count, rows, half).astype(BF)
    else:
        at = pl.multiple_of(column * wide * rows, wide * rows)
        left = grad_down_t[pl.ds(at, wide * rows), :]
        for row in range(count):
            columns = row * half if at_z is None else pl.multiple_of((at_z * 2 + row) * half, half)
            out = dot_nn(left, hidden[:, pl.ds(columns, half)])
            spare[row] = out.reshape(wide, rows, half).astype(BF)


def attention_group(spot, core, part, far_y, at_z, normed_t, grad_mixed, attended_t, grad_proj, spare):
    count, _, rows, half = spare.shape
    column = 2 * lax.rem(spot[2] + far_y, 2) + core
    if part == 0:
        out = dot_nn(normed_t[...], grad_mixed[column, :, :half])
    else:
        out = dot_nn(normed_t[...], grad_mixed[column, :, half:]) + dot_nn(
            attended_t[...], grad_proj[column]
        )
    spare[:, 0] = out.reshape(count, rows, half).astype(BF)


def each_group(fill, steps, ring, spot, core, operands, spare):
    wide = spare.shape[1]
    at_z = lax.rem(spot[0] - steps[0] + ring, ring) if len(steps) == 1 else None
    for part in range(2):
        for far_y in range(2):
            fill(spot, core, part, far_y, at_z, *operands, spare)
            for index, step in enumerate(steps):
                for far_x in range(2):
                    row = row_of(spot, step, far_x, ring) if at_z is None else lax.rem(spot[1] + far_x, 2)
                    for j in range(wide):
                        yield index, part, far_y, far_x, j, spare[row, j]


def place_in(part, far_y, far_x, j, wide):
    return (far_x * 2 + far_y) * wide + j if part == 0 else (4 + far_y * 2 + far_x) * wide + j


def sent_kernel(fill, steps, ring, spot, *refs):
    operands, out, spare = refs[:4], refs[4], refs[5]
    for index, part, far_y, far_x, j, block in each_group(fill, steps, ring, spot, 1 - spot[3], operands, spare):
        out[index, place_in(part, far_y, far_x, j, spare.shape[1])] = block


def kept_kernel(fill, steps, ring, spot, *refs):
    operands, got, outs, spare = refs[:4], refs[4], refs[5:-1], refs[-1]
    wide = spare.shape[1]
    for index, part, far_y, far_x, j, block in each_group(fill, steps, ring, spot, spot[3], operands, spare):
        total = block.astype(F32) + got[index, place_in(part, far_y, far_x, j, wide)].astype(F32)
        across, aside, stays = outs[3 * index : 3 * index + 3]
        if part == 0:
            at = far_y * wide + j
            target = across if far_x else stays
        else:
            at = far_x * wide + j
            target = aside if far_y else stays
            at = at if far_y else 2 * wide + at
        target[at] = total.astype(BF)


def spare_shape(place, steps, wide, rows, half):
    return pltpu.VMEM((2 if len(steps) == 1 else place.n_dp, wide, rows, half), BF)


def sent_part(place, spot, fill, wide, steps, operands):
    rows, half = (operands[0].shape[0] // place.n_dp, operands[0].shape[0] // 2)
    return pl.pallas_call(
        partial(sent_kernel, fill, steps, place.nz),
        in_specs=in_smem(1) + whole_vmem(4),
        out_specs=whole_vmem(1)[0],
        out_shape=jax.ShapeDtypeStruct((len(steps), 8 * wide, rows, half), BF),
        scratch_shapes=[spare_shape(place, steps, wide, rows, half)],
        compiler_params=kernel_params(10),
        cost_estimate=pl.CostEstimate(flops=0, bytes_accessed=0, transcendentals=0),
        name="gradient_sent",
    )(spot, *operands)


def kept_part(place, spot, fill, wide, steps, operands, got):
    rows, half = (operands[0].shape[0] // place.n_dp, operands[0].shape[0] // 2)
    shapes = [
        jax.ShapeDtypeStruct((size * wide, rows, half), BF) for _ in steps for size in (2, 2, 4)
    ]
    outs = pl.pallas_call(
        partial(kept_kernel, fill, steps, place.nz),
        in_specs=in_smem(1) + whole_vmem(5),
        out_specs=whole_vmem(len(shapes)),
        out_shape=shapes,
        scratch_shapes=[spare_shape(place, steps, wide, rows, half)],
        compiler_params=kernel_params(10),
        cost_estimate=pl.CostEstimate(flops=0, bytes_accessed=0, transcendentals=0),
        name="gradient_kept",
    )(spot, *operands, got)
    return {step: list(outs[3 * i : 3 * i + 3]) for i, step in enumerate(steps)}


def ring_kernel(stays, across, aside, *refs):
    out = refs[-1]
    count = across.shape[0]
    for at in range(2 * count):
        side = across[at] if at < count else aside[at - count]
        total = stays[at].astype(F32) + side.astype(F32)
        if len(refs) == 2:
            total = total + refs[0][at].astype(F32)
        out[at] = total.astype(BF)


def ring_block(stays, across, aside, running):
    operands = [stays, across, aside] + ([] if running is None else [running])
    return pl.pallas_call(
        ring_kernel,
        in_specs=whole_vmem(len(operands)),
        out_specs=whole_vmem(1)[0],
        out_shape=jax.ShapeDtypeStruct(stays.shape, BF),
        compiler_params=kernel_params(4),
        cost_estimate=pl.CostEstimate(flops=0, bytes_accessed=0, transcendentals=0),
        name="ring_block",
    )(*operands)


def fence(trees):
    flat = [list(tree.values()) if isinstance(tree, dict) else tree for tree in trees]
    flat = lax.optimization_barrier(flat)
    return [
        dict(zip(tree, values)) if isinstance(tree, dict) else values
        for tree, values in zip(trees, flat)
    ]


def pick(which, low, high):
    return jnp.where(which == 0, low, high)


def attention_groups(place, qkv, proj):
    half = proj.shape[1] // 2

    def of(core):
        parts = [qkv[:, (2 * j + core) * half : (2 * j + core + 1) * half] for j in range(3)]
        return jnp.stack(parts + [proj[:, core * half : (core + 1) * half]])

    return pick(place.core, of(0), of(1))


def feed_groups(place, up, down):
    rows, half = up.shape[0], down.shape[1] // 2

    def of(core):
        parts = [up[:, (core * 4 + j) * half : (core * 4 + j + 1) * half] for j in range(4)]
        return jnp.concatenate(
            [jnp.stack(parts), down[:, core * half : (core + 1) * half].reshape(4, rows, half)]
        )

    return pick(place.core, of(0), of(1))


class Gathered:
    def __init__(self, place, own, extra, turned, chunks):
        groups, rows, half = own.shape
        self.turned = turned
        self.chunks = chunks
        self.first = jnp.concatenate([own[: groups // 2].reshape(-1, half)] + extra)
        self.wide = self.first.shape[0]
        self.mine = pick(
            place.y,
            own[groups // 2 : groups // 2 + groups // 4],
            own[groups // 2 + groups // 4 :],
        ).reshape(-1, half)
        self.blocks = []
        self.across = {}
        self.aside = {}
        self.whole = []
        self.mate = []
        if turned:
            self.begin([])

    def begin(self, crossed):
        self.blocks.append(jnp.concatenate([self.first, self.mine] + crossed))

    def over_x(self, step):
        return self.blocks[step] if self.turned else self.blocks[step][: self.wide]

    def over_y(self, step):
        tails = [self.blocks[step][self.wide :]]
        if self.turned:
            tails.append(self.across[step][self.wide :])
        return tails

    def chunk(self, which, across, aside):
        return jnp.concatenate(
            [
                piece
                for step in self.chunks[which]
                for piece in (self.blocks[step], across.get(step), aside.get(step))
            ]
        )

    def parts(self):
        return self.whole + self.mate


class Reduced:
    def __init__(self, place):
        self.place = place
        self.operands = None
        self.kept = {}
        self.sides = {}
        self.running = None
        self.last = None

    def block(self, step):
        return ring_block(self.kept[step][2], *self.sides[step], self.running)


def pack_vectors(vectors, bias_up, half, rows):
    layers, part = vectors[0].shape
    packed = jnp.concatenate([jnp.stack(vectors, axis=1), bias_up.reshape(layers, -1, part)], axis=1)
    return jnp.pad(packed, ((0, 0), (0, rows - packed.shape[1]), (0, half - part)))


def image_kernel(spot, lengths, before, patches, after, specials, out, window):
    halo, count = before.shape[0], patches.shape[0]
    begin, length = image_frame(spot, lengths, count, halo)
    window[:halo] = before[...]
    window[halo : halo + count] = patches[...]
    window[halo + count : 2 * halo + count] = after[...]
    spare = window.shape[0] - 2 * halo - count
    window[2 * halo + count :] = jnp.zeros((spare, window.shape[1]), F32)
    inside = lax.broadcasted_iota(jnp.int32, (MOST, 1), 0) < length
    turned = pltpu.roll(window[...], lax.rem(window.shape[0] - begin, window.shape[0]), 0)
    out[:MOST] = jnp.where(inside, turned[:MOST], 0.0)
    last = out.shape[0] - MOST
    out[MOST:] = jnp.zeros((last, out.shape[1]), F32)
    out[MOST : MOST + specials.shape[0]] = specials[...]


def take_image(place, where, patches, specials, halo, rows):
    count, width = patches.shape
    before = shift_seq(place, patches[count - halo :], 1)
    after = shift_seq(place, patches[:halo], -1)

    def build(before, patches, after, specials):
        return pl.pallas_call(
            image_kernel,
            in_specs=in_smem(2) + whole_vmem(4),
            out_specs=whole_vmem(1)[0],
            out_shape=jax.ShapeDtypeStruct((rows, width), F32),
            scratch_shapes=[pltpu.VMEM((MOST + 2 * halo, width), F32)],
            compiler_params=kernel_params(6),
        cost_estimate=pl.CostEstimate(flops=0, bytes_accessed=0, transcendentals=0),
            name="take_image",
        )(where[0], where[1], before, patches, after, specials)

    return (before, patches, after, specials), build


def block_kernel(spot, lengths, *refs):
    streams, (before, after), owns, window = refs[:2], refs[2:4], refs[4:8], refs[8]
    for at, stream in enumerate(streams):
        own, specials = owns[2 * at : 2 * at + 2]
        halo, count = before.shape[0] // 2, own.shape[0]
        begin, length = image_frame(spot, lengths, count, halo)
        window[MOST:] = jnp.zeros((window.shape[0] - MOST, window.shape[1]), F32)
        inside = lax.broadcasted_iota(jnp.int32, (MOST, 1), 0) < length
        window[:MOST] = jnp.where(inside, stream[:MOST], 0.0)
        window[...] = pltpu.roll(window[...], begin, 0)
        before[at * halo : (at + 1) * halo] = window[:halo]
        own[...] = window[halo : halo + count]
        after[at * halo : (at + 1) * halo] = window[halo + count : 2 * halo + count]
        specials[...] = stream[MOST : MOST + specials.shape[0]]


def give_images(where, streams, halo, count, special_count):
    width = streams[0].shape[1]
    return pl.pallas_call(
        block_kernel,
        in_specs=in_smem(2) + whole_vmem(2),
        out_specs=whole_vmem(6),
        out_shape=[
            jax.ShapeDtypeStruct((size, width), F32)
            for size in (2 * halo, 2 * halo, count, special_count, count, special_count)
        ],
        scratch_shapes=[pltpu.VMEM((MOST + 2 * halo, width), F32)],
        compiler_params=kernel_params(6),
        cost_estimate=pl.CostEstimate(flops=0, bytes_accessed=0, transcendentals=0),
        name="give_images",
    )(where[0], where[1], *streams)


def finish_kernel(*refs):
    spot, refs = refs[0], refs[1:]
    inputs, outs = refs[: 6 * LAYERS], refs[6 * LAYERS :]
    sums, (own_one, own_two, from_before, from_after), outs = outs[:4], outs[4:8], outs[8:]
    (out_mixed, out_proj, out_up, out_down), (image_one, image_two), out_rows = outs[:4], outs[4:6], outs[6:]
    halo = from_before.shape[0] // 2
    for at, (own, image) in enumerate(((own_one, image_one), (own_two, image_two))):
        count = own.shape[0]
        image[:halo] = own[:halo] + from_before[at * halo : (at + 1) * halo]
        image[halo : count - halo] = own[halo : count - halo]
        image[count - halo :] = own[count - halo :] + from_after[at * halo : (at + 1) * halo]
    layers = LAYERS
    total = sums[0][...]
    for other in sums[1:]:
        total = total + other[...]
    place_dp = 2 * spot[0] + spot[1]
    each, width = total.shape[0] // layers, total.shape[1]
    part = out_rows[0].shape[1]
    turned = pltpu.roll(total, lax.rem(width - place_dp * part, width), 1)
    more = VECTOR_PIECES - BIAS_DOWN - 1
    row_ids = lax.broadcasted_iota(jnp.int32, total.shape, 0)
    half_turned = pltpu.roll(total, lax.rem(width - lax.rem(place_dp * more * part, width), width), 1)
    for layer in range(layers):
        for row in range(BIAS_DOWN + 1):
            at = layer * each + row
            out_rows[row][layer : layer + 1, :] = turned[at : at + 1, :part]
        at = layer * each + BIAS_DOWN + 1 + place_dp * more * part // width
        row = jnp.sum(jnp.where(row_ids == at, half_turned, 0.0), axis=0, keepdims=True)
        out_rows[-1][layer : layer + 1, :] = row[:, : more * part]
    for layer in range(layers):
        last, aside, across = inputs[6 * layer : 6 * layer + 3]
        one = last[0].astype(F32) + aside[0].astype(F32)
        two = last[2].astype(F32) + across[0].astype(F32)
        cut = one.shape[1] // 2
        out_mixed[layer] = jnp.concatenate([one, two[:, :cut]], axis=1)
        out_proj[layer] = two[:, cut:]
        last, aside, across = inputs[6 * layer + 3 : 6 * layer + 6]
        half = last.shape[2]
        for j in range(2):
            out_up[layer, :, j * half : (j + 1) * half] = last[j].astype(F32) + aside[j].astype(F32)
        downs = [last[4 + j].astype(F32) + across[j].astype(F32) for j in range(2)]
        for j in range(2):
            out_down[layer, j * downs[j].shape[0] : (j + 1) * downs[j].shape[0]] = downs[j]


def finish(place, spot, parts, sums, images, rows, width):
    shapes = [
        jax.ShapeDtypeStruct((LAYERS, rows, columns), F32)
        for rows, columns in (
            (rows, 3 * width // 4),
            (rows, width // 4),
            (rows, width),
            (width // 4, 4 * rows),
        )
    ]
    shapes += [jax.ShapeDtypeStruct(images[0].shape, F32)] * 2
    more = VECTOR_PIECES - BIAS_DOWN - 1
    shapes += [jax.ShapeDtypeStruct((LAYERS, rows), F32)] * (BIAS_DOWN + 1)
    shapes += [jax.ShapeDtypeStruct((LAYERS, more * rows), F32)]
    flat_parts = [array for layer in parts for array in layer] + sums + images
    return pl.pallas_call(
        finish_kernel,
        in_specs=in_smem(1) + whole_vmem(len(flat_parts)),
        out_specs=whole_vmem(len(shapes)),
        out_shape=shapes,
        compiler_params=kernel_params(10),
        cost_estimate=pl.CostEstimate(flops=0, bytes_accessed=0, transcendentals=0),
        name="finish",
    )(spot, *flat_parts)


def local_walked(
    place,
    patches,
    specials,
    lengths,
    keep_mask,
    norm1_gain,
    norm1_bias,
    qkv_weight,
    query_bias,
    value_bias,
    proj_weight,
    proj_bias,
    norm2_gain,
    norm2_bias,
    fc1_weight,
    fc1_bias,
    fc2_weight,
    fc2_bias,
    cot_patches,
    cot_specials,
):
    count, width = patches.shape
    special_count = specials.shape[0]
    images = lengths.shape[1]
    halo = (MOST - count) * (images // 2)
    rows = -(-(MOST + special_count) // 16) * 16
    nz = place.nz
    pairs = ((0, 1), (2, 3))
    part_rows = proj_weight.shape[1]
    spot = jnp.stack([place.z, place.x, place.y, place.core, place.seq]).astype(jnp.int32)
    where = (spot, lengths, keep_mask[0])

    shards = (norm1_gain, norm1_bias, query_bias, value_bias, proj_bias, norm2_gain, norm2_bias, fc2_bias)

    extras = pack_vectors(list(shards), fc1_bias, width // 2, EXTRA_ROWS)

    def attention_unit(layer, qkv, proj, extra):
        return Gathered(place, attention_groups(place, qkv, proj), [extra], layer == 0, pairs)

    units = [attention_unit(0, qkv_weight[0], proj_weight[0], extras[0])]
    image, build = take_image(place, where, patches, specials, halo, rows)
    inputs = {
        "weights": (fc1_weight[0], fc2_weight[0], qkv_weight[1], proj_weight[1], extras[1], fc1_weight[1], fc2_weight[1]),
        "cots": (cot_patches, cot_specials),
    }
    vectors, bias_up = ([None] * LAYERS, [None] * LAYERS)
    streams = [None] * (LAYERS + 1)
    middles, normed_one_ts, normed_two_ts, mixeds, attended_ts, hiddens, slopes = (
        [None] * LAYERS for _ in range(7)
    )
    weights = [None] * (2 * LAYERS)
    unit_count = 2 * LAYERS
    last_slot = 3 * unit_count + 1
    at_x, at_y = ([[] for _ in range(last_slot + 2)] for _ in range(2))
    for which in range(unit_count):
        for step in range(nz):
            slot = 3 * which + step
            at_x[slot].append((which, step))
            at_y[slot + (which == 0)].append((which, step))
    at_core = {4: [(0, 0)], 5: [(0, 1), (1, 0)], 7: [(1, 1)], 8: [(2, 0)], 10: [(2, 1)], 11: [(3, 0)], 12: [(3, 1)], 13: [(3, 2)]}
    carried = {}
    grad = None
    for slot in range(last_slot + 1):
        new = {}
        index, step = divmod(slot, 3)
        if index < unit_count:
            new["z"] = place.ring_z(units[index].blocks[step])
        for which, at in at_x[slot]:
            new["x", which, at] = place.swap_x(units[which].over_x(at))
        for which, at in at_y[slot]:
            tails = units[which].over_y(at)
            new["y", which, at] = place.swap_seq(tails[0] if len(tails) == 1 else jnp.concatenate(tails), 2)
        for which, at in at_core.get(slot, []):
            new["core", which, at] = place.swap_seq(units[which].whole[at], 1)
        for which, at in at_y[slot]:
            for index_of, chunk in enumerate(units[which].chunks):
                if chunk[-1] == at:
                    unit = units[which]
                    across = {**unit.across, **{k[2]: v for k, v in new.items() if k[:2] == ("x", which)}}
                    aside = {**unit.aside, **{k[2]: v for k, v in new.items() if k[:2] == ("y", which)}}
                    new["chunk", which, index_of] = unit.chunk(index_of, across, aside)
        later = {1: 1, 4: 2, 8: 3}.get(slot)
        if later:
            new["later"] = place.swap_x(units[later].mine)
        if slot == 0:
            new["image"] = image
        if slot == 5:
            carried["stream"] = build(*image)
        if slot == 3 * unit_count:
            new["image"], build = take_image(place, where, *inputs["cots"], halo, rows)
        if slot == 3 * unit_count + 1:
            grad = build(*image)
        if slot in (9, 11):
            layer = slot // 11
            new["forward"] = forward_attention(
                place, where, 2 * layer, special_count, carried["stream"], units[2 * layer], EXTRA_ROWS
            )
        if slot == 10:
            hidden, slope, crossed, split = forward_up(place, spot, carried["normed"], bias_up[0], units[1])
            output = forward_down(where, 1, carried["middle"], hidden, vectors[0], split)
            new["feed"] = (output, hidden, slope, crossed, split)
        if slot in (3, 5):
            names = [key for key in new if key[0] in ("x", "y")]
            swapped, weights_1 = fence(([new[key] for key in names], weights_1))
            new.update(zip(names, swapped))
            if slot == 3:
                unit = attention_unit(1, *weights_1[:3])
            else:
                unit = Gathered(place, feed_groups(place, *weights_1[3:]), [], False, ((0, 1), (2,), (3,)))
            new["unit"] = (unit.first, unit.mine)
        if step == 2 and index + 1 < len(units) and units[index + 1].blocks:
            carried["begin"] = units[index + 1].blocks[0]
        gate = inputs if slot in (0, 3 * unit_count - 1) else {}
        new, carried, gate = fence((new, carried, gate))
        inputs.update(gate)
        if slot == 0:
            up_0, down_0, *weights_1 = inputs.pop("weights")
            units.append(Gathered(place, feed_groups(place, up_0, down_0), [], False, pairs))
        if "unit" in new:
            unit.first, unit.mine = new["unit"]
            units.append(unit)
        if "begin" in carried:
            units[index + 1].blocks[0] = carried.pop("begin")
        if "image" in new:
            image = new["image"]
        if "later" in new:
            units[later].begin([new["later"]])
        if "z" in new:
            units[index].blocks.append(new["z"])
        for which, at in at_core.get(slot, []):
            units[which].mate.append(new["core", which, at])
        for which, at in at_x[slot]:
            units[which].across[at] = new["x", which, at]
        for which, at in at_y[slot]:
            units[which].aside[at] = new["y", which, at]
        for key in new:
            if key[0] == "chunk":
                units[key[1]].whole.append(new[key])
        if "forward" in new:
            streams[layer] = carried.pop("stream")
            middle, normed, normed_one_ts[layer], normed_two_ts[layer], mixeds[layer], _, attended_ts[layer], crossed, split, vectors[layer], bias_up[layer] = new["forward"]
            weights[2 * layer] = [crossed, split]
            middles[layer] = middle
            carried["middle"], carried["normed"] = middle, normed
        if "feed" in new:
            carried["stream"], hiddens[0], slopes[0], *weights[1] = new["feed"]
            del carried["middle"], carried["normed"]
    hiddens[1], slopes[1], *weights[3] = forward_up(
        place, spot, carried["normed"], bias_up[1], units[3]
    )

    reduces = [Reduced(place) for _ in range(2 * LAYERS)]
    lasts = [None] * (2 * LAYERS)
    back = [{} for _ in range(LAYERS)]

    def feed_back(layer, grad):
        found = back[layer]
        found["down_t"], found["up"], found["sum_down"], found["sum_up"] = backward_feed(
            where, 2 * layer + 1, grad, slopes[layer], weights[2 * layer + 1][1]
        )

    def feed_operands(layer):
        reduces[2 * (LAYERS - 1 - layer)].operands = (
            normed_two_ts[layer], back[layer]["up"], back[layer]["down_t"], hiddens[layer]
        )

    def middle_back(layer, grad):
        found = back[layer]
        found["middle"], found["proj"], found["sum_proj"], found["gain"], found["shift"] = backward_middle(
            where, 2 * layer, grad, found["up"], middles[layer], vectors[layer], weights[2 * layer + 1][0]
        )

    def attention_back(layer):
        found = back[layer]
        others = [found[name] for name in ("sum_proj", "gain", "shift", "sum_down", "sum_up")]
        found["grad"], found["mixed"], found["sums"] = backward_attention(
            where, special_count, found["middle"], found["proj"], mixeds[layer], streams[layer], vectors[layer], others, *weights[2 * layer]
        )

    def attention_operands(layer):
        found = back[layer]
        wide = 3 * width // 4
        cut = width // 4
        mixed = jnp.stack(
            [jnp.pad(found["mixed"][:, i * wide : (i + 1) * wide], ((0, 0), (0, cut))) for i in range(4)]
        )
        proj = jnp.stack([jnp.pad(found["proj"][:, i * cut : (i + 1) * cut], ((0, 0), (cut, 0))) for i in range(4)])
        unit = reduces[2 * (LAYERS - 1 - layer) + 1]
        unit.operands = (normed_one_ts[layer], mixed, attended_ts[layer], proj)

    fills = [(feed_group, 2), (attention_group, 1)] * LAYERS
    all_steps = (1, 2, 3, 0)
    cuts = [((1,), (2, 3, 0))] + [(all_steps,)] * (len(reduces) - 1)

    def sent_cut(which, cut):
        fill, wide = fills[which]
        return sent_part(place, spot, fill, wide, cuts[which][cut], reduces[which].operands)

    def keep_cut(which, cut, got):
        fill, wide = fills[which]
        unit = reduces[which]
        unit.kept.update(kept_part(place, spot, fill, wide, cuts[which][cut], unit.operands, got))

    feed_back(1, grad)
    feed_operands(1)
    sent = [sent_cut(0, 0), None]
    back[1], sent = fence((back[1], sent[:1]))
    final_slot = 3 * len(reduces)
    total = given = None
    rung = []
    got = {}
    sending = {(0, 0): sent[0]}
    for slot in range(-2, final_slot + 1):
        new = {}
        work = {}
        for which, unit in enumerate(reduces):
            at = slot - 3 * which
            if 0 <= at <= 2:
                new["z", which] = place.ring_z(unit.block(at + 1))
            if at == 3:
                unit.last = unit.block(0)
                work["last", which] = unit.last
        for base, group in ((final_slot - 2, range(len(reduces) - 1)), (final_slot, [len(reduces) - 1])):
            if slot == base:
                ends = [reduces[which].last for which in group]
                parts = [end.shape[0] // 4 for end in ends]
                aside = place.swap_seq(
                    jnp.concatenate([end[part : 2 * part] for end, part in zip(ends, parts)]), 2
                )
                across = place.swap_x(jnp.concatenate([end[3 * part :] for end, part in zip(ends, parts)]))
                begins = 0
                for which, end, part in zip(group, ends, parts):
                    lasts[which] = [end, aside[begins : begins + part], across[begins : begins + part]]
                    begins += part
                if slot < final_slot:
                    new["lasts"] = [lasts[which] for which in group]
        if slot == -2:
            sending[0, 1] = sent_cut(0, 1)
            work["sending"] = sending[0, 1]
        if slot == 0:
            keep_cut(0, 1, got.pop((0, 1)))
        if slot == -1:
            keep_cut(0, 0, got.pop((0, 0)))
        for which, base in ((2, 4), (3, 7)):
            if slot == base:
                keep_cut(which, 0, got.pop((which, 0)))
                for step in all_steps:
                    work["kept", which, step] = reduces[which].kept[step]
        for key, base in (((0, 0), -2), ((0, 1), -1), ((1, 0), 2), ((2, 0), 3), ((3, 0), 6)):
            if slot == base:
                new["core", key] = place.swap_seq(sending.pop(key), 1)
        if slot == 2:
            keep_cut(1, 0, new["core", (1, 0)])
        for which, unit in enumerate(reduces):
            at = slot - 3 * which
            if -1 <= at <= 2:
                step = (at + 2) % nz
                new["side", which] = (
                    place.swap_x(unit.kept[step][0]),
                    place.swap_seq(unit.kept[step][1], 2),
                )
        if slot == 3:
            attention_operands(0)
            work["sending"] = sent_cut(3, 0)
        if slot == -1:
            middle_back(1, grad)
            streams[LAYERS] = forward_down(where, 3, carried["middle"], hiddens[1], vectors[1], weights[3][1])
            work["output"] = streams[LAYERS]
        if slot == 0:
            attention_back(1)
        if slot == 1:
            attention_operands(1)
            names = ("down_t", "up", "sum_down", "sum_up", "middle", "proj", "sum_proj", "gain", "shift")
            back[0] = dict(
                zip(
                    names,
                    backward_feed_middle(
                        where, (0, 1), back[1]["grad"], slopes[0], weights[1][1], middles[0], vectors[0], weights[1][0]
                    ),
                )
            )
            feed_operands(0)
            work["sending"] = (sent_cut(1, 0), sent_cut(2, 0))
        if slot == 2:
            attention_back(0)
        if slot in (-1, 0):
            work["back", 1] = back[1]
        if slot in (1, 2):
            work["back", 0] = back[0]
        if slot == 3:
            total = jnp.concatenate([back[layer]["sums"] for layer in range(LAYERS)])
            new["sum"] = place.swap_seq(total, 1)
        if slot == 4:
            new["sum"] = place.swap_seq(total, 2)
        if slot == 6:
            new["sum"] = place.swap_x(total)
        if slot in (7, 9):
            new["ringing"] = [place.ring_z(total, by) for by in ((1,) if slot == 7 else (2, 3))]
        if slot == final_slot - 1:
            work["images"] = give_images(where, given, halo, count, special_count)
        if slot == final_slot:
            images_before, images_after, *owns = images
            new["images"] = (shift_seq(place, images_after, 1), shift_seq(place, images_before, -1))
        pending = {}
        for which, unit in enumerate(reduces):
            at = slot + 1 - 3 * which
            if 0 <= at <= 2:
                step = (at + 2) % nz
                if step in unit.kept:
                    pending["kept", which] = unit.kept[step]
        if slot == final_slot - 2:
            pending["give"] = [streams[LAYERS], back[0]["grad"]]
        for key, base in (((2, 0), 2), ((3, 0), 5)):
            if slot == base:
                pending["sending", key] = sending[key]
        for key, base in (((0, 1), 0), ((2, 0), 4), ((3, 0), 7)):
            if slot == base - 1 and key in got:
                pending["got", key] = got[key]
        new, work, pending = fence((new, work, pending))
        if "sending" in work:
            if slot == 1:
                sending[1, 0], sending[2, 0] = work.pop("sending")
            else:
                sending[(0, 1) if slot == -2 else (3, 0)] = work.pop("sending")
        for key in [key for key in pending if key[0] == "sending"]:
            sending[key[1]] = pending.pop(key)
        if "output" in work:
            streams[LAYERS] = work.pop("output")
        for key, value in work.items():
            if key[0] == "back":
                back[key[1]] = value
            if key[0] == "last":
                reduces[key[1]].last = value
            if key == "images":
                images = value
            if key[0] == "kept":
                reduces[key[1]].kept[key[2]] = value
        if "give" in pending:
            given = pending.pop("give")
        for key in [key for key in pending if key[0] == "got"]:
            got[key[1]] = pending.pop(key)
        for key, value in pending.items():
            reduces[key[1]].kept[(slot + 1 - 3 * key[1] + 2) % nz] = value
        for key, value in new.items():
            if key[0] == "core":
                got[key[1]] = value
            if key[0] == "z":
                reduces[key[1]].running = value
            if key[0] == "side":
                reduces[key[1]].sides[(slot - 3 * key[1] + 2) % nz] = value
        if "images" in new:
            sides = new["images"]
        if "lasts" in new:
            lasts[: len(new["lasts"])] = new["lasts"]
        if "sum" in new:
            total = total + new["sum"]
        if "ringing" in new:
            rung += new["ringing"]

    wm, wp, wu, wd, out_patches, grad_patches, g1, s1, bq, bv, bp, g2, s2, bd, bu = finish(
        place,
        spot,
        [lasts[3] + lasts[2], lasts[1] + lasts[0]],
        [total] + rung,
        [owns[0], owns[2], *sides],
        part_rows,
        width,
    )
    wd = jnp.transpose(wd, (0, 2, 1))
    return (
        out_patches,
        owns[1],
        grad_patches,
        owns[3],
        g1,
        s1,
        wm,
        bq,
        bv,
        wp,
        bp,
        g2,
        s2,
        wu,
        bu,
        wd,
        bd,
    )


def local(*args):
    place = Place()
    if place.walked:
        return local_walked(place, *args)
    return local_plain(place, *args)


def solution(mesh):
    in_specs = (
        P(("dp", "seq"), None),
        P(("dp", "seq"), None),
        P("dp", None),
        P("dp", None, None),
        P(None, "dp"),
        P(None, "dp"),
        P(None, "dp", None),
        P(None, "dp"),
        P(None, "dp"),
        P(None, "dp", None),
        P(None, "dp"),
        P(None, "dp"),
        P(None, "dp"),
        P(None, "dp", None),
        P(None, "dp"),
        P(None, "dp", None),
        P(None, "dp"),
        P(("dp", "seq"), None),
        P(("dp", "seq"), None),
    )
    out_specs = (
        P(("dp", "seq"), None),
        P(("dp", "seq"), None),
        P(("dp", "seq"), None),
        P(("dp", "seq"), None),
        P(None, "dp"),
        P(None, "dp"),
        P(None, "dp", "seq"),
        P(None, "dp"),
        P(None, "dp"),
        P(None, "dp", "seq"),
        P(None, "dp"),
        P(None, "dp"),
        P(None, "dp"),
        P(None, "dp", "seq"),
        P(None, "dp"),
        P(None, "dp", "seq"),
        P(None, "dp"),
    )
    return jax.shard_map(local, mesh=mesh, in_specs=in_specs, out_specs=out_specs, check_vma=False)
```

```python
from functools import partial

import jax
import jax.numpy as jnp
from jax import lax
from jax.experimental import pallas as pl
from jax.experimental.pallas import tpu as pltpu
from jax.sharding import PartitionSpec as P

HD = 64
LAYERS = 2
MOST = 280
KEEP_RATE = 0.9
EPSILON = 1e-06
MASKED = -1e30
GAIN_ONE, SHIFT_ONE, BIAS_QUERY, BIAS_VALUE, BIAS_PROJ, GAIN_TWO, SHIFT_TWO, BIAS_DOWN = range(8)
VECTOR_PIECES = 12
EXTRA_ROWS = 16
MIB = 1024 * 1024
ROOT_HALF = 0.7071067811865476
ROOT_TWO_PI = 0.3989422804014327
BF = jnp.bfloat16
F32 = jnp.float32


def dot_nn(left, right):
    return lax.dot_general(left, right, (((1,), (0,)), ((), ())), preferred_element_type=F32)


def dot_nt(left, right):
    return lax.dot_general(left, right, (((1,), (1,)), ((), ())), preferred_element_type=F32)


def dot_tn(left, right):
    return lax.dot_general(left, right, (((0,), (0,)), ((), ())), preferred_element_type=F32)


class Place:
    def __init__(self):
        self.n_dp = lax.axis_size("dp")
        self.n_seq = lax.axis_size("seq")
        self.walked = self.n_dp == 8 and self.n_seq == 4
        self.dp = lax.axis_index("dp")
        self.seq = lax.axis_index("seq")
        if self.walked:
            self.core = self.seq % 2
            self.y = self.seq // 2
            self.x = self.dp % 2
            self.z = self.dp // 2
            self.nz = self.n_dp // 2

    def swap_seq(self, values, mask):
        return lax.ppermute(values, "seq", [(i, i ^ mask) for i in range(self.n_seq)])

    def swap_x(self, values):
        return lax.ppermute(values, "dp", [(i, i ^ 1) for i in range(self.n_dp)])

    def ring_z(self, values, by=1):
        return lax.ppermute(values, "dp", [(i, (i + 2 * by) % self.n_dp) for i in range(self.n_dp)])


def gather_matrix(shard):
    return lax.all_gather(shard, "dp", axis=0, tiled=True)


def reduce_matrix(acts, grads):
    part = dot_tn(acts, grads).astype(BF)
    part = lax.psum_scatter(part, "dp", scatter_dimension=0, tiled=True)
    return lax.psum_scatter(part, "seq", scatter_dimension=1, tiled=True).astype(F32)


def reduce_vectors(place, vectors):
    packed = jnp.concatenate(
        [vector.reshape(place.n_dp, vector.shape[0] // place.n_dp) for vector in vectors], axis=1
    )
    mask = 1
    while mask < place.n_seq:
        packed = packed + place.swap_seq(packed, mask)
        mask *= 2
    packed = lax.all_to_all(packed, "dp", split_axis=0, concat_axis=0, tiled=True)
    total = jnp.sum(packed, axis=0)
    results, at = [], 0
    for vector in vectors:
        width = vector.shape[0] // place.n_dp
        results.append(total[at : at + width])
        at += width
    return results


def gather_vectors(place, shards):
    widths = [shard.shape[1] for shard in shards]
    packed = jnp.concatenate(shards, axis=1)
    rows = packed.shape[0]
    spread = jnp.broadcast_to(packed[None], (place.n_dp,) + packed.shape)
    spread = lax.all_to_all(spread, "dp", split_axis=0, concat_axis=0, tiled=True)
    results, at = [], 0
    for width in widths:
        piece = spread[:, :, at : at + width]
        results.append(jnp.transpose(piece, (1, 0, 2)).reshape(rows, place.n_dp * width).astype(F32))
        at += width
    return results


def normalize(values):
    center = values - jnp.mean(values, axis=-1, keepdims=True)
    spread = jnp.mean(center * center, axis=-1, keepdims=True)
    scale = lax.rsqrt(spread + EPSILON)
    return (center * scale, scale)


def normalize_back(hat, scale, gain, grad):
    scaled = grad * gain
    first = jnp.mean(scaled, axis=-1, keepdims=True)
    second = jnp.mean(scaled * hat, axis=-1, keepdims=True)
    back = scale * (scaled - first - hat * second)
    return (back, jnp.sum(grad * hat, axis=0), jnp.sum(grad, axis=0))


def heads_of(mixed):
    rows = mixed.shape[0]
    width = mixed.shape[1] // 3
    split = mixed.reshape(rows, 3, width // HD, HD)
    return (split[:, 0], split[:, 1], split[:, 2])


def attend(mixed, key_ok):
    queries, keys, values = heads_of(mixed)
    scores = jnp.einsum("qhd,khd->hqk", queries, keys, preferred_element_type=F32) * 0.125
    scores = jnp.where(key_ok[None, None, :], scores, MASKED)
    top = jnp.max(scores, axis=2, keepdims=True)
    powers = jnp.exp(scores - top)
    probs = powers / jnp.sum(powers, axis=2, keepdims=True)
    out = jnp.einsum("hqk,khd->qhd", probs.astype(BF), values, preferred_element_type=F32)
    return (out.reshape(mixed.shape[0], -1).astype(BF), probs)


def attend_back(mixed, probs, grad_out):
    queries, keys, values = heads_of(mixed)
    rows = mixed.shape[0]
    grads = grad_out.reshape(queries.shape)
    grad_probs = jnp.einsum("qhd,khd->hqk", grads, values, preferred_element_type=F32)
    inner = jnp.sum(probs * grad_probs, axis=2, keepdims=True)
    grad_scores = (probs * (grad_probs - inner)).astype(BF)
    grad_values = jnp.einsum("hqk,qhd->khd", probs.astype(BF), grads, preferred_element_type=F32)
    grad_queries = (
        jnp.einsum("hqk,khd->qhd", grad_scores, keys, preferred_element_type=F32) * 0.125
    )
    grad_keys = (
        jnp.einsum("hqk,qhd->khd", grad_scores, queries, preferred_element_type=F32) * 0.125
    )
    return jnp.concatenate(
        [grad.reshape(rows, -1).astype(BF) for grad in (grad_queries, grad_keys, grad_values)], axis=1
    )


def layer_forward(stream, vectors, matrices, keeps, key_ok):
    gain_one, shift_one, bias_query, bias_value, bias_proj, gain_two, shift_two, bias_down, bias_up = vectors
    w_mixed, w_proj, w_up, w_down = matrices
    hat_one, scale_one = normalize(stream)
    normed_one = (hat_one * gain_one + shift_one).astype(BF)
    bias_mixed = jnp.concatenate([bias_query, jnp.zeros_like(bias_query), bias_value])
    mixed = (dot_nn(normed_one, w_mixed) + bias_mixed).astype(BF)
    attended, probs = attend(mixed, key_ok)
    middle = stream + keeps[0] * (dot_nn(attended, w_proj) + bias_proj) / KEEP_RATE
    hat_two, scale_two = normalize(middle)
    normed_two = (hat_two * gain_two + shift_two).astype(BF)
    hidden_pre = dot_nn(normed_two, w_up) + bias_up
    share = 0.5 * (1.0 + lax.erf(hidden_pre * ROOT_HALF))
    hidden = (hidden_pre * share).astype(BF)
    slope = share + hidden_pre * jnp.exp(-0.5 * hidden_pre * hidden_pre) * ROOT_TWO_PI
    output = middle + keeps[1] * (dot_nn(hidden, w_down) + bias_down) / KEEP_RATE
    saved = (hat_one, scale_one, normed_one, mixed, probs, attended, hat_two, scale_two, normed_two, hidden, slope)
    return (output, saved)


def layer_back(place, grad_stream, saved, vectors, matrices, keeps):
    hat_one, scale_one, normed_one, mixed, probs, attended, hat_two, scale_two, normed_two, hidden, slope = saved
    gain_one, gain_two = (vectors[0], vectors[5])
    w_mixed, w_proj, w_up, w_down = matrices
    width = grad_stream.shape[1]
    grad_down = (keeps[1] * grad_stream / KEEP_RATE).astype(BF)
    total_down = reduce_matrix(hidden, grad_down)
    grad_up = (dot_nt(grad_down, w_down) * slope).astype(BF)
    total_up = reduce_matrix(normed_two, grad_up)
    back_two, grad_gain_two, grad_shift_two = normalize_back(
        hat_two, scale_two, gain_two, dot_nt(grad_up, w_up)
    )
    grad_middle = grad_stream + back_two
    grad_proj = (keeps[0] * grad_middle / KEEP_RATE).astype(BF)
    total_proj = reduce_matrix(attended, grad_proj)
    grad_attended = dot_nt(grad_proj, w_proj).astype(BF)
    grad_mixed = attend_back(mixed, probs, grad_attended)
    total_mixed = reduce_matrix(normed_one, grad_mixed)
    back_one, grad_gain_one, grad_shift_one = normalize_back(
        hat_one, scale_one, gain_one, dot_nt(grad_mixed, w_mixed)
    )
    grad_input = grad_middle + back_one
    sum_mixed = jnp.sum(grad_mixed, axis=0, dtype=F32)
    totals = reduce_vectors(
        place,
        (
            grad_gain_one,
            grad_shift_one,
            sum_mixed[:width],
            sum_mixed[2 * width :],
            jnp.sum(grad_proj, axis=0, dtype=F32),
            grad_gain_two,
            grad_shift_two,
            jnp.sum(grad_down, axis=0, dtype=F32),
            jnp.sum(grad_up, axis=0, dtype=F32),
        ),
    )
    return (grad_input, totals, (total_mixed, total_proj, total_up, total_down))


def shift_seq(place, values, by):
    count = place.n_seq
    return lax.ppermute(values, "seq", [(i, i + by) for i in range(count) if 0 <= i + by < count])


def to_image(place, patches, specials, halo, start, length, rows):
    count, width = patches.shape
    before = shift_seq(place, patches[count - halo :], 1)
    after = shift_seq(place, patches[:halo], -1)
    spare = jnp.zeros((MOST + 2 * halo - count - 2 * halo, width), patches.dtype)
    window = jnp.concatenate([before, patches, after, spare])
    image = lax.dynamic_slice_in_dim(window, start, MOST)
    inside = jnp.arange(MOST, dtype=jnp.int32)[:, None] < length
    image = jnp.where(inside, image, 0.0)
    spare = jnp.zeros((rows - MOST - specials.shape[0], width), patches.dtype)
    return jnp.concatenate([image, specials, spare])


def from_image(place, stream, halo, start, length, count, specials):
    width = stream.shape[1]
    inside = jnp.arange(MOST, dtype=jnp.int32)[:, None] < length
    image = jnp.where(inside, stream[:MOST], 0.0)
    window = jnp.zeros((MOST + 2 * halo, width), stream.dtype)
    window = lax.dynamic_update_slice_in_dim(window, image, start, 0)
    own = window[halo : halo + count]
    from_before = shift_seq(place, window[halo + count : count + 2 * halo], 1)
    from_after = shift_seq(place, window[:halo], -1)
    blank = jnp.zeros((count - halo, width), stream.dtype)
    own = own + jnp.concatenate([from_before, blank]) + jnp.concatenate([blank, from_after])
    return (own, stream[MOST : MOST + specials])


def local_plain(
    place,
    patches,
    specials,
    lengths,
    keep_mask,
    norm1_gain,
    norm1_bias,
    qkv_weight,
    query_bias,
    value_bias,
    proj_weight,
    proj_bias,
    norm2_gain,
    norm2_bias,
    fc1_weight,
    fc1_bias,
    fc2_weight,
    fc2_bias,
    cot_patches,
    cot_specials,
):
    count = patches.shape[0]
    special_count = specials.shape[0]
    images = lengths.shape[1]
    halo = (MOST - count) * (images // 2)
    rows = -(-(MOST + special_count) // 16) * 16
    before = jnp.sum(jnp.where(jnp.arange(images) < place.seq, lengths[0], 0))
    length = lax.dynamic_index_in_dim(lengths[0], place.seq, 0, keepdims=False)
    start = before - place.seq * count + halo
    keeps = lax.dynamic_index_in_dim(keep_mask[0], place.seq, 0, keepdims=False).astype(F32)
    row_ids = jnp.arange(rows, dtype=jnp.int32)
    key_ok = (row_ids < length) | ((row_ids >= MOST) & (row_ids < MOST + special_count))

    shards = (norm1_gain, norm1_bias, query_bias, value_bias, proj_bias, norm2_gain, norm2_bias, fc2_bias, fc1_bias)
    vectors_all = gather_vectors(place, shards)
    stream = to_image(place, patches, specials, halo, start, length, rows)
    matrices = []
    for layer in range(LAYERS):
        matrices.append(
            tuple(
                gather_matrix(shard[layer])
                for shard in (qkv_weight, proj_weight, fc1_weight, fc2_weight)
            )
        )
    vectors = [tuple(vector[layer] for vector in vectors_all) for layer in range(LAYERS)]
    saved = []
    for layer in range(LAYERS):
        stream, kept = layer_forward(
            stream, vectors[layer], matrices[layer], keeps[2 * layer : 2 * layer + 2], key_ok
        )
        saved.append(kept)
    out_patches, out_specials = from_image(place, stream, halo, start, length, count, special_count)
    grad = to_image(place, cot_patches, cot_specials, halo, start, length, rows)
    vector_totals, matrix_totals = ([None] * LAYERS, [None] * LAYERS)
    for layer in reversed(range(LAYERS)):
        grad, vector_totals[layer], matrix_totals[layer] = layer_back(
            place, grad, saved[layer], vectors[layer], matrices[layer], keeps[2 * layer : 2 * layer + 2]
        )
    grad_patches, grad_specials = from_image(place, grad, halo, start, length, count, special_count)
    vector_out = [jnp.stack([vector_totals[layer][i] for layer in range(LAYERS)]) for i in range(9)]
    matrix_out = [jnp.stack([matrix_totals[layer][i] for layer in range(LAYERS)]) for i in range(4)]
    g1, s1, bq, bv, bp, g2, s2, bd, bu = vector_out
    wm, wp, wu, wd = matrix_out
    return (
        out_patches,
        out_specials,
        grad_patches,
        grad_specials,
        g1,
        s1,
        wm,
        bq,
        bv,
        wp,
        bp,
        g2,
        s2,
        wu,
        bu,
        wd,
        bd,
    )


def whole_vmem(count):
    return [pl.BlockSpec(memory_space=pltpu.VMEM)] * count


def in_smem(count):
    return [pl.BlockSpec(memory_space=pltpu.SMEM)] * count


def kernel_params(mib):
    return pltpu.CompilerParams(vmem_limit_bytes=mib * MIB)


def place_pieces(spot, parts, chunks, crossed, split, extra, turned):
    z, x, y, core = (spot[i] for i in range(4))
    steps = sum(len(chunk) for chunk in chunks)
    first, rows = crossed.shape[2:4]
    quarter = split.shape[2] // 2
    more = 0 if extra is None else extra.shape[1]
    wide, piece = first * rows + more, quarter * rows
    block = wide + (piece if turned else 2 * piece)
    spots = {
        (0, 0): wide,
        (1, 0): block + wide if turned else wide + piece,
        (0, 1): 2 * wide + 2 * piece,
        (1, 1): 2 * wide + 3 * piece,
    }
    for side in range(2):
        at_core = core if side == 0 else 1 - core
        for step in range(steps):
            which = next(i for i, chunk in enumerate(chunks) if step in chunk)
            part = parts[side * len(chunks) + which]
            start = chunks[which].index(step) * (2 * wide + 4 * piece)
            at_z = lax.rem(z - step + steps, steps)
            for far_x in range(2):
                row = 2 * at_z + lax.rem(x + far_x, 2)
                base = start + far_x * block
                for j in range(first):
                    crossed[at_core, row, j] = part[base + j * rows : base + (j + 1) * rows]
                if extra is not None and side == 0:
                    extra[row] = part[base + first * rows : base + wide]
                for far_y in range(2):
                    base = start + spots[far_x, far_y]
                    for j in range(quarter):
                        split[at_core, row, lax.rem(y + far_y, 2) * quarter + j] = part[
                            base + j * rows : base + (j + 1) * rows
                        ]


SPOT = 5


def keep_factor(spot, images, branch):
    return spot[SPOT + images + spot[4] * 2 * LAYERS + branch].astype(F32) * (1.0 / KEEP_RATE)


def key_block(spot, rows, special_count):
    ids = lax.broadcasted_iota(jnp.int32, (1, rows), 1)
    inside = (ids < spot[SPOT + spot[4]]) | ((ids >= MOST) & (ids < MOST + special_count))
    return jnp.where(inside, 0.0, MASKED).astype(F32)


def image_frame(spot, images, count, halo):
    before = jnp.int32(0)
    for image in range(images):
        before = before + jnp.where(image < spot[4], spot[SPOT + image], 0)
    return before - spot[4] * count + halo, spot[SPOT + spot[4]]


def flat(block):
    return block.reshape(-1, block.shape[-1])


def moments(values):
    center = values - jnp.mean(values, axis=-1, keepdims=True)
    scale = lax.rsqrt(jnp.mean(center * center, axis=-1, keepdims=True) + EPSILON)
    return (center * scale, scale)


def norm_back(hat, scale, gain, grad):
    scaled = grad * gain
    first = jnp.mean(scaled, axis=-1, keepdims=True)
    second = jnp.mean(scaled * hat, axis=-1, keepdims=True)
    return scale * (scaled - first - hat * second)


def erf_of(values):
    v = jnp.clip(values, -3.7439211627767994, 3.7439211627767994)
    s = v * v
    top = s * 0.00022905065861350646 + 0.0034082910107109506
    top = top * s + 0.050955695062380861
    top = top * s + 0.18520832239976145
    top = top * s + 1.128379143519084
    low = s * -1.1791602954361697e-7 + 0.000023547966471313185
    low = low * s + 0.0010179625278914885
    low = low * s + 0.014070470171167667
    low = low * s + 0.11098505178285362
    low = low * s + 0.49746925110067538
    low = low * s + 1.0
    return v * top / low


def head_probs(queries, keys, blocked):
    scores = dot_nt(queries, keys) + blocked
    powers = jnp.exp(scores - jnp.max(scores, axis=1, keepdims=True))
    return powers * (1.0 / jnp.sum(powers, axis=1, keepdims=True))


def forward_attention_kernel(turned, chunks, images, branch, special_count, spot, stream, *refs):
    keep = keep_factor(spot, images, branch)
    blocked = key_block(spot, stream.shape[0], special_count)
    parts, refs = refs[: 2 * len(chunks)], refs[2 * len(chunks) :]
    middle, normed_two, normed_one_t, normed_two_t, mixed, attended, attended_t, crossed, split, vectors, bias_up, extra = refs
    place_pieces(spot, parts, chunks, crossed, split, extra, turned)
    rows = crossed.shape[3]
    for row in range(extra.shape[0]):
        block = extra[row].astype(F32)
        for piece in range(VECTOR_PIECES):
            values = block[piece : piece + 1, :rows]
            if piece < vectors.shape[0]:
                vectors[piece : piece + 1, row * rows : (row + 1) * rows] = values
            else:
                column = (row * (VECTOR_PIECES - vectors.shape[0]) + piece - vectors.shape[0]) * rows
                bias_up[:, column : column + rows] = values
    hat, _ = moments(stream[...])
    normed = (hat * vectors[GAIN_ONE : GAIN_ONE + 1] + vectors[SHIFT_ONE : SHIFT_ONE + 1]).astype(BF)
    normed_one_t[...] = normed.T
    width = stream.shape[1]
    half = width // 2
    for core in range(2):
        for j in range(3):
            weight = crossed[core, :, j] if j < 2 else split[core, :, 0]
            columns = pl.ds(j * width + core * half, half)
            ahead = dot_nn(normed, flat(weight))
            if j != 1:
                row = BIAS_QUERY if j == 0 else BIAS_VALUE
                ahead = ahead + vectors[row : row + 1, core * half : (core + 1) * half]
            mixed[:, columns] = ahead.astype(BF)
    lane = lax.broadcasted_iota(jnp.int32, (1, 2 * HD), 1)
    for pair in range(width // (2 * HD)):
        queries, keys, values = (
            mixed[:, pl.ds(j * width + pair * 2 * HD, 2 * HD)] for j in range(3)
        )
        outs = []
        for side in range(2):
            mine = ((lane < HD) if side == 0 else (lane >= HD)).astype(F32).astype(BF)
            probs = head_probs(queries * (mine * 0.125), keys, blocked)
            outs.append(dot_nn(probs.astype(BF), values))
        attended[:, pl.ds(pair * 2 * HD, 2 * HD)] = jnp.where(lane < HD, outs[0], outs[1]).astype(BF)
    ahead = attended[...]
    attended_t[...] = ahead.T
    for core in range(2):
        columns = pl.ds(core * half, half)
        added = dot_nn(ahead, flat(split[core, :, 1])) + vectors[BIAS_PROJ : BIAS_PROJ + 1, columns]
        middle[:, columns] = stream[:, columns] + keep * added
    hat, _ = moments(middle[...])
    normed = (hat * vectors[GAIN_TWO : GAIN_TWO + 1] + vectors[SHIFT_TWO : SHIFT_TWO + 1]).astype(BF)
    normed_two[...] = normed
    normed_two_t[...] = normed.T


def forward_attention(place, spot, branch, special_count, stream, unit, extra_rows):
    parts = unit.parts()
    rows, width = stream.shape
    group = (width // place.n_dp, width // 2)
    shapes = [
        jax.ShapeDtypeStruct((rows, width), F32),
        jax.ShapeDtypeStruct((rows, width), BF),
        jax.ShapeDtypeStruct((width, rows), BF),
        jax.ShapeDtypeStruct((width, rows), BF),
        jax.ShapeDtypeStruct((rows, 3 * width), BF),
        jax.ShapeDtypeStruct((rows, width), BF),
        jax.ShapeDtypeStruct((width, rows), BF),
    ] + [jax.ShapeDtypeStruct((2, place.n_dp, 2) + group, BF)] * 2
    shapes += [
        jax.ShapeDtypeStruct((BIAS_DOWN + 1, width), F32),
        jax.ShapeDtypeStruct((1, 4 * width), F32),
    ]
    return pl.pallas_call(
        partial(forward_attention_kernel, unit.turned, unit.chunks, place.n_seq, branch, special_count),
        in_specs=in_smem(1) + whole_vmem(1 + len(parts)),
        out_specs=whole_vmem(len(shapes)),
        out_shape=shapes,
        scratch_shapes=[pltpu.VMEM((place.n_dp, extra_rows, width // 2), BF)],
        compiler_params=kernel_params(12),
        cost_estimate=pl.CostEstimate(flops=0, bytes_accessed=0, transcendentals=0),
        name="forward_attention",
    )(spot, stream, *parts)


def forward_up_kernel(turned, chunks, spot, normed, bias_up, *refs):
    parts, refs = refs[: 2 * len(chunks)], refs[2 * len(chunks) :]
    hidden, slope, crossed, split = refs
    place_pieces(spot, parts, chunks, crossed, split, None, turned)
    values = normed[...]
    half = values.shape[1] // 2
    for core in range(2):
        for j in range(4):
            columns = pl.ds((core * 4 + j) * half, half)
            pre = dot_nn(values, flat(crossed[core, :, j])) + bias_up[:, columns]
            share = 0.5 + 0.5 * erf_of(pre * ROOT_HALF)
            hidden[:, columns] = (pre * share).astype(BF)
            slope[:, columns] = (share + pre * jnp.exp(-0.5 * pre * pre) * ROOT_TWO_PI).astype(BF)


def forward_up(place, spot, normed, bias_up, unit):
    parts = unit.parts()
    rows, width = normed.shape
    group = (width // place.n_dp, width // 2)
    return pl.pallas_call(
        partial(forward_up_kernel, unit.turned, unit.chunks),
        in_specs=in_smem(1) + whole_vmem(2 + len(parts)),
        out_specs=whole_vmem(4),
        out_shape=[jax.ShapeDtypeStruct((rows, 4 * width), BF)] * 2
        + [jax.ShapeDtypeStruct((2, place.n_dp, 4) + group, BF)] * 2,
        compiler_params=kernel_params(8),
        cost_estimate=pl.CostEstimate(flops=0, bytes_accessed=0, transcendentals=0),
        name="forward_up",
    )(spot, normed, bias_up, *parts)


def forward_down_kernel(images, branch, spot, middle, hidden, vectors, split, output):
    keep = keep_factor(spot, images, branch)
    ahead = hidden[...]
    half = middle.shape[1] // 2
    for core in range(2):
        columns = pl.ds(core * half, half)
        added = dot_nn(ahead, flat(split[core])) + vectors[BIAS_DOWN : BIAS_DOWN + 1, columns]
        output[:, columns] = middle[:, columns] + keep * added


def forward_down(place, spot, branch, middle, hidden, vectors, split):
    return pl.pallas_call(
        partial(forward_down_kernel, place.n_seq, branch),
        in_specs=in_smem(1) + whole_vmem(4),
        out_specs=whole_vmem(1)[0],
        out_shape=jax.ShapeDtypeStruct(middle.shape, F32),
        compiler_params=kernel_params(8),
        cost_estimate=pl.CostEstimate(flops=0, bytes_accessed=0, transcendentals=0),
        name="forward_down",
    )(spot, middle, hidden, vectors, split)


def backward_feed_kernel(images, branch, spot, grad, slope, split, grad_down_t, grad_up, sum_down, sum_up):
    keep = keep_factor(spot, images, branch)
    down = (keep * grad[...]).astype(BF)
    grad_down_t[...] = down.T
    sum_down[...] = jnp.sum(down.astype(F32), axis=0, keepdims=True)
    half = grad.shape[1] // 2
    for row in range(split.shape[1]):
        columns = pl.ds(row * half, half)
        ahead = dot_nt(down[:, :half], flat(split[0, row])) + dot_nt(down[:, half:], flat(split[1, row]))
        up = (ahead * slope[:, columns].astype(F32)).astype(BF)
        grad_up[:, columns] = up
        sum_up[:, columns] = jnp.sum(up.astype(F32), axis=0, keepdims=True)


def backward_feed(place, spot, branch, grad, slope, split):
    rows, width = grad.shape
    shapes = [
        jax.ShapeDtypeStruct((width, rows), BF),
        jax.ShapeDtypeStruct((rows, 4 * width), BF),
        jax.ShapeDtypeStruct((1, width), F32),
        jax.ShapeDtypeStruct((1, 4 * width), F32),
    ]
    return pl.pallas_call(
        partial(backward_feed_kernel, place.n_seq, branch),
        in_specs=in_smem(1) + whole_vmem(3),
        out_specs=whole_vmem(len(shapes)),
        out_shape=shapes,
        compiler_params=kernel_params(8),
        cost_estimate=pl.CostEstimate(flops=0, bytes_accessed=0, transcendentals=0),
        name="backward_feed",
    )(spot, grad, slope, split)


def backward_middle_kernel(images, branch, spot, grad, grad_up, middle, vectors, crossed, *refs):
    keep = keep_factor(spot, images, branch)
    grad_middle, grad_proj, sum_proj, grad_gain, grad_shift = refs
    hat, scale = moments(middle[...])
    half = grad.shape[1] // 2
    total = jnp.zeros(grad.shape, F32)
    for core in range(2):
        for j in range(4):
            total += dot_nt(grad_up[:, pl.ds((core * 4 + j) * half, half)], flat(crossed[core, :, j]))
    grad_gain[...] = jnp.sum(total * hat, axis=0, keepdims=True)
    grad_shift[...] = jnp.sum(total, axis=0, keepdims=True)
    after = grad[...] + norm_back(hat, scale, vectors[GAIN_TWO : GAIN_TWO + 1], total)
    grad_middle[...] = after
    proj = (keep * after).astype(BF)
    grad_proj[...] = proj
    sum_proj[...] = jnp.sum(proj.astype(F32), axis=0, keepdims=True)


def backward_middle(place, spot, branch, grad, grad_up, middle, vectors, crossed):
    rows, width = grad.shape
    shapes = [
        jax.ShapeDtypeStruct((rows, width), F32),
        jax.ShapeDtypeStruct((rows, width), BF),
    ] + [jax.ShapeDtypeStruct((1, width), F32)] * 3
    return pl.pallas_call(
        partial(backward_middle_kernel, place.n_seq, branch),
        in_specs=in_smem(1) + whole_vmem(5),
        out_specs=whole_vmem(len(shapes)),
        out_shape=shapes,
        compiler_params=kernel_params(10),
        cost_estimate=pl.CostEstimate(flops=0, bytes_accessed=0, transcendentals=0),
        name="backward_middle",
    )(spot, grad, grad_up, middle, vectors, crossed)


def backward_feed_middle_kernel(images, branches, spot, grad, slope, split, middle, vectors, crossed, *refs):
    backward_feed_kernel(images, branches[1], spot, grad, slope, split, *refs[:4])
    backward_middle_kernel(images, branches[0], spot, grad, refs[1], middle, vectors, crossed, *refs[4:])


def backward_feed_middle(place, spot, branches, grad, slope, split, middle, vectors, crossed):
    rows, width = grad.shape
    shapes = [
        jax.ShapeDtypeStruct((width, rows), BF),
        jax.ShapeDtypeStruct((rows, 4 * width), BF),
        jax.ShapeDtypeStruct((1, width), F32),
        jax.ShapeDtypeStruct((1, 4 * width), F32),
        jax.ShapeDtypeStruct((rows, width), F32),
        jax.ShapeDtypeStruct((rows, width), BF),
    ] + [jax.ShapeDtypeStruct((1, width), F32)] * 3
    return pl.pallas_call(
        partial(backward_feed_middle_kernel, place.n_seq, branches),
        in_specs=in_smem(1) + whole_vmem(6),
        out_specs=whole_vmem(len(shapes)),
        out_shape=shapes,
        compiler_params=kernel_params(12),
        name="backward_feed_middle",
    )(spot, grad, slope, split, middle, vectors, crossed)


def backward_attention_kernel(special_count, spot, grad_middle, grad_proj, mixed, stream, vectors, *refs):
    blocked = key_block(spot, stream.shape[0], special_count)
    others, (crossed, split), refs = refs[:5], refs[5:7], refs[7:]
    grad_stream, grad_mixed, sums, ahead = refs
    sum_proj, gain_two, shift_two, sum_down, sum_up = others
    hat, scale = moments(stream[...])
    width = stream.shape[1]
    half = width // 2
    proj = grad_proj[...]
    ahead[...] = (
        dot_nt(proj[:, :half], flat(split[0, :, 1])) + dot_nt(proj[:, half:], flat(split[1, :, 1]))
    ).astype(BF)
    lane = lax.broadcasted_iota(jnp.int32, (1, 2 * HD), 1)
    for pair in range(width // (2 * HD)):
        queries, keys, values = (
            mixed[:, pl.ds(j * width + pair * 2 * HD, 2 * HD)] for j in range(3)
        )
        grads = ahead[:, pl.ds(pair * 2 * HD, 2 * HD)]
        found = []
        for side in range(2):
            mine = ((lane < HD) if side == 0 else (lane >= HD)).astype(F32).astype(BF)
            probs = head_probs(queries * (mine * 0.125), keys, blocked)
            grad_probs = dot_nt(grads * mine, values)
            inner = jnp.sum(probs * grad_probs, axis=1, keepdims=True)
            grad_scores = (probs * (grad_probs - inner)).astype(BF)
            found.append(
                (
                    dot_nn(grad_scores, keys) * 0.125,
                    dot_tn(grad_scores, queries) * 0.125,
                    dot_tn(probs.astype(BF), grads),
                )
            )
        for j in range(3):
            grad_mixed[:, pl.ds(j * width + pair * 2 * HD, 2 * HD)] = jnp.where(
                lane < HD, found[0][j], found[1][j]
            ).astype(BF)
    total = jnp.zeros(stream.shape, F32)
    for core in range(2):
        for j in range(3):
            weight = crossed[core, :, j] if j < 2 else split[core, :, 0]
            total += dot_nt(grad_mixed[:, pl.ds(j * width + core * half, half)], flat(weight))

    def put(row, values):
        sums[row : row + 1, :] = values

    put(GAIN_ONE, jnp.sum(total * hat, axis=0, keepdims=True))
    put(SHIFT_ONE, jnp.sum(total, axis=0, keepdims=True))
    put(BIAS_QUERY, jnp.sum(grad_mixed[:, :width].astype(F32), axis=0, keepdims=True))
    put(BIAS_VALUE, jnp.sum(grad_mixed[:, 2 * width :].astype(F32), axis=0, keepdims=True))
    put(BIAS_PROJ, sum_proj[...])
    put(GAIN_TWO, gain_two[...])
    put(SHIFT_TWO, shift_two[...])
    put(BIAS_DOWN, sum_down[...])
    for j in range(4):
        put(BIAS_DOWN + 1 + j, sum_up[:, j * width : (j + 1) * width])
    sums[BIAS_DOWN + 5 :, :] = jnp.zeros((sums.shape[0] - BIAS_DOWN - 5, width), F32)
    grad_stream[...] = grad_middle[...] + norm_back(hat, scale, vectors[GAIN_ONE : GAIN_ONE + 1], total)


def backward_attention(spot, special_count, grad_middle, grad_proj, mixed, stream, vectors, others, crossed, split):
    rows, width = stream.shape
    shapes = [
        jax.ShapeDtypeStruct((rows, width), F32),
        jax.ShapeDtypeStruct((rows, 3 * width), BF),
        jax.ShapeDtypeStruct((16, width), F32),
    ]
    return pl.pallas_call(
        partial(backward_attention_kernel, special_count),
        in_specs=in_smem(1) + whole_vmem(5 + 5 + 2),
        out_specs=whole_vmem(len(shapes)),
        out_shape=shapes,
        scratch_shapes=[pltpu.VMEM((rows, width), BF)],
        compiler_params=kernel_params(12),
        cost_estimate=pl.CostEstimate(flops=0, bytes_accessed=0, transcendentals=0),
        name="backward_attention",
    )(spot, grad_middle, grad_proj, mixed, stream, vectors, *others, crossed, split)


def row_of(spot, step, far_x, steps):
    return 2 * lax.rem(spot[0] - step + steps, steps) + lax.rem(spot[1] + far_x, 2)


def feed_group(spot, core, part, far_y, at_z, normed_t, grad_up, grad_down_t, hidden, spare):
    count, wide, rows, half = spare.shape
    column = 2 * lax.rem(spot[2] + far_y, 2) + core
    if part == 0:
        left = normed_t[...] if at_z is None else normed_t[pl.ds(pl.multiple_of(at_z * 2 * rows, 2 * rows), 2 * rows), :]
        for j in range(wide):
            at = pl.multiple_of((column * wide + j) * half, half)
            out = dot_nn(left, grad_up[:, pl.ds(at, half)])
            spare[:, j] = out.reshape(count, rows, half).astype(BF)
    else:
        at = pl.multiple_of(column * wide * rows, wide * rows)
        left = grad_down_t[pl.ds(at, wide * rows), :]
        for row in range(count):
            columns = row * half if at_z is None else pl.multiple_of((at_z * 2 + row) * half, half)
            out = dot_nn(left, hidden[:, pl.ds(columns, half)])
            spare[row] = out.reshape(wide, rows, half).astype(BF)


def attention_group(spot, core, part, far_y, at_z, normed_t, grad_mixed, attended_t, grad_proj, spare):
    count, _, rows, half = spare.shape
    column = 2 * lax.rem(spot[2] + far_y, 2) + core
    if part == 0:
        out = dot_nn(normed_t[...], grad_mixed[column, :, :half])
    else:
        out = dot_nn(normed_t[...], grad_mixed[column, :, half:]) + dot_nn(
            attended_t[...], grad_proj[column]
        )
    spare[:, 0] = out.reshape(count, rows, half).astype(BF)


def each_group(fill, steps, ring, spot, core, operands, spare):
    wide = spare.shape[1]
    at_z = lax.rem(spot[0] - steps[0] + ring, ring) if len(steps) == 1 else None
    for part in range(2):
        for far_y in range(2):
            fill(spot, core, part, far_y, at_z, *operands, spare)
            for index, step in enumerate(steps):
                for far_x in range(2):
                    row = row_of(spot, step, far_x, ring) if at_z is None else lax.rem(spot[1] + far_x, 2)
                    for j in range(wide):
                        yield index, part, far_y, far_x, j, spare[row, j]


def place_in(part, far_y, far_x, j, wide):
    return (far_x * 2 + far_y) * wide + j if part == 0 else (4 + far_y * 2 + far_x) * wide + j


def sent_kernel(fill, steps, ring, spot, *refs):
    operands, out, spare = refs[:4], refs[4], refs[5]
    for index, part, far_y, far_x, j, block in each_group(fill, steps, ring, spot, 1 - spot[3], operands, spare):
        out[index, place_in(part, far_y, far_x, j, spare.shape[1])] = block


def kept_kernel(fill, steps, ring, spot, *refs):
    operands, got, outs, spare = refs[:4], refs[4], refs[5:-1], refs[-1]
    wide = spare.shape[1]
    for index, part, far_y, far_x, j, block in each_group(fill, steps, ring, spot, spot[3], operands, spare):
        total = block.astype(F32) + got[index, place_in(part, far_y, far_x, j, wide)].astype(F32)
        across, aside, stays = outs[3 * index : 3 * index + 3]
        if part == 0:
            at = far_y * wide + j
            target = across if far_x else stays
        else:
            at = far_x * wide + j
            target = aside if far_y else stays
            at = at if far_y else 2 * wide + at
        target[at] = total.astype(BF)


def spare_shape(place, steps, wide, rows, half):
    return pltpu.VMEM((2 if len(steps) == 1 else place.n_dp, wide, rows, half), BF)


def sent_part(place, spot, fill, wide, steps, operands):
    rows, half = (operands[0].shape[0] // place.n_dp, operands[0].shape[0] // 2)
    return pl.pallas_call(
        partial(sent_kernel, fill, steps, place.nz),
        in_specs=in_smem(1) + whole_vmem(4),
        out_specs=whole_vmem(1)[0],
        out_shape=jax.ShapeDtypeStruct((len(steps), 8 * wide, rows, half), BF),
        scratch_shapes=[spare_shape(place, steps, wide, rows, half)],
        compiler_params=kernel_params(10),
        cost_estimate=pl.CostEstimate(flops=0, bytes_accessed=0, transcendentals=0),
        name="gradient_sent",
    )(spot, *operands)


def kept_part(place, spot, fill, wide, steps, operands, got):
    rows, half = (operands[0].shape[0] // place.n_dp, operands[0].shape[0] // 2)
    shapes = [
        jax.ShapeDtypeStruct((size * wide, rows, half), BF) for _ in steps for size in (2, 2, 4)
    ]
    outs = pl.pallas_call(
        partial(kept_kernel, fill, steps, place.nz),
        in_specs=in_smem(1) + whole_vmem(5),
        out_specs=whole_vmem(len(shapes)),
        out_shape=shapes,
        scratch_shapes=[spare_shape(place, steps, wide, rows, half)],
        compiler_params=kernel_params(10),
        cost_estimate=pl.CostEstimate(flops=0, bytes_accessed=0, transcendentals=0),
        name="gradient_kept",
    )(spot, *operands, got)
    return {step: list(outs[3 * i : 3 * i + 3]) for i, step in enumerate(steps)}


def ring_kernel(stays, across, aside, *refs):
    out = refs[-1]
    count = across.shape[0]
    for at in range(2 * count):
        side = across[at] if at < count else aside[at - count]
        total = stays[at].astype(F32) + side.astype(F32)
        if len(refs) == 2:
            total = total + refs[0][at].astype(F32)
        out[at] = total.astype(BF)


def ring_block(stays, across, aside, running):
    operands = [stays, across, aside] + ([] if running is None else [running])
    return pl.pallas_call(
        ring_kernel,
        in_specs=whole_vmem(len(operands)),
        out_specs=whole_vmem(1)[0],
        out_shape=jax.ShapeDtypeStruct(stays.shape, BF),
        compiler_params=kernel_params(4),
        cost_estimate=pl.CostEstimate(flops=0, bytes_accessed=0, transcendentals=0),
        name="ring_block",
    )(*operands)


def fence(trees):
    flat = [list(tree.values()) if isinstance(tree, dict) else tree for tree in trees]
    flat = lax.optimization_barrier(flat)
    return [
        dict(zip(tree, values)) if isinstance(tree, dict) else values
        for tree, values in zip(trees, flat)
    ]


def pick(which, low, high):
    return jnp.where(which == 0, low, high)


def attention_groups(place, qkv, proj):
    half = proj.shape[1] // 2

    def of(core):
        parts = [qkv[:, (2 * j + core) * half : (2 * j + core + 1) * half] for j in range(3)]
        return jnp.stack(parts + [proj[:, core * half : (core + 1) * half]])

    return pick(place.core, of(0), of(1))


def feed_groups(place, up, down):
    rows, half = up.shape[0], down.shape[1] // 2

    def of(core):
        parts = [up[:, (core * 4 + j) * half : (core * 4 + j + 1) * half] for j in range(4)]
        return jnp.concatenate(
            [jnp.stack(parts), down[:, core * half : (core + 1) * half].reshape(4, rows, half)]
        )

    return pick(place.core, of(0), of(1))


class Gathered:
    def __init__(self, place, own, extra, turned, chunks):
        groups, rows, half = own.shape
        self.turned = turned
        self.chunks = chunks
        self.first = jnp.concatenate([own[: groups // 2].reshape(-1, half)] + extra)
        self.wide = self.first.shape[0]
        self.mine = pick(
            place.y,
            own[groups // 2 : groups // 2 + groups // 4],
            own[groups // 2 + groups // 4 :],
        ).reshape(-1, half)
        self.blocks = []
        self.across = {}
        self.aside = {}
        self.whole = []
        self.mate = []
        if turned:
            self.begin([])

    def begin(self, crossed):
        self.blocks.append(jnp.concatenate([self.first, self.mine] + crossed))

    def over_x(self, step):
        return self.blocks[step] if self.turned else self.blocks[step][: self.wide]

    def over_y(self, step):
        tails = [self.blocks[step][self.wide :]]
        if self.turned:
            tails.append(self.across[step][self.wide :])
        return tails

    def chunk(self, which, across, aside):
        return jnp.concatenate(
            [
                piece
                for step in self.chunks[which]
                for piece in (self.blocks[step], across.get(step), aside.get(step))
            ]
        )

    def parts(self):
        return self.whole + self.mate


class Reduced:
    def __init__(self, place):
        self.place = place
        self.operands = None
        self.kept = {}
        self.sides = {}
        self.running = None
        self.last = None

    def block(self, step):
        return ring_block(self.kept[step][2], *self.sides[step], self.running)


def pack_vectors(vectors, bias_up, half, rows):
    layers, part = vectors[0].shape
    packed = jnp.concatenate([jnp.stack(vectors, axis=1), bias_up.reshape(layers, -1, part)], axis=1)
    return jnp.pad(packed, ((0, 0), (0, rows - packed.shape[1]), (0, half - part)))


def image_kernel(images, spot, before, patches, after, specials, out, window):
    halo, count = before.shape[0], patches.shape[0]
    begin, length = image_frame(spot, images, count, halo)
    window[:halo] = before[...]
    window[halo : halo + count] = patches[...]
    window[halo + count : 2 * halo + count] = after[...]
    spare = window.shape[0] - 2 * halo - count
    window[2 * halo + count :] = jnp.zeros((spare, window.shape[1]), F32)
    inside = lax.broadcasted_iota(jnp.int32, (MOST, 1), 0) < length
    turned = pltpu.roll(window[...], lax.rem(window.shape[0] - begin, window.shape[0]), 0)
    out[:MOST] = jnp.where(inside, turned[:MOST], 0.0)
    last = out.shape[0] - MOST
    out[MOST:] = jnp.zeros((last, out.shape[1]), F32)
    out[MOST : MOST + specials.shape[0]] = specials[...]


def take_image(place, spot, patches, specials, halo, rows):
    count, width = patches.shape
    before = shift_seq(place, patches[count - halo :], 1)
    after = shift_seq(place, patches[:halo], -1)

    def build(before, patches, after, specials):
        return pl.pallas_call(
            partial(image_kernel, place.n_seq),
            in_specs=in_smem(1) + whole_vmem(4),
            out_specs=whole_vmem(1)[0],
            out_shape=jax.ShapeDtypeStruct((rows, width), F32),
            scratch_shapes=[pltpu.VMEM((MOST + 2 * halo, width), F32)],
            compiler_params=kernel_params(6),
        cost_estimate=pl.CostEstimate(flops=0, bytes_accessed=0, transcendentals=0),
            name="take_image",
        )(spot, before, patches, after, specials)

    return (before, patches, after, specials), build


def block_kernel(images, spot, *refs):
    streams, (before, after), owns, window = refs[:2], refs[2:4], refs[4:8], refs[8]
    for at, stream in enumerate(streams):
        own, specials = owns[2 * at : 2 * at + 2]
        halo, count = before.shape[0] // 2, own.shape[0]
        begin, length = image_frame(spot, images, count, halo)
        window[MOST:] = jnp.zeros((window.shape[0] - MOST, window.shape[1]), F32)
        inside = lax.broadcasted_iota(jnp.int32, (MOST, 1), 0) < length
        window[:MOST] = jnp.where(inside, stream[:MOST], 0.0)
        window[...] = pltpu.roll(window[...], begin, 0)
        before[at * halo : (at + 1) * halo] = window[:halo]
        own[...] = window[halo : halo + count]
        after[at * halo : (at + 1) * halo] = window[halo + count : 2 * halo + count]
        specials[...] = stream[MOST : MOST + specials.shape[0]]


def give_images(place, spot, streams, halo, count, special_count):
    width = streams[0].shape[1]
    return pl.pallas_call(
        partial(block_kernel, place.n_seq),
        in_specs=in_smem(1) + whole_vmem(2),
        out_specs=whole_vmem(6),
        out_shape=[
            jax.ShapeDtypeStruct((size, width), F32)
            for size in (2 * halo, 2 * halo, count, special_count, count, special_count)
        ],
        scratch_shapes=[pltpu.VMEM((MOST + 2 * halo, width), F32)],
        compiler_params=kernel_params(6),
        cost_estimate=pl.CostEstimate(flops=0, bytes_accessed=0, transcendentals=0),
        name="give_images",
    )(spot, *streams)


def finish_kernel(*refs):
    spot, refs = refs[0], refs[1:]
    inputs, outs = refs[: 6 * LAYERS], refs[6 * LAYERS :]
    sums, (own_one, own_two, from_before, from_after), outs = outs[:4], outs[4:8], outs[8:]
    (out_mixed, out_proj, out_up, out_down), (image_one, image_two), out_rows = outs[:4], outs[4:6], outs[6:]
    halo = from_before.shape[0] // 2
    for at, (own, image) in enumerate(((own_one, image_one), (own_two, image_two))):
        count = own.shape[0]
        image[:halo] = own[:halo] + from_before[at * halo : (at + 1) * halo]
        image[halo : count - halo] = own[halo : count - halo]
        image[count - halo :] = own[count - halo :] + from_after[at * halo : (at + 1) * halo]
    layers = LAYERS
    total = sums[0][...]
    for other in sums[1:]:
        total = total + other[...]
    place_dp = 2 * spot[0] + spot[1]
    each, width = total.shape[0] // layers, total.shape[1]
    part = out_rows[0].shape[1]
    turned = pltpu.roll(total, lax.rem(width - place_dp * part, width), 1)
    more = VECTOR_PIECES - BIAS_DOWN - 1
    row_ids = lax.broadcasted_iota(jnp.int32, total.shape, 0)
    half_turned = pltpu.roll(total, lax.rem(width - lax.rem(place_dp * more * part, width), width), 1)
    for layer in range(layers):
        for row in range(BIAS_DOWN + 1):
            at = layer * each + row
            out_rows[row][layer : layer + 1, :] = turned[at : at + 1, :part]
        at = layer * each + BIAS_DOWN + 1 + place_dp * more * part // width
        row = jnp.sum(jnp.where(row_ids == at, half_turned, 0.0), axis=0, keepdims=True)
        out_rows[-1][layer : layer + 1, :] = row[:, : more * part]
    for layer in range(layers):
        last, aside, across = inputs[6 * layer : 6 * layer + 3]
        one = last[0].astype(F32) + aside[0].astype(F32)
        two = last[2].astype(F32) + across[0].astype(F32)
        cut = one.shape[1] // 2
        out_mixed[layer] = jnp.concatenate([one, two[:, :cut]], axis=1)
        out_proj[layer] = two[:, cut:]
        last, aside, across = inputs[6 * layer + 3 : 6 * layer + 6]
        half = last.shape[2]
        for j in range(2):
            out_up[layer, :, j * half : (j + 1) * half] = last[j].astype(F32) + aside[j].astype(F32)
        downs = [last[4 + j].astype(F32) + across[j].astype(F32) for j in range(2)]
        for j in range(2):
            out_down[layer, j * downs[j].shape[0] : (j + 1) * downs[j].shape[0]] = downs[j]


def finish(place, spot, parts, sums, images, rows, width):
    shapes = [
        jax.ShapeDtypeStruct((LAYERS, rows, columns), F32)
        for rows, columns in (
            (rows, 3 * width // 4),
            (rows, width // 4),
            (rows, width),
            (width // 4, 4 * rows),
        )
    ]
    shapes += [jax.ShapeDtypeStruct(images[0].shape, F32)] * 2
    more = VECTOR_PIECES - BIAS_DOWN - 1
    shapes += [jax.ShapeDtypeStruct((LAYERS, rows), F32)] * (BIAS_DOWN + 1)
    shapes += [jax.ShapeDtypeStruct((LAYERS, more * rows), F32)]
    flat_parts = [array for layer in parts for array in layer] + sums + images
    return pl.pallas_call(
        finish_kernel,
        in_specs=in_smem(1) + whole_vmem(len(flat_parts)),
        out_specs=whole_vmem(len(shapes)),
        out_shape=shapes,
        compiler_params=kernel_params(10),
        cost_estimate=pl.CostEstimate(flops=0, bytes_accessed=0, transcendentals=0),
        name="finish",
    )(spot, *flat_parts)


def local_walked(
    place,
    patches,
    specials,
    lengths,
    keep_mask,
    norm1_gain,
    norm1_bias,
    qkv_weight,
    query_bias,
    value_bias,
    proj_weight,
    proj_bias,
    norm2_gain,
    norm2_bias,
    fc1_weight,
    fc1_bias,
    fc2_weight,
    fc2_bias,
    cot_patches,
    cot_specials,
):
    count, width = patches.shape
    special_count = specials.shape[0]
    images = lengths.shape[1]
    halo = (MOST - count) * (images // 2)
    rows = -(-(MOST + special_count) // 16) * 16
    nz = place.nz
    pairs = ((0, 1), (2, 3))
    part_rows = proj_weight.shape[1]
    spot = jnp.stack([place.z, place.x, place.y, place.core, place.seq]).astype(jnp.int32)
    spot = jnp.concatenate([spot, lengths.reshape(-1), keep_mask.reshape(-1)])

    shards = (norm1_gain, norm1_bias, query_bias, value_bias, proj_bias, norm2_gain, norm2_bias, fc2_bias)

    extras = pack_vectors(list(shards), fc1_bias, width // 2, EXTRA_ROWS)

    def attention_unit(layer, qkv, proj, extra):
        return Gathered(place, attention_groups(place, qkv, proj), [extra], layer == 0, pairs)

    units = [attention_unit(0, qkv_weight[0], proj_weight[0], extras[0])]
    image, build = take_image(place, spot, patches, specials, halo, rows)
    inputs = {
        "weights": (fc1_weight[0], fc2_weight[0], qkv_weight[1], proj_weight[1], extras[1], fc1_weight[1], fc2_weight[1]),
        "cots": (cot_patches, cot_specials),
    }
    vectors, bias_up = ([None] * LAYERS, [None] * LAYERS)
    streams = [None] * (LAYERS + 1)
    middles, normed_one_ts, normed_two_ts, mixeds, attended_ts, hiddens, slopes = (
        [None] * LAYERS for _ in range(7)
    )
    weights = [None] * (2 * LAYERS)
    unit_count = 2 * LAYERS
    last_slot = 3 * unit_count + 1
    at_x, at_y = ([[] for _ in range(last_slot + 2)] for _ in range(2))
    for which in range(unit_count):
        for step in range(nz):
            slot = 3 * which + step
            at_x[slot].append((which, step))
            at_y[slot + (which == 0)].append((which, step))
    at_core = {4: [(0, 0)], 5: [(0, 1), (1, 0)], 7: [(1, 1)], 8: [(2, 0)], 10: [(2, 1)], 11: [(3, 0)], 12: [(3, 1)], 13: [(3, 2)]}
    carried = {}
    grad = None
    for slot in range(last_slot + 1):
        new = {}
        index, step = divmod(slot, 3)
        if index < unit_count:
            new["z"] = place.ring_z(units[index].blocks[step])
        for which, at in at_x[slot]:
            new["x", which, at] = place.swap_x(units[which].over_x(at))
        for which, at in at_y[slot]:
            tails = units[which].over_y(at)
            new["y", which, at] = place.swap_seq(tails[0] if len(tails) == 1 else jnp.concatenate(tails), 2)
        for which, at in at_core.get(slot, []):
            new["core", which, at] = place.swap_seq(units[which].whole[at], 1)
        for which, at in at_y[slot]:
            for index_of, chunk in enumerate(units[which].chunks):
                if chunk[-1] == at:
                    unit = units[which]
                    across = {**unit.across, **{k[2]: v for k, v in new.items() if k[:2] == ("x", which)}}
                    aside = {**unit.aside, **{k[2]: v for k, v in new.items() if k[:2] == ("y", which)}}
                    new["chunk", which, index_of] = unit.chunk(index_of, across, aside)
        later = {1: 1, 4: 2, 8: 3}.get(slot)
        if later:
            new["later"] = place.swap_x(units[later].mine)
        if slot == 0:
            new["image"] = image
        if slot == 5:
            carried["stream"] = build(*image)
        if slot == 3 * unit_count:
            new["image"], build = take_image(place, spot, *inputs["cots"], halo, rows)
        if slot == 3 * unit_count + 1:
            grad = build(*image)
        if slot in (9, 11):
            layer = slot // 11
            new["forward"] = forward_attention(
                place, spot, 2 * layer, special_count, carried["stream"], units[2 * layer], EXTRA_ROWS
            )
        if slot == 10:
            hidden, slope, crossed, split = forward_up(place, spot, carried["normed"], bias_up[0], units[1])
            output = forward_down(place, spot, 1, carried["middle"], hidden, vectors[0], split)
            new["feed"] = (output, hidden, slope, crossed, split)
        if slot in (3, 5):
            names = [key for key in new if key[0] in ("x", "y")]
            swapped, weights_1 = fence(([new[key] for key in names], weights_1))
            new.update(zip(names, swapped))
            if slot == 3:
                unit = attention_unit(1, *weights_1[:3])
            else:
                unit = Gathered(place, feed_groups(place, *weights_1[3:]), [], False, ((0, 1), (2,), (3,)))
            new["unit"] = (unit.first, unit.mine)
        if step == 2 and index + 1 < len(units) and units[index + 1].blocks:
            carried["begin"] = units[index + 1].blocks[0]
        gate = inputs if slot in (0, 3 * unit_count - 1) else {}
        new, carried, gate = fence((new, carried, gate))
        inputs.update(gate)
        if slot == 0:
            up_0, down_0, *weights_1 = inputs.pop("weights")
            units.append(Gathered(place, feed_groups(place, up_0, down_0), [], False, pairs))
        if "unit" in new:
            unit.first, unit.mine = new["unit"]
            units.append(unit)
        if "begin" in carried:
            units[index + 1].blocks[0] = carried.pop("begin")
        if "image" in new:
            image = new["image"]
        if "later" in new:
            units[later].begin([new["later"]])
        if "z" in new:
            units[index].blocks.append(new["z"])
        for which, at in at_core.get(slot, []):
            units[which].mate.append(new["core", which, at])
        for which, at in at_x[slot]:
            units[which].across[at] = new["x", which, at]
        for which, at in at_y[slot]:
            units[which].aside[at] = new["y", which, at]
        for key in new:
            if key[0] == "chunk":
                units[key[1]].whole.append(new[key])
        if "forward" in new:
            streams[layer] = carried.pop("stream")
            middle, normed, normed_one_ts[layer], normed_two_ts[layer], mixeds[layer], _, attended_ts[layer], crossed, split, vectors[layer], bias_up[layer] = new["forward"]
            weights[2 * layer] = [crossed, split]
            middles[layer] = middle
            carried["middle"], carried["normed"] = middle, normed
        if "feed" in new:
            carried["stream"], hiddens[0], slopes[0], *weights[1] = new["feed"]
            del carried["middle"], carried["normed"]
    hiddens[1], slopes[1], *weights[3] = forward_up(
        place, spot, carried["normed"], bias_up[1], units[3]
    )

    reduces = [Reduced(place) for _ in range(2 * LAYERS)]
    lasts = [None] * (2 * LAYERS)
    back = [{} for _ in range(LAYERS)]

    def feed_back(layer, grad):
        found = back[layer]
        found["down_t"], found["up"], found["sum_down"], found["sum_up"] = backward_feed(
            place, spot, 2 * layer + 1, grad, slopes[layer], weights[2 * layer + 1][1]
        )

    def feed_operands(layer):
        reduces[2 * (LAYERS - 1 - layer)].operands = (
            normed_two_ts[layer], back[layer]["up"], back[layer]["down_t"], hiddens[layer]
        )

    def middle_back(layer, grad):
        found = back[layer]
        found["middle"], found["proj"], found["sum_proj"], found["gain"], found["shift"] = backward_middle(
            place, spot, 2 * layer, grad, found["up"], middles[layer], vectors[layer], weights[2 * layer + 1][0]
        )

    def attention_back(layer):
        found = back[layer]
        others = [found[name] for name in ("sum_proj", "gain", "shift", "sum_down", "sum_up")]
        found["grad"], found["mixed"], found["sums"] = backward_attention(
            spot, special_count, found["middle"], found["proj"], mixeds[layer], streams[layer], vectors[layer], others, *weights[2 * layer]
        )

    def attention_operands(layer):
        found = back[layer]
        wide = 3 * width // 4
        cut = width // 4
        mixed = jnp.stack(
            [jnp.pad(found["mixed"][:, i * wide : (i + 1) * wide], ((0, 0), (0, cut))) for i in range(4)]
        )
        proj = jnp.stack([jnp.pad(found["proj"][:, i * cut : (i + 1) * cut], ((0, 0), (cut, 0))) for i in range(4)])
        unit = reduces[2 * (LAYERS - 1 - layer) + 1]
        unit.operands = (normed_one_ts[layer], mixed, attended_ts[layer], proj)

    fills = [(feed_group, 2), (attention_group, 1)] * LAYERS
    all_steps = (1, 2, 3, 0)
    cuts = [((1,), (2, 3, 0))] + [(all_steps,)] * (len(reduces) - 1)

    def sent_cut(which, cut):
        fill, wide = fills[which]
        return sent_part(place, spot, fill, wide, cuts[which][cut], reduces[which].operands)

    def keep_cut(which, cut, got):
        fill, wide = fills[which]
        unit = reduces[which]
        unit.kept.update(kept_part(place, spot, fill, wide, cuts[which][cut], unit.operands, got))

    feed_back(1, grad)
    feed_operands(1)
    sent = [sent_cut(0, 0), None]
    back[1], sent = fence((back[1], sent[:1]))
    final_slot = 3 * len(reduces)
    total = given = None
    rung = []
    got = {}
    sending = {(0, 0): sent[0]}
    for slot in range(-2, final_slot + 1):
        new = {}
        work = {}
        for which, unit in enumerate(reduces):
            at = slot - 3 * which
            if 0 <= at <= 2:
                new["z", which] = place.ring_z(unit.block(at + 1))
            if at == 3:
                unit.last = unit.block(0)
                work["last", which] = unit.last
        for base, group in ((final_slot - 2, range(len(reduces) - 1)), (final_slot, [len(reduces) - 1])):
            if slot == base:
                ends = [reduces[which].last for which in group]
                parts = [end.shape[0] // 4 for end in ends]
                aside = place.swap_seq(
                    jnp.concatenate([end[part : 2 * part] for end, part in zip(ends, parts)]), 2
                )
                across = place.swap_x(jnp.concatenate([end[3 * part :] for end, part in zip(ends, parts)]))
                begins = 0
                for which, end, part in zip(group, ends, parts):
                    lasts[which] = [end, aside[begins : begins + part], across[begins : begins + part]]
                    begins += part
                if slot < final_slot:
                    new["lasts"] = [lasts[which] for which in group]
        if slot == -2:
            sending[0, 1] = sent_cut(0, 1)
            work["sending"] = sending[0, 1]
        if slot == -1:
            keep_cut(0, 0, got.pop((0, 0)))
        for which, base in ((2, 4), (3, 7)):
            if slot == base:
                keep_cut(which, 0, got.pop((which, 0)))
                for step in all_steps:
                    work["kept", which, step] = reduces[which].kept[step]
        for key, base in (((0, 0), -2), ((0, 1), -1), ((1, 0), 2), ((2, 0), 3), ((3, 0), 6)):
            if slot == base:
                new["core", key] = place.swap_seq(sending.pop(key), 1)
        if slot == -1:
            keep_cut(0, 1, new["core", (0, 1)])
            for step in cuts[0][1]:
                work["kept", 0, step] = reduces[0].kept[step]
        if slot == 2:
            keep_cut(1, 0, new["core", (1, 0)])
        for which, unit in enumerate(reduces):
            at = slot - 3 * which
            if -1 <= at <= 2:
                step = (at + 2) % nz
                new["side", which] = (
                    place.swap_x(unit.kept[step][0]),
                    place.swap_seq(unit.kept[step][1], 2),
                )
        if slot == 3:
            attention_operands(0)
            work["sending"] = sent_cut(3, 0)
        if slot == -1:
            middle_back(1, grad)
        if slot == 4:
            streams[LAYERS] = forward_down(place, spot, 3, carried["middle"], hiddens[1], vectors[1], weights[3][1])
            work["output"] = streams[LAYERS]
        if slot == 0:
            attention_back(1)
        if slot == 1:
            attention_operands(1)
            names = ("down_t", "up", "sum_down", "sum_up", "middle", "proj", "sum_proj", "gain", "shift")
            back[0] = dict(
                zip(
                    names,
                    backward_feed_middle(
                        place, spot, (0, 1), back[1]["grad"], slopes[0], weights[1][1], middles[0], vectors[0], weights[1][0]
                    ),
                )
            )
            feed_operands(0)
            work["sending"] = (sent_cut(1, 0), sent_cut(2, 0))
        if slot == 2:
            attention_back(0)
        if slot in (-1, 0):
            work["back", 1] = back[1]
        if slot in (1, 2):
            work["back", 0] = back[0]
        if slot == 3:
            total = jnp.concatenate([back[layer]["sums"] for layer in range(LAYERS)])
            new["sum"] = place.swap_seq(total, 1)
        if slot == 4:
            new["sum"] = place.swap_seq(total, 2)
        if slot == 6:
            new["sum"] = place.swap_x(total)
        if slot in (7, 9, 11):
            new["ringing"] = [place.ring_z(total if slot == 7 else rung[-1])]
        if slot == final_slot - 4:
            work["images"] = give_images(place, spot, given, halo, count, special_count)
        if slot == final_slot - 3:
            images_before, images_after, *owns = images
            new["image_down"] = shift_seq(place, images_before, -1)
        if slot == final_slot - 1:
            new["image_up"] = shift_seq(place, images_after, 1)
        pending = {}
        if slot == final_slot - 2:
            pending["after"] = images_after
        for which, unit in enumerate(reduces):
            at = slot + 1 - 3 * which
            if 0 <= at <= 2:
                step = (at + 2) % nz
                if step in unit.kept and ("kept", which, step) not in work:
                    pending["kept", which] = unit.kept[step]
        if slot == final_slot - 5:
            pending["give"] = [streams[LAYERS], back[0]["grad"]]
        for key, base in (((2, 0), 2), ((3, 0), 5)):
            if slot == base:
                pending["sending", key] = sending[key]
        for key, base in (((2, 0), 4), ((3, 0), 7)):
            if slot == base - 1 and key in got:
                pending["got", key] = got[key]
        new, work, pending = fence((new, work, pending))
        if "sending" in work:
            if slot == 1:
                sending[1, 0], sending[2, 0] = work.pop("sending")
            else:
                sending[(0, 1) if slot == -2 else (3, 0)] = work.pop("sending")
        for key in [key for key in pending if key[0] == "sending"]:
            sending[key[1]] = pending.pop(key)
        if "output" in work:
            streams[LAYERS] = work.pop("output")
        for key, value in work.items():
            if key[0] == "back":
                back[key[1]] = value
            if key[0] == "last":
                reduces[key[1]].last = value
            if key == "images":
                images = value
            if key[0] == "kept":
                reduces[key[1]].kept[key[2]] = value
        if "give" in pending:
            given = pending.pop("give")
        if "after" in pending:
            images_after = pending.pop("after")
        for key in [key for key in pending if key[0] == "got"]:
            got[key[1]] = pending.pop(key)
        for key, value in pending.items():
            reduces[key[1]].kept[(slot + 1 - 3 * key[1] + 2) % nz] = value
        for key, value in new.items():
            if key[0] == "core":
                got[key[1]] = value
            if key[0] == "z":
                reduces[key[1]].running = value
            if key[0] == "side":
                reduces[key[1]].sides[(slot - 3 * key[1] + 2) % nz] = value
        if "image_down" in new:
            image_down = new["image_down"]
        if "image_up" in new:
            sides = (new["image_up"], image_down)
        if "lasts" in new:
            lasts[: len(new["lasts"])] = new["lasts"]
        if "sum" in new:
            total = total + new["sum"]
        if "ringing" in new:
            rung += new["ringing"]

    wm, wp, wu, wd, out_patches, grad_patches, g1, s1, bq, bv, bp, g2, s2, bd, bu = finish(
        place,
        spot,
        [lasts[3] + lasts[2], lasts[1] + lasts[0]],
        [total] + rung,
        [owns[0], owns[2], *sides],
        part_rows,
        width,
    )
    wd = jnp.transpose(wd, (0, 2, 1))
    return (
        out_patches,
        owns[1],
        grad_patches,
        owns[3],
        g1,
        s1,
        wm,
        bq,
        bv,
        wp,
        bp,
        g2,
        s2,
        wu,
        bu,
        wd,
        bd,
    )


def local(*args):
    place = Place()
    if place.walked:
        return local_walked(place, *args)
    return local_plain(place, *args)


def solution(mesh):
    in_specs = (
        P(("dp", "seq"), None),
        P(("dp", "seq"), None),
        P("dp", None),
        P("dp", None, None),
        P(None, "dp"),
        P(None, "dp"),
        P(None, "dp", None),
        P(None, "dp"),
        P(None, "dp"),
        P(None, "dp", None),
        P(None, "dp"),
        P(None, "dp"),
        P(None, "dp"),
        P(None, "dp", None),
        P(None, "dp"),
        P(None, "dp", None),
        P(None, "dp"),
        P(("dp", "seq"), None),
        P(("dp", "seq"), None),
    )
    out_specs = (
        P(("dp", "seq"), None),
        P(("dp", "seq"), None),
        P(("dp", "seq"), None),
        P(("dp", "seq"), None),
        P(None, "dp"),
        P(None, "dp"),
        P(None, "dp", "seq"),
        P(None, "dp"),
        P(None, "dp"),
        P(None, "dp", "seq"),
        P(None, "dp"),
        P(None, "dp"),
        P(None, "dp"),
        P(None, "dp", "seq"),
        P(None, "dp"),
        P(None, "dp", "seq"),
        P(None, "dp"),
    )
    return jax.shard_map(local, mesh=mesh, in_specs=in_specs, out_specs=out_specs, check_vma=False)
```

```python
from functools import partial

import jax
import jax.numpy as jnp
from jax import lax
from jax.experimental import pallas as pl
from jax.experimental.pallas import tpu as pltpu
from jax.sharding import PartitionSpec as P

HD = 64
LAYERS = 2
MOST = 280
KEEP_RATE = 0.9
EPSILON = 1e-06
MASKED = -1e30
GAIN_ONE, SHIFT_ONE, BIAS_QUERY, BIAS_VALUE, BIAS_PROJ, GAIN_TWO, SHIFT_TWO, BIAS_DOWN = range(8)
VECTOR_PIECES = 12
EXTRA_ROWS = 16
MIB = 1024 * 1024
ROOT_HALF = 0.7071067811865476
ROOT_TWO_PI = 0.3989422804014327
BF = jnp.bfloat16
F32 = jnp.float32


def dot_nn(left, right):
    return lax.dot_general(left, right, (((1,), (0,)), ((), ())), preferred_element_type=F32)


def dot_nt(left, right):
    return lax.dot_general(left, right, (((1,), (1,)), ((), ())), preferred_element_type=F32)


def dot_tn(left, right):
    return lax.dot_general(left, right, (((0,), (0,)), ((), ())), preferred_element_type=F32)


class Place:
    def __init__(self):
        self.n_dp = lax.axis_size("dp")
        self.n_seq = lax.axis_size("seq")
        self.walked = self.n_dp == 8 and self.n_seq == 4
        self.dp = lax.axis_index("dp")
        self.seq = lax.axis_index("seq")
        if self.walked:
            self.core = self.seq % 2
            self.y = self.seq // 2
            self.x = self.dp % 2
            self.z = self.dp // 2
            self.nz = self.n_dp // 2

    def swap_seq(self, values, mask):
        return lax.ppermute(values, "seq", [(i, i ^ mask) for i in range(self.n_seq)])

    def swap_x(self, values):
        return lax.ppermute(values, "dp", [(i, i ^ 1) for i in range(self.n_dp)])

    def ring_z(self, values, by=1):
        return lax.ppermute(values, "dp", [(i, (i + 2 * by) % self.n_dp) for i in range(self.n_dp)])


def gather_matrix(shard):
    return lax.all_gather(shard, "dp", axis=0, tiled=True)


def reduce_matrix(acts, grads):
    part = dot_tn(acts, grads).astype(BF)
    part = lax.psum_scatter(part, "dp", scatter_dimension=0, tiled=True)
    return lax.psum_scatter(part, "seq", scatter_dimension=1, tiled=True).astype(F32)


def reduce_vectors(place, vectors):
    packed = jnp.concatenate(
        [vector.reshape(place.n_dp, vector.shape[0] // place.n_dp) for vector in vectors], axis=1
    )
    mask = 1
    while mask < place.n_seq:
        packed = packed + place.swap_seq(packed, mask)
        mask *= 2
    packed = lax.all_to_all(packed, "dp", split_axis=0, concat_axis=0, tiled=True)
    total = jnp.sum(packed, axis=0)
    results, at = [], 0
    for vector in vectors:
        width = vector.shape[0] // place.n_dp
        results.append(total[at : at + width])
        at += width
    return results


def gather_vectors(place, shards):
    widths = [shard.shape[1] for shard in shards]
    packed = jnp.concatenate(shards, axis=1)
    rows = packed.shape[0]
    spread = jnp.broadcast_to(packed[None], (place.n_dp,) + packed.shape)
    spread = lax.all_to_all(spread, "dp", split_axis=0, concat_axis=0, tiled=True)
    results, at = [], 0
    for width in widths:
        piece = spread[:, :, at : at + width]
        results.append(jnp.transpose(piece, (1, 0, 2)).reshape(rows, place.n_dp * width).astype(F32))
        at += width
    return results


def normalize(values):
    center = values - jnp.mean(values, axis=-1, keepdims=True)
    spread = jnp.mean(center * center, axis=-1, keepdims=True)
    scale = lax.rsqrt(spread + EPSILON)
    return (center * scale, scale)


def normalize_back(hat, scale, gain, grad):
    scaled = grad * gain
    first = jnp.mean(scaled, axis=-1, keepdims=True)
    second = jnp.mean(scaled * hat, axis=-1, keepdims=True)
    back = scale * (scaled - first - hat * second)
    return (back, jnp.sum(grad * hat, axis=0), jnp.sum(grad, axis=0))


def heads_of(mixed):
    rows = mixed.shape[0]
    width = mixed.shape[1] // 3
    split = mixed.reshape(rows, 3, width // HD, HD)
    return (split[:, 0], split[:, 1], split[:, 2])


def attend(mixed, key_ok):
    queries, keys, values = heads_of(mixed)
    scores = jnp.einsum("qhd,khd->hqk", queries, keys, preferred_element_type=F32) * 0.125
    scores = jnp.where(key_ok[None, None, :], scores, MASKED)
    top = jnp.max(scores, axis=2, keepdims=True)
    powers = jnp.exp(scores - top)
    probs = powers / jnp.sum(powers, axis=2, keepdims=True)
    out = jnp.einsum("hqk,khd->qhd", probs.astype(BF), values, preferred_element_type=F32)
    return (out.reshape(mixed.shape[0], -1).astype(BF), probs)


def attend_back(mixed, probs, grad_out):
    queries, keys, values = heads_of(mixed)
    rows = mixed.shape[0]
    grads = grad_out.reshape(queries.shape)
    grad_probs = jnp.einsum("qhd,khd->hqk", grads, values, preferred_element_type=F32)
    inner = jnp.sum(probs * grad_probs, axis=2, keepdims=True)
    grad_scores = (probs * (grad_probs - inner)).astype(BF)
    grad_values = jnp.einsum("hqk,qhd->khd", probs.astype(BF), grads, preferred_element_type=F32)
    grad_queries = (
        jnp.einsum("hqk,khd->qhd", grad_scores, keys, preferred_element_type=F32) * 0.125
    )
    grad_keys = (
        jnp.einsum("hqk,qhd->khd", grad_scores, queries, preferred_element_type=F32) * 0.125
    )
    return jnp.concatenate(
        [grad.reshape(rows, -1).astype(BF) for grad in (grad_queries, grad_keys, grad_values)], axis=1
    )


def layer_forward(stream, vectors, matrices, keeps, key_ok):
    gain_one, shift_one, bias_query, bias_value, bias_proj, gain_two, shift_two, bias_down, bias_up = vectors
    w_mixed, w_proj, w_up, w_down = matrices
    hat_one, scale_one = normalize(stream)
    normed_one = (hat_one * gain_one + shift_one).astype(BF)
    bias_mixed = jnp.concatenate([bias_query, jnp.zeros_like(bias_query), bias_value])
    mixed = (dot_nn(normed_one, w_mixed) + bias_mixed).astype(BF)
    attended, probs = attend(mixed, key_ok)
    middle = stream + keeps[0] * (dot_nn(attended, w_proj) + bias_proj) / KEEP_RATE
    hat_two, scale_two = normalize(middle)
    normed_two = (hat_two * gain_two + shift_two).astype(BF)
    hidden_pre = dot_nn(normed_two, w_up) + bias_up
    share = 0.5 * (1.0 + lax.erf(hidden_pre * ROOT_HALF))
    hidden = (hidden_pre * share).astype(BF)
    slope = share + hidden_pre * jnp.exp(-0.5 * hidden_pre * hidden_pre) * ROOT_TWO_PI
    output = middle + keeps[1] * (dot_nn(hidden, w_down) + bias_down) / KEEP_RATE
    saved = (hat_one, scale_one, normed_one, mixed, probs, attended, hat_two, scale_two, normed_two, hidden, slope)
    return (output, saved)


def layer_back(place, grad_stream, saved, vectors, matrices, keeps):
    hat_one, scale_one, normed_one, mixed, probs, attended, hat_two, scale_two, normed_two, hidden, slope = saved
    gain_one, gain_two = (vectors[0], vectors[5])
    w_mixed, w_proj, w_up, w_down = matrices
    width = grad_stream.shape[1]
    grad_down = (keeps[1] * grad_stream / KEEP_RATE).astype(BF)
    total_down = reduce_matrix(hidden, grad_down)
    grad_up = (dot_nt(grad_down, w_down) * slope).astype(BF)
    total_up = reduce_matrix(normed_two, grad_up)
    back_two, grad_gain_two, grad_shift_two = normalize_back(
        hat_two, scale_two, gain_two, dot_nt(grad_up, w_up)
    )
    grad_middle = grad_stream + back_two
    grad_proj = (keeps[0] * grad_middle / KEEP_RATE).astype(BF)
    total_proj = reduce_matrix(attended, grad_proj)
    grad_attended = dot_nt(grad_proj, w_proj).astype(BF)
    grad_mixed = attend_back(mixed, probs, grad_attended)
    total_mixed = reduce_matrix(normed_one, grad_mixed)
    back_one, grad_gain_one, grad_shift_one = normalize_back(
        hat_one, scale_one, gain_one, dot_nt(grad_mixed, w_mixed)
    )
    grad_input = grad_middle + back_one
    sum_mixed = jnp.sum(grad_mixed, axis=0, dtype=F32)
    totals = reduce_vectors(
        place,
        (
            grad_gain_one,
            grad_shift_one,
            sum_mixed[:width],
            sum_mixed[2 * width :],
            jnp.sum(grad_proj, axis=0, dtype=F32),
            grad_gain_two,
            grad_shift_two,
            jnp.sum(grad_down, axis=0, dtype=F32),
            jnp.sum(grad_up, axis=0, dtype=F32),
        ),
    )
    return (grad_input, totals, (total_mixed, total_proj, total_up, total_down))


def shift_seq(place, values, by):
    count = place.n_seq
    return lax.ppermute(values, "seq", [(i, i + by) for i in range(count) if 0 <= i + by < count])


def to_image(place, patches, specials, halo, start, length, rows):
    count, width = patches.shape
    before = shift_seq(place, patches[count - halo :], 1)
    after = shift_seq(place, patches[:halo], -1)
    spare = jnp.zeros((MOST + 2 * halo - count - 2 * halo, width), patches.dtype)
    window = jnp.concatenate([before, patches, after, spare])
    image = lax.dynamic_slice_in_dim(window, start, MOST)
    inside = jnp.arange(MOST, dtype=jnp.int32)[:, None] < length
    image = jnp.where(inside, image, 0.0)
    spare = jnp.zeros((rows - MOST - specials.shape[0], width), patches.dtype)
    return jnp.concatenate([image, specials, spare])


def from_image(place, stream, halo, start, length, count, specials):
    width = stream.shape[1]
    inside = jnp.arange(MOST, dtype=jnp.int32)[:, None] < length
    image = jnp.where(inside, stream[:MOST], 0.0)
    window = jnp.zeros((MOST + 2 * halo, width), stream.dtype)
    window = lax.dynamic_update_slice_in_dim(window, image, start, 0)
    own = window[halo : halo + count]
    from_before = shift_seq(place, window[halo + count : count + 2 * halo], 1)
    from_after = shift_seq(place, window[:halo], -1)
    blank = jnp.zeros((count - halo, width), stream.dtype)
    own = own + jnp.concatenate([from_before, blank]) + jnp.concatenate([blank, from_after])
    return (own, stream[MOST : MOST + specials])


def local_plain(
    place,
    patches,
    specials,
    lengths,
    keep_mask,
    norm1_gain,
    norm1_bias,
    qkv_weight,
    query_bias,
    value_bias,
    proj_weight,
    proj_bias,
    norm2_gain,
    norm2_bias,
    fc1_weight,
    fc1_bias,
    fc2_weight,
    fc2_bias,
    cot_patches,
    cot_specials,
):
    count = patches.shape[0]
    special_count = specials.shape[0]
    images = lengths.shape[1]
    halo = (MOST - count) * (images // 2)
    rows = -(-(MOST + special_count) // 16) * 16
    before = jnp.sum(jnp.where(jnp.arange(images) < place.seq, lengths[0], 0))
    length = lax.dynamic_index_in_dim(lengths[0], place.seq, 0, keepdims=False)
    start = before - place.seq * count + halo
    keeps = lax.dynamic_index_in_dim(keep_mask[0], place.seq, 0, keepdims=False).astype(F32)
    row_ids = jnp.arange(rows, dtype=jnp.int32)
    key_ok = (row_ids < length) | ((row_ids >= MOST) & (row_ids < MOST + special_count))

    shards = (norm1_gain, norm1_bias, query_bias, value_bias, proj_bias, norm2_gain, norm2_bias, fc2_bias, fc1_bias)
    vectors_all = gather_vectors(place, shards)
    stream = to_image(place, patches, specials, halo, start, length, rows)
    matrices = []
    for layer in range(LAYERS):
        matrices.append(
            tuple(
                gather_matrix(shard[layer])
                for shard in (qkv_weight, proj_weight, fc1_weight, fc2_weight)
            )
        )
    vectors = [tuple(vector[layer] for vector in vectors_all) for layer in range(LAYERS)]
    saved = []
    for layer in range(LAYERS):
        stream, kept = layer_forward(
            stream, vectors[layer], matrices[layer], keeps[2 * layer : 2 * layer + 2], key_ok
        )
        saved.append(kept)
    out_patches, out_specials = from_image(place, stream, halo, start, length, count, special_count)
    grad = to_image(place, cot_patches, cot_specials, halo, start, length, rows)
    vector_totals, matrix_totals = ([None] * LAYERS, [None] * LAYERS)
    for layer in reversed(range(LAYERS)):
        grad, vector_totals[layer], matrix_totals[layer] = layer_back(
            place, grad, saved[layer], vectors[layer], matrices[layer], keeps[2 * layer : 2 * layer + 2]
        )
    grad_patches, grad_specials = from_image(place, grad, halo, start, length, count, special_count)
    vector_out = [jnp.stack([vector_totals[layer][i] for layer in range(LAYERS)]) for i in range(9)]
    matrix_out = [jnp.stack([matrix_totals[layer][i] for layer in range(LAYERS)]) for i in range(4)]
    g1, s1, bq, bv, bp, g2, s2, bd, bu = vector_out
    wm, wp, wu, wd = matrix_out
    return (
        out_patches,
        out_specials,
        grad_patches,
        grad_specials,
        g1,
        s1,
        wm,
        bq,
        bv,
        wp,
        bp,
        g2,
        s2,
        wu,
        bu,
        wd,
        bd,
    )


def whole_vmem(count):
    return [pl.BlockSpec(memory_space=pltpu.VMEM)] * count


def in_smem(count):
    return [pl.BlockSpec(memory_space=pltpu.SMEM)] * count


def kernel_params(mib):
    return pltpu.CompilerParams(vmem_limit_bytes=mib * MIB)


def place_pieces(spot, parts, chunks, crossed, split, extra, turned):
    z, x, y, core = (spot[i] for i in range(4))
    steps = sum(len(chunk) for chunk in chunks)
    first, rows = crossed.shape[2:4]
    quarter = split.shape[2] // 2
    more = 0 if extra is None else extra.shape[1]
    wide, piece = first * rows + more, quarter * rows
    block = wide + (piece if turned else 2 * piece)
    spots = {
        (0, 0): wide,
        (1, 0): block + wide if turned else wide + piece,
        (0, 1): 2 * wide + 2 * piece,
        (1, 1): 2 * wide + 3 * piece,
    }
    for side in range(2):
        at_core = core if side == 0 else 1 - core
        for step in range(steps):
            which = next(i for i, chunk in enumerate(chunks) if step in chunk)
            part = parts[side * len(chunks) + which]
            start = chunks[which].index(step) * (2 * wide + 4 * piece)
            at_z = lax.rem(z - step + steps, steps)
            for far_x in range(2):
                row = 2 * at_z + lax.rem(x + far_x, 2)
                base = start + far_x * block
                for j in range(first):
                    crossed[at_core, row, j] = part[base + j * rows : base + (j + 1) * rows]
                if extra is not None and side == 0:
                    extra[row] = part[base + first * rows : base + wide]
                for far_y in range(2):
                    base = start + spots[far_x, far_y]
                    for j in range(quarter):
                        split[at_core, row, lax.rem(y + far_y, 2) * quarter + j] = part[
                            base + j * rows : base + (j + 1) * rows
                        ]


SPOT = 5


def keep_factor(spot, images, branch):
    return spot[SPOT + images + spot[4] * 2 * LAYERS + branch].astype(F32) * (1.0 / KEEP_RATE)


def key_block(spot, rows, special_count):
    ids = lax.broadcasted_iota(jnp.int32, (1, rows), 1)
    inside = (ids < spot[SPOT + spot[4]]) | ((ids >= MOST) & (ids < MOST + special_count))
    return jnp.where(inside, 0.0, MASKED).astype(F32)


def image_frame(spot, images, count, halo):
    before = jnp.int32(0)
    for image in range(images):
        before = before + jnp.where(image < spot[4], spot[SPOT + image], 0)
    return before - spot[4] * count + halo, spot[SPOT + spot[4]]


def flat(block):
    return block.reshape(-1, block.shape[-1])


def moments(values):
    center = values - jnp.mean(values, axis=-1, keepdims=True)
    scale = lax.rsqrt(jnp.mean(center * center, axis=-1, keepdims=True) + EPSILON)
    return (center * scale, scale)


def norm_back(hat, scale, gain, grad):
    scaled = grad * gain
    first = jnp.mean(scaled, axis=-1, keepdims=True)
    second = jnp.mean(scaled * hat, axis=-1, keepdims=True)
    return scale * (scaled - first - hat * second)


def erf_of(values):
    v = jnp.clip(values, -3.7439211627767994, 3.7439211627767994)
    s = v * v
    top = s * 0.00022905065861350646 + 0.0034082910107109506
    top = top * s + 0.050955695062380861
    top = top * s + 0.18520832239976145
    top = top * s + 1.128379143519084
    low = s * -1.1791602954361697e-7 + 0.000023547966471313185
    low = low * s + 0.0010179625278914885
    low = low * s + 0.014070470171167667
    low = low * s + 0.11098505178285362
    low = low * s + 0.49746925110067538
    low = low * s + 1.0
    return v * top / low


def head_probs(queries, keys, blocked):
    scores = dot_nt(queries, keys) + blocked
    powers = jnp.exp(scores - jnp.max(scores, axis=1, keepdims=True))
    return powers * (1.0 / jnp.sum(powers, axis=1, keepdims=True))


def forward_attention_kernel(turned, chunks, images, branch, special_count, spot, stream, *refs):
    keep = keep_factor(spot, images, branch)
    blocked = key_block(spot, stream.shape[0], special_count)
    parts, refs = refs[: 2 * len(chunks)], refs[2 * len(chunks) :]
    middle, normed_two, normed_one_t, normed_two_t, mixed, attended, attended_t, crossed, split, vectors, bias_up, extra = refs
    place_pieces(spot, parts, chunks, crossed, split, extra, turned)
    rows = crossed.shape[3]
    for row in range(extra.shape[0]):
        block = extra[row].astype(F32)
        for piece in range(VECTOR_PIECES):
            values = block[piece : piece + 1, :rows]
            if piece < vectors.shape[0]:
                vectors[piece : piece + 1, row * rows : (row + 1) * rows] = values
            else:
                column = (row * (VECTOR_PIECES - vectors.shape[0]) + piece - vectors.shape[0]) * rows
                bias_up[:, column : column + rows] = values
    hat, _ = moments(stream[...])
    normed = (hat * vectors[GAIN_ONE : GAIN_ONE + 1] + vectors[SHIFT_ONE : SHIFT_ONE + 1]).astype(BF)
    normed_one_t[...] = normed.T
    width = stream.shape[1]
    half = width // 2
    for core in range(2):
        for j in range(3):
            weight = crossed[core, :, j] if j < 2 else split[core, :, 0]
            columns = pl.ds(j * width + core * half, half)
            ahead = dot_nn(normed, flat(weight))
            if j != 1:
                row = BIAS_QUERY if j == 0 else BIAS_VALUE
                ahead = ahead + vectors[row : row + 1, core * half : (core + 1) * half]
            mixed[:, columns] = ahead.astype(BF)
    lane = lax.broadcasted_iota(jnp.int32, (1, 2 * HD), 1)
    for pair in range(width // (2 * HD)):
        queries, keys, values = (
            mixed[:, pl.ds(j * width + pair * 2 * HD, 2 * HD)] for j in range(3)
        )
        outs = []
        for side in range(2):
            mine = ((lane < HD) if side == 0 else (lane >= HD)).astype(F32).astype(BF)
            probs = head_probs(queries * (mine * 0.125), keys, blocked)
            outs.append(dot_nn(probs.astype(BF), values))
        attended[:, pl.ds(pair * 2 * HD, 2 * HD)] = jnp.where(lane < HD, outs[0], outs[1]).astype(BF)
    ahead = attended[...]
    attended_t[...] = ahead.T
    for core in range(2):
        columns = pl.ds(core * half, half)
        added = dot_nn(ahead, flat(split[core, :, 1])) + vectors[BIAS_PROJ : BIAS_PROJ + 1, columns]
        middle[:, columns] = stream[:, columns] + keep * added
    hat, _ = moments(middle[...])
    normed = (hat * vectors[GAIN_TWO : GAIN_TWO + 1] + vectors[SHIFT_TWO : SHIFT_TWO + 1]).astype(BF)
    normed_two[...] = normed
    normed_two_t[...] = normed.T


def forward_attention(place, spot, branch, special_count, stream, unit, extra_rows):
    parts = unit.parts()
    rows, width = stream.shape
    group = (width // place.n_dp, width // 2)
    shapes = [
        jax.ShapeDtypeStruct((rows, width), F32),
        jax.ShapeDtypeStruct((rows, width), BF),
        jax.ShapeDtypeStruct((width, rows), BF),
        jax.ShapeDtypeStruct((width, rows), BF),
        jax.ShapeDtypeStruct((rows, 3 * width), BF),
        jax.ShapeDtypeStruct((rows, width), BF),
        jax.ShapeDtypeStruct((width, rows), BF),
    ] + [jax.ShapeDtypeStruct((2, place.n_dp, 2) + group, BF)] * 2
    shapes += [
        jax.ShapeDtypeStruct((BIAS_DOWN + 1, width), F32),
        jax.ShapeDtypeStruct((1, 4 * width), F32),
    ]
    return pl.pallas_call(
        partial(forward_attention_kernel, unit.turned, unit.chunks, place.n_seq, branch, special_count),
        in_specs=in_smem(1) + whole_vmem(1 + len(parts)),
        out_specs=whole_vmem(len(shapes)),
        out_shape=shapes,
        scratch_shapes=[pltpu.VMEM((place.n_dp, extra_rows, width // 2), BF)],
        compiler_params=kernel_params(12),
        cost_estimate=pl.CostEstimate(flops=0, bytes_accessed=0, transcendentals=0),
    )(spot, stream, *parts)


def forward_up_kernel(turned, chunks, spot, normed, bias_up, *refs):
    parts, refs = refs[: 2 * len(chunks)], refs[2 * len(chunks) :]
    hidden, slope, crossed, split = refs
    place_pieces(spot, parts, chunks, crossed, split, None, turned)
    values = normed[...]
    half = values.shape[1] // 2
    for core in range(2):
        for j in range(4):
            columns = pl.ds((core * 4 + j) * half, half)
            pre = dot_nn(values, flat(crossed[core, :, j])) + bias_up[:, columns]
            share = 0.5 + 0.5 * erf_of(pre * ROOT_HALF)
            hidden[:, columns] = (pre * share).astype(BF)
            slope[:, columns] = (share + pre * jnp.exp(-0.5 * pre * pre) * ROOT_TWO_PI).astype(BF)


def forward_up(place, spot, normed, bias_up, unit):
    parts = unit.parts()
    rows, width = normed.shape
    group = (width // place.n_dp, width // 2)
    return pl.pallas_call(
        partial(forward_up_kernel, unit.turned, unit.chunks),
        in_specs=in_smem(1) + whole_vmem(2 + len(parts)),
        out_specs=whole_vmem(4),
        out_shape=[jax.ShapeDtypeStruct((rows, 4 * width), BF)] * 2
        + [jax.ShapeDtypeStruct((2, place.n_dp, 4) + group, BF)] * 2,
        compiler_params=kernel_params(8),
        cost_estimate=pl.CostEstimate(flops=0, bytes_accessed=0, transcendentals=0),
    )(spot, normed, bias_up, *parts)


def forward_down_kernel(images, branch, spot, middle, hidden, vectors, split, output):
    keep = keep_factor(spot, images, branch)
    ahead = hidden[...]
    half = middle.shape[1] // 2
    for core in range(2):
        columns = pl.ds(core * half, half)
        added = dot_nn(ahead, flat(split[core])) + vectors[BIAS_DOWN : BIAS_DOWN + 1, columns]
        output[:, columns] = middle[:, columns] + keep * added


def forward_down(place, spot, branch, middle, hidden, vectors, split):
    return pl.pallas_call(
        partial(forward_down_kernel, place.n_seq, branch),
        in_specs=in_smem(1) + whole_vmem(4),
        out_specs=whole_vmem(1)[0],
        out_shape=jax.ShapeDtypeStruct(middle.shape, F32),
        compiler_params=kernel_params(8),
        cost_estimate=pl.CostEstimate(flops=0, bytes_accessed=0, transcendentals=0),
    )(spot, middle, hidden, vectors, split)


def backward_feed_kernel(images, branch, spot, grad, slope, split, grad_down_t, grad_up, sum_down, sum_up):
    keep = keep_factor(spot, images, branch)
    down = (keep * grad[...]).astype(BF)
    grad_down_t[...] = down.T
    sum_down[...] = jnp.sum(down.astype(F32), axis=0, keepdims=True)
    half = grad.shape[1] // 2
    for row in range(split.shape[1]):
        columns = pl.ds(row * half, half)
        ahead = dot_nt(down[:, :half], flat(split[0, row])) + dot_nt(down[:, half:], flat(split[1, row]))
        up = (ahead * slope[:, columns].astype(F32)).astype(BF)
        grad_up[:, columns] = up
        sum_up[:, columns] = jnp.sum(up.astype(F32), axis=0, keepdims=True)


def backward_feed(place, spot, branch, grad, slope, split):
    rows, width = grad.shape
    shapes = [
        jax.ShapeDtypeStruct((width, rows), BF),
        jax.ShapeDtypeStruct((rows, 4 * width), BF),
        jax.ShapeDtypeStruct((1, width), F32),
        jax.ShapeDtypeStruct((1, 4 * width), F32),
    ]
    return pl.pallas_call(
        partial(backward_feed_kernel, place.n_seq, branch),
        in_specs=in_smem(1) + whole_vmem(3),
        out_specs=whole_vmem(len(shapes)),
        out_shape=shapes,
        compiler_params=kernel_params(8),
        cost_estimate=pl.CostEstimate(flops=0, bytes_accessed=0, transcendentals=0),
    )(spot, grad, slope, split)


def backward_middle_kernel(images, branch, spot, grad, grad_up, middle, vectors, crossed, *refs):
    keep = keep_factor(spot, images, branch)
    grad_middle, grad_proj, sum_proj, grad_gain, grad_shift = refs
    hat, scale = moments(middle[...])
    half = grad.shape[1] // 2
    total = jnp.zeros(grad.shape, F32)
    for core in range(2):
        for j in range(4):
            total += dot_nt(grad_up[:, pl.ds((core * 4 + j) * half, half)], flat(crossed[core, :, j]))
    grad_gain[...] = jnp.sum(total * hat, axis=0, keepdims=True)
    grad_shift[...] = jnp.sum(total, axis=0, keepdims=True)
    after = grad[...] + norm_back(hat, scale, vectors[GAIN_TWO : GAIN_TWO + 1], total)
    grad_middle[...] = after
    proj = (keep * after).astype(BF)
    grad_proj[...] = proj
    sum_proj[...] = jnp.sum(proj.astype(F32), axis=0, keepdims=True)


def backward_middle(place, spot, branch, grad, grad_up, middle, vectors, crossed):
    rows, width = grad.shape
    shapes = [
        jax.ShapeDtypeStruct((rows, width), F32),
        jax.ShapeDtypeStruct((rows, width), BF),
    ] + [jax.ShapeDtypeStruct((1, width), F32)] * 3
    return pl.pallas_call(
        partial(backward_middle_kernel, place.n_seq, branch),
        in_specs=in_smem(1) + whole_vmem(5),
        out_specs=whole_vmem(len(shapes)),
        out_shape=shapes,
        compiler_params=kernel_params(10),
        cost_estimate=pl.CostEstimate(flops=0, bytes_accessed=0, transcendentals=0),
    )(spot, grad, grad_up, middle, vectors, crossed)


def backward_feed_middle_kernel(images, branches, spot, grad, slope, split, middle, vectors, crossed, *refs):
    backward_feed_kernel(images, branches[1], spot, grad, slope, split, *refs[:4])
    backward_middle_kernel(images, branches[0], spot, grad, refs[1], middle, vectors, crossed, *refs[4:])


def backward_feed_middle(place, spot, branches, grad, slope, split, middle, vectors, crossed):
    rows, width = grad.shape
    shapes = [
        jax.ShapeDtypeStruct((width, rows), BF),
        jax.ShapeDtypeStruct((rows, 4 * width), BF),
        jax.ShapeDtypeStruct((1, width), F32),
        jax.ShapeDtypeStruct((1, 4 * width), F32),
        jax.ShapeDtypeStruct((rows, width), F32),
        jax.ShapeDtypeStruct((rows, width), BF),
    ] + [jax.ShapeDtypeStruct((1, width), F32)] * 3
    return pl.pallas_call(
        partial(backward_feed_middle_kernel, place.n_seq, branches),
        in_specs=in_smem(1) + whole_vmem(6),
        out_specs=whole_vmem(len(shapes)),
        out_shape=shapes,
        compiler_params=kernel_params(12),
    )(spot, grad, slope, split, middle, vectors, crossed)


def backward_attention_kernel(special_count, spot, grad_middle, grad_proj, mixed, stream, vectors, *refs):
    blocked = key_block(spot, stream.shape[0], special_count)
    others, (crossed, split), refs = refs[:5], refs[5:7], refs[7:]
    grad_stream, grad_mixed, sums, ahead = refs
    sum_proj, gain_two, shift_two, sum_down, sum_up = others
    hat, scale = moments(stream[...])
    width = stream.shape[1]
    half = width // 2
    proj = grad_proj[...]
    ahead[...] = (
        dot_nt(proj[:, :half], flat(split[0, :, 1])) + dot_nt(proj[:, half:], flat(split[1, :, 1]))
    ).astype(BF)
    lane = lax.broadcasted_iota(jnp.int32, (1, 2 * HD), 1)
    for pair in range(width // (2 * HD)):
        queries, keys, values = (
            mixed[:, pl.ds(j * width + pair * 2 * HD, 2 * HD)] for j in range(3)
        )
        grads = ahead[:, pl.ds(pair * 2 * HD, 2 * HD)]
        found = []
        for side in range(2):
            mine = ((lane < HD) if side == 0 else (lane >= HD)).astype(F32).astype(BF)
            probs = head_probs(queries * (mine * 0.125), keys, blocked)
            grad_probs = dot_nt(grads * mine, values)
            inner = jnp.sum(probs * grad_probs, axis=1, keepdims=True)
            grad_scores = (probs * (grad_probs - inner)).astype(BF)
            found.append(
                (
                    dot_nn(grad_scores, keys) * 0.125,
                    dot_tn(grad_scores, queries) * 0.125,
                    dot_tn(probs.astype(BF), grads),
                )
            )
        for j in range(3):
            grad_mixed[:, pl.ds(j * width + pair * 2 * HD, 2 * HD)] = jnp.where(
                lane < HD, found[0][j], found[1][j]
            ).astype(BF)
    total = jnp.zeros(stream.shape, F32)
    for core in range(2):
        for j in range(3):
            weight = crossed[core, :, j] if j < 2 else split[core, :, 0]
            total += dot_nt(grad_mixed[:, pl.ds(j * width + core * half, half)], flat(weight))

    def put(row, values):
        sums[row : row + 1, :] = values

    put(GAIN_ONE, jnp.sum(total * hat, axis=0, keepdims=True))
    put(SHIFT_ONE, jnp.sum(total, axis=0, keepdims=True))
    put(BIAS_QUERY, jnp.sum(grad_mixed[:, :width].astype(F32), axis=0, keepdims=True))
    put(BIAS_VALUE, jnp.sum(grad_mixed[:, 2 * width :].astype(F32), axis=0, keepdims=True))
    put(BIAS_PROJ, sum_proj[...])
    put(GAIN_TWO, gain_two[...])
    put(SHIFT_TWO, shift_two[...])
    put(BIAS_DOWN, sum_down[...])
    for j in range(4):
        put(BIAS_DOWN + 1 + j, sum_up[:, j * width : (j + 1) * width])
    sums[BIAS_DOWN + 5 :, :] = jnp.zeros((sums.shape[0] - BIAS_DOWN - 5, width), F32)
    grad_stream[...] = grad_middle[...] + norm_back(hat, scale, vectors[GAIN_ONE : GAIN_ONE + 1], total)


def backward_attention(spot, special_count, grad_middle, grad_proj, mixed, stream, vectors, others, crossed, split):
    rows, width = stream.shape
    shapes = [
        jax.ShapeDtypeStruct((rows, width), F32),
        jax.ShapeDtypeStruct((rows, 3 * width), BF),
        jax.ShapeDtypeStruct((16, width), F32),
    ]
    return pl.pallas_call(
        partial(backward_attention_kernel, special_count),
        in_specs=in_smem(1) + whole_vmem(5 + 5 + 2),
        out_specs=whole_vmem(len(shapes)),
        out_shape=shapes,
        scratch_shapes=[pltpu.VMEM((rows, width), BF)],
        compiler_params=kernel_params(12),
        cost_estimate=pl.CostEstimate(flops=0, bytes_accessed=0, transcendentals=0),
    )(spot, grad_middle, grad_proj, mixed, stream, vectors, *others, crossed, split)


def row_of(spot, step, far_x, steps):
    return 2 * lax.rem(spot[0] - step + steps, steps) + lax.rem(spot[1] + far_x, 2)


def feed_group(spot, core, part, far_y, at_z, normed_t, grad_up, grad_down_t, hidden, spare):
    count, wide, rows, half = spare.shape
    column = 2 * lax.rem(spot[2] + far_y, 2) + core
    if part == 0:
        left = normed_t[...] if at_z is None else normed_t[pl.ds(pl.multiple_of(at_z * 2 * rows, 2 * rows), 2 * rows), :]
        for j in range(wide):
            at = pl.multiple_of((column * wide + j) * half, half)
            out = dot_nn(left, grad_up[:, pl.ds(at, half)])
            spare[:, j] = out.reshape(count, rows, half).astype(BF)
    else:
        at = pl.multiple_of(column * wide * rows, wide * rows)
        left = grad_down_t[pl.ds(at, wide * rows), :]
        for row in range(count):
            columns = row * half if at_z is None else pl.multiple_of((at_z * 2 + row) * half, half)
            out = dot_nn(left, hidden[:, pl.ds(columns, half)])
            spare[row] = out.reshape(wide, rows, half).astype(BF)


def attention_group(spot, core, part, far_y, at_z, normed_t, grad_mixed, attended_t, grad_proj, spare):
    count, _, rows, half = spare.shape
    column = 2 * lax.rem(spot[2] + far_y, 2) + core
    if part == 0:
        out = dot_nn(normed_t[...], grad_mixed[column, :, :half])
    else:
        out = dot_nn(normed_t[...], grad_mixed[column, :, half:]) + dot_nn(
            attended_t[...], grad_proj[column]
        )
    spare[:, 0] = out.reshape(count, rows, half).astype(BF)


def each_group(fill, steps, ring, spot, core, operands, spare):
    wide = spare.shape[1]
    at_z = lax.rem(spot[0] - steps[0] + ring, ring) if len(steps) == 1 else None
    for part in range(2):
        for far_y in range(2):
            fill(spot, core, part, far_y, at_z, *operands, spare)
            for index, step in enumerate(steps):
                for far_x in range(2):
                    row = row_of(spot, step, far_x, ring) if at_z is None else lax.rem(spot[1] + far_x, 2)
                    for j in range(wide):
                        yield index, part, far_y, far_x, j, spare[row, j]


def place_in(part, far_y, far_x, j, wide):
    return (far_x * 2 + far_y) * wide + j if part == 0 else (4 + far_y * 2 + far_x) * wide + j


def sent_kernel(fill, steps, ring, spot, *refs):
    operands, out, spare = refs[:4], refs[4], refs[5]
    for index, part, far_y, far_x, j, block in each_group(fill, steps, ring, spot, 1 - spot[3], operands, spare):
        out[index, place_in(part, far_y, far_x, j, spare.shape[1])] = block


def kept_kernel(fill, steps, ring, spot, *refs):
    operands, got, outs, spare = refs[:4], refs[4], refs[5:-1], refs[-1]
    wide = spare.shape[1]
    for index, part, far_y, far_x, j, block in each_group(fill, steps, ring, spot, spot[3], operands, spare):
        total = block.astype(F32) + got[index, place_in(part, far_y, far_x, j, wide)].astype(F32)
        across, aside, stays = outs[3 * index : 3 * index + 3]
        if part == 0:
            at = far_y * wide + j
            target = across if far_x else stays
        else:
            at = far_x * wide + j
            target = aside if far_y else stays
            at = at if far_y else 2 * wide + at
        target[at] = total.astype(BF)


def spare_shape(place, steps, wide, rows, half):
    return pltpu.VMEM((2 if len(steps) == 1 else place.n_dp, wide, rows, half), BF)


def sent_part(place, spot, fill, wide, steps, operands):
    rows, half = (operands[0].shape[0] // place.n_dp, operands[0].shape[0] // 2)
    return pl.pallas_call(
        partial(sent_kernel, fill, steps, place.nz),
        in_specs=in_smem(1) + whole_vmem(4),
        out_specs=whole_vmem(1)[0],
        out_shape=jax.ShapeDtypeStruct((len(steps), 8 * wide, rows, half), BF),
        scratch_shapes=[spare_shape(place, steps, wide, rows, half)],
        compiler_params=kernel_params(10),
        cost_estimate=pl.CostEstimate(flops=0, bytes_accessed=0, transcendentals=0),
    )(spot, *operands)


def kept_part(place, spot, fill, wide, steps, operands, got):
    rows, half = (operands[0].shape[0] // place.n_dp, operands[0].shape[0] // 2)
    shapes = [
        jax.ShapeDtypeStruct((size * wide, rows, half), BF) for _ in steps for size in (2, 2, 4)
    ]
    outs = pl.pallas_call(
        partial(kept_kernel, fill, steps, place.nz),
        in_specs=in_smem(1) + whole_vmem(5),
        out_specs=whole_vmem(len(shapes)),
        out_shape=shapes,
        scratch_shapes=[spare_shape(place, steps, wide, rows, half)],
        compiler_params=kernel_params(10),
        cost_estimate=pl.CostEstimate(flops=0, bytes_accessed=0, transcendentals=0),
    )(spot, *operands, got)
    return {step: list(outs[3 * i : 3 * i + 3]) for i, step in enumerate(steps)}


def ring_kernel(stays, across, aside, *refs):
    out = refs[-1]
    count = across.shape[0]
    for at in range(2 * count):
        side = across[at] if at < count else aside[at - count]
        total = stays[at].astype(F32) + side.astype(F32)
        if len(refs) == 2:
            total = total + refs[0][at].astype(F32)
        out[at] = total.astype(BF)


def ring_block(stays, across, aside, running):
    operands = [stays, across, aside] + ([] if running is None else [running])
    return pl.pallas_call(
        ring_kernel,
        in_specs=whole_vmem(len(operands)),
        out_specs=whole_vmem(1)[0],
        out_shape=jax.ShapeDtypeStruct(stays.shape, BF),
        compiler_params=kernel_params(4),
        cost_estimate=pl.CostEstimate(flops=0, bytes_accessed=0, transcendentals=0),
    )(*operands)


def fence(trees):
    flat = [list(tree.values()) if isinstance(tree, dict) else tree for tree in trees]
    flat = lax.optimization_barrier(flat)
    return [
        dict(zip(tree, values)) if isinstance(tree, dict) else values
        for tree, values in zip(trees, flat)
    ]


def pick(which, low, high):
    return jnp.where(which == 0, low, high)


def attention_groups(place, qkv, proj):
    half = proj.shape[1] // 2

    def of(core):
        parts = [qkv[:, (2 * j + core) * half : (2 * j + core + 1) * half] for j in range(3)]
        return jnp.stack(parts + [proj[:, core * half : (core + 1) * half]])

    return pick(place.core, of(0), of(1))


def feed_groups(place, up, down):
    rows, half = up.shape[0], down.shape[1] // 2

    def of(core):
        parts = [up[:, (core * 4 + j) * half : (core * 4 + j + 1) * half] for j in range(4)]
        return jnp.concatenate(
            [jnp.stack(parts), down[:, core * half : (core + 1) * half].reshape(4, rows, half)]
        )

    return pick(place.core, of(0), of(1))


class Gathered:
    def __init__(self, place, own, extra, turned, chunks):
        groups, rows, half = own.shape
        self.turned = turned
        self.chunks = chunks
        self.first = jnp.concatenate([own[: groups // 2].reshape(-1, half)] + extra)
        self.wide = self.first.shape[0]
        self.mine = pick(
            place.y,
            own[groups // 2 : groups // 2 + groups // 4],
            own[groups // 2 + groups // 4 :],
        ).reshape(-1, half)
        self.blocks = []
        self.across = {}
        self.aside = {}
        self.whole = []
        self.mate = []
        if turned:
            self.begin([])

    def begin(self, crossed):
        self.blocks.append(jnp.concatenate([self.first, self.mine] + crossed))

    def over_x(self, step):
        return self.blocks[step] if self.turned else self.blocks[step][: self.wide]

    def over_y(self, step):
        tails = [self.blocks[step][self.wide :]]
        if self.turned:
            tails.append(self.across[step][self.wide :])
        return tails

    def chunk(self, which, across, aside):
        return jnp.concatenate(
            [
                piece
                for step in self.chunks[which]
                for piece in (self.blocks[step], across.get(step), aside.get(step))
            ]
        )

    def parts(self):
        return self.whole + self.mate


class Reduced:
    def __init__(self, place):
        self.place = place
        self.operands = None
        self.kept = {}
        self.sides = {}
        self.running = None
        self.last = None

    def block(self, step):
        return ring_block(self.kept[step][2], *self.sides[step], self.running)


def pack_vectors(vectors, bias_up, half, rows):
    layers, part = vectors[0].shape
    packed = jnp.concatenate([jnp.stack(vectors, axis=1), bias_up.reshape(layers, -1, part)], axis=1)
    return jnp.pad(packed, ((0, 0), (0, rows - packed.shape[1]), (0, half - part)))


def image_kernel(images, spot, before, patches, after, specials, out, window):
    halo, count = before.shape[0], patches.shape[0]
    begin, length = image_frame(spot, images, count, halo)
    window[:halo] = before[...]
    window[halo : halo + count] = patches[...]
    window[halo + count : 2 * halo + count] = after[...]
    spare = window.shape[0] - 2 * halo - count
    window[2 * halo + count :] = jnp.zeros((spare, window.shape[1]), F32)
    inside = lax.broadcasted_iota(jnp.int32, (MOST, 1), 0) < length
    turned = pltpu.roll(window[...], lax.rem(window.shape[0] - begin, window.shape[0]), 0)
    out[:MOST] = jnp.where(inside, turned[:MOST], 0.0)
    last = out.shape[0] - MOST
    out[MOST:] = jnp.zeros((last, out.shape[1]), F32)
    out[MOST : MOST + specials.shape[0]] = specials[...]


def take_image(place, spot, patches, specials, halo, rows):
    count, width = patches.shape
    before = shift_seq(place, patches[count - halo :], 1)
    after = shift_seq(place, patches[:halo], -1)

    def build(before, patches, after, specials):
        return pl.pallas_call(
            partial(image_kernel, place.n_seq),
            in_specs=in_smem(1) + whole_vmem(4),
            out_specs=whole_vmem(1)[0],
            out_shape=jax.ShapeDtypeStruct((rows, width), F32),
            scratch_shapes=[pltpu.VMEM((MOST + 2 * halo, width), F32)],
            compiler_params=kernel_params(6),
        cost_estimate=pl.CostEstimate(flops=0, bytes_accessed=0, transcendentals=0),
        )(spot, before, patches, after, specials)

    return (before, patches, after, specials), build


def block_kernel(images, spot, *refs):
    streams, (before, after), owns, window = refs[:2], refs[2:4], refs[4:8], refs[8]
    for at, stream in enumerate(streams):
        own, specials = owns[2 * at : 2 * at + 2]
        halo, count = before.shape[0] // 2, own.shape[0]
        begin, length = image_frame(spot, images, count, halo)
        window[MOST:] = jnp.zeros((window.shape[0] - MOST, window.shape[1]), F32)
        inside = lax.broadcasted_iota(jnp.int32, (MOST, 1), 0) < length
        window[:MOST] = jnp.where(inside, stream[:MOST], 0.0)
        window[...] = pltpu.roll(window[...], begin, 0)
        before[at * halo : (at + 1) * halo] = window[:halo]
        own[...] = window[halo : halo + count]
        after[at * halo : (at + 1) * halo] = window[halo + count : 2 * halo + count]
        specials[...] = stream[MOST : MOST + specials.shape[0]]


def give_images(place, spot, streams, halo, count, special_count):
    width = streams[0].shape[1]
    return pl.pallas_call(
        partial(block_kernel, place.n_seq),
        in_specs=in_smem(1) + whole_vmem(2),
        out_specs=whole_vmem(6),
        out_shape=[
            jax.ShapeDtypeStruct((size, width), F32)
            for size in (2 * halo, 2 * halo, count, special_count, count, special_count)
        ],
        scratch_shapes=[pltpu.VMEM((MOST + 2 * halo, width), F32)],
        compiler_params=kernel_params(6),
        cost_estimate=pl.CostEstimate(flops=0, bytes_accessed=0, transcendentals=0),
    )(spot, *streams)


def finish_attention_kernel(*refs):
    inputs, (out_mixed, out_proj) = refs[:-2], refs[-2:]
    for layer in range(LAYERS):
        last, aside, across = inputs[3 * layer : 3 * layer + 3]
        one = last[0].astype(F32) + aside[0].astype(F32)
        two = last[2].astype(F32) + across[0].astype(F32)
        cut = one.shape[1] // 2
        out_mixed[layer] = jnp.concatenate([one, two[:, :cut]], axis=1)
        out_proj[layer] = two[:, cut:]


def finish_attention(parts, rows, width):
    flat_parts = [array for layer in parts for array in layer]
    return pl.pallas_call(
        finish_attention_kernel,
        in_specs=whole_vmem(len(flat_parts)),
        out_specs=whole_vmem(2),
        out_shape=[
            jax.ShapeDtypeStruct((LAYERS, rows, columns), F32) for columns in (3 * width // 4, width // 4)
        ],
        compiler_params=kernel_params(6),
    )(*flat_parts)


def finish_kernel(spot, *refs):
    inputs, refs = refs[: 3 * LAYERS], refs[3 * LAYERS :]
    sums, (own_one, own_two, from_before, from_after), refs = refs[:4], refs[4:8], refs[8:]
    (out_up, out_down, image_one, image_two), out_rows = refs[:4], refs[4:]
    halo = from_before.shape[0] // 2
    for at, (own, image) in enumerate(((own_one, image_one), (own_two, image_two))):
        count = own.shape[0]
        image[:halo] = own[:halo] + from_before[at * halo : (at + 1) * halo]
        image[halo : count - halo] = own[halo : count - halo]
        image[count - halo :] = own[count - halo :] + from_after[at * halo : (at + 1) * halo]
    total = sums[0][...]
    for other in sums[1:]:
        total = total + other[...]
    place_dp = 2 * spot[0] + spot[1]
    each, width = total.shape[0] // LAYERS, total.shape[1]
    part = out_rows[0].shape[1]
    turned = pltpu.roll(total, lax.rem(width - place_dp * part, width), 1)
    more = VECTOR_PIECES - BIAS_DOWN - 1
    row_ids = lax.broadcasted_iota(jnp.int32, total.shape, 0)
    half_turned = pltpu.roll(total, lax.rem(width - lax.rem(place_dp * more * part, width), width), 1)
    for layer in range(LAYERS):
        for row in range(BIAS_DOWN + 1):
            at = layer * each + row
            out_rows[row][layer : layer + 1, :] = turned[at : at + 1, :part]
        at = layer * each + BIAS_DOWN + 1 + place_dp * more * part // width
        row = jnp.sum(jnp.where(row_ids == at, half_turned, 0.0), axis=0, keepdims=True)
        out_rows[-1][layer : layer + 1, :] = row[:, : more * part]
        last, aside, across = inputs[3 * layer : 3 * layer + 3]
        rows, half = last.shape[1:]
        for j in range(2):
            out_up[layer, :, j * half : (j + 1) * half] = last[j].astype(F32) + aside[j].astype(F32)
            out_down[layer, j * rows : (j + 1) * rows] = last[4 + j].astype(F32) + across[j].astype(F32)


def finish(spot, parts, sums, images, rows, width):
    more = VECTOR_PIECES - BIAS_DOWN - 1
    shapes = [
        jax.ShapeDtypeStruct((LAYERS, rows, width), F32),
        jax.ShapeDtypeStruct((LAYERS, width // 4, 4 * rows), F32),
    ]
    shapes += [jax.ShapeDtypeStruct(images[0].shape, F32)] * 2
    shapes += [jax.ShapeDtypeStruct((LAYERS, rows), F32)] * (BIAS_DOWN + 1)
    shapes += [jax.ShapeDtypeStruct((LAYERS, more * rows), F32)]
    flat_parts = [array for layer in parts for array in layer] + sums + images
    return pl.pallas_call(
        finish_kernel,
        in_specs=in_smem(1) + whole_vmem(len(flat_parts)),
        out_specs=whole_vmem(len(shapes)),
        out_shape=shapes,
        compiler_params=kernel_params(10),
    )(spot, *flat_parts)


def local_walked(
    place,
    patches,
    specials,
    lengths,
    keep_mask,
    norm1_gain,
    norm1_bias,
    qkv_weight,
    query_bias,
    value_bias,
    proj_weight,
    proj_bias,
    norm2_gain,
    norm2_bias,
    fc1_weight,
    fc1_bias,
    fc2_weight,
    fc2_bias,
    cot_patches,
    cot_specials,
):
    count, width = patches.shape
    special_count = specials.shape[0]
    images = lengths.shape[1]
    halo = (MOST - count) * (images // 2)
    rows = -(-(MOST + special_count) // 16) * 16
    nz = place.nz
    pairs = ((0, 1), (2, 3))
    part_rows = proj_weight.shape[1]
    spot = jnp.stack([place.z, place.x, place.y, place.core, place.seq]).astype(jnp.int32)
    spot = jnp.concatenate([spot, lengths.reshape(-1), keep_mask.reshape(-1)])

    shards = (norm1_gain, norm1_bias, query_bias, value_bias, proj_bias, norm2_gain, norm2_bias, fc2_bias)

    extras = pack_vectors(list(shards), fc1_bias, width // 2, EXTRA_ROWS)

    def attention_unit(layer, qkv, proj, extra):
        return Gathered(place, attention_groups(place, qkv, proj), [extra], layer == 0, pairs)

    units = [attention_unit(0, qkv_weight[0], proj_weight[0], extras[0])]
    image, build = take_image(place, spot, patches, specials, halo, rows)
    inputs = {
        "weights": (fc1_weight[0], fc2_weight[0], qkv_weight[1], proj_weight[1], extras[1], fc1_weight[1], fc2_weight[1]),
        "cots": (cot_patches, cot_specials),
    }
    vectors, bias_up = ([None] * LAYERS, [None] * LAYERS)
    streams = [None] * (LAYERS + 1)
    middles, normed_one_ts, normed_two_ts, mixeds, attended_ts, hiddens, slopes = (
        [None] * LAYERS for _ in range(7)
    )
    weights = [None] * (2 * LAYERS)
    unit_count = 2 * LAYERS
    last_slot = 3 * unit_count + 1
    at_x, at_y = ([[] for _ in range(last_slot + 2)] for _ in range(2))
    for which in range(unit_count):
        for step in range(nz):
            slot = 3 * which + step
            at_x[slot].append((which, step))
            at_y[slot + (which == 0)].append((which, step))
    at_core = {4: [(0, 0)], 5: [(0, 1), (1, 0)], 7: [(1, 1)], 8: [(2, 0)], 10: [(2, 1)], 11: [(3, 0)], 12: [(3, 1)], 13: [(3, 2)]}
    carried = {}
    grad = None
    for slot in range(last_slot + 1):
        new = {}
        index, step = divmod(slot, 3)
        if index < unit_count:
            new["z"] = place.ring_z(units[index].blocks[step])
        for which, at in at_x[slot]:
            new["x", which, at] = place.swap_x(units[which].over_x(at))
        for which, at in at_y[slot]:
            tails = units[which].over_y(at)
            new["y", which, at] = place.swap_seq(tails[0] if len(tails) == 1 else jnp.concatenate(tails), 2)
        for which, at in at_core.get(slot, []):
            new["core", which, at] = place.swap_seq(units[which].whole[at], 1)
        for which, at in at_y[slot]:
            for index_of, chunk in enumerate(units[which].chunks):
                if chunk[-1] == at:
                    unit = units[which]
                    across = {**unit.across, **{k[2]: v for k, v in new.items() if k[:2] == ("x", which)}}
                    aside = {**unit.aside, **{k[2]: v for k, v in new.items() if k[:2] == ("y", which)}}
                    new["chunk", which, index_of] = unit.chunk(index_of, across, aside)
        later = {1: 1, 4: 2, 8: 3}.get(slot)
        if later:
            new["later"] = place.swap_x(units[later].mine)
        if slot == 0:
            new["image"] = image
        if slot == 4:
            carried["stream"] = build(*image)
        if slot == 3 * unit_count:
            new["image"], build = take_image(place, spot, *inputs["cots"], halo, rows)
        if slot == 3 * unit_count + 1:
            grad = build(*image)
        if slot in (9, 11):
            layer = slot // 11
            new["forward"] = forward_attention(
                place, spot, 2 * layer, special_count, carried["stream"], units[2 * layer], EXTRA_ROWS
            )
        if slot == 10:
            hidden, slope, crossed, split = forward_up(place, spot, carried["normed"], bias_up[0], units[1])
            output = forward_down(place, spot, 1, carried["middle"], hidden, vectors[0], split)
            new["feed"] = (output, hidden, slope, crossed, split)
        if slot in (3, 5):
            names = [key for key in new if key[0] in ("x", "y")]
            swapped, weights_1 = fence(([new[key] for key in names], weights_1))
            new.update(zip(names, swapped))
            if slot == 3:
                unit = attention_unit(1, *weights_1[:3])
            else:
                unit = Gathered(place, feed_groups(place, *weights_1[3:]), [], False, ((0, 1), (2,), (3,)))
            new["unit"] = (unit.first, unit.mine)
        if step == 2 and index + 1 < len(units) and units[index + 1].blocks:
            carried["begin"] = units[index + 1].blocks[0]
        gate = inputs if slot in (0, 3 * unit_count - 1) else {}
        new, carried, gate = fence((new, carried, gate))
        inputs.update(gate)
        if slot == 0:
            up_0, down_0, *weights_1 = inputs.pop("weights")
            units.append(Gathered(place, feed_groups(place, up_0, down_0), [], False, pairs))
        if "unit" in new:
            unit.first, unit.mine = new["unit"]
            units.append(unit)
        if "begin" in carried:
            units[index + 1].blocks[0] = carried.pop("begin")
        if "image" in new:
            image = new["image"]
        if "later" in new:
            units[later].begin([new["later"]])
        if "z" in new:
            units[index].blocks.append(new["z"])
        for which, at in at_core.get(slot, []):
            units[which].mate.append(new["core", which, at])
        for which, at in at_x[slot]:
            units[which].across[at] = new["x", which, at]
        for which, at in at_y[slot]:
            units[which].aside[at] = new["y", which, at]
        for key in new:
            if key[0] == "chunk":
                units[key[1]].whole.append(new[key])
        if "forward" in new:
            streams[layer] = carried.pop("stream")
            middle, normed, normed_one_ts[layer], normed_two_ts[layer], mixeds[layer], _, attended_ts[layer], crossed, split, vectors[layer], bias_up[layer] = new["forward"]
            weights[2 * layer] = [crossed, split]
            middles[layer] = middle
            carried["middle"], carried["normed"] = middle, normed
        if "feed" in new:
            carried["stream"], hiddens[0], slopes[0], *weights[1] = new["feed"]
            del carried["middle"], carried["normed"]
    hiddens[1], slopes[1], *weights[3] = forward_up(
        place, spot, carried["normed"], bias_up[1], units[3]
    )

    reduces = [Reduced(place) for _ in range(2 * LAYERS)]
    lasts = [None] * (2 * LAYERS)
    back = [{} for _ in range(LAYERS)]

    def feed_back(layer, grad):
        found = back[layer]
        found["down_t"], found["up"], found["sum_down"], found["sum_up"] = backward_feed(
            place, spot, 2 * layer + 1, grad, slopes[layer], weights[2 * layer + 1][1]
        )

    def feed_operands(layer):
        reduces[2 * (LAYERS - 1 - layer)].operands = (
            normed_two_ts[layer], back[layer]["up"], back[layer]["down_t"], hiddens[layer]
        )

    def middle_back(layer, grad):
        found = back[layer]
        found["middle"], found["proj"], found["sum_proj"], found["gain"], found["shift"] = backward_middle(
            place, spot, 2 * layer, grad, found["up"], middles[layer], vectors[layer], weights[2 * layer + 1][0]
        )

    def attention_back(layer):
        found = back[layer]
        others = [found[name] for name in ("sum_proj", "gain", "shift", "sum_down", "sum_up")]
        found["grad"], found["mixed"], found["sums"] = backward_attention(
            spot, special_count, found["middle"], found["proj"], mixeds[layer], streams[layer], vectors[layer], others, *weights[2 * layer]
        )

    def attention_operands(layer):
        found = back[layer]
        wide = 3 * width // 4
        cut = width // 4
        mixed = jnp.stack(
            [jnp.pad(found["mixed"][:, i * wide : (i + 1) * wide], ((0, 0), (0, cut))) for i in range(4)]
        )
        proj = jnp.stack([jnp.pad(found["proj"][:, i * cut : (i + 1) * cut], ((0, 0), (cut, 0))) for i in range(4)])
        unit = reduces[2 * (LAYERS - 1 - layer) + 1]
        unit.operands = (normed_one_ts[layer], mixed, attended_ts[layer], proj)

    fills = [(feed_group, 2), (attention_group, 1)] * LAYERS
    all_steps = (1, 2, 3, 0)
    cuts = [((1,), (2, 3, 0))] + [(all_steps,)] * (len(reduces) - 1)

    def sent_cut(which, cut):
        fill, wide = fills[which]
        return sent_part(place, spot, fill, wide, cuts[which][cut], reduces[which].operands)

    def keep_cut(which, cut, got):
        fill, wide = fills[which]
        unit = reduces[which]
        unit.kept.update(kept_part(place, spot, fill, wide, cuts[which][cut], unit.operands, got))

    feed_back(1, grad)
    feed_operands(1)
    sent = [sent_cut(0, 0), None]
    back[1], sent = fence((back[1], sent[:1]))
    final_slot = 3 * len(reduces)
    total = given = None
    first_last = []
    rung = []
    got = {}
    sending = {(0, 0): sent[0]}
    for slot in range(-2, final_slot + 1):
        new = {}
        work = {}
        for which, unit in enumerate(reduces):
            at = slot - 3 * which
            if 0 <= at <= 2:
                new["z", which] = place.ring_z(unit.block(at + 1))
            if at == 3:
                unit.last = unit.block(0)
                work["last", which] = unit.last
        if slot in (4, 7):
            end = reduces[0].last
            part = end.shape[0] // 4
            if slot == 4:
                new["last"] = place.swap_seq(end[part : 2 * part], 2)
            else:
                new["last"] = place.swap_x(end[3 * part :])
        for base, group in ((final_slot - 2, range(1, len(reduces) - 1)), (final_slot, [len(reduces) - 1])):
            if slot == base:
                ends = [reduces[which].last for which in group]
                parts = [end.shape[0] // 4 for end in ends]
                aside = place.swap_seq(
                    jnp.concatenate([end[part : 2 * part] for end, part in zip(ends, parts)]), 2
                )
                across = place.swap_x(jnp.concatenate([end[3 * part :] for end, part in zip(ends, parts)]))
                begins = 0
                for which, end, part in zip(group, ends, parts):
                    lasts[which] = [end, aside[begins : begins + part], across[begins : begins + part]]
                    begins += part
                if slot < final_slot:
                    new["lasts"] = [lasts[which] for which in group]
        if slot == -2:
            sending[0, 1] = sent_cut(0, 1)
            work["sending"] = sending[0, 1]
        if slot == -1:
            keep_cut(0, 0, got.pop((0, 0)))
        for which, base in ((2, 4), (3, 7)):
            if slot == base:
                keep_cut(which, 0, got.pop((which, 0)))
                for step in all_steps:
                    work["kept", which, step] = reduces[which].kept[step]
        for key, base in (((0, 0), -2), ((0, 1), -1), ((1, 0), 2), ((2, 0), 3), ((3, 0), 6)):
            if slot == base:
                new["core", key] = place.swap_seq(sending.pop(key), 1)
        if slot == -1:
            keep_cut(0, 1, new["core", (0, 1)])
            for step in cuts[0][1]:
                work["kept", 0, step] = reduces[0].kept[step]
        if slot == 2:
            keep_cut(1, 0, new["core", (1, 0)])
        for which, unit in enumerate(reduces):
            at = slot - 3 * which
            if -1 <= at <= 2:
                step = (at + 2) % nz
                new["side", which] = (
                    place.swap_x(unit.kept[step][0]),
                    place.swap_seq(unit.kept[step][1], 2),
                )
        if slot == 3:
            attention_operands(0)
            work["sending"] = sent_cut(3, 0)
        if slot == -1:
            middle_back(1, grad)
        if slot == 4:
            streams[LAYERS] = forward_down(place, spot, 3, carried["middle"], hiddens[1], vectors[1], weights[3][1])
            work["output"] = streams[LAYERS]
        if slot == 0:
            attention_back(1)
        if slot == 1:
            attention_operands(1)
            names = ("down_t", "up", "sum_down", "sum_up", "middle", "proj", "sum_proj", "gain", "shift")
            back[0] = dict(
                zip(
                    names,
                    backward_feed_middle(
                        place, spot, (0, 1), back[1]["grad"], slopes[0], weights[1][1], middles[0], vectors[0], weights[1][0]
                    ),
                )
            )
            feed_operands(0)
            work["sending"] = (sent_cut(1, 0), sent_cut(2, 0))
        if slot == 2:
            attention_back(0)
        if slot in (-1, 0):
            work["back", 1] = back[1]
        if slot in (1, 2):
            work["back", 0] = back[0]
        if slot == 3:
            total = jnp.concatenate([back[layer]["sums"] for layer in range(LAYERS)])
            new["sum"] = place.swap_seq(total, 1)
        if slot == 4:
            new["sum"] = place.swap_seq(total, 2)
        if slot == 6:
            new["sum"] = place.swap_x(total)
        if slot in (7, 9, 11):
            new["ringing"] = [place.ring_z(total if slot == 7 else rung[-1])]
        if slot == final_slot - 4:
            work["images"] = give_images(place, spot, given, halo, count, special_count)
        if slot == final_slot - 3:
            images_before, images_after, *owns = images
            new["image_down"] = shift_seq(place, images_before, -1)
        if slot == final_slot - 1:
            new["image_up"] = shift_seq(place, images_after, 1)
        pending = {}
        if slot == final_slot - 2:
            pending["after"] = images_after
        for which, unit in enumerate(reduces):
            at = slot + 1 - 3 * which
            if 0 <= at <= 2:
                step = (at + 2) % nz
                if step in unit.kept and ("kept", which, step) not in work:
                    pending["kept", which] = unit.kept[step]
        if slot == final_slot - 5:
            pending["give"] = [streams[LAYERS], back[0]["grad"]]
        for key, base in (((2, 0), 2), ((3, 0), 5)):
            if slot == base:
                pending["sending", key] = sending[key]
        for key, base in (((2, 0), 4), ((3, 0), 7)):
            if slot == base - 1 and key in got:
                pending["got", key] = got[key]
        new, work, pending = fence((new, work, pending))
        if "sending" in work:
            if slot == 1:
                sending[1, 0], sending[2, 0] = work.pop("sending")
            else:
                sending[(0, 1) if slot == -2 else (3, 0)] = work.pop("sending")
        for key in [key for key in pending if key[0] == "sending"]:
            sending[key[1]] = pending.pop(key)
        if "output" in work:
            streams[LAYERS] = work.pop("output")
        for key, value in work.items():
            if key[0] == "back":
                back[key[1]] = value
            if key[0] == "last":
                reduces[key[1]].last = value
            if key == "images":
                images = value
            if key[0] == "kept":
                reduces[key[1]].kept[key[2]] = value
        if "give" in pending:
            given = pending.pop("give")
        if "after" in pending:
            images_after = pending.pop("after")
        for key in [key for key in pending if key[0] == "got"]:
            got[key[1]] = pending.pop(key)
        for key, value in pending.items():
            reduces[key[1]].kept[(slot + 1 - 3 * key[1] + 2) % nz] = value
        for key, value in new.items():
            if key[0] == "core":
                got[key[1]] = value
            if key[0] == "z":
                reduces[key[1]].running = value
            if key[0] == "side":
                reduces[key[1]].sides[(slot - 3 * key[1] + 2) % nz] = value
        if "image_down" in new:
            image_down = new["image_down"]
        if "image_up" in new:
            sides = (new["image_up"], image_down)
        if "lasts" in new:
            lasts[1 : 1 + len(new["lasts"])] = new["lasts"]
        if "last" in new:
            first_last.append(new["last"])
            lasts[0] = [reduces[0].last] + first_last
        if "sum" in new:
            total = total + new["sum"]
        if "ringing" in new:
            rung += new["ringing"]

    wu, wd, out_patches, grad_patches, g1, s1, bq, bv, bp, g2, s2, bd, bu = finish(
        spot,
        [lasts[2], lasts[0]],
        [total] + rung,
        [owns[0], owns[2], *sides],
        part_rows,
        width,
    )
    wm, wp = finish_attention([lasts[3], lasts[1]], part_rows, width)
    wd = jnp.transpose(wd, (0, 2, 1))
    return (
        out_patches,
        owns[1],
        grad_patches,
        owns[3],
        g1,
        s1,
        wm,
        bq,
        bv,
        wp,
        bp,
        g2,
        s2,
        wu,
        bu,
        wd,
        bd,
    )


def local(*args):
    place = Place()
    if place.walked:
        return local_walked(place, *args)
    return local_plain(place, *args)


def solution(mesh):
    in_specs = (
        P(("dp", "seq"), None),
        P(("dp", "seq"), None),
        P("dp", None),
        P("dp", None, None),
        P(None, "dp"),
        P(None, "dp"),
        P(None, "dp", None),
        P(None, "dp"),
        P(None, "dp"),
        P(None, "dp", None),
        P(None, "dp"),
        P(None, "dp"),
        P(None, "dp"),
        P(None, "dp", None),
        P(None, "dp"),
        P(None, "dp", None),
        P(None, "dp"),
        P(("dp", "seq"), None),
        P(("dp", "seq"), None),
    )
    out_specs = (
        P(("dp", "seq"), None),
        P(("dp", "seq"), None),
        P(("dp", "seq"), None),
        P(("dp", "seq"), None),
        P(None, "dp"),
        P(None, "dp"),
        P(None, "dp", "seq"),
        P(None, "dp"),
        P(None, "dp"),
        P(None, "dp", "seq"),
        P(None, "dp"),
        P(None, "dp"),
        P(None, "dp"),
        P(None, "dp", "seq"),
        P(None, "dp"),
        P(None, "dp", "seq"),
        P(None, "dp"),
    )
    return jax.shard_map(local, mesh=mesh, in_specs=in_specs, out_specs=out_specs, check_vma=False)
```

```python
from functools import partial

import jax
import jax.numpy as jnp
from jax import lax
from jax.experimental import pallas as pl
from jax.experimental.pallas import tpu as pltpu
from jax.sharding import PartitionSpec as P

HD = 64
LAYERS = 2
MOST = 280
KEEP_RATE = 0.9
EPSILON = 1e-06
MASKED = -1e30
GAIN_ONE, SHIFT_ONE, BIAS_QUERY, BIAS_VALUE, BIAS_PROJ, GAIN_TWO, SHIFT_TWO, BIAS_DOWN = range(8)
VECTOR_PIECES = 12
EXTRA_ROWS = 16
MIB = 1024 * 1024
ROOT_HALF = 0.7071067811865476
ROOT_TWO_PI = 0.3989422804014327
BF = jnp.bfloat16
F32 = jnp.float32


def dot_nn(left, right):
    return lax.dot_general(left, right, (((1,), (0,)), ((), ())), preferred_element_type=F32)


def dot_nt(left, right):
    return lax.dot_general(left, right, (((1,), (1,)), ((), ())), preferred_element_type=F32)


def dot_tn(left, right):
    return lax.dot_general(left, right, (((0,), (0,)), ((), ())), preferred_element_type=F32)


class Place:
    def __init__(self):
        self.n_dp = lax.axis_size("dp")
        self.n_seq = lax.axis_size("seq")
        self.walked = self.n_dp == 8 and self.n_seq == 4
        self.dp = lax.axis_index("dp")
        self.seq = lax.axis_index("seq")
        if self.walked:
            self.core = self.seq % 2
            self.y = self.seq // 2
            self.x = self.dp % 2
            self.z = self.dp // 2
            self.nz = self.n_dp // 2

    def swap_seq(self, values, mask):
        return lax.ppermute(values, "seq", [(i, i ^ mask) for i in range(self.n_seq)])

    def swap_x(self, values):
        return lax.ppermute(values, "dp", [(i, i ^ 1) for i in range(self.n_dp)])

    def ring_z(self, values, by=1):
        return lax.ppermute(values, "dp", [(i, (i + 2 * by) % self.n_dp) for i in range(self.n_dp)])


def gather_matrix(shard):
    return lax.all_gather(shard, "dp", axis=0, tiled=True)


def reduce_matrix(acts, grads):
    part = dot_tn(acts, grads).astype(BF)
    part = lax.psum_scatter(part, "dp", scatter_dimension=0, tiled=True)
    return lax.psum_scatter(part, "seq", scatter_dimension=1, tiled=True).astype(F32)


def reduce_vectors(place, vectors):
    packed = jnp.concatenate(
        [vector.reshape(place.n_dp, vector.shape[0] // place.n_dp) for vector in vectors], axis=1
    )
    mask = 1
    while mask < place.n_seq:
        packed = packed + place.swap_seq(packed, mask)
        mask *= 2
    packed = lax.all_to_all(packed, "dp", split_axis=0, concat_axis=0, tiled=True)
    total = jnp.sum(packed, axis=0)
    results, at = [], 0
    for vector in vectors:
        width = vector.shape[0] // place.n_dp
        results.append(total[at : at + width])
        at += width
    return results


def gather_vectors(place, shards):
    widths = [shard.shape[1] for shard in shards]
    packed = jnp.concatenate(shards, axis=1)
    rows = packed.shape[0]
    spread = jnp.broadcast_to(packed[None], (place.n_dp,) + packed.shape)
    spread = lax.all_to_all(spread, "dp", split_axis=0, concat_axis=0, tiled=True)
    results, at = [], 0
    for width in widths:
        piece = spread[:, :, at : at + width]
        results.append(jnp.transpose(piece, (1, 0, 2)).reshape(rows, place.n_dp * width).astype(F32))
        at += width
    return results


def normalize(values):
    center = values - jnp.mean(values, axis=-1, keepdims=True)
    spread = jnp.mean(center * center, axis=-1, keepdims=True)
    scale = lax.rsqrt(spread + EPSILON)
    return (center * scale, scale)


def normalize_back(hat, scale, gain, grad):
    scaled = grad * gain
    first = jnp.mean(scaled, axis=-1, keepdims=True)
    second = jnp.mean(scaled * hat, axis=-1, keepdims=True)
    back = scale * (scaled - first - hat * second)
    return (back, jnp.sum(grad * hat, axis=0), jnp.sum(grad, axis=0))


def heads_of(mixed):
    rows = mixed.shape[0]
    width = mixed.shape[1] // 3
    split = mixed.reshape(rows, 3, width // HD, HD)
    return (split[:, 0], split[:, 1], split[:, 2])


def attend(mixed, key_ok):
    queries, keys, values = heads_of(mixed)
    scores = jnp.einsum("qhd,khd->hqk", queries, keys, preferred_element_type=F32) * 0.125
    scores = jnp.where(key_ok[None, None, :], scores, MASKED)
    top = jnp.max(scores, axis=2, keepdims=True)
    powers = jnp.exp(scores - top)
    probs = powers / jnp.sum(powers, axis=2, keepdims=True)
    out = jnp.einsum("hqk,khd->qhd", probs.astype(BF), values, preferred_element_type=F32)
    return (out.reshape(mixed.shape[0], -1).astype(BF), probs)


def attend_back(mixed, probs, grad_out):
    queries, keys, values = heads_of(mixed)
    rows = mixed.shape[0]
    grads = grad_out.reshape(queries.shape)
    grad_probs = jnp.einsum("qhd,khd->hqk", grads, values, preferred_element_type=F32)
    inner = jnp.sum(probs * grad_probs, axis=2, keepdims=True)
    grad_scores = (probs * (grad_probs - inner)).astype(BF)
    grad_values = jnp.einsum("hqk,qhd->khd", probs.astype(BF), grads, preferred_element_type=F32)
    grad_queries = (
        jnp.einsum("hqk,khd->qhd", grad_scores, keys, preferred_element_type=F32) * 0.125
    )
    grad_keys = (
        jnp.einsum("hqk,qhd->khd", grad_scores, queries, preferred_element_type=F32) * 0.125
    )
    return jnp.concatenate(
        [grad.reshape(rows, -1).astype(BF) for grad in (grad_queries, grad_keys, grad_values)], axis=1
    )


def layer_forward(stream, vectors, matrices, keeps, key_ok):
    gain_one, shift_one, bias_query, bias_value, bias_proj, gain_two, shift_two, bias_down, bias_up = vectors
    w_mixed, w_proj, w_up, w_down = matrices
    hat_one, scale_one = normalize(stream)
    normed_one = (hat_one * gain_one + shift_one).astype(BF)
    bias_mixed = jnp.concatenate([bias_query, jnp.zeros_like(bias_query), bias_value])
    mixed = (dot_nn(normed_one, w_mixed) + bias_mixed).astype(BF)
    attended, probs = attend(mixed, key_ok)
    middle = stream + keeps[0] * (dot_nn(attended, w_proj) + bias_proj) / KEEP_RATE
    hat_two, scale_two = normalize(middle)
    normed_two = (hat_two * gain_two + shift_two).astype(BF)
    hidden_pre = dot_nn(normed_two, w_up) + bias_up
    share = 0.5 * (1.0 + lax.erf(hidden_pre * ROOT_HALF))
    hidden = (hidden_pre * share).astype(BF)
    slope = share + hidden_pre * jnp.exp(-0.5 * hidden_pre * hidden_pre) * ROOT_TWO_PI
    output = middle + keeps[1] * (dot_nn(hidden, w_down) + bias_down) / KEEP_RATE
    saved = (hat_one, scale_one, normed_one, mixed, probs, attended, hat_two, scale_two, normed_two, hidden, slope)
    return (output, saved)


def layer_back(place, grad_stream, saved, vectors, matrices, keeps):
    hat_one, scale_one, normed_one, mixed, probs, attended, hat_two, scale_two, normed_two, hidden, slope = saved
    gain_one, gain_two = (vectors[0], vectors[5])
    w_mixed, w_proj, w_up, w_down = matrices
    width = grad_stream.shape[1]
    grad_down = (keeps[1] * grad_stream / KEEP_RATE).astype(BF)
    total_down = reduce_matrix(hidden, grad_down)
    grad_up = (dot_nt(grad_down, w_down) * slope).astype(BF)
    total_up = reduce_matrix(normed_two, grad_up)
    back_two, grad_gain_two, grad_shift_two = normalize_back(
        hat_two, scale_two, gain_two, dot_nt(grad_up, w_up)
    )
    grad_middle = grad_stream + back_two
    grad_proj = (keeps[0] * grad_middle / KEEP_RATE).astype(BF)
    total_proj = reduce_matrix(attended, grad_proj)
    grad_attended = dot_nt(grad_proj, w_proj).astype(BF)
    grad_mixed = attend_back(mixed, probs, grad_attended)
    total_mixed = reduce_matrix(normed_one, grad_mixed)
    back_one, grad_gain_one, grad_shift_one = normalize_back(
        hat_one, scale_one, gain_one, dot_nt(grad_mixed, w_mixed)
    )
    grad_input = grad_middle + back_one
    sum_mixed = jnp.sum(grad_mixed, axis=0, dtype=F32)
    totals = reduce_vectors(
        place,
        (
            grad_gain_one,
            grad_shift_one,
            sum_mixed[:width],
            sum_mixed[2 * width :],
            jnp.sum(grad_proj, axis=0, dtype=F32),
            grad_gain_two,
            grad_shift_two,
            jnp.sum(grad_down, axis=0, dtype=F32),
            jnp.sum(grad_up, axis=0, dtype=F32),
        ),
    )
    return (grad_input, totals, (total_mixed, total_proj, total_up, total_down))


def shift_seq(place, values, by):
    count = place.n_seq
    return lax.ppermute(values, "seq", [(i, i + by) for i in range(count) if 0 <= i + by < count])


def to_image(place, patches, specials, halo, start, length, rows):
    count, width = patches.shape
    before = shift_seq(place, patches[count - halo :], 1)
    after = shift_seq(place, patches[:halo], -1)
    spare = jnp.zeros((MOST + 2 * halo - count - 2 * halo, width), patches.dtype)
    window = jnp.concatenate([before, patches, after, spare])
    image = lax.dynamic_slice_in_dim(window, start, MOST)
    inside = jnp.arange(MOST, dtype=jnp.int32)[:, None] < length
    image = jnp.where(inside, image, 0.0)
    spare = jnp.zeros((rows - MOST - specials.shape[0], width), patches.dtype)
    return jnp.concatenate([image, specials, spare])


def from_image(place, stream, halo, start, length, count, specials):
    width = stream.shape[1]
    inside = jnp.arange(MOST, dtype=jnp.int32)[:, None] < length
    image = jnp.where(inside, stream[:MOST], 0.0)
    window = jnp.zeros((MOST + 2 * halo, width), stream.dtype)
    window = lax.dynamic_update_slice_in_dim(window, image, start, 0)
    own = window[halo : halo + count]
    from_before = shift_seq(place, window[halo + count : count + 2 * halo], 1)
    from_after = shift_seq(place, window[:halo], -1)
    blank = jnp.zeros((count - halo, width), stream.dtype)
    own = own + jnp.concatenate([from_before, blank]) + jnp.concatenate([blank, from_after])
    return (own, stream[MOST : MOST + specials])


def local_plain(
    place,
    patches,
    specials,
    lengths,
    keep_mask,
    norm1_gain,
    norm1_bias,
    qkv_weight,
    query_bias,
    value_bias,
    proj_weight,
    proj_bias,
    norm2_gain,
    norm2_bias,
    fc1_weight,
    fc1_bias,
    fc2_weight,
    fc2_bias,
    cot_patches,
    cot_specials,
):
    count = patches.shape[0]
    special_count = specials.shape[0]
    images = lengths.shape[1]
    halo = (MOST - count) * (images // 2)
    rows = -(-(MOST + special_count) // 16) * 16
    before = jnp.sum(jnp.where(jnp.arange(images) < place.seq, lengths[0], 0))
    length = lax.dynamic_index_in_dim(lengths[0], place.seq, 0, keepdims=False)
    start = before - place.seq * count + halo
    keeps = lax.dynamic_index_in_dim(keep_mask[0], place.seq, 0, keepdims=False).astype(F32)
    row_ids = jnp.arange(rows, dtype=jnp.int32)
    key_ok = (row_ids < length) | ((row_ids >= MOST) & (row_ids < MOST + special_count))

    shards = (norm1_gain, norm1_bias, query_bias, value_bias, proj_bias, norm2_gain, norm2_bias, fc2_bias, fc1_bias)
    vectors_all = gather_vectors(place, shards)
    stream = to_image(place, patches, specials, halo, start, length, rows)
    matrices = []
    for layer in range(LAYERS):
        matrices.append(
            tuple(
                gather_matrix(shard[layer])
                for shard in (qkv_weight, proj_weight, fc1_weight, fc2_weight)
            )
        )
    vectors = [tuple(vector[layer] for vector in vectors_all) for layer in range(LAYERS)]
    saved = []
    for layer in range(LAYERS):
        stream, kept = layer_forward(
            stream, vectors[layer], matrices[layer], keeps[2 * layer : 2 * layer + 2], key_ok
        )
        saved.append(kept)
    out_patches, out_specials = from_image(place, stream, halo, start, length, count, special_count)
    grad = to_image(place, cot_patches, cot_specials, halo, start, length, rows)
    vector_totals, matrix_totals = ([None] * LAYERS, [None] * LAYERS)
    for layer in reversed(range(LAYERS)):
        grad, vector_totals[layer], matrix_totals[layer] = layer_back(
            place, grad, saved[layer], vectors[layer], matrices[layer], keeps[2 * layer : 2 * layer + 2]
        )
    grad_patches, grad_specials = from_image(place, grad, halo, start, length, count, special_count)
    vector_out = [jnp.stack([vector_totals[layer][i] for layer in range(LAYERS)]) for i in range(9)]
    matrix_out = [jnp.stack([matrix_totals[layer][i] for layer in range(LAYERS)]) for i in range(4)]
    g1, s1, bq, bv, bp, g2, s2, bd, bu = vector_out
    wm, wp, wu, wd = matrix_out
    return (
        out_patches,
        out_specials,
        grad_patches,
        grad_specials,
        g1,
        s1,
        wm,
        bq,
        bv,
        wp,
        bp,
        g2,
        s2,
        wu,
        bu,
        wd,
        bd,
    )


def whole_vmem(count):
    return [pl.BlockSpec(memory_space=pltpu.VMEM)] * count


def in_smem(count):
    return [pl.BlockSpec(memory_space=pltpu.SMEM)] * count


def kernel_params(mib):
    return pltpu.CompilerParams(vmem_limit_bytes=mib * MIB)


def place_pieces(spot, parts, chunks, crossed, split, extra, turned):
    z, x, y, core = (spot[i] for i in range(4))
    steps = sum(len(chunk) for chunk in chunks)
    first, rows = crossed.shape[2:4]
    quarter = split.shape[2] // 2
    more = 0 if extra is None else extra.shape[1]
    wide, piece = first * rows + more, quarter * rows
    block = wide + (piece if turned else 2 * piece)
    spots = {
        (0, 0): wide,
        (1, 0): block + wide if turned else wide + piece,
        (0, 1): 2 * wide + 2 * piece,
        (1, 1): 2 * wide + 3 * piece,
    }
    for side in range(2):
        at_core = core if side == 0 else 1 - core
        for step in range(steps):
            which = next(i for i, chunk in enumerate(chunks) if step in chunk)
            part = parts[side * len(chunks) + which]
            start = chunks[which].index(step) * (2 * wide + 4 * piece)
            at_z = lax.rem(z - step + steps, steps)
            for far_x in range(2):
                row = 2 * at_z + lax.rem(x + far_x, 2)
                base = start + far_x * block
                for j in range(first):
                    crossed[at_core, row, j] = part[base + j * rows : base + (j + 1) * rows]
                if extra is not None and side == 0:
                    extra[row] = part[base + first * rows : base + wide]
                for far_y in range(2):
                    base = start + spots[far_x, far_y]
                    for j in range(quarter):
                        split[at_core, row, lax.rem(y + far_y, 2) * quarter + j] = part[
                            base + j * rows : base + (j + 1) * rows
                        ]


SPOT = 5


def keep_factor(spot, images, branch):
    return spot[SPOT + images + spot[4] * 2 * LAYERS + branch].astype(F32) * (1.0 / KEEP_RATE)


def key_block(spot, rows, special_count):
    ids = lax.broadcasted_iota(jnp.int32, (1, rows), 1)
    inside = (ids < spot[SPOT + spot[4]]) | ((ids >= MOST) & (ids < MOST + special_count))
    return jnp.where(inside, 0.0, MASKED).astype(F32)


def image_frame(spot, images, count, halo):
    before = jnp.int32(0)
    for image in range(images):
        before = before + jnp.where(image < spot[4], spot[SPOT + image], 0)
    return before - spot[4] * count + halo, spot[SPOT + spot[4]]


def flat(block):
    return block.reshape(-1, block.shape[-1])


def moments(values):
    center = values - jnp.mean(values, axis=-1, keepdims=True)
    scale = lax.rsqrt(jnp.mean(center * center, axis=-1, keepdims=True) + EPSILON)
    return (center * scale, scale)


def norm_back(hat, scale, gain, grad):
    scaled = grad * gain
    first = jnp.mean(scaled, axis=-1, keepdims=True)
    second = jnp.mean(scaled * hat, axis=-1, keepdims=True)
    return scale * (scaled - first - hat * second)


def erf_of(values):
    v = jnp.clip(values, -3.7439211627767994, 3.7439211627767994)
    s = v * v
    top = s * 0.00022905065861350646 + 0.0034082910107109506
    top = top * s + 0.050955695062380861
    top = top * s + 0.18520832239976145
    top = top * s + 1.128379143519084
    low = s * -1.1791602954361697e-7 + 0.000023547966471313185
    low = low * s + 0.0010179625278914885
    low = low * s + 0.014070470171167667
    low = low * s + 0.11098505178285362
    low = low * s + 0.49746925110067538
    low = low * s + 1.0
    return v * top / low


def head_probs(queries, keys, blocked):
    scores = dot_nt(queries, keys) + blocked
    powers = jnp.exp(scores - jnp.max(scores, axis=1, keepdims=True))
    return powers * (1.0 / jnp.sum(powers, axis=1, keepdims=True))


def forward_attention_kernel(turned, chunks, images, branch, special_count, spot, stream, *refs):
    keep = keep_factor(spot, images, branch)
    blocked = key_block(spot, stream.shape[0], special_count)
    parts, refs = refs[: 2 * len(chunks)], refs[2 * len(chunks) :]
    middle, normed_two, normed_one_t, normed_two_t, mixed, attended, attended_t, crossed, split, vectors, bias_up, extra = refs
    place_pieces(spot, parts, chunks, crossed, split, extra, turned)
    rows = crossed.shape[3]
    for row in range(extra.shape[0]):
        block = extra[row].astype(F32)
        for piece in range(VECTOR_PIECES):
            values = block[piece : piece + 1, :rows]
            if piece < vectors.shape[0]:
                vectors[piece : piece + 1, row * rows : (row + 1) * rows] = values
            else:
                column = (row * (VECTOR_PIECES - vectors.shape[0]) + piece - vectors.shape[0]) * rows
                bias_up[:, column : column + rows] = values
    hat, _ = moments(stream[...])
    normed = (hat * vectors[GAIN_ONE : GAIN_ONE + 1] + vectors[SHIFT_ONE : SHIFT_ONE + 1]).astype(BF)
    normed_one_t[...] = normed.T
    width = stream.shape[1]
    half = width // 2
    for core in range(2):
        for j in range(3):
            weight = crossed[core, :, j] if j < 2 else split[core, :, 0]
            columns = pl.ds(j * width + core * half, half)
            ahead = dot_nn(normed, flat(weight))
            if j != 1:
                row = BIAS_QUERY if j == 0 else BIAS_VALUE
                ahead = ahead + vectors[row : row + 1, core * half : (core + 1) * half]
            mixed[:, columns] = ahead.astype(BF)
    lane = lax.broadcasted_iota(jnp.int32, (1, 2 * HD), 1)
    for pair in range(width // (2 * HD)):
        queries, keys, values = (
            mixed[:, pl.ds(j * width + pair * 2 * HD, 2 * HD)] for j in range(3)
        )
        outs = []
        for side in range(2):
            mine = ((lane < HD) if side == 0 else (lane >= HD)).astype(F32).astype(BF)
            probs = head_probs(queries * (mine * 0.125), keys, blocked)
            outs.append(dot_nn(probs.astype(BF), values))
        attended[:, pl.ds(pair * 2 * HD, 2 * HD)] = jnp.where(lane < HD, outs[0], outs[1]).astype(BF)
    ahead = attended[...]
    attended_t[...] = ahead.T
    for core in range(2):
        columns = pl.ds(core * half, half)
        added = dot_nn(ahead, flat(split[core, :, 1])) + vectors[BIAS_PROJ : BIAS_PROJ + 1, columns]
        middle[:, columns] = stream[:, columns] + keep * added
    hat, _ = moments(middle[...])
    normed = (hat * vectors[GAIN_TWO : GAIN_TWO + 1] + vectors[SHIFT_TWO : SHIFT_TWO + 1]).astype(BF)
    normed_two[...] = normed
    normed_two_t[...] = normed.T


def forward_attention(place, spot, branch, special_count, stream, unit, extra_rows):
    parts = unit.parts()
    rows, width = stream.shape
    group = (width // place.n_dp, width // 2)
    shapes = [
        jax.ShapeDtypeStruct((rows, width), F32),
        jax.ShapeDtypeStruct((rows, width), BF),
        jax.ShapeDtypeStruct((width, rows), BF),
        jax.ShapeDtypeStruct((width, rows), BF),
        jax.ShapeDtypeStruct((rows, 3 * width), BF),
        jax.ShapeDtypeStruct((rows, width), BF),
        jax.ShapeDtypeStruct((width, rows), BF),
    ] + [jax.ShapeDtypeStruct((2, place.n_dp, 2) + group, BF)] * 2
    shapes += [
        jax.ShapeDtypeStruct((BIAS_DOWN + 1, width), F32),
        jax.ShapeDtypeStruct((1, 4 * width), F32),
    ]
    return pl.pallas_call(
        partial(forward_attention_kernel, unit.turned, unit.chunks, place.n_seq, branch, special_count),
        in_specs=in_smem(1) + whole_vmem(1 + len(parts)),
        out_specs=whole_vmem(len(shapes)),
        out_shape=shapes,
        scratch_shapes=[pltpu.VMEM((place.n_dp, extra_rows, width // 2), BF)],
        compiler_params=kernel_params(12),
        cost_estimate=pl.CostEstimate(flops=0, bytes_accessed=0, transcendentals=0),
    )(spot, stream, *parts)


def forward_up_kernel(turned, chunks, spot, normed, bias_up, *refs):
    parts, refs = refs[: 2 * len(chunks)], refs[2 * len(chunks) :]
    hidden, slope, crossed, split = refs
    place_pieces(spot, parts, chunks, crossed, split, None, turned)
    values = normed[...]
    half = values.shape[1] // 2
    for core in range(2):
        for j in range(4):
            columns = pl.ds((core * 4 + j) * half, half)
            pre = dot_nn(values, flat(crossed[core, :, j])) + bias_up[:, columns]
            share = 0.5 + 0.5 * erf_of(pre * ROOT_HALF)
            hidden[:, columns] = (pre * share).astype(BF)
            slope[:, columns] = (share + pre * jnp.exp(-0.5 * pre * pre) * ROOT_TWO_PI).astype(BF)


def forward_up(place, spot, normed, bias_up, unit):
    parts = unit.parts()
    rows, width = normed.shape
    group = (width // place.n_dp, width // 2)
    return pl.pallas_call(
        partial(forward_up_kernel, unit.turned, unit.chunks),
        in_specs=in_smem(1) + whole_vmem(2 + len(parts)),
        out_specs=whole_vmem(4),
        out_shape=[jax.ShapeDtypeStruct((rows, 4 * width), BF)] * 2
        + [jax.ShapeDtypeStruct((2, place.n_dp, 4) + group, BF)] * 2,
        compiler_params=kernel_params(8),
        cost_estimate=pl.CostEstimate(flops=0, bytes_accessed=0, transcendentals=0),
    )(spot, normed, bias_up, *parts)


def forward_down_kernel(images, branch, spot, middle, hidden, vectors, split, output):
    keep = keep_factor(spot, images, branch)
    ahead = hidden[...]
    half = middle.shape[1] // 2
    for core in range(2):
        columns = pl.ds(core * half, half)
        added = dot_nn(ahead, flat(split[core])) + vectors[BIAS_DOWN : BIAS_DOWN + 1, columns]
        output[:, columns] = middle[:, columns] + keep * added


def forward_down(place, spot, branch, middle, hidden, vectors, split):
    return pl.pallas_call(
        partial(forward_down_kernel, place.n_seq, branch),
        in_specs=in_smem(1) + whole_vmem(4),
        out_specs=whole_vmem(1)[0],
        out_shape=jax.ShapeDtypeStruct(middle.shape, F32),
        compiler_params=kernel_params(8),
        cost_estimate=pl.CostEstimate(flops=0, bytes_accessed=0, transcendentals=0),
    )(spot, middle, hidden, vectors, split)


def backward_feed_kernel(images, branch, spot, grad, slope, split, grad_down_t, grad_up, sum_down, sum_up):
    keep = keep_factor(spot, images, branch)
    down = (keep * grad[...]).astype(BF)
    grad_down_t[...] = down.T
    sum_down[...] = jnp.sum(down.astype(F32), axis=0, keepdims=True)
    half = grad.shape[1] // 2
    for row in range(split.shape[1]):
        columns = pl.ds(row * half, half)
        ahead = dot_nt(down[:, :half], flat(split[0, row])) + dot_nt(down[:, half:], flat(split[1, row]))
        up = (ahead * slope[:, columns].astype(F32)).astype(BF)
        grad_up[:, columns] = up
        sum_up[:, columns] = jnp.sum(up.astype(F32), axis=0, keepdims=True)


def backward_feed(place, spot, branch, grad, slope, split):
    rows, width = grad.shape
    shapes = [
        jax.ShapeDtypeStruct((width, rows), BF),
        jax.ShapeDtypeStruct((rows, 4 * width), BF),
        jax.ShapeDtypeStruct((1, width), F32),
        jax.ShapeDtypeStruct((1, 4 * width), F32),
    ]
    return pl.pallas_call(
        partial(backward_feed_kernel, place.n_seq, branch),
        in_specs=in_smem(1) + whole_vmem(3),
        out_specs=whole_vmem(len(shapes)),
        out_shape=shapes,
        compiler_params=kernel_params(8),
        cost_estimate=pl.CostEstimate(flops=0, bytes_accessed=0, transcendentals=0),
    )(spot, grad, slope, split)


def forward_up_back_kernel(turned, chunks, images, branch, spot, normed, bias_up, grad, *refs):
    parts, refs = refs[: 2 * len(chunks)], refs[2 * len(chunks) :]
    hidden, crossed, split, backs, slope = refs[0], refs[1], refs[2], refs[3:7], refs[7]
    forward_up_kernel(turned, chunks, spot, normed, bias_up, *parts, hidden, slope, crossed, split)
    backward_feed_kernel(images, branch, spot, grad, slope, split, *backs)


def forward_up_back(place, spot, branch, normed, bias_up, unit, grad):
    parts = unit.parts()
    rows, width = normed.shape
    group = (width // place.n_dp, width // 2)
    shapes = [jax.ShapeDtypeStruct((rows, 4 * width), BF)]
    shapes += [jax.ShapeDtypeStruct((2, place.n_dp, 4) + group, BF)] * 2
    shapes += [
        jax.ShapeDtypeStruct((width, rows), BF),
        jax.ShapeDtypeStruct((rows, 4 * width), BF),
        jax.ShapeDtypeStruct((1, width), F32),
        jax.ShapeDtypeStruct((1, 4 * width), F32),
    ]
    return pl.pallas_call(
        partial(forward_up_back_kernel, unit.turned, unit.chunks, place.n_seq, branch),
        in_specs=in_smem(1) + whole_vmem(3 + len(parts)),
        out_specs=whole_vmem(len(shapes)),
        out_shape=shapes,
        scratch_shapes=[pltpu.VMEM((rows, 4 * width), BF)],
        compiler_params=kernel_params(12),
    )(spot, normed, bias_up, grad, *parts)


def backward_middle_kernel(images, branch, spot, grad, grad_up, middle, vectors, crossed, *refs):
    keep = keep_factor(spot, images, branch)
    grad_middle, grad_proj, sum_proj, grad_gain, grad_shift = refs
    hat, scale = moments(middle[...])
    half = grad.shape[1] // 2
    total = jnp.zeros(grad.shape, F32)
    for core in range(2):
        for j in range(4):
            total += dot_nt(grad_up[:, pl.ds((core * 4 + j) * half, half)], flat(crossed[core, :, j]))
    grad_gain[...] = jnp.sum(total * hat, axis=0, keepdims=True)
    grad_shift[...] = jnp.sum(total, axis=0, keepdims=True)
    after = grad[...] + norm_back(hat, scale, vectors[GAIN_TWO : GAIN_TWO + 1], total)
    grad_middle[...] = after
    proj = (keep * after).astype(BF)
    grad_proj[...] = proj
    sum_proj[...] = jnp.sum(proj.astype(F32), axis=0, keepdims=True)


def backward_middle(place, spot, branch, grad, grad_up, middle, vectors, crossed):
    rows, width = grad.shape
    shapes = [
        jax.ShapeDtypeStruct((rows, width), F32),
        jax.ShapeDtypeStruct((rows, width), BF),
    ] + [jax.ShapeDtypeStruct((1, width), F32)] * 3
    return pl.pallas_call(
        partial(backward_middle_kernel, place.n_seq, branch),
        in_specs=in_smem(1) + whole_vmem(5),
        out_specs=whole_vmem(len(shapes)),
        out_shape=shapes,
        compiler_params=kernel_params(10),
        cost_estimate=pl.CostEstimate(flops=0, bytes_accessed=0, transcendentals=0),
    )(spot, grad, grad_up, middle, vectors, crossed)


def backward_feed_middle_kernel(images, branches, spot, grad, slope, split, middle, vectors, crossed, *refs):
    backward_feed_kernel(images, branches[1], spot, grad, slope, split, *refs[:4])
    backward_middle_kernel(images, branches[0], spot, grad, refs[1], middle, vectors, crossed, *refs[4:])


def backward_feed_middle(place, spot, branches, grad, slope, split, middle, vectors, crossed):
    rows, width = grad.shape
    shapes = [
        jax.ShapeDtypeStruct((width, rows), BF),
        jax.ShapeDtypeStruct((rows, 4 * width), BF),
        jax.ShapeDtypeStruct((1, width), F32),
        jax.ShapeDtypeStruct((1, 4 * width), F32),
        jax.ShapeDtypeStruct((rows, width), F32),
        jax.ShapeDtypeStruct((rows, width), BF),
    ] + [jax.ShapeDtypeStruct((1, width), F32)] * 3
    return pl.pallas_call(
        partial(backward_feed_middle_kernel, place.n_seq, branches),
        in_specs=in_smem(1) + whole_vmem(6),
        out_specs=whole_vmem(len(shapes)),
        out_shape=shapes,
        compiler_params=kernel_params(12),
    )(spot, grad, slope, split, middle, vectors, crossed)


def backward_attention_kernel(special_count, spot, grad_middle, grad_proj, mixed, stream, vectors, *refs):
    blocked = key_block(spot, stream.shape[0], special_count)
    others, (crossed, split), refs = refs[:5], refs[5:7], refs[7:]
    grad_stream, grad_mixed, sums, ahead = refs
    sum_proj, gain_two, shift_two, sum_down, sum_up = others
    hat, scale = moments(stream[...])
    width = stream.shape[1]
    half = width // 2
    proj = grad_proj[...]
    ahead[...] = (
        dot_nt(proj[:, :half], flat(split[0, :, 1])) + dot_nt(proj[:, half:], flat(split[1, :, 1]))
    ).astype(BF)
    lane = lax.broadcasted_iota(jnp.int32, (1, 2 * HD), 1)
    for pair in range(width // (2 * HD)):
        queries, keys, values = (
            mixed[:, pl.ds(j * width + pair * 2 * HD, 2 * HD)] for j in range(3)
        )
        grads = ahead[:, pl.ds(pair * 2 * HD, 2 * HD)]
        found = []
        for side in range(2):
            mine = ((lane < HD) if side == 0 else (lane >= HD)).astype(F32).astype(BF)
            probs = head_probs(queries * (mine * 0.125), keys, blocked)
            grad_probs = dot_nt(grads * mine, values)
            inner = jnp.sum(probs * grad_probs, axis=1, keepdims=True)
            grad_scores = (probs * (grad_probs - inner)).astype(BF)
            found.append(
                (
                    dot_nn(grad_scores, keys) * 0.125,
                    dot_tn(grad_scores, queries) * 0.125,
                    dot_tn(probs.astype(BF), grads),
                )
            )
        for j in range(3):
            grad_mixed[:, pl.ds(j * width + pair * 2 * HD, 2 * HD)] = jnp.where(
                lane < HD, found[0][j], found[1][j]
            ).astype(BF)
    total = jnp.zeros(stream.shape, F32)
    for core in range(2):
        for j in range(3):
            weight = crossed[core, :, j] if j < 2 else split[core, :, 0]
            total += dot_nt(grad_mixed[:, pl.ds(j * width + core * half, half)], flat(weight))

    def put(row, values):
        sums[row : row + 1, :] = values

    put(GAIN_ONE, jnp.sum(total * hat, axis=0, keepdims=True))
    put(SHIFT_ONE, jnp.sum(total, axis=0, keepdims=True))
    put(BIAS_QUERY, jnp.sum(grad_mixed[:, :width].astype(F32), axis=0, keepdims=True))
    put(BIAS_VALUE, jnp.sum(grad_mixed[:, 2 * width :].astype(F32), axis=0, keepdims=True))
    put(BIAS_PROJ, sum_proj[...])
    put(GAIN_TWO, gain_two[...])
    put(SHIFT_TWO, shift_two[...])
    put(BIAS_DOWN, sum_down[...])
    for j in range(4):
        put(BIAS_DOWN + 1 + j, sum_up[:, j * width : (j + 1) * width])
    sums[BIAS_DOWN + 5 :, :] = jnp.zeros((sums.shape[0] - BIAS_DOWN - 5, width), F32)
    grad_stream[...] = grad_middle[...] + norm_back(hat, scale, vectors[GAIN_ONE : GAIN_ONE + 1], total)


def backward_attention(spot, special_count, grad_middle, grad_proj, mixed, stream, vectors, others, crossed, split):
    rows, width = stream.shape
    shapes = [
        jax.ShapeDtypeStruct((rows, width), F32),
        jax.ShapeDtypeStruct((rows, 3 * width), BF),
        jax.ShapeDtypeStruct((16, width), F32),
    ]
    return pl.pallas_call(
        partial(backward_attention_kernel, special_count),
        in_specs=in_smem(1) + whole_vmem(5 + 5 + 2),
        out_specs=whole_vmem(len(shapes)),
        out_shape=shapes,
        scratch_shapes=[pltpu.VMEM((rows, width), BF)],
        compiler_params=kernel_params(12),
        cost_estimate=pl.CostEstimate(flops=0, bytes_accessed=0, transcendentals=0),
    )(spot, grad_middle, grad_proj, mixed, stream, vectors, *others, crossed, split)


def row_of(spot, step, far_x, steps):
    return 2 * lax.rem(spot[0] - step + steps, steps) + lax.rem(spot[1] + far_x, 2)


def feed_group(spot, core, part, far_y, at_z, normed_t, grad_up, grad_down_t, hidden, spare):
    count, wide, rows, half = spare.shape
    column = 2 * lax.rem(spot[2] + far_y, 2) + core
    if part == 0:
        left = normed_t[...] if at_z is None else normed_t[pl.ds(pl.multiple_of(at_z * 2 * rows, 2 * rows), 2 * rows), :]
        for j in range(wide):
            at = pl.multiple_of((column * wide + j) * half, half)
            out = dot_nn(left, grad_up[:, pl.ds(at, half)])
            spare[:, j] = out.reshape(count, rows, half).astype(BF)
    else:
        at = pl.multiple_of(column * wide * rows, wide * rows)
        left = grad_down_t[pl.ds(at, wide * rows), :]
        for row in range(count):
            columns = row * half if at_z is None else pl.multiple_of((at_z * 2 + row) * half, half)
            out = dot_nn(left, hidden[:, pl.ds(columns, half)])
            spare[row] = out.reshape(wide, rows, half).astype(BF)


def attention_group(spot, core, part, far_y, at_z, normed_t, grad_mixed, attended_t, grad_proj, spare):
    count, _, rows, half = spare.shape
    column = 2 * lax.rem(spot[2] + far_y, 2) + core
    if part == 0:
        out = dot_nn(normed_t[...], grad_mixed[column, :, :half])
    else:
        out = dot_nn(normed_t[...], grad_mixed[column, :, half:]) + dot_nn(
            attended_t[...], grad_proj[column]
        )
    spare[:, 0] = out.reshape(count, rows, half).astype(BF)


def each_group(fill, steps, ring, spot, core, operands, spare):
    wide = spare.shape[1]
    at_z = lax.rem(spot[0] - steps[0] + ring, ring) if len(steps) == 1 else None
    for part in range(2):
        for far_y in range(2):
            fill(spot, core, part, far_y, at_z, *operands, spare)
            for index, step in enumerate(steps):
                for far_x in range(2):
                    row = row_of(spot, step, far_x, ring) if at_z is None else lax.rem(spot[1] + far_x, 2)
                    for j in range(wide):
                        yield index, part, far_y, far_x, j, spare[row, j]


def place_in(part, far_y, far_x, j, wide):
    return (far_x * 2 + far_y) * wide + j if part == 0 else (4 + far_y * 2 + far_x) * wide + j


def sent_kernel(fill, steps, ring, spot, *refs):
    operands, out, spare = refs[:4], refs[4], refs[5]
    for index, part, far_y, far_x, j, block in each_group(fill, steps, ring, spot, 1 - spot[3], operands, spare):
        out[index, place_in(part, far_y, far_x, j, spare.shape[1])] = block


def kept_kernel(fill, steps, ring, spot, *refs):
    operands, got, outs, spare = refs[:4], refs[4], refs[5:-1], refs[-1]
    wide = spare.shape[1]
    for index, part, far_y, far_x, j, block in each_group(fill, steps, ring, spot, spot[3], operands, spare):
        total = block.astype(F32) + got[index, place_in(part, far_y, far_x, j, wide)].astype(F32)
        across, aside, stays = outs[3 * index : 3 * index + 3]
        if part == 0:
            at = far_y * wide + j
            target = across if far_x else stays
        else:
            at = far_x * wide + j
            target = aside if far_y else stays
            at = at if far_y else 2 * wide + at
        target[at] = total.astype(BF)


def spare_shape(place, steps, wide, rows, half):
    return pltpu.VMEM((2 if len(steps) == 1 else place.n_dp, wide, rows, half), BF)


def sent_part(place, spot, fill, wide, steps, operands):
    rows, half = (operands[0].shape[0] // place.n_dp, operands[0].shape[0] // 2)
    return pl.pallas_call(
        partial(sent_kernel, fill, steps, place.nz),
        in_specs=in_smem(1) + whole_vmem(4),
        out_specs=whole_vmem(1)[0],
        out_shape=jax.ShapeDtypeStruct((len(steps), 8 * wide, rows, half), BF),
        scratch_shapes=[spare_shape(place, steps, wide, rows, half)],
        compiler_params=kernel_params(10),
        cost_estimate=pl.CostEstimate(flops=0, bytes_accessed=0, transcendentals=0),
    )(spot, *operands)


def kept_part(place, spot, fill, wide, steps, operands, got):
    rows, half = (operands[0].shape[0] // place.n_dp, operands[0].shape[0] // 2)
    shapes = [
        jax.ShapeDtypeStruct((size * wide, rows, half), BF) for _ in steps for size in (2, 2, 4)
    ]
    outs = pl.pallas_call(
        partial(kept_kernel, fill, steps, place.nz),
        in_specs=in_smem(1) + whole_vmem(5),
        out_specs=whole_vmem(len(shapes)),
        out_shape=shapes,
        scratch_shapes=[spare_shape(place, steps, wide, rows, half)],
        compiler_params=kernel_params(10),
        cost_estimate=pl.CostEstimate(flops=0, bytes_accessed=0, transcendentals=0),
    )(spot, *operands, got)
    return {step: list(outs[3 * i : 3 * i + 3]) for i, step in enumerate(steps)}


def ring_kernel(stays, across, aside, *refs):
    out = refs[-1]
    count = across.shape[0]
    for at in range(2 * count):
        side = across[at] if at < count else aside[at - count]
        total = stays[at].astype(F32) + side.astype(F32)
        if len(refs) == 2:
            total = total + refs[0][at].astype(F32)
        out[at] = total.astype(BF)


def ring_block(stays, across, aside, running):
    operands = [stays, across, aside] + ([] if running is None else [running])
    return pl.pallas_call(
        ring_kernel,
        in_specs=whole_vmem(len(operands)),
        out_specs=whole_vmem(1)[0],
        out_shape=jax.ShapeDtypeStruct(stays.shape, BF),
        compiler_params=kernel_params(4),
        cost_estimate=pl.CostEstimate(flops=0, bytes_accessed=0, transcendentals=0),
    )(*operands)


def fence(trees):
    flat = [list(tree.values()) if isinstance(tree, dict) else tree for tree in trees]
    flat = lax.optimization_barrier(flat)
    return [
        dict(zip(tree, values)) if isinstance(tree, dict) else values
        for tree, values in zip(trees, flat)
    ]


def pick(which, low, high):
    return jnp.where(which == 0, low, high)


def attention_groups(place, qkv, proj):
    half = proj.shape[1] // 2

    def of(core):
        parts = [qkv[:, (2 * j + core) * half : (2 * j + core + 1) * half] for j in range(3)]
        return jnp.stack(parts + [proj[:, core * half : (core + 1) * half]])

    return pick(place.core, of(0), of(1))


def feed_groups(place, up, down):
    rows, half = up.shape[0], down.shape[1] // 2

    def of(core):
        parts = [up[:, (core * 4 + j) * half : (core * 4 + j + 1) * half] for j in range(4)]
        return jnp.concatenate(
            [jnp.stack(parts), down[:, core * half : (core + 1) * half].reshape(4, rows, half)]
        )

    return pick(place.core, of(0), of(1))


class Gathered:
    def __init__(self, place, own, extra, turned, chunks):
        groups, rows, half = own.shape
        self.turned = turned
        self.chunks = chunks
        self.first = jnp.concatenate([own[: groups // 2].reshape(-1, half)] + extra)
        self.wide = self.first.shape[0]
        self.mine = pick(
            place.y,
            own[groups // 2 : groups // 2 + groups // 4],
            own[groups // 2 + groups // 4 :],
        ).reshape(-1, half)
        self.blocks = []
        self.across = {}
        self.aside = {}
        self.whole = []
        self.mate = []
        if turned:
            self.begin([])

    def begin(self, crossed):
        self.blocks.append(jnp.concatenate([self.first, self.mine] + crossed))

    def over_x(self, step):
        return self.blocks[step] if self.turned else self.blocks[step][: self.wide]

    def over_y(self, step):
        tails = [self.blocks[step][self.wide :]]
        if self.turned:
            tails.append(self.across[step][self.wide :])
        return tails

    def chunk(self, which, across, aside):
        return jnp.concatenate(
            [
                piece
                for step in self.chunks[which]
                for piece in (self.blocks[step], across.get(step), aside.get(step))
            ]
        )

    def parts(self):
        return self.whole + self.mate


class Reduced:
    def __init__(self, place):
        self.place = place
        self.operands = None
        self.kept = {}
        self.sides = {}
        self.running = None
        self.last = None

    def block(self, step):
        return ring_block(self.kept[step][2], *self.sides[step], self.running)


def pack_vectors(vectors, bias_up, half, rows):
    layers, part = vectors[0].shape
    packed = jnp.concatenate([jnp.stack(vectors, axis=1), bias_up.reshape(layers, -1, part)], axis=1)
    return jnp.pad(packed, ((0, 0), (0, rows - packed.shape[1]), (0, half - part)))


def image_kernel(images, spot, before, patches, after, specials, out, window):
    halo, count = before.shape[0], patches.shape[0]
    begin, length = image_frame(spot, images, count, halo)
    window[:halo] = before[...]
    window[halo : halo + count] = patches[...]
    window[halo + count : 2 * halo + count] = after[...]
    spare = window.shape[0] - 2 * halo - count
    window[2 * halo + count :] = jnp.zeros((spare, window.shape[1]), F32)
    inside = lax.broadcasted_iota(jnp.int32, (MOST, 1), 0) < length
    turned = pltpu.roll(window[...], lax.rem(window.shape[0] - begin, window.shape[0]), 0)
    out[:MOST] = jnp.where(inside, turned[:MOST], 0.0)
    last = out.shape[0] - MOST
    out[MOST:] = jnp.zeros((last, out.shape[1]), F32)
    out[MOST : MOST + specials.shape[0]] = specials[...]


def take_image(place, spot, patches, specials, halo, rows):
    count, width = patches.shape
    before = shift_seq(place, patches[count - halo :], 1)
    after = shift_seq(place, patches[:halo], -1)

    def build(before, patches, after, specials):
        return pl.pallas_call(
            partial(image_kernel, place.n_seq),
            in_specs=in_smem(1) + whole_vmem(4),
            out_specs=whole_vmem(1)[0],
            out_shape=jax.ShapeDtypeStruct((rows, width), F32),
            scratch_shapes=[pltpu.VMEM((MOST + 2 * halo, width), F32)],
            compiler_params=kernel_params(6),
        cost_estimate=pl.CostEstimate(flops=0, bytes_accessed=0, transcendentals=0),
        )(spot, before, patches, after, specials)

    return (before, patches, after, specials), build


def block_kernel(images, spot, *refs):
    streams, (before, after), owns, window = refs[:2], refs[2:4], refs[4:8], refs[8]
    for at, stream in enumerate(streams):
        own, specials = owns[2 * at : 2 * at + 2]
        halo, count = before.shape[0] // 2, own.shape[0]
        begin, length = image_frame(spot, images, count, halo)
        window[MOST:] = jnp.zeros((window.shape[0] - MOST, window.shape[1]), F32)
        inside = lax.broadcasted_iota(jnp.int32, (MOST, 1), 0) < length
        window[:MOST] = jnp.where(inside, stream[:MOST], 0.0)
        window[...] = pltpu.roll(window[...], begin, 0)
        before[at * halo : (at + 1) * halo] = window[:halo]
        own[...] = window[halo : halo + count]
        after[at * halo : (at + 1) * halo] = window[halo + count : 2 * halo + count]
        specials[...] = stream[MOST : MOST + specials.shape[0]]


def give_images(place, spot, streams, halo, count, special_count):
    width = streams[0].shape[1]
    return pl.pallas_call(
        partial(block_kernel, place.n_seq),
        in_specs=in_smem(1) + whole_vmem(2),
        out_specs=whole_vmem(6),
        out_shape=[
            jax.ShapeDtypeStruct((size, width), F32)
            for size in (2 * halo, 2 * halo, count, special_count, count, special_count)
        ],
        scratch_shapes=[pltpu.VMEM((MOST + 2 * halo, width), F32)],
        compiler_params=kernel_params(6),
        cost_estimate=pl.CostEstimate(flops=0, bytes_accessed=0, transcendentals=0),
    )(spot, *streams)


def finish_attention_kernel(*refs):
    inputs, (out_mixed, out_proj) = refs[:-2], refs[-2:]
    for layer in range(LAYERS):
        last, aside, across = inputs[3 * layer : 3 * layer + 3]
        one = last[0].astype(F32) + aside[0].astype(F32)
        two = last[2].astype(F32) + across[0].astype(F32)
        cut = one.shape[1] // 2
        out_mixed[layer] = jnp.concatenate([one, two[:, :cut]], axis=1)
        out_proj[layer] = two[:, cut:]


def finish_attention(parts, rows, width):
    flat_parts = [array for layer in parts for array in layer]
    return pl.pallas_call(
        finish_attention_kernel,
        in_specs=whole_vmem(len(flat_parts)),
        out_specs=whole_vmem(2),
        out_shape=[
            jax.ShapeDtypeStruct((LAYERS, rows, columns), F32) for columns in (3 * width // 4, width // 4)
        ],
        compiler_params=kernel_params(6),
    )(*flat_parts)


def finish_kernel(spot, *refs):
    inputs, refs = refs[: 3 * LAYERS], refs[3 * LAYERS :]
    sums, (own_one, own_two, from_before, from_after), refs = refs[:4], refs[4:8], refs[8:]
    (out_up, out_down, image_one, image_two), out_rows = refs[:4], refs[4:]
    halo = from_before.shape[0] // 2
    for at, (own, image) in enumerate(((own_one, image_one), (own_two, image_two))):
        count = own.shape[0]
        image[:halo] = own[:halo] + from_before[at * halo : (at + 1) * halo]
        image[halo : count - halo] = own[halo : count - halo]
        image[count - halo :] = own[count - halo :] + from_after[at * halo : (at + 1) * halo]
    total = sums[0][...]
    for other in sums[1:]:
        total = total + other[...]
    place_dp = 2 * spot[0] + spot[1]
    each, width = total.shape[0] // LAYERS, total.shape[1]
    part = out_rows[0].shape[1]
    turned = pltpu.roll(total, lax.rem(width - place_dp * part, width), 1)
    more = VECTOR_PIECES - BIAS_DOWN - 1
    row_ids = lax.broadcasted_iota(jnp.int32, total.shape, 0)
    half_turned = pltpu.roll(total, lax.rem(width - lax.rem(place_dp * more * part, width), width), 1)
    for layer in range(LAYERS):
        for row in range(BIAS_DOWN + 1):
            at = layer * each + row
            out_rows[row][layer : layer + 1, :] = turned[at : at + 1, :part]
        at = layer * each + BIAS_DOWN + 1 + place_dp * more * part // width
        row = jnp.sum(jnp.where(row_ids == at, half_turned, 0.0), axis=0, keepdims=True)
        out_rows[-1][layer : layer + 1, :] = row[:, : more * part]
        last, aside, across = inputs[3 * layer : 3 * layer + 3]
        rows, half = last.shape[1:]
        for j in range(2):
            out_up[layer, :, j * half : (j + 1) * half] = last[j].astype(F32) + aside[j].astype(F32)
            out_down[layer, j * rows : (j + 1) * rows] = last[4 + j].astype(F32) + across[j].astype(F32)


def finish(spot, parts, sums, images, rows, width):
    more = VECTOR_PIECES - BIAS_DOWN - 1
    shapes = [
        jax.ShapeDtypeStruct((LAYERS, rows, width), F32),
        jax.ShapeDtypeStruct((LAYERS, width // 4, 4 * rows), F32),
    ]
    shapes += [jax.ShapeDtypeStruct(images[0].shape, F32)] * 2
    shapes += [jax.ShapeDtypeStruct((LAYERS, rows), F32)] * (BIAS_DOWN + 1)
    shapes += [jax.ShapeDtypeStruct((LAYERS, more * rows), F32)]
    flat_parts = [array for layer in parts for array in layer] + sums + images
    return pl.pallas_call(
        finish_kernel,
        in_specs=in_smem(1) + whole_vmem(len(flat_parts)),
        out_specs=whole_vmem(len(shapes)),
        out_shape=shapes,
        compiler_params=kernel_params(10),
    )(spot, *flat_parts)


def local_walked(
    place,
    patches,
    specials,
    lengths,
    keep_mask,
    norm1_gain,
    norm1_bias,
    qkv_weight,
    query_bias,
    value_bias,
    proj_weight,
    proj_bias,
    norm2_gain,
    norm2_bias,
    fc1_weight,
    fc1_bias,
    fc2_weight,
    fc2_bias,
    cot_patches,
    cot_specials,
):
    count, width = patches.shape
    special_count = specials.shape[0]
    images = lengths.shape[1]
    halo = (MOST - count) * (images // 2)
    rows = -(-(MOST + special_count) // 16) * 16
    nz = place.nz
    pairs = ((0, 1), (2, 3))
    part_rows = proj_weight.shape[1]
    spot = jnp.stack([place.z, place.x, place.y, place.core, place.seq]).astype(jnp.int32)
    spot = jnp.concatenate([spot, lengths.reshape(-1), keep_mask.reshape(-1)])

    shards = (norm1_gain, norm1_bias, query_bias, value_bias, proj_bias, norm2_gain, norm2_bias, fc2_bias)

    extras = pack_vectors(list(shards), fc1_bias, width // 2, EXTRA_ROWS)

    def attention_unit(layer, qkv, proj, extra):
        return Gathered(place, attention_groups(place, qkv, proj), [extra], layer == 0, pairs)

    units = [attention_unit(0, qkv_weight[0], proj_weight[0], extras[0])]
    image, build = take_image(place, spot, patches, specials, halo, rows)
    inputs = {
        "weights": (fc1_weight[0], fc2_weight[0], qkv_weight[1], proj_weight[1], extras[1], fc1_weight[1], fc2_weight[1]),
        "cots": (cot_patches, cot_specials),
    }
    vectors, bias_up = ([None] * LAYERS, [None] * LAYERS)
    streams = [None] * (LAYERS + 1)
    middles, normed_one_ts, normed_two_ts, mixeds, attended_ts, hiddens, slopes = (
        [None] * LAYERS for _ in range(7)
    )
    weights = [None] * (2 * LAYERS)
    unit_count = 2 * LAYERS
    last_slot = 3 * unit_count + 1
    at_x, at_y = ([[] for _ in range(last_slot + 2)] for _ in range(2))
    for which in range(unit_count):
        for step in range(nz):
            slot = 3 * which + step
            at_x[slot].append((which, step))
            at_y[slot + (which == 0)].append((which, step))
    at_core = {4: [(0, 0)], 5: [(0, 1), (1, 0)], 7: [(1, 1)], 8: [(2, 0)], 10: [(2, 1)], 11: [(3, 0)], 12: [(3, 1)], 13: [(3, 2)]}
    carried = {}
    grad = None
    for slot in range(last_slot + 1):
        new = {}
        index, step = divmod(slot, 3)
        if index < unit_count:
            new["z"] = place.ring_z(units[index].blocks[step])
        for which, at in at_x[slot]:
            new["x", which, at] = place.swap_x(units[which].over_x(at))
        for which, at in at_y[slot]:
            tails = units[which].over_y(at)
            new["y", which, at] = place.swap_seq(tails[0] if len(tails) == 1 else jnp.concatenate(tails), 2)
        for which, at in at_core.get(slot, []):
            new["core", which, at] = place.swap_seq(units[which].whole[at], 1)
        for which, at in at_y[slot]:
            for index_of, chunk in enumerate(units[which].chunks):
                if chunk[-1] == at:
                    unit = units[which]
                    across = {**unit.across, **{k[2]: v for k, v in new.items() if k[:2] == ("x", which)}}
                    aside = {**unit.aside, **{k[2]: v for k, v in new.items() if k[:2] == ("y", which)}}
                    new["chunk", which, index_of] = unit.chunk(index_of, across, aside)
        later = {1: 1, 4: 2, 8: 3}.get(slot)
        if later:
            new["later"] = place.swap_x(units[later].mine)
        if slot == 0:
            new["image"] = image
        if slot == 4:
            carried["stream"] = build(*image)
        if slot == 3 * unit_count:
            new["image"], build = take_image(place, spot, *inputs["cots"], halo, rows)
        if slot == 3 * unit_count + 1:
            grad = build(*image)
        if slot in (9, 11):
            layer = slot // 11
            new["forward"] = forward_attention(
                place, spot, 2 * layer, special_count, carried["stream"], units[2 * layer], EXTRA_ROWS
            )
        if slot == 10:
            hidden, slope, crossed, split = forward_up(place, spot, carried["normed"], bias_up[0], units[1])
            output = forward_down(place, spot, 1, carried["middle"], hidden, vectors[0], split)
            new["feed"] = (output, hidden, slope, crossed, split)
        if slot in (3, 5):
            names = [key for key in new if key[0] in ("x", "y")]
            swapped, weights_1 = fence(([new[key] for key in names], weights_1))
            new.update(zip(names, swapped))
            if slot == 3:
                unit = attention_unit(1, *weights_1[:3])
            else:
                unit = Gathered(place, feed_groups(place, *weights_1[3:]), [], False, ((0, 1), (2,), (3,)))
            new["unit"] = (unit.first, unit.mine)
        if step == 2 and index + 1 < len(units) and units[index + 1].blocks:
            carried["begin"] = units[index + 1].blocks[0]
        gate = inputs if slot in (0, 3 * unit_count - 1) else {}
        new, carried, gate = fence((new, carried, gate))
        inputs.update(gate)
        if slot == 0:
            up_0, down_0, *weights_1 = inputs.pop("weights")
            units.append(Gathered(place, feed_groups(place, up_0, down_0), [], False, pairs))
        if "unit" in new:
            unit.first, unit.mine = new["unit"]
            units.append(unit)
        if "begin" in carried:
            units[index + 1].blocks[0] = carried.pop("begin")
        if "image" in new:
            image = new["image"]
        if "later" in new:
            units[later].begin([new["later"]])
        if "z" in new:
            units[index].blocks.append(new["z"])
        for which, at in at_core.get(slot, []):
            units[which].mate.append(new["core", which, at])
        for which, at in at_x[slot]:
            units[which].across[at] = new["x", which, at]
        for which, at in at_y[slot]:
            units[which].aside[at] = new["y", which, at]
        for key in new:
            if key[0] == "chunk":
                units[key[1]].whole.append(new[key])
        if "forward" in new:
            streams[layer] = carried.pop("stream")
            middle, normed, normed_one_ts[layer], normed_two_ts[layer], mixeds[layer], _, attended_ts[layer], crossed, split, vectors[layer], bias_up[layer] = new["forward"]
            weights[2 * layer] = [crossed, split]
            middles[layer] = middle
            carried["middle"], carried["normed"] = middle, normed
        if "feed" in new:
            carried["stream"], hiddens[0], slopes[0], *weights[1] = new["feed"]
            del carried["middle"], carried["normed"]
    hiddens[1], *found_1 = forward_up_back(place, spot, 3, carried["normed"], bias_up[1], units[3], grad)
    weights[3] = found_1[:2]

    reduces = [Reduced(place) for _ in range(2 * LAYERS)]
    lasts = [None] * (2 * LAYERS)
    back = [{} for _ in range(LAYERS)]

    def feed_operands(layer):
        reduces[2 * (LAYERS - 1 - layer)].operands = (
            normed_two_ts[layer], back[layer]["up"], back[layer]["down_t"], hiddens[layer]
        )

    def middle_back(layer, grad):
        found = back[layer]
        found["middle"], found["proj"], found["sum_proj"], found["gain"], found["shift"] = backward_middle(
            place, spot, 2 * layer, grad, found["up"], middles[layer], vectors[layer], weights[2 * layer + 1][0]
        )

    def attention_back(layer):
        found = back[layer]
        others = [found[name] for name in ("sum_proj", "gain", "shift", "sum_down", "sum_up")]
        found["grad"], found["mixed"], found["sums"] = backward_attention(
            spot, special_count, found["middle"], found["proj"], mixeds[layer], streams[layer], vectors[layer], others, *weights[2 * layer]
        )

    def attention_operands(layer):
        found = back[layer]
        wide = 3 * width // 4
        cut = width // 4
        mixed = jnp.stack(
            [jnp.pad(found["mixed"][:, i * wide : (i + 1) * wide], ((0, 0), (0, cut))) for i in range(4)]
        )
        proj = jnp.stack([jnp.pad(found["proj"][:, i * cut : (i + 1) * cut], ((0, 0), (cut, 0))) for i in range(4)])
        unit = reduces[2 * (LAYERS - 1 - layer) + 1]
        unit.operands = (normed_one_ts[layer], mixed, attended_ts[layer], proj)

    fills = [(feed_group, 2), (attention_group, 1)] * LAYERS
    all_steps = (1, 2, 3, 0)
    cuts = [((1,), (2, 3, 0))] + [(all_steps,)] * (len(reduces) - 1)

    def sent_cut(which, cut):
        fill, wide = fills[which]
        return sent_part(place, spot, fill, wide, cuts[which][cut], reduces[which].operands)

    def keep_cut(which, cut, got):
        fill, wide = fills[which]
        unit = reduces[which]
        unit.kept.update(kept_part(place, spot, fill, wide, cuts[which][cut], unit.operands, got))

    found = back[1]
    found["down_t"], found["up"], found["sum_down"], found["sum_up"] = found_1[2:]
    feed_operands(1)
    sent = [sent_cut(0, 0), None]
    back[1], sent = fence((back[1], sent[:1]))
    final_slot = 3 * len(reduces)
    total = given = None
    first_last = []
    rung = []
    got = {}
    sending = {(0, 0): sent[0]}
    for slot in range(-2, final_slot + 1):
        new = {}
        work = {}
        for which, unit in enumerate(reduces):
            at = slot - 3 * which
            if 0 <= at <= 2:
                new["z", which] = place.ring_z(unit.block(at + 1))
            if at == 3:
                unit.last = unit.block(0)
                work["last", which] = unit.last
        if slot in (4, 7):
            end = reduces[0].last
            part = end.shape[0] // 4
            if slot == 4:
                new["last"] = place.swap_seq(end[part : 2 * part], 2)
            else:
                new["last"] = place.swap_x(end[3 * part :])
        for base, group in ((final_slot - 2, range(1, len(reduces) - 1)), (final_slot, [len(reduces) - 1])):
            if slot == base:
                ends = [reduces[which].last for which in group]
                parts = [end.shape[0] // 4 for end in ends]
                aside = place.swap_seq(
                    jnp.concatenate([end[part : 2 * part] for end, part in zip(ends, parts)]), 2
                )
                across = place.swap_x(jnp.concatenate([end[3 * part :] for end, part in zip(ends, parts)]))
                begins = 0
                for which, end, part in zip(group, ends, parts):
                    lasts[which] = [end, aside[begins : begins + part], across[begins : begins + part]]
                    begins += part
                if slot < final_slot:
                    new["lasts"] = [lasts[which] for which in group]
        if slot == -2:
            sending[0, 1] = sent_cut(0, 1)
            work["sending"] = sending[0, 1]
        if slot == -1:
            keep_cut(0, 0, got.pop((0, 0)))
        for which, base in ((2, 4), (3, 7)):
            if slot == base:
                keep_cut(which, 0, got.pop((which, 0)))
                for step in all_steps:
                    work["kept", which, step] = reduces[which].kept[step]
        for key, base in (((0, 0), -2), ((0, 1), -1), ((1, 0), 2), ((2, 0), 3), ((3, 0), 6)):
            if slot == base:
                new["core", key] = place.swap_seq(sending.pop(key), 1)
        if slot == -1:
            keep_cut(0, 1, new["core", (0, 1)])
            for step in cuts[0][1]:
                work["kept", 0, step] = reduces[0].kept[step]
        if slot == 2:
            keep_cut(1, 0, new["core", (1, 0)])
        for which, unit in enumerate(reduces):
            at = slot - 3 * which
            if -1 <= at <= 2:
                step = (at + 2) % nz
                new["side", which] = (
                    place.swap_x(unit.kept[step][0]),
                    place.swap_seq(unit.kept[step][1], 2),
                )
        if slot == 3:
            attention_operands(0)
            work["sending"] = sent_cut(3, 0)
        if slot == -1:
            middle_back(1, grad)
        if slot == 4:
            streams[LAYERS] = forward_down(place, spot, 3, carried["middle"], hiddens[1], vectors[1], weights[3][1])
            work["output"] = streams[LAYERS]
        if slot == 0:
            attention_back(1)
        if slot == 1:
            attention_operands(1)
            names = ("down_t", "up", "sum_down", "sum_up", "middle", "proj", "sum_proj", "gain", "shift")
            back[0] = dict(
                zip(
                    names,
                    backward_feed_middle(
                        place, spot, (0, 1), back[1]["grad"], slopes[0], weights[1][1], middles[0], vectors[0], weights[1][0]
                    ),
                )
            )
            feed_operands(0)
            work["sending"] = (sent_cut(1, 0), sent_cut(2, 0))
        if slot == 2:
            attention_back(0)
        if slot in (-1, 0):
            work["back", 1] = back[1]
        if slot in (1, 2):
            work["back", 0] = back[0]
        if slot == 3:
            total = jnp.concatenate([back[layer]["sums"] for layer in range(LAYERS)])
            new["sum"] = place.swap_seq(total, 1)
        if slot == 4:
            new["sum"] = place.swap_seq(total, 2)
        if slot == 6:
            new["sum"] = place.swap_x(total)
        if slot in (7, 9, 11):
            new["ringing"] = [place.ring_z(total if slot == 7 else rung[-1])]
        if slot == final_slot - 4:
            work["images"] = give_images(place, spot, given, halo, count, special_count)
        if slot == final_slot - 3:
            images_before, images_after, *owns = images
            new["image_down"] = shift_seq(place, images_before, -1)
        if slot == final_slot - 1:
            new["image_up"] = shift_seq(place, images_after, 1)
        pending = {}
        if slot == final_slot - 2:
            pending["after"] = images_after
        for which, unit in enumerate(reduces):
            at = slot + 1 - 3 * which
            if 0 <= at <= 2:
                step = (at + 2) % nz
                if step in unit.kept and ("kept", which, step) not in work:
                    pending["kept", which] = unit.kept[step]
        if slot == final_slot - 5:
            pending["give"] = [streams[LAYERS], back[0]["grad"]]
        for key, base in (((2, 0), 2), ((3, 0), 5)):
            if slot == base:
                pending["sending", key] = sending[key]
        for key, base in (((2, 0), 4), ((3, 0), 7)):
            if slot == base - 1 and key in got:
                pending["got", key] = got[key]
        new, work, pending = fence((new, work, pending))
        if "sending" in work:
            if slot == 1:
                sending[1, 0], sending[2, 0] = work.pop("sending")
            else:
                sending[(0, 1) if slot == -2 else (3, 0)] = work.pop("sending")
        for key in [key for key in pending if key[0] == "sending"]:
            sending[key[1]] = pending.pop(key)
        if "output" in work:
            streams[LAYERS] = work.pop("output")
        for key, value in work.items():
            if key[0] == "back":
                back[key[1]] = value
            if key[0] == "last":
                reduces[key[1]].last = value
            if key == "images":
                images = value
            if key[0] == "kept":
                reduces[key[1]].kept[key[2]] = value
        if "give" in pending:
            given = pending.pop("give")
        if "after" in pending:
            images_after = pending.pop("after")
        for key in [key for key in pending if key[0] == "got"]:
            got[key[1]] = pending.pop(key)
        for key, value in pending.items():
            reduces[key[1]].kept[(slot + 1 - 3 * key[1] + 2) % nz] = value
        for key, value in new.items():
            if key[0] == "core":
                got[key[1]] = value
            if key[0] == "z":
                reduces[key[1]].running = value
            if key[0] == "side":
                reduces[key[1]].sides[(slot - 3 * key[1] + 2) % nz] = value
        if "image_down" in new:
            image_down = new["image_down"]
        if "image_up" in new:
            sides = (new["image_up"], image_down)
        if "lasts" in new:
            lasts[1 : 1 + len(new["lasts"])] = new["lasts"]
        if "last" in new:
            first_last.append(new["last"])
            lasts[0] = [reduces[0].last] + first_last
        if "sum" in new:
            total = total + new["sum"]
        if "ringing" in new:
            rung += new["ringing"]

    wu, wd, out_patches, grad_patches, g1, s1, bq, bv, bp, g2, s2, bd, bu = finish(
        spot,
        [lasts[2], lasts[0]],
        [total] + rung,
        [owns[0], owns[2], *sides],
        part_rows,
        width,
    )
    wm, wp = finish_attention([lasts[3], lasts[1]], part_rows, width)
    wd = jnp.transpose(wd, (0, 2, 1))
    return (
        out_patches,
        owns[1],
        grad_patches,
        owns[3],
        g1,
        s1,
        wm,
        bq,
        bv,
        wp,
        bp,
        g2,
        s2,
        wu,
        bu,
        wd,
        bd,
    )


def local(*args):
    place = Place()
    if place.walked:
        return local_walked(place, *args)
    return local_plain(place, *args)


def solution(mesh):
    in_specs = (
        P(("dp", "seq"), None),
        P(("dp", "seq"), None),
        P("dp", None),
        P("dp", None, None),
        P(None, "dp"),
        P(None, "dp"),
        P(None, "dp", None),
        P(None, "dp"),
        P(None, "dp"),
        P(None, "dp", None),
        P(None, "dp"),
        P(None, "dp"),
        P(None, "dp"),
        P(None, "dp", None),
        P(None, "dp"),
        P(None, "dp", None),
        P(None, "dp"),
        P(("dp", "seq"), None),
        P(("dp", "seq"), None),
    )
    out_specs = (
        P(("dp", "seq"), None),
        P(("dp", "seq"), None),
        P(("dp", "seq"), None),
        P(("dp", "seq"), None),
        P(None, "dp"),
        P(None, "dp"),
        P(None, "dp", "seq"),
        P(None, "dp"),
        P(None, "dp"),
        P(None, "dp", "seq"),
        P(None, "dp"),
        P(None, "dp"),
        P(None, "dp"),
        P(None, "dp", "seq"),
        P(None, "dp"),
        P(None, "dp", "seq"),
        P(None, "dp"),
    )
    return jax.shard_map(local, mesh=mesh, in_specs=in_specs, out_specs=out_specs, check_vma=False)
```
